32 devices in a mesh: parts: 2 (over y), layer: 4 (over x, core), node: 4 (over z).
Axes of the slice: x: 2, y: 2, z: 4, core: 2. Of those that a mesh axis runs over, the one named last changes fastest.
Arguments:
- blocks: bfloat16 [16, 2048, 4096], P(('parts', 'layer'), 'node'), parts along dimension 0, may hold values from -6 to 6
- block_rows: int32 [16, 2048], P(('parts', 'layer'), 'node'), parts along dimension 0, may hold values from 0 to 7, as said below
- block_cols: int32 [16, 2048], P(('parts', 'layer'), 'node'), parts along dimension 0, may hold values from 0 to 31
- counts: int32 [16, 4], P(('parts', 'layer'), 'node'), parts along dimension 0, may hold values from 256 to 512, as said below
- start: float32 [16, 32, 2048], P(('parts', 'layer'), None, 'node'), parts along dimension 0, may hold values from -6 to 6
Outputs:
- joint_basis: float32 [16, 32, 2048], P(('parts', 'layer'), None, 'node'), parts along dimension 0
- scores: float32 [16, 32, 32], P(('parts', 'layer')), parts along dimension 0
The draws below stay inside these ranges and needn't reach their ends.
There are 2 independent parts, one for each index of `parts`. The reference program is written for one: setup_inputs(seed, part) draws one part's arguments, and reference() takes and returns one part's arrays. A program takes and returns all parts, laid end to end along the dimension named above; each array names one. Nothing has to cross between parts.
Inputs may be any that keep to these rules, and one draw needn't show every extreme that they name: `block_rows`: each device's 512 slots of one layer name each of its 8 block rows exactly 64 times. `counts`: in every layer one device has all 512 slots live and another exactly half of them.
All inputs are finite; a program needn't handle non-finite values.
Results may differ from the reference program's by a relative error of at most 0.0014.
The reference program's roundings to bfloat16 on the way count: a program that leaves them out, or rounds other values in their place, can miss the bound.
Values may be sent and summed in bfloat16 or wider, within the bound.
No kernel may reach another device: no remote copies, remote signals or barrier semaphores. Data moves between devices by JAX's collectives and lax.ppermute only.
A program may use at most 128 MiB of HBM per device.

```python
import jax
import jax.numpy as jnp
from jax import lax

K = 32
BLK = 64
ITERS = 2
ROWS_DEV = 512
SLOTS = 512
ALL_SLOTS = 2048
NODES = 2048
LAYERS = 8


def draw_block_rows(key, part):
    key = jax.random.fold_in(key, 1)
    shards = NODES // ROWS_DEV
    baseline = jnp.arange(SLOTS, dtype=jnp.int32) % (ROWS_DEV // BLK)
    baseline = jnp.broadcast_to(baseline, (LAYERS, shards, SLOTS))
    shuffled = jax.random.permutation(key, baseline, axis=2, independent=True)
    return shuffled.reshape(LAYERS, shards * SLOTS).astype(jnp.int32)


def draw_block_cols(key, part):
    key = jax.random.fold_in(key, 2)
    shards = NODES // ROWS_DEV
    return jax.random.randint(key, (LAYERS, shards * SLOTS), 0, NODES // BLK).astype(jnp.int32)


def draw_counts(key, part):
    key = jax.random.fold_in(key, 3)
    first_key, second_key = jax.random.split(key)
    shards = NODES // ROWS_DEV
    baseline = SLOTS - jax.random.randint(first_key, (LAYERS, shards), 0, SLOTS // 2 + 1)
    layer_keys = jax.random.split(second_key, LAYERS)
    ranking = jax.vmap(lambda single: jax.random.permutation(single, shards))(layer_keys)
    baseline = jnp.where(ranking == 0, SLOTS, baseline)
    baseline = jnp.where(ranking == 1, SLOTS // 2, baseline)
    return baseline.astype(jnp.int32)


def block_scale(stream_key, extent, cuts, least, high):
    gain = 1.0
    for axis_at, blocks in cuts:
        heights = jax.random.uniform(jax.random.fold_in(jax.random.fold_in(stream_key, 6), axis_at), (blocks,), jnp.float32, least / len(cuts), high / len(cuts))
        gain = gain * jnp.repeat(jnp.exp(heights), extent[axis_at] // blocks).reshape((-1,) + (1,) * (len(extent) - 1 - axis_at))
    return gain


def normal_values(key, dims, scale, most, cuts=(), kind=jnp.bfloat16):
    entries = jax.random.normal(key, dims, jnp.float32) * scale
    if len(cuts) > 0:
        entries = block_scale(key, dims, cuts, -0.22, 0.18) * entries
    return jnp.clip(entries, min=-most, max=most).astype(kind)


def setup_inputs(seed: int = 0, part: int = 0) -> dict:
    arg_keys = jax.random.split(jax.random.key(seed), 6)
    part_splits = jax.random.split(jax.random.fold_in(arg_keys[5], part), 6)
    blocks = normal_values(part_splits[0], (LAYERS, ALL_SLOTS, BLK * BLK), 1.0, 6.0, ((0, 4), (1, 4)))
    block_rows = draw_block_rows(jax.random.fold_in(jax.random.fold_in(arg_keys[5], part), 71), part)
    block_cols = draw_block_cols(jax.random.fold_in(jax.random.fold_in(arg_keys[5], part), 71), part)
    counts = draw_counts(jax.random.fold_in(jax.random.fold_in(arg_keys[5], part), 71), part)
    start = normal_values(part_splits[4], (LAYERS, K, NODES), 1.0, 6.0, ((0, 4), (2, 4)), jnp.float32)
    return {"blocks": blocks, "block_rows": block_rows, "block_cols": block_cols, "counts": counts, "start": start}


def apply_layer(values_f, rows_l, cols_l, counts_l, basis_b):
    shards = NODES // ROWS_DEV
    brows = ROWS_DEV // BLK
    column_table = basis_b.astype(jnp.float32).reshape(K, NODES // BLK, BLK)
    picked = jnp.take(column_table, cols_l, axis=1)
    products = jnp.einsum('ksj,sij->ski', picked, values_f, precision=lax.Precision.HIGHEST)
    live_mask = (jnp.arange(SLOTS, dtype=jnp.int32)[None, :] < counts_l[:, None]).reshape(-1)
    global_row = (jnp.arange(shards, dtype=jnp.int32)[:, None] * brows + rows_l.reshape(shards, SLOTS)).reshape(-1)
    onehot = ((global_row[:, None] == jnp.arange(shards * brows, dtype=jnp.int32)[None, :]) & live_mask[:, None]).astype(jnp.float32)
    result = jnp.einsum('ski,sb->kbi', products, onehot, precision=lax.Precision.HIGHEST)
    return result.reshape(K, NODES)

def orthonormal(matrix):
    gram_matrix = jnp.dot(matrix, matrix.T, precision=lax.Precision.HIGHEST)
    lower_factor = jnp.linalg.cholesky(gram_matrix)
    return lax.linalg.triangular_solve(lower_factor, matrix, left_side=True, lower=True)

def reference(blocks, block_rows, block_cols, counts, start):
    bases = []
    for layer_idx in range(LAYERS):
        values_f = blocks[layer_idx].astype(jnp.float32).reshape(-1, BLK, BLK)
        current = start[layer_idx]
        for step_idx in range(ITERS):
            image = apply_layer(values_f, block_rows[layer_idx], block_cols[layer_idx], counts[layer_idx], current.astype(jnp.bfloat16))
            current = orthonormal(image)
        bases.append(current)
    stacked = jnp.stack(bases).reshape(LAYERS * K, NODES)
    joint_basis = orthonormal(stacked).reshape(LAYERS, K, NODES)
    score_list = []
    for layer_idx in range(LAYERS):
        values_f = blocks[layer_idx].astype(jnp.float32).reshape(-1, BLK, BLK)
        chosen = joint_basis[layer_idx]
        image = apply_layer(values_f, block_rows[layer_idx], block_cols[layer_idx], counts[layer_idx], chosen.astype(jnp.bfloat16))
        score_list.append(jnp.dot(chosen, image.T, precision=lax.Precision.HIGHEST))
    return (joint_basis, jnp.stack(score_list))
```

```python
import functools

import jax
import jax.numpy as jnp
from jax import lax
from jax.experimental import pallas as pl
from jax.experimental.pallas import tpu as pltpu
from jax.sharding import PartitionSpec as P

BLK = 64
ROWS_DEV = 512
BROWS = ROWS_DEV // BLK
CHUNK_COLS = 8
CHUNK_LANES = CHUNK_COLS * 2 * BLK
TALL = BROWS * BLK // 2
MIB = 1024 * 1024
F32 = jnp.float32
BF16 = jnp.bfloat16
HIGHEST = lax.Precision.HIGHEST
TRANS_B = (((1,), (1,)), ((), ()))
TRANS_A = (((0,), (0,)), ((), ()))


def params(mib):
    return pltpu.CompilerParams(vmem_limit_bytes=mib * MIB)


def vmem_specs(count):
    return [pl.BlockSpec(memory_space=pltpu.VMEM)] * count


def build_kernel(key_ref, blocks_ref, hi_ref, lo_ref):
    chunks = hi_ref.shape[1]
    slots = key_ref.shape[2]
    positions = chunks * CHUNK_COLS * BROWS
    base = pl.program_id(1) * positions
    position = lax.broadcasted_iota(jnp.int32, (positions, slots), 0) + base
    onehot = jnp.where(position == key_ref[0], 1.0, 0.0).astype(BF16)

    def step(u, carry):
        cols = pl.ds(pl.multiple_of(u * 256, 256), 256)
        z = jnp.dot(onehot, blocks_ref[0, :, cols], preferred_element_type=F32)
        out_rows = pl.ds(pl.multiple_of(u * 16, 16), 16)
        for c in range(chunks * CHUNK_COLS):
            piece = z[c * 8 : c * 8 + 8]
            piece = jnp.concatenate([piece[:, :128], piece[:, 128:]], axis=0)
            hi = piece.astype(BF16)
            lo = (piece - hi.astype(F32)).astype(BF16)
            lanes = slice((c % CHUNK_COLS) * 128, (c % CHUNK_COLS) * 128 + 128)
            hi_ref[0, c // CHUNK_COLS, out_rows, lanes] = hi
            lo_ref[0, c // CHUNK_COLS, out_rows, lanes] = lo
        return carry

    lax.fori_loop(0, BLK * BLK // 256, step, 0)


def build_dense(key, blocks, chunk_total):
    layers, slots, width = blocks.shape
    per_step = min(4, chunk_total)
    dense = jax.ShapeDtypeStruct((layers, chunk_total, TALL, CHUNK_LANES), BF16)
    out_spec = pl.BlockSpec((1, per_step, TALL, CHUNK_LANES), lambda l, s: (l, s, 0, 0))
    return pl.pallas_call(
        build_kernel,
        grid=(layers, chunk_total // per_step),
        in_specs=[
            pl.BlockSpec((1, 1, slots), lambda l, s: (l, 0, 0)),
            pl.BlockSpec((1, slots, width), lambda l, s: (l, 0, 0)),
        ],
        out_specs=[out_spec, out_spec],
        out_shape=[dense, dense],
        compiler_params=params(40),
        name="build_dense",
    )(key.reshape(layers, 1, slots), blocks)


def split3(x):
    a = x.astype(BF16)
    r = x - a.astype(F32)
    b = r.astype(BF16)
    c = (r - b.astype(F32)).astype(BF16)
    return a, b, c


def apply_kernel(mode, piece_count, *refs):
    pieces = refs[:piece_count]
    refs = refs[piece_count:]
    if mode == "score":
        left_ref, refs = refs[0], refs[1:]
    hi_ref, lo_ref, out_ref = refs[:3]
    gram_ref = refs[3] if mode != "plain" else None
    basis, perm, acc = refs[-3:]
    layer, chunk = pl.program_id(0), pl.program_id(1)
    k = pieces[0].shape[1]

    @pl.when((layer == 0) & (chunk == 0))
    def _():
        at = 0
        for piece in pieces:
            basis[:, :, at : at + piece.shape[2]] = piece[...].astype(BF16)
            at += piece.shape[2]
        row = lax.broadcasted_iota(jnp.int32, (ROWS_DEV, ROWS_DEV), 0)
        col = lax.broadcasted_iota(jnp.int32, (ROWS_DEV, ROWS_DEV), 1)
        target = (row % 8) * BLK + 2 * ((row % TALL) // 8) + row // TALL
        perm[...] = jnp.where(target == col, 1.0, 0.0).astype(BF16)

    width = CHUNK_COLS * BLK
    here = basis[layer, :, pl.ds(pl.multiple_of(chunk * width, width), width)].astype(F32)
    low = lax.broadcasted_iota(jnp.int32, (k, 128), 1) < BLK
    first, second = [], []
    for q in range(width // 128):
        b = here[:, q * 128 : q * 128 + 128]
        br = pltpu.roll(b, BLK, 1)
        first += [jnp.where(low, b, 0.0), jnp.where(low, br, 0.0)]
        second += [jnp.where(low, 0.0, br), jnp.where(low, 0.0, b)]
    weights = jnp.concatenate(
        [
            jnp.concatenate(first, axis=1),
            jnp.concatenate(second, axis=1),
            jnp.zeros((128 - 2 * k, CHUNK_LANES), F32),
        ],
        axis=0,
    ).astype(BF16)
    total = lax.dot_general(hi_ref[0, 0], weights, TRANS_B, preferred_element_type=F32)
    total += lax.dot_general(lo_ref[0, 0], weights, TRANS_B, preferred_element_type=F32)

    @pl.when(chunk == 0)
    def _():
        acc[...] = total

    @pl.when(chunk > 0)
    def _():
        acc[...] += total

    @pl.when(chunk == pl.num_programs(1) - 1)
    def _():
        turned = acc[...].T
        wide = jnp.concatenate([turned[:k], turned[k : 2 * k]], axis=1)
        parts = jnp.concatenate(split3(wide), axis=0)
        moved = jnp.dot(parts, perm[...], preferred_element_type=F32)
        image = moved[:k] + moved[k : 2 * k] + moved[2 * k :]
        out_ref[0] = image
        if mode == "gram":
            gram_ref[0] = lax.dot_general(image, image, TRANS_B, precision=HIGHEST, preferred_element_type=F32)
        if mode == "score":
            gram_ref[0] = lax.dot_general(
                left_ref[0], image, TRANS_B, precision=HIGHEST, preferred_element_type=F32
            )


def apply_dense(mode, pieces, hi, lo, left=None):
    layers, chunks = hi.shape[:2]
    k = pieces[0].shape[1]
    nodes = sum(piece.shape[2] for piece in pieces)
    dense_spec = pl.BlockSpec((1, 1, TALL, CHUNK_LANES), lambda l, s: (l, s, 0, 0))
    image_spec = pl.BlockSpec((1, k, ROWS_DEV), lambda l, s: (l, 0, 0))
    small_spec = pl.BlockSpec((1, k, k), lambda l, s: (l, 0, 0))
    out_shape = [jax.ShapeDtypeStruct((layers, k, ROWS_DEV), F32)]
    out_specs = [image_spec]
    if mode != "plain":
        out_shape.append(jax.ShapeDtypeStruct((layers, k, k), F32))
        out_specs.append(small_spec)
    operands = list(pieces) + ([left] if mode == "score" else []) + [hi, lo]
    in_specs = vmem_specs(len(pieces)) + ([image_spec] if mode == "score" else []) + [dense_spec, dense_spec]
    return pl.pallas_call(
        functools.partial(apply_kernel, mode, len(pieces)),
        grid=(layers, chunks),
        in_specs=in_specs,
        out_specs=out_specs,
        out_shape=out_shape,
        scratch_shapes=[
            pltpu.VMEM((layers, k, nodes), BF16),
            pltpu.VMEM((ROWS_DEV, ROWS_DEV), BF16),
            pltpu.VMEM((TALL, 128), F32),
        ],
        compiler_params=params(40),
        name="apply_" + mode,
    )(*operands)


def eliminate(panel, tail, offset):
    k = panel.shape[0]
    row_at = lax.broadcasted_iota(jnp.int32, (k, 1), 0)
    for j in range(k):
        row = panel[j : j + 1]
        pivot = row[:, offset + j : offset + j + 1]
        column = panel[:, offset + j : offset + j + 1]
        factor = jnp.where(row_at > j, column / pivot, 0.0)
        panel = panel - factor * row
        tail = tail - factor * tail[j : j + 1]
    lane = lax.broadcasted_iota(jnp.int32, panel.shape, 1)
    sub = lax.broadcasted_iota(jnp.int32, panel.shape, 0)
    diagonal = jnp.sum(jnp.where(lane == sub + offset, panel, 0.0), axis=1, keepdims=True)
    scale = 1.0 / jnp.sqrt(diagonal)
    return panel * scale, tail * scale


def solve_kernel(piece_count, *refs):
    grams, image_ref, out_ref = refs[:piece_count], refs[piece_count], refs[piece_count + 1]
    layers, k = image_ref.shape[:2]
    lane = lax.broadcasted_iota(jnp.int32, (k, 128), 1)
    sub = lax.broadcasted_iota(jnp.int32, (k, 128), 0)
    eye = jnp.where(lane == sub, 1.0, 0.0)
    for layer in range(layers):
        values = [ref[layer] for ref in grams]
        if piece_count == 4:
            gram = (values[0] + values[2]) + (values[1] + values[3])
        else:
            gram = values[0]
        gram = jnp.concatenate([gram, jnp.zeros((k, 128 - k), F32)], axis=1)
        inverse = eliminate(gram, eye, 0)[1][:, :k]
        solved = jnp.dot(inverse, image_ref[layer], precision=HIGHEST, preferred_element_type=F32)
        out_ref[layer] = solved.astype(BF16)


def solve(grams, image):
    return pl.pallas_call(
        functools.partial(solve_kernel, len(grams)),
        in_specs=vmem_specs(len(grams) + 1),
        out_specs=pl.BlockSpec(memory_space=pltpu.VMEM),
        out_shape=jax.ShapeDtypeStruct(image.shape, BF16),
        name="solve_layers",
    )(*grams, image)


def stack_rows(refs, scratch):
    g = lax.axis_index("layer")
    rows = scratch.shape[0] // len(refs)
    for d, ref in enumerate(refs):
        at = lax.rem(g + d, len(refs)) * rows
        scratch[pl.ds(pl.multiple_of(at, rows), rows)] = ref[...].reshape(rows, ref.shape[-1])


def cross_kernel(piece_count, *refs):
    pieces, out_ref, stacked = refs[:piece_count], refs[piece_count], refs[piece_count + 1]
    stack_rows(pieces, stacked)
    own = pieces[0][...].reshape(-1, stacked.shape[1])
    out_ref[...] = lax.dot_general(
        own, stacked[...], TRANS_B, precision=HIGHEST, preferred_element_type=F32
    )


def cross(pieces):
    layers, k, width = pieces[0].shape
    rows = layers * k
    return pl.pallas_call(
        functools.partial(cross_kernel, len(pieces)),
        in_specs=vmem_specs(len(pieces)),
        out_specs=pl.BlockSpec(memory_space=pltpu.VMEM),
        out_shape=jax.ShapeDtypeStruct((rows, rows * len(pieces)), F32),
        scratch_shapes=[pltpu.VMEM((rows * len(pieces), width), F32)],
        name="cross_gram",
    )(*pieces)


def joint_kernel(piece_count, k, *refs):
    gram_refs, image_refs = refs[:piece_count], refs[piece_count : 2 * piece_count]
    out_ref, rounded_ref, work, stacked = refs[2 * piece_count :]
    stack_rows(gram_refs, work)
    stack_rows(image_refs, stacked)
    size = work.shape[0]
    steps = size // k
    lane = lax.broadcasted_iota(jnp.int32, (k, size), 1)
    sub = lax.broadcasted_iota(jnp.int32, (k, size), 0)
    lane_all = lax.broadcasted_iota(jnp.int32, (size, size), 1)
    for s in range(steps):
        lo, hi = s * k, (s + 1) * k
        here = (lane >= lo) & (lane < hi)
        panel = work[lo:hi]
        tail = jnp.where(here, jnp.where(lane == sub + lo, 1.0, 0.0), 0.0)
        panel, tail = eliminate(panel, tail, lo)
        panel = jnp.where(here, tail, panel)
        work[lo:hi] = jnp.where(lane < hi, panel, 0.0)
        if s + 1 < steps:
            ahead = jnp.where(lane >= hi, panel, 0.0)
            update = lax.dot_general(ahead, panel, TRANS_A, precision=HIGHEST, preferred_element_type=F32)
            rest = work[hi:]
            rest = jnp.where((lane_all[hi:] >= lo) & (lane_all[hi:] < hi), 0.0, rest)
            work[hi:] = rest - update[hi:]
    rows = size // piece_count
    own = work[pl.ds(pl.multiple_of(lax.axis_index("layer") * rows, rows), rows)]
    joint = jnp.dot(own, stacked[...], precision=HIGHEST, preferred_element_type=F32)
    joint = joint.reshape(out_ref.shape)
    out_ref[...] = joint
    rounded_ref[...] = joint.astype(BF16)


def joint_solve(grams, images):
    layers, k, width = images[0].shape
    size = layers * k * len(images)
    return pl.pallas_call(
        functools.partial(joint_kernel, len(images), k),
        in_specs=vmem_specs(2 * len(images)),
        out_specs=vmem_specs(2),
        out_shape=[
            jax.ShapeDtypeStruct(images[0].shape, F32),
            jax.ShapeDtypeStruct(images[0].shape, BF16),
        ],
        scratch_shapes=[pltpu.VMEM((size, size), F32), pltpu.VMEM((size, width), F32)],
        compiler_params=params(32),
        name="joint_solve",
    )(*grams, *images)


def around(x, axis, count):
    pieces = [x]
    for d in range(1, count):
        pieces.append(lax.ppermute(x, axis, [((m + d) % count, m) for m in range(count)]))
    return pieces


def add4(pieces):
    return (pieces[0] + pieces[2]) + (pieces[1] + pieces[3])


def per_device(shards, groups, blocks, block_rows, block_cols, counts, start):
    relative = shards == 4
    cols_total = shards * BROWS
    live = jnp.arange(block_rows.shape[1], dtype=jnp.int32)[None, :] < counts
    cols = block_cols
    if relative:
        cols = (cols - lax.axis_index("node") * BROWS + cols_total) % cols_total
    key = jnp.where(live, cols * BROWS + block_rows, -1)

    def gather(x):
        if relative:
            return around(x, "node", shards)
        return [lax.all_gather(x, "node", axis=2, tiled=True)]

    def total(x):
        return add4(around(x, "node", shards)) if relative else lax.psum(x, "node")

    first = gather(start.astype(BF16))
    hi, lo = build_dense(key, blocks, cols_total // CHUNK_COLS)
    image, gram = apply_dense("gram", first, hi, lo)
    grams = around(gram, "node", shards) if relative else [lax.psum(gram, "node")]
    (image,) = apply_dense("plain", gather(solve(grams, image)), hi, lo)
    images = around(image, "layer", groups)
    grams = around(total(cross(images)), "layer", groups)
    joint_basis, rounded = joint_solve(grams, images)
    _, partial = apply_dense("score", gather(rounded), hi, lo, joint_basis)
    return joint_basis, total(partial)


def solution(mesh):
    in_specs = (
        P(("parts", "layer"), "node", None),
        P(("parts", "layer"), "node"),
        P(("parts", "layer"), "node"),
        P(("parts", "layer"), "node"),
        P(("parts", "layer"), None, "node"),
    )
    out_specs = (P(("parts", "layer"), None, "node"), P(("parts", "layer"), None, None))
    return jax.shard_map(
        functools.partial(per_device, mesh.shape["node"], mesh.shape["layer"]),
        mesh=mesh,
        in_specs=in_specs,
        out_specs=out_specs,
        check_vma=False,
    )
```

```python
import functools

import jax
import jax.numpy as jnp
from jax import lax
from jax.experimental import pallas as pl
from jax.experimental.pallas import tpu as pltpu
from jax.sharding import PartitionSpec as P

BLK = 64
ROWS_DEV = 512
BROWS = ROWS_DEV // BLK
CHUNK_COLS = 8
CHUNK_LANES = CHUNK_COLS * 2 * BLK
TALL = BROWS * BLK // 2
MIB = 1024 * 1024
F32 = jnp.float32
BF16 = jnp.bfloat16
HIGHEST = lax.Precision.HIGHEST
TRANS_B = (((1,), (1,)), ((), ()))
TRANS_A = (((0,), (0,)), ((), ()))


def params(mib):
    return pltpu.CompilerParams(vmem_limit_bytes=mib * MIB)


def vmem_specs(count):
    return [pl.BlockSpec(memory_space=pltpu.VMEM)] * count


def build_kernel(key_ref, blocks_ref, hi_ref, lo_ref):
    chunks = hi_ref.shape[1]
    slots = key_ref.shape[2]
    positions = chunks * CHUNK_COLS * BROWS
    base = pl.program_id(1) * positions
    position = lax.broadcasted_iota(jnp.int32, (positions, slots), 0) + base
    onehot = jnp.where(position == key_ref[0], 1.0, 0.0).astype(BF16)

    def step(u, carry):
        cols = pl.ds(pl.multiple_of(u * 256, 256), 256)
        z = jnp.dot(onehot, blocks_ref[0, :, cols], preferred_element_type=F32)
        out_rows = pl.ds(pl.multiple_of(u * 16, 16), 16)
        for c in range(chunks * CHUNK_COLS):
            piece = z[c * 8 : c * 8 + 8]
            piece = jnp.concatenate([piece[:, :128], piece[:, 128:]], axis=0)
            hi = piece.astype(BF16)
            lo = (piece - hi.astype(F32)).astype(BF16)
            lanes = slice((c % CHUNK_COLS) * 128, (c % CHUNK_COLS) * 128 + 128)
            hi_ref[0, c // CHUNK_COLS, out_rows, lanes] = hi
            lo_ref[0, c // CHUNK_COLS, out_rows, lanes] = lo
        return carry

    lax.fori_loop(0, BLK * BLK // 256, step, 0)


def build_dense(key, blocks, chunk_total):
    layers, slots, width = blocks.shape
    per_step = min(4, chunk_total)
    dense = jax.ShapeDtypeStruct((layers, chunk_total, TALL, CHUNK_LANES), BF16)
    out_spec = pl.BlockSpec((1, per_step, TALL, CHUNK_LANES), lambda l, s: (l, s, 0, 0))
    return pl.pallas_call(
        build_kernel,
        grid=(layers, chunk_total // per_step),
        in_specs=[
            pl.BlockSpec((1, 1, slots), lambda l, s: (l, 0, 0)),
            pl.BlockSpec((1, slots, width), lambda l, s: (l, 0, 0)),
        ],
        out_specs=[out_spec, out_spec],
        out_shape=[dense, dense],
        compiler_params=params(24),
        name="build_dense",
    )(key.reshape(layers, 1, slots), blocks)


def split3(x):
    a = x.astype(BF16)
    r = x - a.astype(F32)
    b = r.astype(BF16)
    c = (r - b.astype(F32)).astype(BF16)
    return a, b, c


def apply_kernel(mode, piece_count, *refs):
    pieces = refs[:piece_count]
    refs = refs[piece_count:]
    if mode == "score":
        left_ref, refs = refs[0], refs[1:]
    hi_ref, lo_ref, out_ref = refs[:3]
    gram_ref = refs[3] if mode != "plain" else None
    basis, perm, acc = refs[-3:]
    layer, chunk = pl.program_id(0), pl.program_id(1)
    k = pieces[0].shape[1]

    @pl.when((layer == 0) & (chunk == 0))
    def _():
        at = 0
        for piece in pieces:
            basis[:, :, at : at + piece.shape[2]] = piece[...].astype(BF16)
            at += piece.shape[2]
        row = lax.broadcasted_iota(jnp.int32, (ROWS_DEV, ROWS_DEV), 0)
        col = lax.broadcasted_iota(jnp.int32, (ROWS_DEV, ROWS_DEV), 1)
        target = (row % 8) * BLK + 2 * ((row % TALL) // 8) + row // TALL
        perm[...] = jnp.where(target == col, 1.0, 0.0).astype(BF16)

    width = CHUNK_COLS * BLK
    here = basis[layer, :, pl.ds(pl.multiple_of(chunk * width, width), width)].astype(F32)
    low = lax.broadcasted_iota(jnp.int32, (k, 128), 1) < BLK
    first, second = [], []
    for q in range(width // 128):
        b = here[:, q * 128 : q * 128 + 128]
        br = pltpu.roll(b, BLK, 1)
        first += [jnp.where(low, b, 0.0), jnp.where(low, br, 0.0)]
        second += [jnp.where(low, 0.0, br), jnp.where(low, 0.0, b)]
    weights = jnp.concatenate(
        [
            jnp.concatenate(first, axis=1),
            jnp.concatenate(second, axis=1),
            jnp.zeros((128 - 2 * k, CHUNK_LANES), F32),
        ],
        axis=0,
    ).astype(BF16)
    total = lax.dot_general(hi_ref[0, 0], weights, TRANS_B, preferred_element_type=F32)
    total += lax.dot_general(lo_ref[0, 0], weights, TRANS_B, preferred_element_type=F32)

    @pl.when(chunk == 0)
    def _():
        acc[...] = total

    @pl.when(chunk > 0)
    def _():
        acc[...] += total

    @pl.when(chunk == pl.num_programs(1) - 1)
    def _():
        turned = acc[...].T
        wide = jnp.concatenate([turned[:k], turned[k : 2 * k]], axis=1)
        parts = jnp.concatenate(split3(wide), axis=0)
        moved = jnp.dot(parts, perm[...], preferred_element_type=F32)
        image = moved[:k] + moved[k : 2 * k] + moved[2 * k :]
        out_ref[0] = image
        if mode == "gram":
            gram_ref[0] = lax.dot_general(image, image, TRANS_B, precision=HIGHEST, preferred_element_type=F32)
        if mode == "score":
            gram_ref[0] = lax.dot_general(
                left_ref[0], image, TRANS_B, precision=HIGHEST, preferred_element_type=F32
            )


def apply_dense(mode, pieces, hi, lo, left=None):
    layers, chunks = hi.shape[:2]
    k = pieces[0].shape[1]
    nodes = sum(piece.shape[2] for piece in pieces)
    dense_spec = pl.BlockSpec((1, 1, TALL, CHUNK_LANES), lambda l, s: (l, s, 0, 0))
    image_spec = pl.BlockSpec((1, k, ROWS_DEV), lambda l, s: (l, 0, 0))
    small_spec = pl.BlockSpec((1, k, k), lambda l, s: (l, 0, 0))
    out_shape = [jax.ShapeDtypeStruct((layers, k, ROWS_DEV), F32)]
    out_specs = [image_spec]
    if mode != "plain":
        out_shape.append(jax.ShapeDtypeStruct((layers, k, k), F32))
        out_specs.append(small_spec)
    operands = list(pieces) + ([left] if mode == "score" else []) + [hi, lo]
    in_specs = vmem_specs(len(pieces)) + ([image_spec] if mode == "score" else []) + [dense_spec, dense_spec]
    return pl.pallas_call(
        functools.partial(apply_kernel, mode, len(pieces)),
        grid=(layers, chunks),
        in_specs=in_specs,
        out_specs=out_specs,
        out_shape=out_shape,
        scratch_shapes=[
            pltpu.VMEM((layers, k, nodes), BF16),
            pltpu.VMEM((ROWS_DEV, ROWS_DEV), BF16),
            pltpu.VMEM((TALL, 128), F32),
        ],
        compiler_params=params(12),
        name="apply_" + mode,
    )(*operands)


def eliminate(panel, tail, offset):
    k = panel.shape[0]
    row_at = lax.broadcasted_iota(jnp.int32, (k, 1), 0)
    for j in range(k):
        row = panel[j : j + 1]
        pivot = row[:, offset + j : offset + j + 1]
        column = panel[:, offset + j : offset + j + 1]
        factor = jnp.where(row_at > j, column / pivot, 0.0)
        panel = panel - factor * row
        tail = tail - factor * tail[j : j + 1]
    lane = lax.broadcasted_iota(jnp.int32, panel.shape, 1)
    sub = lax.broadcasted_iota(jnp.int32, panel.shape, 0)
    diagonal = jnp.sum(jnp.where(lane == sub + offset, panel, 0.0), axis=1, keepdims=True)
    scale = 1.0 / jnp.sqrt(diagonal)
    return panel * scale, tail * scale


def solve_kernel(piece_count, *refs):
    grams, image_ref, out_ref = refs[:piece_count], refs[piece_count], refs[piece_count + 1]
    layers, k = image_ref.shape[:2]
    lane = lax.broadcasted_iota(jnp.int32, (k, 128), 1)
    sub = lax.broadcasted_iota(jnp.int32, (k, 128), 0)
    eye = jnp.where(lane == sub, 1.0, 0.0)
    for layer in range(layers):
        values = [ref[layer] for ref in grams]
        if piece_count == 4:
            gram = (values[0] + values[2]) + (values[1] + values[3])
        else:
            gram = values[0]
        gram = jnp.concatenate([gram, jnp.zeros((k, 128 - k), F32)], axis=1)
        inverse = eliminate(gram, eye, 0)[1][:, :k]
        solved = jnp.dot(inverse, image_ref[layer], precision=HIGHEST, preferred_element_type=F32)
        out_ref[layer] = solved.astype(BF16)


def solve(grams, image):
    return pl.pallas_call(
        functools.partial(solve_kernel, len(grams)),
        in_specs=vmem_specs(len(grams) + 1),
        out_specs=pl.BlockSpec(memory_space=pltpu.VMEM),
        out_shape=jax.ShapeDtypeStruct(image.shape, BF16),
        compiler_params=params(4),
        name="solve_layers",
    )(*grams, image)


def stack_rows(refs, scratch):
    g = lax.axis_index("layer")
    rows = scratch.shape[0] // len(refs)
    for d, ref in enumerate(refs):
        at = lax.rem(g + d, len(refs)) * rows
        scratch[pl.ds(pl.multiple_of(at, rows), rows)] = ref[...].reshape(rows, ref.shape[-1])


def cross_kernel(piece_count, *refs):
    pieces, out_ref, stacked = refs[:piece_count], refs[piece_count], refs[piece_count + 1]
    stack_rows(pieces, stacked)
    own = pieces[0][...].reshape(-1, stacked.shape[1])
    out_ref[...] = lax.dot_general(
        own, stacked[...], TRANS_B, precision=HIGHEST, preferred_element_type=F32
    )


def cross(pieces):
    layers, k, width = pieces[0].shape
    rows = layers * k
    return pl.pallas_call(
        functools.partial(cross_kernel, len(pieces)),
        in_specs=vmem_specs(len(pieces)),
        out_specs=pl.BlockSpec(memory_space=pltpu.VMEM),
        out_shape=jax.ShapeDtypeStruct((rows, rows * len(pieces)), F32),
        scratch_shapes=[pltpu.VMEM((rows * len(pieces), width), F32)],
        compiler_params=params(6),
        name="cross_gram",
    )(*pieces)


def joint_kernel(piece_count, k, *refs):
    gram_refs, image_refs = refs[:piece_count], refs[piece_count : 2 * piece_count]
    out_ref, rounded_ref, work, stacked = refs[2 * piece_count :]
    stack_rows(gram_refs, work)
    stack_rows(image_refs, stacked)
    size = work.shape[0]
    steps = size // k
    lane = lax.broadcasted_iota(jnp.int32, (k, size), 1)
    sub = lax.broadcasted_iota(jnp.int32, (k, size), 0)
    lane_all = lax.broadcasted_iota(jnp.int32, (size, size), 1)
    for s in range(steps):
        lo, hi = s * k, (s + 1) * k
        here = (lane >= lo) & (lane < hi)
        panel = work[lo:hi]
        tail = jnp.where(here, jnp.where(lane == sub + lo, 1.0, 0.0), 0.0)
        panel, tail = eliminate(panel, tail, lo)
        panel = jnp.where(here, tail, panel)
        work[lo:hi] = jnp.where(lane < hi, panel, 0.0)
        if s + 1 < steps:
            ahead = jnp.where(lane >= hi, panel, 0.0)
            update = lax.dot_general(ahead, panel, TRANS_A, precision=HIGHEST, preferred_element_type=F32)
            rest = work[hi:]
            rest = jnp.where((lane_all[hi:] >= lo) & (lane_all[hi:] < hi), 0.0, rest)
            work[hi:] = rest - update[hi:]
    rows = size // piece_count
    own = work[pl.ds(pl.multiple_of(lax.axis_index("layer") * rows, rows), rows)]
    joint = jnp.dot(own, stacked[...], precision=HIGHEST, preferred_element_type=F32)
    joint = joint.reshape(out_ref.shape)
    out_ref[...] = joint
    rounded_ref[...] = joint.astype(BF16)


def joint_solve(grams, images):
    layers, k, width = images[0].shape
    size = layers * k * len(images)
    return pl.pallas_call(
        functools.partial(joint_kernel, len(images), k),
        in_specs=vmem_specs(2 * len(images)),
        out_specs=vmem_specs(2),
        out_shape=[
            jax.ShapeDtypeStruct(images[0].shape, F32),
            jax.ShapeDtypeStruct(images[0].shape, BF16),
        ],
        scratch_shapes=[pltpu.VMEM((size, size), F32), pltpu.VMEM((size, width), F32)],
        compiler_params=params(8),
        name="joint_solve",
    )(*grams, *images)


def around(x, axis, count):
    pieces = [x]
    for d in range(1, count):
        pieces.append(lax.ppermute(x, axis, [((m + d) % count, m) for m in range(count)]))
    return pieces


def add4(pieces):
    return (pieces[0] + pieces[2]) + (pieces[1] + pieces[3])


def per_device(shards, groups, blocks, block_rows, block_cols, counts, start):
    relative = shards == 4
    cols_total = shards * BROWS
    live = jnp.arange(block_rows.shape[1], dtype=jnp.int32)[None, :] < counts
    cols = block_cols
    if relative:
        cols = (cols - lax.axis_index("node") * BROWS + cols_total) % cols_total
    key = jnp.where(live, cols * BROWS + block_rows, -1)

    def gather(x):
        if relative:
            return around(x, "node", shards)
        return [lax.all_gather(x, "node", axis=2, tiled=True)]

    def total(x):
        return add4(around(x, "node", shards)) if relative else lax.psum(x, "node")

    first = gather(start.astype(BF16))
    hi, lo = build_dense(key, blocks, cols_total // CHUNK_COLS)
    image, gram = apply_dense("gram", first, hi, lo)
    grams = around(gram, "node", shards) if relative else [lax.psum(gram, "node")]
    (image,) = apply_dense("plain", gather(solve(grams, image)), hi, lo)
    images = around(image, "layer", groups)
    grams = around(total(cross(images)), "layer", groups)
    joint_basis, rounded = joint_solve(grams, images)
    _, partial = apply_dense("score", gather(rounded), hi, lo, joint_basis)
    return joint_basis, total(partial)


def solution(mesh):
    in_specs = (
        P(("parts", "layer"), "node", None),
        P(("parts", "layer"), "node"),
        P(("parts", "layer"), "node"),
        P(("parts", "layer"), "node"),
        P(("parts", "layer"), None, "node"),
    )
    out_specs = (P(("parts", "layer"), None, "node"), P(("parts", "layer"), None, None))
    return jax.shard_map(
        functools.partial(per_device, mesh.shape["node"], mesh.shape["layer"]),
        mesh=mesh,
        in_specs=in_specs,
        out_specs=out_specs,
        check_vma=False,
    )
```

```python
import functools

import jax
import jax.numpy as jnp
from jax import lax
from jax.experimental import pallas as pl
from jax.experimental.pallas import tpu as pltpu
from jax.sharding import PartitionSpec as P

BLK = 64
ROWS_DEV = 512
BROWS = ROWS_DEV // BLK
CHUNK_COLS = 8
CHUNK_LANES = CHUNK_COLS * 2 * BLK
TALL = BROWS * BLK // 2
MIB = 1024 * 1024
F32 = jnp.float32
BF16 = jnp.bfloat16
HIGHEST = lax.Precision.HIGHEST
TRANS_B = (((1,), (1,)), ((), ()))
TRANS_A = (((0,), (0,)), ((), ()))


def params(mib):
    return pltpu.CompilerParams(vmem_limit_bytes=mib * MIB)


def vmem_specs(count):
    return [pl.BlockSpec(memory_space=pltpu.VMEM)] * count


def build_kernel(key_ref, blocks_ref, hi_ref, lo_ref):
    chunks = hi_ref.shape[1]
    slots = key_ref.shape[2]
    positions = chunks * CHUNK_COLS * BROWS
    base = pl.program_id(1) * positions
    position = lax.broadcasted_iota(jnp.int32, (positions, slots), 0) + base
    onehot = jnp.where(position == key_ref[0], 1.0, 0.0).astype(BF16)

    def step(u, carry):
        cols = pl.ds(pl.multiple_of(u * 256, 256), 256)
        z = jnp.dot(onehot, blocks_ref[0, :, cols], preferred_element_type=F32)
        out_rows = pl.ds(pl.multiple_of(u * 16, 16), 16)
        for c in range(chunks * CHUNK_COLS):
            piece = z[c * 8 : c * 8 + 8]
            piece = jnp.concatenate([piece[:, :128], piece[:, 128:]], axis=0)
            hi = piece.astype(BF16)
            lo = (piece - hi.astype(F32)).astype(BF16)
            lanes = slice((c % CHUNK_COLS) * 128, (c % CHUNK_COLS) * 128 + 128)
            hi_ref[0, c // CHUNK_COLS, out_rows, lanes] = hi
            lo_ref[0, c // CHUNK_COLS, out_rows, lanes] = lo
        return carry

    lax.fori_loop(0, BLK * BLK // 256, step, 0)


def build_dense(key, blocks, chunk_total):
    layers, slots, width = blocks.shape
    per_step = min(4, chunk_total)
    dense = jax.ShapeDtypeStruct((layers, chunk_total, TALL, CHUNK_LANES), BF16)
    out_spec = pl.BlockSpec((1, per_step, TALL, CHUNK_LANES), lambda l, s: (l, s, 0, 0))
    return pl.pallas_call(
        build_kernel,
        grid=(layers, chunk_total // per_step),
        in_specs=[
            pl.BlockSpec((1, 1, slots), lambda l, s: (l, 0, 0)),
            pl.BlockSpec((1, slots, width), lambda l, s: (l, 0, 0)),
        ],
        out_specs=[out_spec, out_spec],
        out_shape=[dense, dense],
        compiler_params=params(24),
        name="build_dense",
    )(key.reshape(layers, 1, slots), blocks)


def split3(x):
    a = x.astype(BF16)
    r = x - a.astype(F32)
    b = r.astype(BF16)
    c = (r - b.astype(F32)).astype(BF16)
    return a, b, c


def spread_copies(x, ref):
    return jnp.broadcast_to(x[None, None], ref.shape)


def apply_kernel(mode, *refs):
    pieces, refs = refs[0], refs[1:]
    if mode == "score":
        left_ref, refs = refs[0], refs[1:]
    hi_ref, lo_ref, out_ref = refs[:3]
    gram_ref = refs[3] if mode != "plain" else None
    perm, acc = refs[-2:]
    layer, chunk = pl.program_id(0), pl.program_id(1)
    k = pieces.shape[2]

    @pl.when((layer == 0) & (chunk == 0))
    def _():
        row = lax.broadcasted_iota(jnp.int32, (ROWS_DEV, ROWS_DEV), 0)
        col = lax.broadcasted_iota(jnp.int32, (ROWS_DEV, ROWS_DEV), 1)
        target = (row % 8) * BLK + 2 * ((row % TALL) // 8) + row // TALL
        perm[...] = jnp.where(target == col, 1.0, 0.0).astype(BF16)

    width = CHUNK_COLS * BLK
    here = pieces[chunk, layer].astype(F32)
    low = lax.broadcasted_iota(jnp.int32, (k, 128), 1) < BLK
    first, second = [], []
    for q in range(width // 128):
        b = here[:, q * 128 : q * 128 + 128]
        br = pltpu.roll(b, BLK, 1)
        first += [jnp.where(low, b, 0.0), jnp.where(low, br, 0.0)]
        second += [jnp.where(low, 0.0, br), jnp.where(low, 0.0, b)]
    weights = jnp.concatenate(
        [
            jnp.concatenate(first, axis=1),
            jnp.concatenate(second, axis=1),
            jnp.zeros((128 - 2 * k, CHUNK_LANES), F32),
        ],
        axis=0,
    ).astype(BF16)
    total = lax.dot_general(hi_ref[0, 0], weights, TRANS_B, preferred_element_type=F32)
    total += lax.dot_general(lo_ref[0, 0], weights, TRANS_B, preferred_element_type=F32)

    @pl.when(chunk == 0)
    def _():
        acc[...] = total

    @pl.when(chunk > 0)
    def _():
        acc[...] += total

    @pl.when(chunk == pl.num_programs(1) - 1)
    def _():
        turned = acc[...].T
        wide = jnp.concatenate([turned[:k], turned[k : 2 * k]], axis=1)
        parts = jnp.concatenate(split3(wide), axis=0)
        moved = jnp.dot(parts, perm[...], preferred_element_type=F32)
        image = moved[:k] + moved[k : 2 * k] + moved[2 * k :]
        out_ref[0] = image
        if mode == "gram":
            gram_ref[...] = spread_copies(lax.dot_general(image, image, TRANS_B, precision=HIGHEST, preferred_element_type=F32), gram_ref)
        if mode == "score":
            gram_ref[...] = spread_copies(lax.dot_general(left_ref[0], image, TRANS_B, precision=HIGHEST, preferred_element_type=F32), gram_ref)


def apply_dense(mode, basis, hi, lo, left=None):
    layers, chunks = hi.shape[:2]
    k = basis.shape[2]
    dense_spec = pl.BlockSpec((1, 1, TALL, CHUNK_LANES), lambda l, s: (l, s, 0, 0))
    image_spec = pl.BlockSpec((1, k, ROWS_DEV), lambda l, s: (l, 0, 0))
    small_spec = pl.BlockSpec((chunks, 1, k, k), lambda l, s: (0, l, 0, 0))
    out_shape = [jax.ShapeDtypeStruct((layers, k, ROWS_DEV), F32)]
    out_specs = [image_spec]
    if mode != "plain":
        out_shape.append(jax.ShapeDtypeStruct((chunks, layers, k, k), F32))
        out_specs.append(small_spec)
    operands = [basis] + ([left] if mode == "score" else []) + [hi, lo]
    in_specs = vmem_specs(1) + ([image_spec] if mode == "score" else []) + [dense_spec, dense_spec]
    return pl.pallas_call(
        functools.partial(apply_kernel, mode),
        grid=(layers, chunks),
        in_specs=in_specs,
        out_specs=out_specs,
        out_shape=out_shape,
        scratch_shapes=[pltpu.VMEM((ROWS_DEV, ROWS_DEV), BF16), pltpu.VMEM((TALL, 128), F32)],
        compiler_params=params(12),
        name="apply_" + mode,
    )(*operands)


def reciprocal(x):
    r = pl.reciprocal(x, approx=True)
    r = r * (2.0 - x * r)
    return r * (2.0 - x * r)


def eliminate(rows, offset):
    k, width = rows.shape
    groups = [rows[g * 8 : g * 8 + 8] for g in range(k // 8)]
    sub = lax.broadcasted_iota(jnp.int32, (8, 128), 0)

    def spread(x, size):
        return jnp.broadcast_to(x, (8, size))

    for base in range(0, k, 4):
        active = range(base // 8, k // 8)
        home, at = base // 8, base % 8
        cols = [
            {g: spread(groups[g][:, offset + base + q : offset + base + q + 1], 128) for g in active}
            for q in range(4)
        ]
        row = [spread(groups[home][at + q : at + q + 1], width) for q in range(4)]
        cell = {}
        for q in range(4):
            for p in range(q + 1):
                cell[p, q] = spread(cols[p][home][at + q : at + q + 1], 128)
        pairs = []
        for m in (0, 2):
            a, b, c = cell[m, m], cell[m, m + 1], cell[m + 1, m + 1]
            r = reciprocal(a * c - b * b)
            i00, i01, i11 = c * r, -b * r, a * r
            f0 = {g: cols[m][g] * i00 + cols[m + 1][g] * i01 for g in active}
            f1 = {g: cols[m][g] * i01 + cols[m + 1][g] * i11 for g in active}
            if m == 0:
                e0 = [cell[0, q] * i00 + cell[1, q] * i01 for q in (2, 3)]
                e1 = [cell[0, q] * i01 + cell[1, q] * i11 for q in (2, 3)]
                for q in (2, 3):
                    for p in range(2, q + 1):
                        cell[p, q] = cell[p, q] - e0[p - 2] * cell[0, q] - e1[p - 2] * cell[1, q]
                    cols[q] = {g: cols[q][g] - f0[g] * cell[0, q] - f1[g] * cell[1, q] for g in active}
                    row[q] = (
                        row[q]
                        - jnp.tile(e0[q - 2], (1, width // 128)) * row[0]
                        - jnp.tile(e1[q - 2], (1, width // 128)) * row[1]
                    )
            f0 = {g: jnp.where(sub > base + m + 1 - 8 * g, f0[g], 0.0) for g in active}
            f1 = {g: jnp.where(sub > base + m + 1 - 8 * g, f1[g], 0.0) for g in active}
            f0[home] = jnp.where(sub == at + m + 1, b * reciprocal(a), f0[home])
            pairs.append((f0, f1))
        for g in active:
            x = groups[g]
            for m, (f0, f1) in enumerate(pairs):
                x = x - jnp.tile(f0[g], (1, width // 128)) * row[2 * m]
                x = x - jnp.tile(f1[g], (1, width // 128)) * row[2 * m + 1]
            groups[g] = x
    rows = jnp.concatenate(groups, axis=0)
    tile = offset // 128 * 128
    diagonal = diagonal_of(rows[:, tile : tile + 128], offset - tile)
    return rows * (1.0 / jnp.sqrt(diagonal))


def diagonal_of(block, offset):
    lane = lax.broadcasted_iota(jnp.int32, block.shape, 1)
    sub = lax.broadcasted_iota(jnp.int32, block.shape, 0)
    return jnp.sum(jnp.where(lane == sub + offset, block, 0.0), axis=1, keepdims=True)


def unit_scale(gram):
    lane = lax.broadcasted_iota(jnp.int32, gram.shape, 1)
    sub = lax.broadcasted_iota(jnp.int32, gram.shape, 0)
    kept = jnp.where(lane == sub, gram, 0.0)
    down = 1.0 / jnp.sqrt(jnp.sum(kept, axis=1, keepdims=True))
    across = jnp.sum(kept, axis=0, keepdims=True)
    across = 1.0 / jnp.sqrt(jnp.where(across == 0.0, 1.0, across))
    return gram * down * across, across


def gram_update(left, right):
    a, b = split3(left), split3(right)
    left = jnp.concatenate([a[0], a[0], a[1], a[1], a[0], a[2]], axis=0)
    right = jnp.concatenate([b[0], b[1], b[0], b[1], b[2], b[0]], axis=0)
    return lax.dot_general(left, right, TRANS_A, preferred_element_type=F32)


def solve_kernel(grams_ref, image_ref, out_ref):
    layers, k = image_ref.shape[:2]
    lane = lax.broadcasted_iota(jnp.int32, (k, 128), 1)
    sub = lax.broadcasted_iota(jnp.int32, (k, 128), 0)
    eye = jnp.where(lane == sub, 1.0, 0.0)
    for layer in range(layers):
        gram = sum(grams_ref[m, layer] for m in range(grams_ref.shape[0]))
        gram = jnp.concatenate([gram, jnp.zeros((k, 128 - k), F32)], axis=1)
        gram, across = unit_scale(gram)
        inverse = eliminate(jnp.concatenate([gram, eye], axis=1), 0)[:, 128:] * across
        solved = jnp.dot(inverse[:, :k], image_ref[layer], precision=HIGHEST, preferred_element_type=F32)
        for copy in range(out_ref.shape[0]):
            out_ref[copy, layer] = solved.astype(BF16)


def solve(grams, image, copies):
    return pl.pallas_call(
        solve_kernel,
        in_specs=vmem_specs(2),
        out_specs=pl.BlockSpec(memory_space=pltpu.VMEM),
        out_shape=jax.ShapeDtypeStruct((copies, *image.shape), BF16),
        compiler_params=params(6),
        name="solve_layers",
    )(grams, image)


def stack_rows(refs, scratch):
    g = lax.axis_index("layer")
    rows = scratch.shape[0] // len(refs)
    for d, ref in enumerate(refs):
        at = lax.rem(g + d, len(refs)) * rows
        scratch[pl.ds(pl.multiple_of(at, rows), rows)] = ref[...].reshape(rows, ref.shape[-1])


def cross_kernel(piece_count, *refs):
    pieces, out_ref, stacked = refs[:piece_count], refs[piece_count], refs[piece_count + 1]
    stack_rows(pieces, stacked)
    own = pieces[0][...].reshape(-1, stacked.shape[1])
    out_ref[...] = lax.dot_general(
        own, stacked[...], TRANS_B, precision=HIGHEST, preferred_element_type=F32
    )


def cross(pieces):
    layers, k, width = pieces[0].shape
    rows = layers * k
    return pl.pallas_call(
        functools.partial(cross_kernel, len(pieces)),
        in_specs=vmem_specs(len(pieces)),
        out_specs=pl.BlockSpec(memory_space=pltpu.VMEM),
        out_shape=jax.ShapeDtypeStruct((rows, rows * len(pieces)), F32),
        scratch_shapes=[pltpu.VMEM((rows * len(pieces), width), F32)],
        compiler_params=params(6),
        name="cross_gram",
    )(*pieces)


def joint_kernel(piece_count, k, *refs):
    gram_refs, image_refs = refs[:piece_count], refs[piece_count : 2 * piece_count]
    out_ref, rounded_ref, work, stacked = refs[2 * piece_count :]
    stack_rows(gram_refs, work)
    stack_rows(image_refs, stacked)
    size = work.shape[0]
    steps = size // k
    lane = lax.broadcasted_iota(jnp.int32, (k, size), 1)
    lane_128 = lax.broadcasted_iota(jnp.int32, (k, 128), 1)
    sub_128 = lax.broadcasted_iota(jnp.int32, (k, 128), 0)
    gram, across = unit_scale(work[...])
    work[...] = gram
    for s in range(steps):
        lo, hi = s * k, (s + 1) * k
        here = (lane >= lo) & (lane < hi)
        eye = jnp.where(lane_128 == sub_128 + lo % 128, 1.0, 0.0)
        panel = work[lo:hi]
        solved = eliminate(jnp.concatenate([panel, eye], axis=1), lo)
        panel, tail = solved[:, :size], solved[:, size:]
        panel = jnp.where(here, jnp.concatenate([tail] * (size // 128), axis=1), panel)
        work[lo:hi] = jnp.where(lane < hi, panel, 0.0)
        if s + 1 < steps:
            update = gram_update(jnp.where(lane >= hi, panel, 0.0), panel)
            for r in range(s + 1, steps):
                rows = work[r * k : r * k + k]
                work[r * k : r * k + k] = jnp.where(here, 0.0, rows) - update[r * k : r * k + k]
    rows = size // piece_count
    own = work[pl.ds(pl.multiple_of(lax.axis_index("layer") * rows, rows), rows)] * across
    joint = jnp.dot(own, stacked[...], precision=HIGHEST, preferred_element_type=F32)
    joint = joint.reshape(out_ref.shape)
    out_ref[...] = joint
    for copy in range(rounded_ref.shape[0]):
        rounded_ref[copy] = joint.astype(BF16)


def joint_solve(grams, images, copies):
    layers, k, width = images[0].shape
    size = layers * k * len(images)
    return pl.pallas_call(
        functools.partial(joint_kernel, len(images), k),
        in_specs=vmem_specs(2 * len(images)),
        out_specs=vmem_specs(2),
        out_shape=[
            jax.ShapeDtypeStruct(images[0].shape, F32),
            jax.ShapeDtypeStruct((copies, *images[0].shape), BF16),
        ],
        scratch_shapes=[pltpu.VMEM((size, size), F32), pltpu.VMEM((size, width), F32)],
        compiler_params=params(8),
        name="joint_solve",
    )(*grams, *images)


def around(x, axis, count):
    pieces = [x]
    for d in range(1, count):
        pieces.append(lax.ppermute(x, axis, [((m + d) % count, m) for m in range(count)]))
    return pieces


def gather(copies):
    return lax.all_to_all(copies, "node", 0, 0)


def per_device(shards, groups, blocks, block_rows, block_cols, counts, start):
    cols_total = shards * BROWS
    live = jnp.arange(block_rows.shape[1], dtype=jnp.int32)[None, :] < counts
    key = jnp.where(live, block_cols * BROWS + block_rows, -1)

    def copied(x):
        return jnp.broadcast_to(x[None], (shards, *x.shape))

    first = gather(copied(start.astype(BF16)))
    hi, lo = build_dense(key, blocks, cols_total // CHUNK_COLS)
    image, gram = apply_dense("gram", first, hi, lo)
    (image,) = apply_dense("plain", gather(solve(gather(gram), image, shards)), hi, lo)
    images = around(image, "layer", groups)
    grams = around(jnp.sum(gather(copied(cross(images))), axis=0), "layer", groups)
    joint_basis, rounded = joint_solve(grams, images, shards)
    _, partial = apply_dense("score", gather(rounded), hi, lo, joint_basis)
    return joint_basis, jnp.sum(gather(partial), axis=0)


def solution(mesh):
    in_specs = (
        P(("parts", "layer"), "node", None),
        P(("parts", "layer"), "node"),
        P(("parts", "layer"), "node"),
        P(("parts", "layer"), "node"),
        P(("parts", "layer"), None, "node"),
    )
    out_specs = (P(("parts", "layer"), None, "node"), P(("parts", "layer"), None, None))
    return jax.shard_map(
        functools.partial(per_device, mesh.shape["node"], mesh.shape["layer"]),
        mesh=mesh,
        in_specs=in_specs,
        out_specs=out_specs,
        check_vma=False,
    )
```

```python
import functools

import jax
import jax.numpy as jnp
from jax import lax
from jax.experimental import pallas as pl
from jax.experimental.pallas import tpu as pltpu
from jax.sharding import PartitionSpec as P

BLK = 64
ROWS_DEV = 512
BROWS = ROWS_DEV // BLK
CHUNK_COLS = 8
CHUNK_LANES = CHUNK_COLS * 2 * BLK
TALL = BROWS * BLK // 2
MIB = 1024 * 1024
F32 = jnp.float32
BF16 = jnp.bfloat16
HIGHEST = lax.Precision.HIGHEST
TRANS_B = (((1,), (1,)), ((), ()))
TRANS_A = (((0,), (0,)), ((), ()))


def params(mib):
    return pltpu.CompilerParams(vmem_limit_bytes=mib * MIB)


def vmem_specs(count):
    return [pl.BlockSpec(memory_space=pltpu.VMEM)] * count


def place(z, chunks, u, hi_ref, lo_ref, layer):
    out_rows = pl.ds(pl.multiple_of(u * 16, 16), 16)
    for c in range(chunks * CHUNK_COLS):
        piece = z[c * 8 : c * 8 + 8]
        piece = jnp.concatenate([piece[:, :128], piece[:, 128:]], axis=0)
        hi = piece.astype(BF16)
        lo = (piece - hi.astype(F32)).astype(BF16)
        lanes = slice((c % CHUNK_COLS) * 128, (c % CHUNK_COLS) * 128 + 128)
        hi_ref[layer, c // CHUNK_COLS, out_rows, lanes] = hi
        lo_ref[layer, c // CHUNK_COLS, out_rows, lanes] = lo


def one_hot(key, base, positions):
    position = lax.broadcasted_iota(jnp.int32, (positions, key.shape[1]), 0) + base
    return jnp.where(position == key, 1.0, 0.0).astype(BF16)


def build_kernel(key_ref, blocks_ref, hi_ref, lo_ref):
    chunks = hi_ref.shape[1]
    positions = chunks * CHUNK_COLS * BROWS
    onehot = one_hot(key_ref[0], pl.program_id(1) * positions, positions)

    def step(u, carry):
        cols = pl.ds(pl.multiple_of(u * 256, 256), 256)
        z = jnp.dot(onehot, blocks_ref[0, :, cols], preferred_element_type=F32)
        place(z, chunks, u, hi_ref, lo_ref, 0)
        return carry

    lax.fori_loop(0, BLK * BLK // 256, step, 0)


def build_whole_kernel(key_ref, blocks_ref, hi_ref, lo_ref, held, arrived):
    layers, chunks = hi_ref.shape[:2]
    pieces = arrived.shape[1]
    width = held.shape[2] // pieces
    inner = width // 256

    def fetch(layer, piece):
        cols = pl.ds(pl.multiple_of(piece * width, width), width)
        return pltpu.make_async_copy(
            blocks_ref.at[layer, :, cols], held.at[layer, :, cols], arrived.at[layer, piece]
        )

    for layer in range(layers):
        for piece in range(pieces):
            fetch(layer, piece).start()
    for layer in range(layers):
        onehot = one_hot(key_ref[layer], 0, chunks * CHUNK_COLS * BROWS)

        def step(piece, carry):
            fetch(layer, piece).wait()
            for v in range(inner):
                cols = pl.ds(pl.multiple_of(piece * width + v * 256, 256), 256)
                z = jnp.dot(onehot, held[layer, :, cols], preferred_element_type=F32)
                place(z, chunks, piece * inner + v, hi_ref, lo_ref, layer)
            return carry

        lax.fori_loop(0, pieces, step, 0)


def build_dense(key, blocks, chunk_total):
    layers, slots, width = blocks.shape
    dense = jax.ShapeDtypeStruct((layers, chunk_total, TALL, CHUNK_LANES), BF16)
    key = key.reshape(layers, 1, slots)
    if chunk_total <= 4:
        pieces = 4
        return pl.pallas_call(
            build_whole_kernel,
            in_specs=[pl.BlockSpec(memory_space=pltpu.VMEM), pl.BlockSpec(memory_space=pltpu.HBM)],
            out_specs=vmem_specs(2),
            out_shape=[dense, dense],
            scratch_shapes=[pltpu.VMEM(blocks.shape, BF16), pltpu.SemaphoreType.DMA((layers, pieces))],
            compiler_params=params(24),
            name="build_dense",
        )(key, blocks)
    out_spec = pl.BlockSpec((1, 4, TALL, CHUNK_LANES), lambda l, s: (l, s, 0, 0))
    return pl.pallas_call(
        build_kernel,
        grid=(layers, chunk_total // 4),
        in_specs=[
            pl.BlockSpec((1, 1, slots), lambda l, s: (l, 0, 0)),
            pl.BlockSpec((1, slots, width), lambda l, s: (l, 0, 0)),
        ],
        out_specs=[out_spec, out_spec],
        out_shape=[dense, dense],
        compiler_params=params(24),
        name="build_dense",
    )(key, blocks)


def split3(x):
    a = x.astype(BF16)
    r = x - a.astype(F32)
    b = r.astype(BF16)
    c = (r - b.astype(F32)).astype(BF16)
    return a, b, c


def image_part(basis, hi, lo):
    k, width = basis.shape
    basis = basis.astype(F32)
    low = lax.broadcasted_iota(jnp.int32, (k, 128), 1) < BLK
    first, second = [], []
    for q in range(width // 128):
        b = basis[:, q * 128 : q * 128 + 128]
        br = pltpu.roll(b, BLK, 1)
        first += [jnp.where(low, b, 0.0), jnp.where(low, br, 0.0)]
        second += [jnp.where(low, 0.0, br), jnp.where(low, 0.0, b)]
    weights = jnp.concatenate(
        [
            jnp.concatenate(first, axis=1),
            jnp.concatenate(second, axis=1),
            jnp.zeros((128 - 2 * k, CHUNK_LANES), F32),
        ],
        axis=0,
    ).astype(BF16)
    total = lax.dot_general(hi, weights, TRANS_B, preferred_element_type=F32)
    return total + lax.dot_general(lo, weights, TRANS_B, preferred_element_type=F32)


def node_order():
    row = lax.broadcasted_iota(jnp.int32, (ROWS_DEV, ROWS_DEV), 0)
    col = lax.broadcasted_iota(jnp.int32, (ROWS_DEV, ROWS_DEV), 1)
    target = (row % 8) * BLK + 2 * ((row % TALL) // 8) + row // TALL
    return jnp.where(target == col, 1.0, 0.0).astype(BF16)


def to_wide(total, perm, k):
    turned = total.T
    wide = jnp.concatenate([turned[:k], turned[k : 2 * k]], axis=1)
    moved = jnp.dot(jnp.concatenate(split3(wide), axis=0), perm, preferred_element_type=F32)
    return moved[:k] + moved[k : 2 * k] + moved[2 * k :]


def dot_rows(a, b):
    return lax.dot_general(a, b, TRANS_B, precision=HIGHEST, preferred_element_type=F32)


def apply_kernel(mode, *refs):
    basis_ref, refs = refs[0], refs[1:]
    if mode == "score":
        left_ref, refs = refs[0], refs[1:]
    hi_ref, lo_ref, out_ref = refs[:3]
    perm, acc = refs[-2:]
    layer, chunk = pl.program_id(0), pl.program_id(1)

    @pl.when((layer == 0) & (chunk == 0))
    def _():
        perm[...] = node_order()

    total = image_part(basis_ref[chunk, layer], hi_ref[0, 0], lo_ref[0, 0])

    @pl.when(chunk == 0)
    def _():
        acc[...] = total

    @pl.when(chunk > 0)
    def _():
        acc[...] += total

    @pl.when(chunk == pl.num_programs(1) - 1)
    def _():
        image = to_wide(acc[...], perm[...], basis_ref.shape[2])
        if mode != "score":
            out_ref[0] = image
        if mode == "gram":
            refs[3][0] = dot_rows(image, image)
        if mode == "score":
            out_ref[0] = dot_rows(left_ref[0], image)


def apply_whole_kernel(mode, piece_count, *refs):
    pieces, refs = refs[:piece_count], refs[piece_count:]
    if mode == "score":
        left_ref, refs = refs[0], refs[1:]
    hi_ref, lo_ref, out_ref = refs[:3]
    perm = node_order()
    for layer in range(hi_ref.shape[0]):
        total = sum(
            image_part(piece[layer], hi_ref[layer, chunk], lo_ref[layer, chunk])
            for chunk, piece in enumerate(pieces)
        )
        image = to_wide(total, perm, pieces[0].shape[1])
        if mode != "score":
            out_ref[layer] = image
        if mode == "gram":
            refs[3][layer] = dot_rows(image, image)
        if mode == "score":
            out_ref[layer] = dot_rows(left_ref[layer], image)


def apply_dense(mode, pieces, hi, lo, left=None):
    layers, chunks = hi.shape[:2]
    k = pieces[0].shape[-2]
    image = jax.ShapeDtypeStruct((layers, k, ROWS_DEV), F32)
    small = jax.ShapeDtypeStruct((layers, k, k), F32)
    out_shape = {"gram": [image, small], "plain": [image], "score": [small]}[mode]
    operands = list(pieces) + ([left] if mode == "score" else []) + [hi, lo]
    if len(pieces) == chunks:
        return pl.pallas_call(
            functools.partial(apply_whole_kernel, mode, chunks),
            in_specs=vmem_specs(len(operands)),
            out_specs=vmem_specs(len(out_shape)),
            out_shape=out_shape,
            compiler_params=params(14),
            name="apply_" + mode,
        )(*operands)
    dense_spec = pl.BlockSpec((1, 1, TALL, CHUNK_LANES), lambda l, s: (l, s, 0, 0))
    image_spec = pl.BlockSpec((1, k, ROWS_DEV), lambda l, s: (l, 0, 0))
    small_spec = pl.BlockSpec((1, k, k), lambda l, s: (l, 0, 0))
    return pl.pallas_call(
        functools.partial(apply_kernel, mode),
        grid=(layers, chunks),
        in_specs=vmem_specs(1) + ([image_spec] if mode == "score" else []) + [dense_spec, dense_spec],
        out_specs={"gram": [image_spec, small_spec], "plain": [image_spec], "score": [small_spec]}[mode],
        out_shape=out_shape,
        scratch_shapes=[pltpu.VMEM((ROWS_DEV, ROWS_DEV), BF16), pltpu.VMEM((TALL, 128), F32)],
        compiler_params=params(12),
        name="apply_" + mode,
    )(*operands)


def spread(x):
    return jnp.broadcast_to(x, (8, 128))


def eliminate(rows, offset):
    groups, tiles = len(rows), len(rows[0])
    rows = [list(row) for row in rows]
    home, at = offset // 128, offset % 128
    sub = lax.broadcasted_iota(jnp.int32, (8, 128), 0)
    solved = []
    for h in range(groups):
        below = range(h + 1, groups)
        lane = at + 8 * h
        col = [{g: spread(rows[g][home][:, lane + q : lane + q + 1]) for g in range(h, groups)} for q in range(8)]
        cell = {(p, q): spread(col[p][h][q : q + 1]) for q in range(8) for p in range(q + 1)}
        row = [[spread(rows[h][t][q : q + 1]) for t in range(tiles)] for q in range(8)]
        done = []
        for m in range(0, 8, 2):
            n = m + 1
            a, b, c = cell[m, m], cell[m, n], cell[n, n]
            det = a * c - b * b
            r = pl.reciprocal(det, approx=True)
            later = range(m + 2, 8)
            u = {q: c * cell[m, q] - b * cell[n, q] for q in later}
            v = {q: a * cell[n, q] - b * cell[m, q] for q in later}
            for q in later:
                for p in range(m + 2, q + 1):
                    cell[p, q] = cell[p, q] - r * (cell[m, p] * u[q] + cell[n, p] * v[q])
            for q in later:
                for g in below:
                    col[q][g] = col[q][g] - r * (col[m][g] * u[q] + col[n][g] * v[q])
            for t in range(tiles):
                x = r * (c * row[m][t] - b * row[n][t])
                y = r * (a * row[n][t] - b * row[m][t])
                for q in later:
                    row[q][t] = row[q][t] - (cell[m, q] * x + cell[n, q] * y)
                for g in below:
                    rows[g][t] = rows[g][t] - (col[m][g] * x + col[n][g] * y)
            over = pl.reciprocal(a, approx=True)
            done.append([lax.rsqrt(a) * x for x in row[m]])
            scale = lax.rsqrt(det * over)
            done.append([scale * (x - (b * over) * w) for x, w in zip(row[n], row[m])])
        finished = []
        for t in range(tiles):
            x = done[7][t]
            for q in range(7):
                x = jnp.where(sub == q, done[q][t], x)
            finished.append(x)
        solved.append(finished)
    return solved


def tiled(x):
    return [
        [x[g * 8 : g * 8 + 8, t * 128 : t * 128 + 128] for t in range(x.shape[1] // 128)]
        for g in range(x.shape[0] // 8)
    ]


def joined(tiles):
    return jnp.concatenate([jnp.concatenate(row, axis=1) for row in tiles], axis=0)


def unit_scale(gram):
    lane = lax.broadcasted_iota(jnp.int32, gram.shape, 1)
    sub = lax.broadcasted_iota(jnp.int32, gram.shape, 0)
    kept = jnp.where(lane == sub, gram, 0.0)
    down = 1.0 / jnp.sqrt(jnp.sum(kept, axis=1, keepdims=True))
    across = jnp.sum(kept, axis=0, keepdims=True)
    across = 1.0 / jnp.sqrt(jnp.where(across == 0.0, 1.0, across))
    return gram * down * across, across


def gram_update(panel, first):
    a, b, c = split3(panel)
    left = jnp.concatenate([a, a, b, b, a, c], axis=0)
    right = jnp.concatenate([a, b, a, b, c, a], axis=0)
    parts = {
        at: lax.dot_general(left[:, at : at + 128], right, TRANS_A, preferred_element_type=F32)
        for at in range(first, panel.shape[1], 128)
    }
    return lambda at, count: parts[at // 128 * 128][at % 128 : at % 128 + count]


def solve_kernel(piece_count, *refs):
    grams, image_ref, out_ref = refs[:piece_count], refs[piece_count], refs[piece_count + 1]
    layers, k = image_ref.shape[:2]
    lane = lax.broadcasted_iota(jnp.int32, (k, 128), 1)
    sub = lax.broadcasted_iota(jnp.int32, (k, 128), 0)
    eye = jnp.where(lane == sub, 1.0, 0.0)
    for layer in range(layers):
        gram = add_pieces([ref[layer] for ref in grams])
        gram = jnp.concatenate([gram, jnp.zeros((k, 128 - k), F32)], axis=1)
        gram, across = unit_scale(gram)
        solved = eliminate(tiled(jnp.concatenate([gram, eye], axis=1)), 0)
        inverse = joined(solved)[:, 128:] * across
        solved = jnp.dot(inverse[:, :k], image_ref[layer], precision=HIGHEST, preferred_element_type=F32)
        out_ref[layer] = solved.astype(BF16)


def solve(grams, image):
    return pl.pallas_call(
        functools.partial(solve_kernel, len(grams)),
        in_specs=vmem_specs(len(grams) + 1),
        out_specs=pl.BlockSpec(memory_space=pltpu.VMEM),
        out_shape=jax.ShapeDtypeStruct(image.shape, BF16),
        compiler_params=params(4),
        name="solve_layers",
    )(*grams, image)


def stack_rows(refs, scratch):
    g = lax.axis_index("layer")
    rows = scratch.shape[0] // len(refs)
    for d, ref in enumerate(refs):
        at = lax.rem(g + d, len(refs)) * rows
        scratch[pl.ds(pl.multiple_of(at, rows), rows)] = ref[...].reshape(rows, ref.shape[-1])


def cross_kernel(piece_count, *refs):
    pieces, out_ref, stacked = refs[:piece_count], refs[piece_count], refs[piece_count + 1]
    stack_rows(pieces, stacked)
    own = pieces[0][...].reshape(-1, stacked.shape[1])
    out_ref[...] = lax.dot_general(
        own, stacked[...], TRANS_B, precision=HIGHEST, preferred_element_type=F32
    )


def cross(pieces):
    layers, k, width = pieces[0].shape
    rows = layers * k
    return pl.pallas_call(
        functools.partial(cross_kernel, len(pieces)),
        in_specs=vmem_specs(len(pieces)),
        out_specs=pl.BlockSpec(memory_space=pltpu.VMEM),
        out_shape=jax.ShapeDtypeStruct((rows, rows * len(pieces)), F32),
        scratch_shapes=[pltpu.VMEM((rows * len(pieces), width), F32)],
        compiler_params=params(6),
        name="cross_gram",
    )(*pieces)


def joint_kernel(piece_count, k, *refs):
    gram_refs, image_refs = refs[:piece_count], refs[piece_count : 2 * piece_count]
    out_ref, rounded_ref, work, stacked = refs[2 * piece_count :]
    stack_rows(gram_refs, work)
    stack_rows(image_refs, stacked)
    size = work.shape[0]
    steps = size // k
    lane = lax.broadcasted_iota(jnp.int32, (k, size), 1)
    lane_128 = lax.broadcasted_iota(jnp.int32, (k, 128), 1)
    sub_128 = lax.broadcasted_iota(jnp.int32, (k, 128), 0)
    gram, across = unit_scale(work[...])
    work[...] = gram
    for s in range(steps):
        lo, hi = s * k, (s + 1) * k
        here = (lane >= lo) & (lane < hi)
        eye = jnp.where(lane_128 == sub_128 + lo % 128, 1.0, 0.0)
        solved = joined(eliminate(tiled(jnp.concatenate([work[lo:hi], eye], axis=1)), lo))
        panel, tail = solved[:, :size], solved[:, size:]
        panel = jnp.where(here, jnp.concatenate([tail] * (size // 128), axis=1), panel)
        work[lo:hi] = jnp.where(lane < hi, panel, 0.0)
        if s + 1 < steps:
            update = gram_update(panel, hi // 128 * 128)
            for r in range(s + 1, steps):
                rows = work[r * k : r * k + k]
                work[r * k : r * k + k] = jnp.where(here, 0.0, rows) - update(r * k, k)
    rows = size // piece_count
    own = work[pl.ds(pl.multiple_of(lax.axis_index("layer") * rows, rows), rows)] * across
    joint = jnp.dot(own, stacked[...], precision=HIGHEST, preferred_element_type=F32)
    joint = joint.reshape(out_ref.shape)
    out_ref[...] = joint
    rounded_ref[...] = joint.astype(BF16)


def joint_solve(grams, images):
    layers, k, width = images[0].shape
    size = layers * k * len(images)
    return pl.pallas_call(
        functools.partial(joint_kernel, len(images), k),
        in_specs=vmem_specs(2 * len(images)),
        out_specs=vmem_specs(2),
        out_shape=[
            jax.ShapeDtypeStruct(images[0].shape, F32),
            jax.ShapeDtypeStruct(images[0].shape, BF16),
        ],
        scratch_shapes=[pltpu.VMEM((size, size), F32), pltpu.VMEM((size, width), F32)],
        compiler_params=params(8),
        name="joint_solve",
    )(*grams, *images)


def around(x, axis, count):
    pieces = [x]
    for d in range(1, count):
        pieces.append(lax.ppermute(x, axis, [((m + d) % count, m) for m in range(count)]))
    return pieces


def add_pieces(pieces):
    if len(pieces) == 1:
        return pieces[0]
    return (pieces[0] + pieces[2]) + (pieces[1] + pieces[3])


def per_device(shards, groups, blocks, block_rows, block_cols, counts, start):
    few = shards == 4
    cols_total = shards * BROWS
    live = jnp.arange(block_rows.shape[1], dtype=jnp.int32)[None, :] < counts
    cols = block_cols
    if few:
        cols = (cols - lax.axis_index("node") * BROWS + cols_total) % cols_total
    key = jnp.where(live, cols * BROWS + block_rows, -1)

    def gather(x):
        return around(x, "node", shards) if few else [lax.all_gather(x, "node")]

    def partials(x):
        return around(x, "node", shards) if few else [lax.psum(x, "node")]

    first = gather(start.astype(BF16))
    hi, lo = build_dense(key, blocks, cols_total // CHUNK_COLS)
    image, gram = apply_dense("gram", first, hi, lo)
    (image,) = apply_dense("plain", gather(solve(partials(gram), image)), hi, lo)
    images = around(image, "layer", groups)
    grams = around(add_pieces(partials(cross(images))), "layer", groups)
    joint_basis, rounded = joint_solve(grams, images)
    (partial,) = apply_dense("score", gather(rounded), hi, lo, joint_basis)
    return joint_basis, add_pieces(partials(partial))


def solution(mesh):
    in_specs = (
        P(("parts", "layer"), "node", None),
        P(("parts", "layer"), "node"),
        P(("parts", "layer"), "node"),
        P(("parts", "layer"), "node"),
        P(("parts", "layer"), None, "node"),
    )
    out_specs = (P(("parts", "layer"), None, "node"), P(("parts", "layer"), None, None))
    return jax.shard_map(
        functools.partial(per_device, mesh.shape["node"], mesh.shape["layer"]),
        mesh=mesh,
        in_specs=in_specs,
        out_specs=out_specs,
        check_vma=False,
    )
```

```python
import functools

import jax
import jax.numpy as jnp
from jax import lax
from jax.experimental import pallas as pl
from jax.experimental.pallas import tpu as pltpu
from jax.sharding import PartitionSpec as P

BLK = 64
ROWS_DEV = 512
BROWS = ROWS_DEV // BLK
CHUNK_COLS = 8
CHUNK_LANES = CHUNK_COLS * 2 * BLK
TALL = BROWS * BLK // 2
MIB = 1024 * 1024
F32 = jnp.float32
BF16 = jnp.bfloat16
HIGHEST = lax.Precision.HIGHEST
TRANS_B = (((1,), (1,)), ((), ()))
TRANS_A = (((0,), (0,)), ((), ()))


def params(mib):
    return pltpu.CompilerParams(vmem_limit_bytes=mib * MIB)


def vmem_specs(count):
    return [pl.BlockSpec(memory_space=pltpu.VMEM)] * count


def place(z, chunks, u, dense_ref, layer):
    for c in range(chunks * CHUNK_COLS):
        piece = z[c * 8 : c * 8 + 8]
        piece = jnp.concatenate([piece[:, :128], piece[:, 128:]], axis=0)
        hi = piece.astype(BF16)
        lo = (piece - hi.astype(F32)).astype(BF16)
        lanes = slice((c % CHUNK_COLS) * 128, (c % CHUNK_COLS) * 128 + 128)
        dense_ref[layer, c // CHUNK_COLS, pl.ds(pl.multiple_of(u * 16, 16), 16), lanes] = hi
        dense_ref[layer, c // CHUNK_COLS, pl.ds(pl.multiple_of(u * 16 + TALL, 16), 16), lanes] = lo


def one_hot(rows_ref, cols_ref, counts_ref, layer, flip, base, positions):
    slot = lax.broadcasted_iota(jnp.int32, (1, rows_ref.shape[2]), 1)
    key = (cols_ref[layer] ^ flip) * BROWS + rows_ref[layer]
    key = jnp.where(slot < counts_ref[layer], key, -1)
    position = lax.broadcasted_iota(jnp.int32, (positions, key.shape[1]), 0) + base
    return jnp.where(position == key, 1.0, 0.0).astype(BF16)


def build_kernel(rows_ref, cols_ref, counts_ref, blocks_ref, dense_ref):
    chunks = dense_ref.shape[1]
    positions = chunks * CHUNK_COLS * BROWS
    base = pl.program_id(1) * positions
    onehot = one_hot(rows_ref, cols_ref, counts_ref, pl.program_id(0), 0, base, positions)

    def step(u, carry):
        cols = pl.ds(pl.multiple_of(u * 256, 256), 256)
        z = jnp.dot(onehot, blocks_ref[0, :, cols], preferred_element_type=F32)
        place(z, chunks, u, dense_ref, 0)
        return carry

    lax.fori_loop(0, BLK * BLK // 256, step, 0)


def build_whole_kernel(rows_ref, cols_ref, counts_ref, blocks_ref, dense_ref, held, arrived):
    layers, chunks = dense_ref.shape[:2]
    pieces = arrived.shape[1]
    width = held.shape[2] // pieces
    inner = width // 256

    def fetch(layer, piece):
        cols = pl.ds(pl.multiple_of(piece * width, width), width)
        return pltpu.make_async_copy(
            blocks_ref.at[layer, :, cols], held.at[layer, :, cols], arrived.at[layer, piece]
        )

    for layer in range(layers):
        for piece in range(pieces):
            fetch(layer, piece).start()
    flip = lax.axis_index("node") * CHUNK_COLS
    for layer in range(layers):
        onehot = one_hot(rows_ref, cols_ref, counts_ref, layer, flip, 0, chunks * CHUNK_COLS * BROWS)

        def step(piece, carry):
            fetch(layer, piece).wait()
            for v in range(inner):
                cols = pl.ds(pl.multiple_of(piece * width + v * 256, 256), 256)
                z = jnp.dot(onehot, held[layer, :, cols], preferred_element_type=F32)
                place(z, chunks, piece * inner + v, dense_ref, layer)
            return carry

        lax.fori_loop(0, pieces, step, 0)


def build_dense(block_rows, block_cols, counts, blocks, chunk_total):
    layers, slots, width = blocks.shape
    dense = jax.ShapeDtypeStruct((layers, chunk_total, 2 * TALL, CHUNK_LANES), BF16)
    operands = (block_rows[:, None], block_cols[:, None], counts[:, 0], pltpu.with_memory_space_constraint(blocks, pltpu.HBM))
    if chunk_total <= 4:
        pieces = 4
        return pl.pallas_call(
            build_whole_kernel,
            in_specs=vmem_specs(2)
            + [pl.BlockSpec(memory_space=pltpu.SMEM), pl.BlockSpec(memory_space=pltpu.HBM)],
            out_specs=pl.BlockSpec(memory_space=pltpu.VMEM),
            out_shape=dense,
            scratch_shapes=[pltpu.VMEM(blocks.shape, BF16), pltpu.SemaphoreType.DMA((layers, pieces))],
            compiler_params=params(28),
            name="build_dense",
        )(*operands)
    return pl.pallas_call(
        build_kernel,
        grid=(layers, chunk_total // 4),
        in_specs=vmem_specs(2)
        + [
            pl.BlockSpec(memory_space=pltpu.SMEM),
            pl.BlockSpec((1, slots, width), lambda l, s: (l, 0, 0)),
        ],
        out_specs=pl.BlockSpec((1, 4, 2 * TALL, CHUNK_LANES), lambda l, s: (l, s, 0, 0)),
        out_shape=dense,
        compiler_params=params(24),
        name="build_dense",
    )(*operands)


def split3(x):
    a = x.astype(BF16)
    r = x - a.astype(F32)
    b = r.astype(BF16)
    c = (r - b.astype(F32)).astype(BF16)
    return a, b, c


def image_part(basis, dense):
    k, width = basis.shape
    basis = basis.astype(F32)
    tall = jnp.concatenate([basis, basis, jnp.zeros((128 - 2 * k, width), F32)], axis=0).T
    lane = lax.broadcasted_iota(jnp.int32, tall.shape, 1)
    first = jnp.where(lane < k, tall, 0.0).astype(BF16)
    second = jnp.where(lane < k, 0.0, tall).astype(BF16)
    weights = []
    for c in range(width // BLK):
        weights += [first[c * BLK : c * BLK + BLK], second[c * BLK : c * BLK + BLK]]
    return jnp.dot(dense, jnp.concatenate(weights, axis=0), preferred_element_type=F32)


def to_wide(total, k, halves, tall):
    halves[...] = total[:TALL] + total[TALL:]
    for b in range(BROWS):
        part = halves[pl.ds(b, BLK // 2, stride=BROWS), :]
        tall[pl.ds(BLK * b, BLK // 2, stride=2), :] = part
        tall[pl.ds(BLK * b + 1, BLK // 2, stride=2), :] = pltpu.roll(part, 128 - k, 1)
    return tall[...].T[:k]


def dot_rows(a, b):
    return lax.dot_general(a, b, TRANS_B, precision=HIGHEST, preferred_element_type=F32)


def apply_kernel(mode, *refs):
    basis_ref, refs = refs[0], refs[1:]
    if mode == "score":
        left_ref, refs = refs[0], refs[1:]
    dense_ref, out_ref = refs[:2]
    halves, tall, acc = refs[-3:]
    layer, chunk = pl.program_id(0), pl.program_id(1)
    total = image_part(basis_ref[chunk, layer], dense_ref[0, 0])

    @pl.when(chunk == 0)
    def _():
        acc[...] = total

    @pl.when(chunk > 0)
    def _():
        acc[...] += total

    @pl.when(chunk == pl.num_programs(1) - 1)
    def _():
        image = to_wide(acc[...], basis_ref.shape[2], halves, tall)
        if mode != "score":
            out_ref[0] = image
        if mode == "gram":
            refs[2][0] = dot_rows(image, image)
        if mode == "score":
            out_ref[0] = dot_rows(left_ref[0], image)


def apply_whole_kernel(mode, piece_count, *refs):
    pieces, refs = refs[:piece_count], refs[piece_count:]
    if mode == "score":
        left_ref, refs = refs[0], refs[1:]
    dense_ref, out_ref = refs[:2]
    halves, tall = refs[-2:]
    for layer in range(dense_ref.shape[0]):
        total = sum(
            image_part(piece[layer], dense_ref[layer, chunk]) for chunk, piece in enumerate(pieces)
        )
        image = to_wide(total, pieces[0].shape[1], halves.at[layer], tall.at[layer])
        if mode != "score":
            out_ref[layer] = image
        if mode == "gram":
            refs[2][layer] = dot_rows(image, image)
        if mode == "score":
            out_ref[layer] = dot_rows(left_ref[layer], image)


def apply_dense(mode, pieces, dense, left=None):
    layers, chunks = dense.shape[:2]
    k = pieces[0].shape[-2]
    image = jax.ShapeDtypeStruct((layers, k, ROWS_DEV), F32)
    small = jax.ShapeDtypeStruct((layers, k, k), F32)
    out_shape = {"gram": [image, small], "plain": [image], "score": [small]}[mode]
    operands = list(pieces) + ([left] if mode == "score" else []) + [dense]
    if len(pieces) == chunks:
        return pl.pallas_call(
            functools.partial(apply_whole_kernel, mode, chunks),
            in_specs=vmem_specs(len(operands)),
            out_specs=vmem_specs(len(out_shape)),
            out_shape=out_shape,
            scratch_shapes=[pltpu.VMEM((layers, TALL, 128), F32), pltpu.VMEM((layers, ROWS_DEV, 128), F32)],
            compiler_params=params(14),
            name="apply_" + mode,
        )(*operands)
    dense_spec = pl.BlockSpec((1, 1, 2 * TALL, CHUNK_LANES), lambda l, s: (l, s, 0, 0))
    image_spec = pl.BlockSpec((1, k, ROWS_DEV), lambda l, s: (l, 0, 0))
    small_spec = pl.BlockSpec((1, k, k), lambda l, s: (l, 0, 0))
    return pl.pallas_call(
        functools.partial(apply_kernel, mode),
        grid=(layers, chunks),
        in_specs=vmem_specs(1) + ([image_spec] if mode == "score" else []) + [dense_spec],
        out_specs={"gram": [image_spec, small_spec], "plain": [image_spec], "score": [small_spec]}[mode],
        out_shape=out_shape,
        scratch_shapes=[
            pltpu.VMEM((TALL, 128), F32),
            pltpu.VMEM((ROWS_DEV, 128), F32),
            pltpu.VMEM((2 * TALL, 128), F32),
        ],
        compiler_params=params(12),
        name="apply_" + mode,
    )(*operands)


def spread(x):
    return jnp.broadcast_to(x, (8, 128))


def eliminate(rows, offset):
    groups, tiles = len(rows), len(rows[0])
    rows = [list(row) for row in rows]
    home, at = offset // 128, offset % 128
    sub = lax.broadcasted_iota(jnp.int32, (8, 128), 0)
    solved = []
    for h in range(groups):
        below = range(h + 1, groups)
        lane = at + 8 * h
        col = [{g: spread(rows[g][home][:, lane + q : lane + q + 1]) for g in range(h, groups)} for q in range(8)]
        cell = {(p, q): spread(col[p][h][q : q + 1]) for q in range(8) for p in range(q + 1)}
        row = [[spread(rows[h][t][q : q + 1]) for t in range(tiles)] for q in range(8)]
        done = []
        for m in range(0, 8, 2):
            n = m + 1
            a, b, c = cell[m, m], cell[m, n], cell[n, n]
            det = a * c - b * b
            r = pl.reciprocal(det, approx=True)
            later = range(m + 2, 8)
            u = {q: c * cell[m, q] - b * cell[n, q] for q in later}
            v = {q: a * cell[n, q] - b * cell[m, q] for q in later}
            for q in later:
                for p in range(m + 2, q + 1):
                    cell[p, q] = cell[p, q] - r * (cell[m, p] * u[q] + cell[n, p] * v[q])
            for q in later:
                for g in below:
                    col[q][g] = col[q][g] - r * (col[m][g] * u[q] + col[n][g] * v[q])
            for t in range(tiles):
                x = r * (c * row[m][t] - b * row[n][t])
                y = r * (a * row[n][t] - b * row[m][t])
                for q in later:
                    row[q][t] = row[q][t] - (cell[m, q] * x + cell[n, q] * y)
                for g in below:
                    rows[g][t] = rows[g][t] - (col[m][g] * x + col[n][g] * y)
            over = pl.reciprocal(a, approx=True)
            done.append([lax.rsqrt(a) * x for x in row[m]])
            scale = lax.rsqrt(det * over)
            done.append([scale * (x - (b * over) * w) for x, w in zip(row[n], row[m])])
        finished = []
        for t in range(tiles):
            x = done[7][t]
            for q in range(7):
                x = jnp.where(sub == q, done[q][t], x)
            finished.append(x)
        solved.append(finished)
    return solved


def tiled(x):
    return [
        [x[g * 8 : g * 8 + 8, t * 128 : t * 128 + 128] for t in range(x.shape[1] // 128)]
        for g in range(x.shape[0] // 8)
    ]


def joined(tiles):
    return jnp.concatenate([jnp.concatenate(row, axis=1) for row in tiles], axis=0)


def unit_scale(gram):
    lane = lax.broadcasted_iota(jnp.int32, gram.shape, 1)
    sub = lax.broadcasted_iota(jnp.int32, gram.shape, 0)
    kept = jnp.where(lane == sub, gram, 0.0)
    down = 1.0 / jnp.sqrt(jnp.sum(kept, axis=1, keepdims=True))
    across = jnp.sum(kept, axis=0, keepdims=True)
    across = 1.0 / jnp.sqrt(jnp.where(across == 0.0, 1.0, across))
    return gram * down * across, across


def gram_update(panel, first):
    a, b, c = split3(panel)
    left = jnp.concatenate([a, a, b, b, a, c], axis=0)
    right = jnp.concatenate([a, b, a, b, c, a], axis=0)
    parts = {
        at: lax.dot_general(left[:, at : at + 128], right, TRANS_A, preferred_element_type=F32)
        for at in range(first, panel.shape[1], 128)
    }
    return lambda at, count: parts[at // 128 * 128][at % 128 : at % 128 + count]


def solve_kernel(piece_count, *refs):
    grams, image_ref, out_ref = refs[:piece_count], refs[piece_count], refs[piece_count + 1]
    layers, k = image_ref.shape[:2]
    lane = lax.broadcasted_iota(jnp.int32, (k, 128), 1)
    sub = lax.broadcasted_iota(jnp.int32, (k, 128), 0)
    eye = jnp.where(lane == sub, 1.0, 0.0)
    for layer in range(layers):
        gram = add_pieces([ref[layer] for ref in grams])
        gram = jnp.concatenate([gram, jnp.zeros((k, 128 - k), F32)], axis=1)
        gram, across = unit_scale(gram)
        solved = eliminate(tiled(jnp.concatenate([gram, eye], axis=1)), 0)
        inverse = joined(solved)[:, 128:] * across
        solved = jnp.dot(inverse[:, :k], image_ref[layer], precision=HIGHEST, preferred_element_type=F32)
        out_ref[layer] = solved.astype(BF16)


def solve(grams, image):
    return pl.pallas_call(
        functools.partial(solve_kernel, len(grams)),
        in_specs=vmem_specs(len(grams) + 1),
        out_specs=pl.BlockSpec(memory_space=pltpu.VMEM),
        out_shape=jax.ShapeDtypeStruct(image.shape, BF16),
        compiler_params=params(4),
        name="solve_layers",
    )(*grams, image)


def stack_rows(refs, scratch):
    g = lax.axis_index("layer")
    rows = scratch.shape[0] // len(refs)
    for d, ref in enumerate(refs):
        at = (g ^ d) * rows
        scratch[pl.ds(pl.multiple_of(at, rows), rows)] = ref[...].reshape(rows, ref.shape[-1])


def cross_kernel(piece_count, *refs):
    pieces, out_ref, stacked = refs[:piece_count], refs[piece_count], refs[piece_count + 1]
    stack_rows(pieces, stacked)
    own = pieces[0][...].reshape(-1, stacked.shape[1])
    out_ref[...] = lax.dot_general(
        own, stacked[...], TRANS_B, precision=HIGHEST, preferred_element_type=F32
    )


def cross(pieces):
    layers, k, width = pieces[0].shape
    rows = layers * k
    return pl.pallas_call(
        functools.partial(cross_kernel, len(pieces)),
        in_specs=vmem_specs(len(pieces)),
        out_specs=pl.BlockSpec(memory_space=pltpu.VMEM),
        out_shape=jax.ShapeDtypeStruct((rows, rows * len(pieces)), F32),
        scratch_shapes=[pltpu.VMEM((rows * len(pieces), width), F32)],
        compiler_params=params(6),
        name="cross_gram",
    )(*pieces)


def joint_kernel(piece_count, k, *refs):
    gram_refs, image_refs = refs[:piece_count], refs[piece_count : 2 * piece_count]
    out_ref, again_ref, rounded_ref, work, stacked = refs[2 * piece_count :]
    stack_rows(gram_refs, work)
    stack_rows(image_refs, stacked)
    size = work.shape[0]
    steps = size // k
    lane = lax.broadcasted_iota(jnp.int32, (k, size), 1)
    lane_128 = lax.broadcasted_iota(jnp.int32, (k, 128), 1)
    sub_128 = lax.broadcasted_iota(jnp.int32, (k, 128), 0)
    gram, across = unit_scale(work[...])
    work[...] = gram
    for s in range(steps):
        lo, hi = s * k, (s + 1) * k
        here = (lane >= lo) & (lane < hi)
        eye = jnp.where(lane_128 == sub_128 + lo % 128, 1.0, 0.0)
        solved = joined(eliminate(tiled(jnp.concatenate([work[lo:hi], eye], axis=1)), lo))
        panel, tail = solved[:, :size], solved[:, size:]
        panel = jnp.where(here, jnp.concatenate([tail] * (size // 128), axis=1), panel)
        work[lo:hi] = jnp.where(lane < hi, panel, 0.0)
        if s + 1 < steps:
            update = gram_update(panel, hi // 128 * 128)
            for r in range(s + 1, steps):
                rows = work[r * k : r * k + k]
                work[r * k : r * k + k] = jnp.where(here, 0.0, rows) - update(r * k, k)
    rows = size // piece_count
    own = work[pl.ds(pl.multiple_of(lax.axis_index("layer") * rows, rows), rows)] * across
    joint = jnp.dot(own, stacked[...], precision=HIGHEST, preferred_element_type=F32)
    joint = joint.reshape(out_ref.shape)
    out_ref[...] = joint
    again_ref[...] = joint
    rounded_ref[...] = joint.astype(BF16)


def joint_solve(grams, images):
    layers, k, width = images[0].shape
    size = layers * k * len(images)
    return pl.pallas_call(
        functools.partial(joint_kernel, len(images), k),
        in_specs=vmem_specs(2 * len(images)),
        out_specs=vmem_specs(3),
        out_shape=[
            jax.ShapeDtypeStruct(images[0].shape, F32),
            jax.ShapeDtypeStruct(images[0].shape, F32),
            jax.ShapeDtypeStruct(images[0].shape, BF16),
        ],
        scratch_shapes=[pltpu.VMEM((size, size), F32), pltpu.VMEM((size, width), F32)],
        compiler_params=params(8),
        name="joint_solve",
    )(*grams, *images)


def around(x, axis, count):
    pieces = [x]
    for d in range(1, count):
        pieces.append(lax.ppermute(x, axis, [(m ^ d, m) for m in range(count)]))
    return pieces


def add_pieces(pieces):
    if len(pieces) == 1:
        return pieces[0]
    return (pieces[0] + pieces[1]) + (pieces[2] + pieces[3])


def per_device(shards, groups, blocks, block_rows, block_cols, counts, start):
    few = shards == 4

    def gather(x):
        return around(x, "node", shards) if few else [lax.all_gather(x, "node")]

    def partials(x):
        return around(x, "node", shards) if few else [lax.psum(x, "node")]

    first = gather(start.astype(BF16))
    dense = build_dense(block_rows, block_cols, counts, blocks, shards * BROWS // CHUNK_COLS)
    image, gram = apply_dense("gram", first, dense)
    (image,) = apply_dense("plain", gather(solve(partials(gram), image)), dense)
    images = around(image, "layer", groups)
    grams = around(add_pieces(partials(cross(images))), "layer", groups)
    joint_basis, again, rounded = joint_solve(grams, images)
    (partial,) = apply_dense("score", gather(rounded), dense, again)
    return joint_basis, add_pieces(partials(partial))


def solution(mesh):
    in_specs = (
        P(("parts", "layer"), "node", None),
        P(("parts", "layer"), "node"),
        P(("parts", "layer"), "node"),
        P(("parts", "layer"), "node"),
        P(("parts", "layer"), None, "node"),
    )
    out_specs = (P(("parts", "layer"), None, "node"), P(("parts", "layer"), None, None))
    return jax.shard_map(
        functools.partial(per_device, mesh.shape["node"], mesh.shape["layer"]),
        mesh=mesh,
        in_specs=in_specs,
        out_specs=out_specs,
        check_vma=False,
    )
```

```python
import functools

import jax
import jax.numpy as jnp
from jax import lax
from jax.experimental import pallas as pl
from jax.experimental.pallas import tpu as pltpu
from jax.sharding import PartitionSpec as P

BLK = 64
ROWS_DEV = 512
BROWS = ROWS_DEV // BLK
CHUNK_COLS = 8
CHUNK_LANES = CHUNK_COLS * 2 * BLK
TALL = BROWS * BLK // 2
MIB = 1024 * 1024
F32 = jnp.float32
BF16 = jnp.bfloat16
HIGHEST = lax.Precision.HIGHEST
TRANS_B = (((1,), (1,)), ((), ()))
TRANS_A = (((0,), (0,)), ((), ()))


def params(mib):
    return pltpu.CompilerParams(vmem_limit_bytes=mib * MIB)


def vmem_specs(count):
    return [pl.BlockSpec(memory_space=pltpu.VMEM)] * count


def place(z, chunks, u, dense_ref, layer):
    for c in range(chunks * CHUNK_COLS):
        piece = z[c * 8 : c * 8 + 8]
        piece = jnp.concatenate([piece[:, :128], piece[:, 128:]], axis=0)
        hi = piece.astype(BF16)
        lo = (piece - hi.astype(F32)).astype(BF16)
        lanes = slice((c % CHUNK_COLS) * 128, (c % CHUNK_COLS) * 128 + 128)
        dense_ref[layer, c // CHUNK_COLS, pl.ds(pl.multiple_of(u * 16, 16), 16), lanes] = hi
        dense_ref[layer, c // CHUNK_COLS, pl.ds(pl.multiple_of(u * 16 + TALL, 16), 16), lanes] = lo


def one_hot(rows_ref, cols_ref, counts_ref, layer, flip, base, positions):
    slot = lax.broadcasted_iota(jnp.int32, (1, rows_ref.shape[1]), 1)
    key = (cols_ref[pl.ds(layer, 1), :] ^ flip) * BROWS + rows_ref[pl.ds(layer, 1), :]
    key = jnp.where(slot < counts_ref[0, layer], key, -1)
    position = lax.broadcasted_iota(jnp.int32, (positions, key.shape[1]), 0) + base
    return jnp.where(position == key, 1.0, 0.0).astype(BF16)


def build_kernel(rows_ref, cols_ref, counts_ref, blocks_ref, dense_ref):
    chunks = dense_ref.shape[1]
    positions = chunks * CHUNK_COLS * BROWS
    base = pl.program_id(1) * positions
    onehot = one_hot(rows_ref, cols_ref, counts_ref, pl.program_id(0), 0, base, positions)

    def step(u, carry):
        cols = pl.ds(pl.multiple_of(u * 256, 256), 256)
        z = jnp.dot(onehot, blocks_ref[0, :, cols], preferred_element_type=F32)
        place(z, chunks, u, dense_ref, 0)
        return carry

    lax.fori_loop(0, BLK * BLK // 256, step, 0)


def build_whole_kernel(rows_ref, cols_ref, counts_ref, blocks_ref, dense_ref, held, arrived):
    layers, chunks = dense_ref.shape[:2]
    pieces = arrived.shape[1]
    width = held.shape[2] // pieces
    inner = width // 256

    def fetch(layer, piece):
        cols = pl.ds(pl.multiple_of(piece * width, width), width)
        return pltpu.make_async_copy(
            blocks_ref.at[layer, :, cols], held.at[layer, :, cols], arrived.at[layer, piece]
        )

    for layer in range(layers):
        for piece in range(pieces):
            fetch(layer, piece).start()
    flip = lax.axis_index("node") * CHUNK_COLS
    for layer in range(layers):
        onehot = one_hot(rows_ref, cols_ref, counts_ref, layer, flip, 0, chunks * CHUNK_COLS * BROWS)

        def step(piece, carry):
            fetch(layer, piece).wait()
            for v in range(inner):
                cols = pl.ds(pl.multiple_of(piece * width + v * 256, 256), 256)
                z = jnp.dot(onehot, held[layer, :, cols], preferred_element_type=F32)
                place(z, chunks, piece * inner + v, dense_ref, layer)
            return carry

        lax.fori_loop(0, pieces, step, 0)


def build_dense(block_rows, block_cols, counts, blocks, chunk_total):
    layers, slots, width = blocks.shape
    dense = jax.ShapeDtypeStruct((layers, chunk_total, 2 * TALL, CHUNK_LANES), BF16)
    operands = (block_rows, block_cols, counts.T, blocks)
    if chunk_total <= 4:
        operands = (*operands[:3], pltpu.with_memory_space_constraint(blocks, pltpu.HBM))
        pieces = 4
        return pl.pallas_call(
            build_whole_kernel,
            in_specs=vmem_specs(2)
            + [pl.BlockSpec(memory_space=pltpu.SMEM), pl.BlockSpec(memory_space=pltpu.HBM)],
            out_specs=pl.BlockSpec(memory_space=pltpu.VMEM),
            out_shape=dense,
            scratch_shapes=[pltpu.VMEM(blocks.shape, BF16), pltpu.SemaphoreType.DMA((layers, pieces))],
            compiler_params=params(28),
            name="build_dense",
        )(*operands)
    return pl.pallas_call(
        build_kernel,
        grid=(layers, chunk_total // 4),
        in_specs=vmem_specs(2)
        + [
            pl.BlockSpec(memory_space=pltpu.SMEM),
            pl.BlockSpec((1, slots, width), lambda l, s: (l, 0, 0)),
        ],
        out_specs=pl.BlockSpec((1, 4, 2 * TALL, CHUNK_LANES), lambda l, s: (l, s, 0, 0)),
        out_shape=dense,
        compiler_params=params(24),
        name="build_dense",
    )(*operands)


def split3(x):
    a = x.astype(BF16)
    r = x - a.astype(F32)
    b = r.astype(BF16)
    c = (r - b.astype(F32)).astype(BF16)
    return a, b, c


def image_part(basis, dense):
    k, width = basis.shape
    basis = basis.astype(F32)
    tall = jnp.concatenate([basis, basis, jnp.zeros((128 - 2 * k, width), F32)], axis=0).T
    lane = lax.broadcasted_iota(jnp.int32, tall.shape, 1)
    first = jnp.where(lane < k, tall, 0.0).astype(BF16)
    second = jnp.where(lane < k, 0.0, tall).astype(BF16)
    weights = []
    for c in range(width // BLK):
        weights += [first[c * BLK : c * BLK + BLK], second[c * BLK : c * BLK + BLK]]
    return jnp.dot(dense, jnp.concatenate(weights, axis=0), preferred_element_type=F32)


def to_wide(total, k, halves, tall):
    halves[...] = total[:TALL] + total[TALL:]
    for b in range(BROWS):
        part = halves[pl.ds(b, BLK // 2, stride=BROWS), :]
        tall[pl.ds(BLK * b, BLK // 2, stride=2), :] = part
        tall[pl.ds(BLK * b + 1, BLK // 2, stride=2), :] = pltpu.roll(part, 128 - k, 1)
    return tall[...].T[:k]


def against(left, tall):
    k = left.shape[0]
    lane = lax.broadcasted_iota(jnp.int32, tall.shape, 1)
    a, b, c = split3(jnp.where(lane < k, tall, 0.0))
    right = a.astype(F32) + pltpu.roll(b.astype(F32), k, 1) + pltpu.roll(c.astype(F32), 2 * k, 1)
    pieces = jnp.dot(jnp.concatenate(split3(left), axis=0), right.astype(BF16), preferred_element_type=F32)
    top, middle, bottom = pieces[:k], pieces[k : 2 * k], pieces[2 * k :]
    total = top[:, :k] + (top[:, k : 2 * k] + middle[:, :k])
    return total + (middle[:, k : 2 * k] + (top[:, 2 * k : 3 * k] + bottom[:, :k]))


def apply_kernel(mode, *refs):
    basis_ref, refs = refs[0], refs[1:]
    if mode == "score":
        left_ref, refs = refs[0], refs[1:]
    dense_ref, out_ref = refs[:2]
    halves, tall, acc = refs[-3:]
    layer, chunk = pl.program_id(0), pl.program_id(1)
    total = image_part(basis_ref[chunk, layer], dense_ref[0, 0])

    @pl.when(chunk == 0)
    def _():
        acc[...] = total

    @pl.when(chunk > 0)
    def _():
        acc[...] += total

    @pl.when(chunk == pl.num_programs(1) - 1)
    def _():
        image = to_wide(acc[...], basis_ref.shape[2], halves, tall)
        if mode != "score":
            out_ref[0] = image
        if mode == "gram":
            refs[2][0] = against(image, tall[...])
        if mode == "score":
            out_ref[0] = against(left_ref[0], tall[...])


def apply_whole_kernel(mode, piece_count, *refs):
    pieces, refs = refs[:piece_count], refs[piece_count:]
    if mode == "score":
        left_ref, refs = refs[0], refs[1:]
    dense_ref, out_ref = refs[:2]
    halves, tall = refs[-2:]
    for layer in range(dense_ref.shape[0]):
        total = sum(
            image_part(piece[layer], dense_ref[layer, chunk]) for chunk, piece in enumerate(pieces)
        )
        image = to_wide(total, pieces[0].shape[1], halves.at[layer], tall.at[layer])
        if mode != "score":
            out_ref[layer] = image
        if mode == "gram":
            refs[2][layer] = against(image, tall[layer])
        if mode == "score":
            out_ref[layer] = against(left_ref[layer], tall[layer])


def apply_dense(mode, pieces, dense, left=None):
    layers, chunks = dense.shape[:2]
    k = pieces[0].shape[-2]
    image = jax.ShapeDtypeStruct((layers, k, ROWS_DEV), F32)
    small = jax.ShapeDtypeStruct((layers, k, k), F32)
    out_shape = {"gram": [image, small], "plain": [image], "score": [small]}[mode]
    operands = list(pieces) + ([left] if mode == "score" else []) + [dense]
    if len(pieces) == chunks:
        return pl.pallas_call(
            functools.partial(apply_whole_kernel, mode, chunks),
            in_specs=vmem_specs(len(operands)),
            out_specs=vmem_specs(len(out_shape)),
            out_shape=out_shape,
            scratch_shapes=[pltpu.VMEM((layers, TALL, 128), F32), pltpu.VMEM((layers, ROWS_DEV, 128), F32)],
            compiler_params=params(14),
            name="apply_" + mode,
        )(*operands)
    dense_spec = pl.BlockSpec((1, 1, 2 * TALL, CHUNK_LANES), lambda l, s: (l, s, 0, 0))
    image_spec = pl.BlockSpec((1, k, ROWS_DEV), lambda l, s: (l, 0, 0))
    small_spec = pl.BlockSpec((1, k, k), lambda l, s: (l, 0, 0))
    return pl.pallas_call(
        functools.partial(apply_kernel, mode),
        grid=(layers, chunks),
        in_specs=vmem_specs(1) + ([image_spec] if mode == "score" else []) + [dense_spec],
        out_specs={"gram": [image_spec, small_spec], "plain": [image_spec], "score": [small_spec]}[mode],
        out_shape=out_shape,
        scratch_shapes=[
            pltpu.VMEM((TALL, 128), F32),
            pltpu.VMEM((ROWS_DEV, 128), F32),
            pltpu.VMEM((2 * TALL, 128), F32),
        ],
        compiler_params=params(12),
        name="apply_" + mode,
    )(*operands)


def spread(x):
    return jnp.broadcast_to(x, (8, 128))


def eliminate(rows, offset):
    groups, tiles = len(rows), len(rows[0])
    rows = [list(row) for row in rows]
    home, at = offset // 128, offset % 128
    sub = lax.broadcasted_iota(jnp.int32, (8, 128), 0)
    solved = []
    for h in range(groups):
        below = range(h + 1, groups)
        lane = at + 8 * h
        col = [{g: spread(rows[g][home][:, lane + q : lane + q + 1]) for g in range(h, groups)} for q in range(8)]
        cell = {(p, q): spread(col[p][h][q : q + 1]) for q in range(8) for p in range(q + 1)}
        row = [[spread(rows[h][t][q : q + 1]) for t in range(tiles)] for q in range(8)]
        done = []
        for m in range(0, 8, 2):
            n = m + 1
            a, b, c = cell[m, m], cell[m, n], cell[n, n]
            det = a * c - b * b
            r = pl.reciprocal(det, approx=True)
            later = range(m + 2, 8)
            u = {q: c * cell[m, q] - b * cell[n, q] for q in later}
            v = {q: a * cell[n, q] - b * cell[m, q] for q in later}
            for q in later:
                for p in range(m + 2, q + 1):
                    cell[p, q] = cell[p, q] - r * (cell[m, p] * u[q] + cell[n, p] * v[q])
            for q in later:
                for g in below:
                    col[q][g] = col[q][g] - r * (col[m][g] * u[q] + col[n][g] * v[q])
            for t in range(tiles):
                x = r * (c * row[m][t] - b * row[n][t])
                y = r * (a * row[n][t] - b * row[m][t])
                for q in later:
                    row[q][t] = row[q][t] - (cell[m, q] * x + cell[n, q] * y)
                for g in below:
                    rows[g][t] = rows[g][t] - (col[m][g] * x + col[n][g] * y)
            over = pl.reciprocal(a, approx=True)
            done.append([lax.rsqrt(a) * x for x in row[m]])
            scale = lax.rsqrt(det * over)
            done.append([scale * (x - (b * over) * w) for x, w in zip(row[n], row[m])])
        finished = []
        for t in range(tiles):
            x = done[7][t]
            for q in range(7):
                x = jnp.where(sub == q, done[q][t], x)
            finished.append(x)
        solved.append(finished)
    return solved


def tiled(x):
    return [
        [x[g * 8 : g * 8 + 8, t * 128 : t * 128 + 128] for t in range(x.shape[1] // 128)]
        for g in range(x.shape[0] // 8)
    ]


def joined(tiles):
    return jnp.concatenate([jnp.concatenate(row, axis=1) for row in tiles], axis=0)


def unit_scale(gram):
    lane = lax.broadcasted_iota(jnp.int32, gram.shape, 1)
    sub = lax.broadcasted_iota(jnp.int32, gram.shape, 0)
    kept = jnp.where(lane == sub, gram, 0.0)
    down = 1.0 / jnp.sqrt(jnp.sum(kept, axis=1, keepdims=True))
    across = jnp.sum(kept, axis=0, keepdims=True)
    across = 1.0 / jnp.sqrt(jnp.where(across == 0.0, 1.0, across))
    return gram * down * across, across


def gram_update(panel, first):
    a, b, c = split3(panel)
    left = jnp.concatenate([a, a, b, b, a, c], axis=0)
    right = jnp.concatenate([a, b, a, b, c, a], axis=0)
    parts = {
        at: lax.dot_general(left[:, at : at + 128], right, TRANS_A, preferred_element_type=F32)
        for at in range(first, panel.shape[1], 128)
    }
    return lambda at, count: parts[at // 128 * 128][at % 128 : at % 128 + count]


def solve_kernel(piece_count, *refs):
    grams, image_ref, out_ref = refs[:piece_count], refs[piece_count], refs[piece_count + 1]
    layers, k = image_ref.shape[:2]
    lane = lax.broadcasted_iota(jnp.int32, (k, 128), 1)
    sub = lax.broadcasted_iota(jnp.int32, (k, 128), 0)
    eye = jnp.where(lane == sub, 1.0, 0.0)
    for layer in range(layers):
        gram = sum(ref[layer] for ref in grams)
        gram = jnp.concatenate([gram, jnp.zeros((k, 128 - k), F32)], axis=1)
        gram, across = unit_scale(gram)
        solved = eliminate(tiled(jnp.concatenate([gram, eye], axis=1)), 0)
        inverse = joined(solved)[:, 128:] * across
        solved = jnp.dot(inverse[:, :k], image_ref[layer], precision=HIGHEST, preferred_element_type=F32)
        out_ref[layer] = solved.astype(BF16)


def solve(grams, image):
    return pl.pallas_call(
        functools.partial(solve_kernel, len(grams)),
        in_specs=vmem_specs(len(grams) + 1),
        out_specs=pl.BlockSpec(memory_space=pltpu.VMEM),
        out_shape=jax.ShapeDtypeStruct(image.shape, BF16),
        compiler_params=params(4),
        name="solve_layers",
    )(*grams, image)


def stack_rows(refs, scratch):
    g = lax.axis_index("layer")
    rows = scratch.shape[0] // len(refs)
    for d, ref in enumerate(refs):
        at = (g ^ d) * rows
        scratch[pl.ds(pl.multiple_of(at, rows), rows)] = ref[...].reshape(rows, ref.shape[-1])


def cross_kernel(own_ref, all_ref, out_ref):
    own = own_ref[...].reshape(-1, own_ref.shape[2])
    every = all_ref[...].reshape(-1, own_ref.shape[2])
    out_ref[...] = lax.dot_general(own, every, TRANS_B, precision=HIGHEST, preferred_element_type=F32)


def cross(own, every):
    rows = own.shape[0] * own.shape[1]
    return pl.pallas_call(
        cross_kernel,
        in_specs=vmem_specs(2),
        out_specs=pl.BlockSpec(memory_space=pltpu.VMEM),
        out_shape=jax.ShapeDtypeStruct((rows, every.shape[0] * every.shape[1]), F32),
        compiler_params=params(6),
        name="cross_gram",
    )(own, every)


def joint_kernel(piece_count, k, *refs):
    gram_refs, (images_ref, out_ref, again_ref, rounded_ref, work) = refs[:piece_count], refs[piece_count:]
    stack_rows(gram_refs, work)
    size = work.shape[0]
    steps = size // k
    lane = lax.broadcasted_iota(jnp.int32, (k, size), 1)
    lane_128 = lax.broadcasted_iota(jnp.int32, (k, 128), 1)
    sub_128 = lax.broadcasted_iota(jnp.int32, (k, 128), 0)
    gram, across = unit_scale(work[...])
    work[...] = gram
    for s in range(steps):
        lo, hi = s * k, (s + 1) * k
        here = (lane >= lo) & (lane < hi)
        eye = jnp.where(lane_128 == sub_128 + lo % 128, 1.0, 0.0)
        solved = joined(eliminate(tiled(jnp.concatenate([work[lo:hi], eye], axis=1)), lo))
        panel, tail = solved[:, :size], solved[:, size:]
        panel = jnp.where(here, jnp.concatenate([tail] * (size // 128), axis=1), panel)
        work[lo:hi] = jnp.where(lane < hi, panel, 0.0)
        if s + 1 < steps:
            update = gram_update(panel, hi // 128 * 128)
            for r in range(s + 1, steps):
                rows = work[r * k : r * k + k]
                work[r * k : r * k + k] = jnp.where(here, 0.0, rows) - update(r * k, k)
    rows = size // piece_count
    own = work[pl.ds(pl.multiple_of(lax.axis_index("layer") * rows, rows), rows)] * across
    images = images_ref[...].reshape(size, -1)
    joint = jnp.dot(own, images, precision=HIGHEST, preferred_element_type=F32)
    joint = joint.reshape(out_ref.shape)
    out_ref[...] = joint
    again_ref[...] = joint
    rounded_ref[...] = joint.astype(BF16)


def joint_solve(grams, images):
    groups = len(grams)
    _, k, width = images.shape
    size = grams[0].shape[1]
    shape = (images.shape[0] // groups, k, width)
    return pl.pallas_call(
        functools.partial(joint_kernel, groups, k),
        in_specs=vmem_specs(groups + 1),
        out_specs=vmem_specs(3),
        out_shape=[
            jax.ShapeDtypeStruct(shape, F32),
            jax.ShapeDtypeStruct(shape, F32),
            jax.ShapeDtypeStruct(shape, BF16),
        ],
        scratch_shapes=[pltpu.VMEM((size, size), F32)],
        compiler_params=params(8),
        name="joint_solve",
    )(*grams, images)


def around(x, axis, count):
    pieces = [x]
    for d in range(1, count):
        pieces.append(lax.ppermute(x, axis, [(m ^ d, m) for m in range(count)]))
    return pieces


def add_pieces(pieces):
    return (pieces[0] + pieces[1]) + (pieces[2] + pieces[3])


def per_device(shards, groups, blocks, block_rows, block_cols, counts, start):
    few = shards == 4

    def gather(x):
        return around(x, "node", shards) if few else [lax.all_gather(x, "node")]

    def partials(x):
        if not few:
            return [lax.psum(x, "node")]
        near = x + lax.ppermute(x, "node", [(m ^ 1, m) for m in range(shards)])
        return [near, lax.ppermute(near, "node", [(m ^ 2, m) for m in range(shards)])]

    def total(x):
        return add_pieces(around(x, "node", shards)) if few else lax.psum(x, "node")

    first = gather(start.astype(BF16))
    dense = build_dense(block_rows, block_cols, counts, blocks, shards * BROWS // CHUNK_COLS)
    image, gram = apply_dense("gram", first, dense)
    (image,) = apply_dense("plain", gather(solve(partials(gram), image)), dense)
    images = lax.all_gather(image, "layer", axis=0, tiled=True)
    grams = around(total(cross(image, images)), "layer", groups)
    joint_basis, again, rounded = joint_solve(grams, images)
    (partial,) = apply_dense("score", gather(rounded), dense, again)
    return joint_basis, sum(partials(partial))


def solution(mesh):
    in_specs = (
        P(("parts", "layer"), "node", None),
        P(("parts", "layer"), "node"),
        P(("parts", "layer"), "node"),
        P(("parts", "layer"), "node"),
        P(("parts", "layer"), None, "node"),
    )
    out_specs = (P(("parts", "layer"), None, "node"), P(("parts", "layer"), None, None))
    return jax.shard_map(
        functools.partial(per_device, mesh.shape["node"], mesh.shape["layer"]),
        mesh=mesh,
        in_specs=in_specs,
        out_specs=out_specs,
        check_vma=False,
    )
```

```python
import functools

import jax
import jax.numpy as jnp
from jax import lax
from jax.experimental import pallas as pl
from jax.experimental.pallas import tpu as pltpu
from jax.sharding import PartitionSpec as P

BLK = 64
ROWS_DEV = 512
BROWS = ROWS_DEV // BLK
CHUNK_COLS = 8
CHUNK_LANES = CHUNK_COLS * 2 * BLK
TALL = BROWS * BLK // 2
MIB = 1024 * 1024
F32 = jnp.float32
BF16 = jnp.bfloat16
HIGHEST = lax.Precision.HIGHEST
TRANS_B = (((1,), (1,)), ((), ()))
TRANS_A = (((0,), (0,)), ((), ()))


def params(mib):
    return pltpu.CompilerParams(vmem_limit_bytes=mib * MIB)


def vmem_specs(count):
    return [pl.BlockSpec(memory_space=pltpu.VMEM)] * count


def place(z, chunks, u, dense_ref, layer):
    for c in range(chunks * CHUNK_COLS):
        piece = z[c * 8 : c * 8 + 8]
        piece = jnp.concatenate([piece[:, :128], piece[:, 128:]], axis=0)
        hi = piece.astype(BF16)
        lo = (piece - hi.astype(F32)).astype(BF16)
        lanes = slice((c % CHUNK_COLS) * 128, (c % CHUNK_COLS) * 128 + 128)
        dense_ref[layer, c // CHUNK_COLS, pl.ds(pl.multiple_of(u * 16, 16), 16), lanes] = hi
        dense_ref[layer, c // CHUNK_COLS, pl.ds(pl.multiple_of(u * 16 + TALL, 16), 16), lanes] = lo


def one_hot(rows_ref, cols_ref, counts_ref, layer, flip, base, positions):
    slot = lax.broadcasted_iota(jnp.int32, (1, rows_ref.shape[1]), 1)
    key = (cols_ref[pl.ds(layer, 1), :] ^ flip) * BROWS + rows_ref[pl.ds(layer, 1), :]
    key = jnp.where(slot < counts_ref[0, layer], key, -1)
    position = lax.broadcasted_iota(jnp.int32, (positions, key.shape[1]), 0) + base
    return jnp.where(position == key, 1.0, 0.0).astype(BF16)


def build_kernel(rows_ref, cols_ref, counts_ref, blocks_ref, dense_ref):
    chunks = dense_ref.shape[1]
    positions = chunks * CHUNK_COLS * BROWS
    base = pl.program_id(1) * positions
    onehot = one_hot(rows_ref, cols_ref, counts_ref, pl.program_id(0), 0, base, positions)

    def step(u, carry):
        cols = pl.ds(pl.multiple_of(u * 256, 256), 256)
        z = jnp.dot(onehot, blocks_ref[0, :, cols], preferred_element_type=F32)
        place(z, chunks, u, dense_ref, 0)
        return carry

    lax.fori_loop(0, BLK * BLK // 256, step, 0)


def build_whole_kernel(
    rows_hbm, cols_hbm, counts_hbm, blocks_ref, dense_ref, held, rows_ref, cols_ref, counts_ref, arrived, index_arrived
):
    layers, chunks = dense_ref.shape[:2]
    index_copies = [
        pltpu.make_async_copy(source, target, index_arrived.at[i])
        for i, (source, target) in enumerate(
            [(rows_hbm, rows_ref), (cols_hbm, cols_ref), (counts_hbm, counts_ref)]
        )
    ]
    for copy in index_copies:
        copy.start()
    pieces = arrived.shape[1]
    width = held.shape[2] // pieces
    inner = width // 256

    def fetch(layer, piece):
        cols = pl.ds(pl.multiple_of(piece * width, width), width)
        return pltpu.make_async_copy(
            blocks_ref.at[layer, :, cols], held.at[layer, :, cols], arrived.at[layer, piece]
        )

    for layer in range(layers):
        for piece in range(pieces):
            fetch(layer, piece).start()
    flip = lax.axis_index("node") * CHUNK_COLS
    for copy in index_copies:
        copy.wait()
    for layer in range(layers):
        onehot = one_hot(rows_ref, cols_ref, counts_ref, layer, flip, 0, chunks * CHUNK_COLS * BROWS)

        def step(piece, carry):
            fetch(layer, piece).wait()
            for v in range(inner):
                cols = pl.ds(pl.multiple_of(piece * width + v * 256, 256), 256)
                z = jnp.dot(onehot, held[layer, :, cols], preferred_element_type=F32)
                place(z, chunks, piece * inner + v, dense_ref, layer)
            return carry

        lax.fori_loop(0, pieces, step, 0)


def build_dense(block_rows, block_cols, counts, blocks, chunk_total):
    layers, slots, width = blocks.shape
    dense = jax.ShapeDtypeStruct((layers, chunk_total, 2 * TALL, CHUNK_LANES), BF16)
    operands = (block_rows, block_cols, counts.T, blocks)
    if chunk_total <= 4:
        pieces = 4
        return pl.pallas_call(
            build_whole_kernel,
            in_specs=[pl.BlockSpec(memory_space=pltpu.HBM)] * 4,
            out_specs=pl.BlockSpec(memory_space=pltpu.VMEM),
            out_shape=dense,
            scratch_shapes=[
                pltpu.VMEM(blocks.shape, BF16),
                pltpu.VMEM(block_rows.shape, jnp.int32),
                pltpu.VMEM(block_cols.shape, jnp.int32),
                pltpu.SMEM((1, layers), jnp.int32),
                pltpu.SemaphoreType.DMA((layers, pieces)),
                pltpu.SemaphoreType.DMA((3,)),
            ],
            compiler_params=params(28),
            name="build_dense",
        )(*[pltpu.with_memory_space_constraint(x, pltpu.HBM) for x in operands])
    return pl.pallas_call(
        build_kernel,
        grid=(layers, chunk_total // 4),
        in_specs=vmem_specs(2)
        + [
            pl.BlockSpec(memory_space=pltpu.SMEM),
            pl.BlockSpec((1, slots, width), lambda l, s: (l, 0, 0)),
        ],
        out_specs=pl.BlockSpec((1, 4, 2 * TALL, CHUNK_LANES), lambda l, s: (l, s, 0, 0)),
        out_shape=dense,
        compiler_params=params(24),
        name="build_dense",
    )(*operands)


def split3(x):
    a = x.astype(BF16)
    r = x - a.astype(F32)
    b = r.astype(BF16)
    c = (r - b.astype(F32)).astype(BF16)
    return a, b, c


def image_part(basis, dense):
    k, width = basis.shape
    basis = basis.astype(F32)
    tall = jnp.concatenate([basis, basis], axis=0).T
    lane = lax.broadcasted_iota(jnp.int32, tall.shape, 1)
    first = jnp.where(lane < k, tall, 0.0).astype(BF16)
    second = jnp.where(lane < k, 0.0, tall).astype(BF16)
    weights = []
    for c in range(width // BLK):
        weights += [first[c * BLK : c * BLK + BLK], second[c * BLK : c * BLK + BLK]]
    return jnp.dot(dense, jnp.concatenate(weights, axis=0), preferred_element_type=F32)


def to_wide(total, k, halves, tall):
    halves[:, : 2 * k] = total[:TALL] + total[TALL:]
    halves[:, 2 * k :] = jnp.zeros((TALL, 128 - 2 * k), F32)
    for b in range(BROWS):
        part = halves[pl.ds(b, BLK // 2, stride=BROWS), :]
        tall[pl.ds(BLK * b, BLK // 2, stride=2), :] = part
        tall[pl.ds(BLK * b + 1, BLK // 2, stride=2), :] = pltpu.roll(part, 128 - k, 1)
    return tall[...].T[:k]


def against(left, tall):
    k = left.shape[0]
    lane = lax.broadcasted_iota(jnp.int32, tall.shape, 1)
    a, b, c = split3(jnp.where(lane < k, tall, 0.0))
    right = a.astype(F32) + pltpu.roll(b.astype(F32), k, 1) + pltpu.roll(c.astype(F32), 2 * k, 1)
    pieces = jnp.dot(jnp.concatenate(split3(left), axis=0), right.astype(BF16), preferred_element_type=F32)
    top, middle, bottom = pieces[:k], pieces[k : 2 * k], pieces[2 * k :]
    total = top[:, :k] + (top[:, k : 2 * k] + middle[:, :k])
    return total + (middle[:, k : 2 * k] + (top[:, 2 * k : 3 * k] + bottom[:, :k]))


def apply_kernel(mode, *refs):
    basis_ref, refs = refs[0], refs[1:]
    if mode == "score":
        left_ref, refs = refs[0], refs[1:]
    dense_ref, out_ref = refs[:2]
    halves, tall, acc = refs[-3:]
    layer, chunk = pl.program_id(0), pl.program_id(1)
    total = image_part(basis_ref[chunk, layer], dense_ref[0, 0])

    @pl.when(chunk == 0)
    def _():
        acc[...] = total

    @pl.when(chunk > 0)
    def _():
        acc[...] += total

    @pl.when(chunk == pl.num_programs(1) - 1)
    def _():
        image = to_wide(acc[...], basis_ref.shape[2], halves, tall)
        if mode != "score":
            out_ref[0] = image
        if mode == "gram":
            refs[2][0] = against(image, tall[...])
        if mode == "score":
            out_ref[0] = against(left_ref[0], tall[...])


def product(a, b):
    k = a.shape[0]
    left = jnp.concatenate(split3(a), axis=0)
    right = left if b is a else jnp.concatenate(split3(b), axis=0)
    pieces = lax.dot_general(left, right, TRANS_B, preferred_element_type=F32)
    top, middle, bottom = pieces[:k], pieces[k : 2 * k], pieces[2 * k :]
    total = top[:, :k] + (top[:, k : 2 * k] + middle[:, :k])
    return total + (middle[:, k : 2 * k] + (top[:, 2 * k : 3 * k] + bottom[:, :k]))


def apply_whole_kernel(mode, piece_count, *refs):
    pieces, refs = refs[:piece_count], refs[piece_count:]
    if mode == "score":
        left_ref, refs = refs[0], refs[1:]
    dense_ref, out_ref, halves, tall = refs
    layers, k = pieces[0].shape[:2]
    if mode == "solved":
        images = [jnp.concatenate([piece[layer] for piece in pieces], axis=1) for layer in range(layers)]
        grams = [product(image, image) for image in images]
        inverses = [inverse_factor(gram) for gram in grams]
        bases = [
            jnp.dot(inverse, image, precision=HIGHEST, preferred_element_type=F32)
            for inverse, image in zip(inverses, images)
        ]
        parts = [[basis[:, d * ROWS_DEV : d * ROWS_DEV + ROWS_DEV] for d in range(piece_count)] for basis in bases]
    else:
        parts = [[piece[layer] for piece in pieces] for layer in range(layers)]
    totals = [
        sum(image_part(part, dense_ref[layer, chunk]) for chunk, part in enumerate(parts[layer]))
        for layer in range(layers)
    ]
    wide = [to_wide(totals[layer], k, halves.at[layer], tall.at[layer]) for layer in range(layers)]
    for layer in range(layers):
        out_ref[layer] = product(left_ref[layer], wide[layer]) if mode == "score" else wide[layer]


def apply_dense(mode, pieces, dense, left=None):
    layers, chunks = dense.shape[:2]
    k = pieces[0].shape[-2]
    image = jax.ShapeDtypeStruct((layers, k, ROWS_DEV), F32)
    small = jax.ShapeDtypeStruct((layers, k, k), F32)
    out_shape = {"gram": [image, small], "plain": [image], "solved": [image], "score": [small]}[mode]
    operands = list(pieces) + ([left] if mode == "score" else []) + [dense]
    if len(pieces) == chunks:
        return pl.pallas_call(
            functools.partial(apply_whole_kernel, mode, chunks),
            in_specs=vmem_specs(len(operands)),
            out_specs=vmem_specs(len(out_shape)),
            out_shape=out_shape,
            scratch_shapes=[pltpu.VMEM((layers, TALL, 128), F32), pltpu.VMEM((layers, ROWS_DEV, 128), F32)],
            compiler_params=params(14),
            name="apply_" + mode,
        )(*operands)
    dense_spec = pl.BlockSpec((1, 1, 2 * TALL, CHUNK_LANES), lambda l, s: (l, s, 0, 0))
    image_spec = pl.BlockSpec((1, k, ROWS_DEV), lambda l, s: (l, 0, 0))
    small_spec = pl.BlockSpec((1, k, k), lambda l, s: (l, 0, 0))
    return pl.pallas_call(
        functools.partial(apply_kernel, mode),
        grid=(layers, chunks),
        in_specs=vmem_specs(1) + ([image_spec] if mode == "score" else []) + [dense_spec],
        out_specs={"gram": [image_spec, small_spec], "plain": [image_spec], "score": [small_spec]}[mode],
        out_shape=out_shape,
        scratch_shapes=[
            pltpu.VMEM((TALL, 128), F32),
            pltpu.VMEM((ROWS_DEV, 128), F32),
            pltpu.VMEM((2 * TALL, 2 * k), F32),
        ],
        compiler_params=params(12),
        name="apply_" + mode,
    )(*operands)


def spread(x):
    return jnp.broadcast_to(x, (8, 128))


def eliminate(rows, offset):
    groups, tiles = len(rows), len(rows[0])
    rows = [list(row) for row in rows]
    home, at = offset // 128, offset % 128
    sub = lax.broadcasted_iota(jnp.int32, (8, 128), 0)
    solved = []
    for h in range(groups):
        below = range(h + 1, groups)
        lane = at + 8 * h
        col = [{g: spread(rows[g][home][:, lane + q : lane + q + 1]) for g in range(h, groups)} for q in range(8)]
        cell = {(p, q): spread(col[p][h][q : q + 1]) for q in range(8) for p in range(q + 1)}
        row = [[spread(rows[h][t][q : q + 1]) for t in range(tiles)] for q in range(8)]
        done = []
        for m in range(0, 8, 2):
            n = m + 1
            a, b, c = cell[m, m], cell[m, n], cell[n, n]
            det = a * c - b * b
            r = pl.reciprocal(det, approx=True)
            later = range(m + 2, 8)
            u = {q: c * cell[m, q] - b * cell[n, q] for q in later}
            v = {q: a * cell[n, q] - b * cell[m, q] for q in later}
            for q in later:
                for p in range(m + 2, q + 1):
                    cell[p, q] = cell[p, q] - r * (cell[m, p] * u[q] + cell[n, p] * v[q])
            for q in later:
                for g in below:
                    col[q][g] = col[q][g] - r * (col[m][g] * u[q] + col[n][g] * v[q])
            for t in range(tiles):
                x = r * (c * row[m][t] - b * row[n][t])
                y = r * (a * row[n][t] - b * row[m][t])
                for q in later:
                    row[q][t] = row[q][t] - (cell[m, q] * x + cell[n, q] * y)
                for g in below:
                    rows[g][t] = rows[g][t] - (col[m][g] * x + col[n][g] * y)
            over = pl.reciprocal(a, approx=True)
            done.append([lax.rsqrt(a) * x for x in row[m]])
            scale = lax.rsqrt(det * over)
            done.append([scale * (x - (b * over) * w) for x, w in zip(row[n], row[m])])
        finished = []
        for t in range(tiles):
            x = done[7][t]
            for q in range(7):
                x = jnp.where(sub == q, done[q][t], x)
            finished.append(x)
        solved.append(finished)
    return solved


def tiled(x):
    return [
        [x[g * 8 : g * 8 + 8, t * 128 : t * 128 + 128] for t in range(x.shape[1] // 128)]
        for g in range(x.shape[0] // 8)
    ]


def joined(tiles):
    return jnp.concatenate([jnp.concatenate(row, axis=1) for row in tiles], axis=0)


def unit_scale(gram):
    lane = lax.broadcasted_iota(jnp.int32, gram.shape, 1)
    sub = lax.broadcasted_iota(jnp.int32, gram.shape, 0)
    kept = jnp.where(lane == sub, gram, 0.0)
    down = 1.0 / jnp.sqrt(jnp.sum(kept, axis=1, keepdims=True))
    across = jnp.sum(kept, axis=0, keepdims=True)
    across = 1.0 / jnp.sqrt(jnp.where(across == 0.0, 1.0, across))
    return gram * down * across, across


def gram_update(panel, first):
    a, b, c = split3(panel)
    left = jnp.concatenate([a, a, b, b, a, c], axis=0)
    right = jnp.concatenate([a, b, a, b, c, a], axis=0)
    parts = {
        at: lax.dot_general(left[:, at : at + 128], right, TRANS_A, preferred_element_type=F32)
        for at in range(first, panel.shape[1], 128)
    }
    return lambda at, count: parts[at // 128 * 128][at % 128 : at % 128 + count]


def inverse_factor(gram):
    k = gram.shape[0]
    lane = lax.broadcasted_iota(jnp.int32, (k, 128), 1)
    sub = lax.broadcasted_iota(jnp.int32, (k, 128), 0)
    eye = jnp.where(lane == sub, 1.0, 0.0)
    gram, across = unit_scale(jnp.concatenate([gram, jnp.zeros((k, 128 - k), F32)], axis=1))
    solved = eliminate(tiled(jnp.concatenate([gram, eye], axis=1)), 0)
    return (joined(solved)[:, 128:] * across)[:, :k]


def solve_kernel(gram_ref, image_ref, out_ref):
    for layer in range(image_ref.shape[0]):
        inverse = inverse_factor(gram_ref[layer])
        solved = jnp.dot(inverse, image_ref[layer], precision=HIGHEST, preferred_element_type=F32)
        out_ref[layer] = solved.astype(BF16)


def solve(gram, image):
    return pl.pallas_call(
        solve_kernel,
        in_specs=vmem_specs(2),
        out_specs=pl.BlockSpec(memory_space=pltpu.VMEM),
        out_shape=jax.ShapeDtypeStruct(image.shape, BF16),
        compiler_params=params(4),
        name="solve_layers",
    )(gram, image)


def cross_kernel(k, all_ref, out_ref):
    every = all_ref[...].reshape(-1, all_ref.shape[2])
    gram = lax.dot_general(every, every, TRANS_B, precision=HIGHEST, preferred_element_type=F32)
    half = gram.shape[0] // 2
    first, last = gram[:half, :half], gram[half:, half:]
    row = lax.broadcasted_iota(jnp.int32, (half, half), 0) // k
    col = lax.broadcasted_iota(jnp.int32, (half, half), 1) // k
    out_ref[:half] = gram[:half, half:]
    out_ref[half : 2 * half] = jnp.where(col >= row, first, last)
    diagonal = jnp.where(col == row, last, 0.0)
    out_ref[2 * half :] = sum(diagonal[r * k : r * k + k] for r in range(half // k))


def cross(every):
    _, k, _ = every.shape
    half = every.shape[0] * k // 2
    return pl.pallas_call(
        functools.partial(cross_kernel, k),
        in_specs=vmem_specs(1),
        out_specs=pl.BlockSpec(memory_space=pltpu.VMEM),
        out_shape=jax.ShapeDtypeStruct((2 * half + k, half), F32),
        compiler_params=params(6),
        name="cross_gram",
    )(every)


def unpack(packed, k, work):
    half = packed.shape[1]
    row = lax.broadcasted_iota(jnp.int32, (half, half), 0) // k
    col = lax.broadcasted_iota(jnp.int32, (half, half), 1) // k
    mixed = packed[half : 2 * half]
    under = jnp.where(col < row, mixed, 0.0)
    diagonal = jnp.concatenate([packed[2 * half :]] * (half // k), axis=0)
    work[:half, :half] = jnp.where(col >= row, mixed, 0.0)
    work[:half, half:] = packed[:half]
    work[half:, :half] = jnp.zeros((half, half), F32)
    work[half:, half:] = under.T + jnp.where(col == row, diagonal, 0.0)


def joint_kernel(piece_count, k, *refs):
    packed_refs, (images_ref, out_ref, again_ref, rounded_ref, work) = refs[:piece_count], refs[piece_count:]
    unpack(add_pieces([ref[...] for ref in packed_refs]), k, work)
    size = work.shape[0]
    steps = size // k
    lane = lax.broadcasted_iota(jnp.int32, (k, size), 1)
    lane_128 = lax.broadcasted_iota(jnp.int32, (k, 128), 1)
    sub_128 = lax.broadcasted_iota(jnp.int32, (k, 128), 0)
    gram, across = unit_scale(work[...])
    work[...] = gram
    for s in range(steps):
        lo, hi = s * k, (s + 1) * k
        here = (lane >= lo) & (lane < hi)
        eye = jnp.where(lane_128 == sub_128 + lo % 128, 1.0, 0.0)
        solved = joined(eliminate(tiled(jnp.concatenate([work[lo:hi], eye], axis=1)), lo))
        panel, tail = solved[:, :size], solved[:, size:]
        panel = jnp.where(here, jnp.concatenate([tail] * (size // 128), axis=1), panel)
        work[lo:hi] = jnp.where(lane < hi, panel, 0.0)
        if s + 1 < steps:
            update = gram_update(panel, hi // 128 * 128)
            for r in range(s + 1, steps):
                rows = work[r * k : r * k + k]
                work[r * k : r * k + k] = jnp.where(here, 0.0, rows) - update(r * k, k)
    rows = out_ref.shape[0] * k
    own = work[pl.ds(pl.multiple_of(lax.axis_index("layer") * rows, rows), rows)] * across
    images = images_ref[...].reshape(size, -1)
    joint = jnp.dot(own, images, precision=HIGHEST, preferred_element_type=F32)
    joint = joint.reshape(out_ref.shape)
    out_ref[...] = joint
    again_ref[...] = joint
    rounded_ref[...] = joint.astype(BF16)


def joint_solve(packed, images, layers):
    _, k, width = images.shape
    size = images.shape[0] * k
    shape = (layers, k, width)
    return pl.pallas_call(
        functools.partial(joint_kernel, len(packed), k),
        in_specs=vmem_specs(len(packed) + 1),
        out_specs=vmem_specs(3),
        out_shape=[
            jax.ShapeDtypeStruct(shape, F32),
            jax.ShapeDtypeStruct(shape, F32),
            jax.ShapeDtypeStruct(shape, BF16),
        ],
        scratch_shapes=[pltpu.VMEM((size, size), F32)],
        compiler_params=params(8),
        name="joint_solve",
    )(*packed, images)


def around(x, axis, count):
    pieces = [x]
    for d in range(1, count):
        pieces.append(lax.ppermute(x, axis, [(m ^ d, m) for m in range(count)]))
    return pieces


def add_pieces(pieces):
    if len(pieces) == 1:
        return pieces[0]
    return (pieces[0] + pieces[1]) + (pieces[2] + pieces[3])


def per_device(shards, blocks, block_rows, block_cols, counts, start):
    few = shards == 4

    def gather(x):
        return around(x, "node", shards) if few else [lax.all_gather(x, "node")]

    def partials(x):
        return around(x, "node", shards) if few else [lax.psum(x, "node")]

    first = gather(start if few else start.astype(BF16))
    dense = build_dense(block_rows, block_cols, counts, blocks, shards * BROWS // CHUNK_COLS)
    if few:
        (image,) = apply_dense("plain", first, dense)
        (image,) = apply_dense("solved", gather(image), dense)
    else:
        image, gram = apply_dense("gram", first, dense)
        (image,) = apply_dense("plain", gather(solve(lax.psum(gram, "node"), image)), dense)
    images = lax.all_gather(image, "layer", axis=0, tiled=True)
    joint_basis, again, rounded = joint_solve(partials(cross(images)), images, start.shape[0])
    (partial,) = apply_dense("score", gather(rounded), dense, again)
    return joint_basis, add_pieces(partials(partial))


def solution(mesh):
    in_specs = (
        P(("parts", "layer"), "node", None),
        P(("parts", "layer"), "node"),
        P(("parts", "layer"), "node"),
        P(("parts", "layer"), "node"),
        P(("parts", "layer"), None, "node"),
    )
    out_specs = (P(("parts", "layer"), None, "node"), P(("parts", "layer"), None, None))
    return jax.shard_map(
        functools.partial(per_device, mesh.shape["node"]),
        mesh=mesh,
        in_specs=in_specs,
        out_specs=out_specs,
        check_vma=False,
    )
```

```python
import functools

import jax
import jax.numpy as jnp
from jax import lax
from jax.experimental import pallas as pl
from jax.experimental.pallas import tpu as pltpu
from jax.sharding import PartitionSpec as P

BLK = 64
ROWS_DEV = 512
BROWS = ROWS_DEV // BLK
CHUNK_COLS = 8
CHUNK_LANES = CHUNK_COLS * 2 * BLK
TALL = BROWS * BLK // 2
MIB = 1024 * 1024
F32 = jnp.float32
BF16 = jnp.bfloat16
HIGHEST = lax.Precision.HIGHEST
TRANS_B = (((1,), (1,)), ((), ()))
TRANS_A = (((0,), (0,)), ((), ()))


def params(mib):
    return pltpu.CompilerParams(vmem_limit_bytes=mib * MIB)


def vmem_specs(count):
    return [pl.BlockSpec(memory_space=pltpu.VMEM)] * count


def place(z, chunks, u, dense_ref):
    for c in range(chunks * CHUNK_COLS):
        piece = z[c * 8 : c * 8 + 8]
        piece = jnp.concatenate([piece[:, :128], piece[:, 128:]], axis=0)
        hi = piece.astype(BF16)
        lo = (piece - hi.astype(F32)).astype(BF16)
        lanes = slice((c % CHUNK_COLS) * 128, (c % CHUNK_COLS) * 128 + 128)
        dense_ref[c // CHUNK_COLS, pl.ds(pl.multiple_of(u * 16, 16), 16), lanes] = hi
        dense_ref[c // CHUNK_COLS, pl.ds(pl.multiple_of(u * 16 + TALL, 16), 16), lanes] = lo


def one_hot(rows_ref, cols_ref, counts_ref, layer, flip, base, positions):
    slot = lax.broadcasted_iota(jnp.int32, (1, rows_ref.shape[1]), 1)
    key = (cols_ref[pl.ds(layer, 1), :] ^ flip) * BROWS + rows_ref[pl.ds(layer, 1), :]
    key = jnp.where(slot < counts_ref[0, layer], key, -1)
    position = lax.broadcasted_iota(jnp.int32, (positions, key.shape[1]), 0) + base
    return jnp.where(position == key, 1.0, 0.0).astype(BF16)


def build_kernel(rows_ref, cols_ref, counts_ref, blocks_ref, dense_ref):
    chunks = dense_ref.shape[1]
    positions = chunks * CHUNK_COLS * BROWS
    base = pl.program_id(1) * positions
    onehot = one_hot(rows_ref, cols_ref, counts_ref, pl.program_id(0), 0, base, positions)

    def step(u, carry):
        cols = pl.ds(pl.multiple_of(u * 256, 256), 256)
        z = jnp.dot(onehot, blocks_ref[0, :, cols], preferred_element_type=F32)
        place(z, chunks, u, dense_ref.at[0])
        return carry

    lax.fori_loop(0, BLK * BLK // 256, step, 0)


def build_whole_kernel(rows_hbm, cols_hbm, counts_hbm, blocks_ref, *refs):
    *dense_refs, held, rows_ref, cols_ref, counts_ref, arrived, index_arrived = refs
    layers, chunks = len(dense_refs), dense_refs[0].shape[0]
    index_copies = [
        pltpu.make_async_copy(source, target, index_arrived.at[i])
        for i, (source, target) in enumerate(
            [(rows_hbm, rows_ref), (cols_hbm, cols_ref), (counts_hbm, counts_ref)]
        )
    ]
    for copy in index_copies:
        copy.start()
    pieces = arrived.shape[1]
    width = held.shape[2] // pieces
    inner = width // 256

    def fetch(layer, piece):
        cols = pl.ds(pl.multiple_of(piece * width, width), width)
        return pltpu.make_async_copy(
            blocks_ref.at[layer, :, cols], held.at[layer, :, cols], arrived.at[layer, piece]
        )

    for layer in range(layers):
        for piece in range(pieces):
            fetch(layer, piece).start()
    flip = lax.axis_index("node") * CHUNK_COLS
    for copy in index_copies:
        copy.wait()
    for layer in range(layers):
        onehot = one_hot(rows_ref, cols_ref, counts_ref, layer, flip, 0, chunks * CHUNK_COLS * BROWS)

        def step(piece, carry):
            fetch(layer, piece).wait()
            for v in range(inner):
                cols = pl.ds(pl.multiple_of(piece * width + v * 256, 256), 256)
                z = jnp.dot(onehot, held[layer, :, cols], preferred_element_type=F32)
                place(z, chunks, piece * inner + v, dense_refs[layer])
            return carry

        lax.fori_loop(0, pieces, step, 0)


def build_dense(block_rows, block_cols, counts, blocks, chunk_total):
    layers, slots, width = blocks.shape
    dense = jax.ShapeDtypeStruct((layers, chunk_total, 2 * TALL, CHUNK_LANES), BF16)
    operands = (block_rows, block_cols, counts.T, blocks)
    if chunk_total <= 4:
        pieces = 4
        return pl.pallas_call(
            build_whole_kernel,
            in_specs=[pl.BlockSpec(memory_space=pltpu.HBM)] * 4,
            out_specs=vmem_specs(layers),
            out_shape=[jax.ShapeDtypeStruct(dense.shape[1:], BF16)] * layers,
            scratch_shapes=[
                pltpu.VMEM(blocks.shape, BF16),
                pltpu.VMEM(block_rows.shape, jnp.int32),
                pltpu.VMEM(block_cols.shape, jnp.int32),
                pltpu.SMEM((1, layers), jnp.int32),
                pltpu.SemaphoreType.DMA((layers, pieces)),
                pltpu.SemaphoreType.DMA((3,)),
            ],
            compiler_params=params(28),
            name="build_dense",
        )(*[pltpu.with_memory_space_constraint(x, pltpu.HBM) for x in operands])
    return pl.pallas_call(
        build_kernel,
        grid=(layers, chunk_total // 4),
        in_specs=vmem_specs(2)
        + [
            pl.BlockSpec(memory_space=pltpu.SMEM),
            pl.BlockSpec((1, slots, width), lambda l, s: (l, 0, 0)),
        ],
        out_specs=pl.BlockSpec((1, 4, 2 * TALL, CHUNK_LANES), lambda l, s: (l, s, 0, 0)),
        out_shape=dense,
        compiler_params=params(24),
        name="build_dense",
    )(*operands)


def split3(x):
    a = x.astype(BF16)
    r = x - a.astype(F32)
    b = r.astype(BF16)
    c = (r - b.astype(F32)).astype(BF16)
    return a, b, c


def image_part(basis, dense):
    k, width = basis.shape
    basis = basis.astype(F32)
    tall = jnp.concatenate([basis, basis], axis=0).T
    lane = lax.broadcasted_iota(jnp.int32, tall.shape, 1)
    first = jnp.where(lane < k, tall, 0.0).astype(BF16)
    second = jnp.where(lane < k, 0.0, tall).astype(BF16)
    weights = []
    for c in range(width // BLK):
        weights += [first[c * BLK : c * BLK + BLK], second[c * BLK : c * BLK + BLK]]
    return jnp.dot(dense, jnp.concatenate(weights, axis=0), preferred_element_type=F32)


def to_wide(total, k, halves, tall):
    halves[:, : 2 * k] = total[:TALL] + total[TALL:]
    halves[:, 2 * k :] = jnp.zeros((TALL, 128 - 2 * k), F32)
    for b in range(BROWS):
        part = halves[pl.ds(b, BLK // 2, stride=BROWS), :]
        tall[pl.ds(BLK * b, BLK // 2, stride=2), :] = part
        tall[pl.ds(BLK * b + 1, BLK // 2, stride=2), :] = pltpu.roll(part, 128 - k, 1)
    return tall[...].T[:k]


def against(left, tall):
    k = left.shape[0]
    lane = lax.broadcasted_iota(jnp.int32, tall.shape, 1)
    a, b, c = split3(jnp.where(lane < k, tall, 0.0))
    right = a.astype(F32) + pltpu.roll(b.astype(F32), k, 1) + pltpu.roll(c.astype(F32), 2 * k, 1)
    pieces = jnp.dot(jnp.concatenate(split3(left), axis=0), right.astype(BF16), preferred_element_type=F32)
    top, middle, bottom = pieces[:k], pieces[k : 2 * k], pieces[2 * k :]
    total = top[:, :k] + (top[:, k : 2 * k] + middle[:, :k])
    return total + (middle[:, k : 2 * k] + (top[:, 2 * k : 3 * k] + bottom[:, :k]))


def apply_kernel(mode, *refs):
    basis_ref, refs = refs[0], refs[1:]
    if mode == "score":
        left_ref, refs = refs[0], refs[1:]
    dense_ref, out_ref = refs[:2]
    halves, tall, acc = refs[-3:]
    layer, chunk = pl.program_id(0), pl.program_id(1)
    total = image_part(basis_ref[chunk, layer], dense_ref[0, 0])

    @pl.when(chunk == 0)
    def _():
        acc[...] = total

    @pl.when(chunk > 0)
    def _():
        acc[...] += total

    @pl.when(chunk == pl.num_programs(1) - 1)
    def _():
        image = to_wide(acc[...], basis_ref.shape[2], halves, tall)
        if mode != "score":
            out_ref[0] = image
        if mode == "gram":
            refs[2][0] = against(image, tall[...])
        if mode == "score":
            out_ref[0] = against(left_ref[0], tall[...])


def product(a, b):
    k = a.shape[0]
    left = jnp.concatenate(split3(a), axis=0)
    right = left if b is a else jnp.concatenate(split3(b), axis=0)
    pieces = lax.dot_general(left, right, TRANS_B, preferred_element_type=F32)
    top, middle, bottom = pieces[:k], pieces[k : 2 * k], pieces[2 * k :]
    total = top[:, :k] + (top[:, k : 2 * k] + middle[:, :k])
    return total + (middle[:, k : 2 * k] + (top[:, 2 * k : 3 * k] + bottom[:, :k]))


def image_of(parts, dense_ref):
    return sum(image_part(part, dense_ref[chunk]) for chunk, part in enumerate(parts))


def first_kernel(layer, piece_count, *refs):
    pieces, (dense_ref, out_ref, halves, tall) = refs[:piece_count], refs[piece_count:]
    total = image_of([piece[layer] for piece in pieces], dense_ref)
    out_ref[...] = to_wide(total, out_ref.shape[0], halves, tall)


def second_kernel(piece_count, *refs):
    pieces, (dense_ref, out_ref, halves, tall) = refs[:piece_count], refs[piece_count:]
    image = jnp.concatenate([piece[...] for piece in pieces], axis=1)
    inverse = inverse_factor(product(image, image))
    basis = jnp.dot(inverse, image, precision=HIGHEST, preferred_element_type=F32)
    parts = [basis[:, d * ROWS_DEV : d * ROWS_DEV + ROWS_DEV] for d in range(piece_count)]
    out_ref[...] = to_wide(image_of(parts, dense_ref), out_ref.shape[0], halves, tall)


def score_kernel(layers, piece_count, *refs):
    pieces, left_ref, refs = refs[:piece_count], refs[piece_count], refs[piece_count + 1 :]
    dense_refs, (out_ref, halves, tall) = refs[:layers], refs[layers:]
    totals = [image_of([piece[layer] for piece in pieces], dense_refs[layer]) for layer in range(layers)]
    wide = [
        to_wide(totals[layer], left_ref.shape[1], halves.at[layer], tall.at[layer]) for layer in range(layers)
    ]
    for layer in range(layers):
        out_ref[layer] = product(left_ref[layer], wide[layer])


def apply_whole(kernel, name, operands, out_shape, *lead):
    return pl.pallas_call(
        kernel,
        in_specs=vmem_specs(len(operands)),
        out_specs=pl.BlockSpec(memory_space=pltpu.VMEM),
        out_shape=jax.ShapeDtypeStruct(out_shape, F32),
        scratch_shapes=[pltpu.VMEM((*lead, TALL, 128), F32), pltpu.VMEM((*lead, ROWS_DEV, 128), F32)],
        compiler_params=params(14),
        cost_estimate=pl.CostEstimate(flops=0, bytes_accessed=4 * MIB, transcendentals=0),
        name=name,
    )(*operands)


def apply_first(layer, pieces, dense):
    kernel = functools.partial(first_kernel, layer, len(pieces))
    return apply_whole(kernel, "apply_first", [*pieces, dense], pieces[0].shape[1:])


def apply_second(pieces, dense):
    kernel = functools.partial(second_kernel, len(pieces))
    return apply_whole(kernel, "apply_second", [*pieces, dense], pieces[0].shape)


def apply_score(pieces, left, dense):
    kernel = functools.partial(score_kernel, len(dense), len(pieces))
    layers, k = left.shape[:2]
    return apply_whole(kernel, "apply_score", [*pieces, left, *dense], (layers, k, k), layers)


def apply_dense(mode, basis, dense, left=None):
    layers, chunks = dense.shape[:2]
    k = basis.shape[-2]
    image = jax.ShapeDtypeStruct((layers, k, ROWS_DEV), F32)
    small = jax.ShapeDtypeStruct((layers, k, k), F32)
    out_shape = {"gram": [image, small], "plain": [image], "score": [small]}[mode]
    operands = [basis] + ([left] if mode == "score" else []) + [dense]
    dense_spec = pl.BlockSpec((1, 1, 2 * TALL, CHUNK_LANES), lambda l, s: (l, s, 0, 0))
    image_spec = pl.BlockSpec((1, k, ROWS_DEV), lambda l, s: (l, 0, 0))
    small_spec = pl.BlockSpec((1, k, k), lambda l, s: (l, 0, 0))
    return pl.pallas_call(
        functools.partial(apply_kernel, mode),
        grid=(layers, chunks),
        in_specs=vmem_specs(1) + ([image_spec] if mode == "score" else []) + [dense_spec],
        out_specs={"gram": [image_spec, small_spec], "plain": [image_spec], "score": [small_spec]}[mode],
        out_shape=out_shape,
        scratch_shapes=[
            pltpu.VMEM((TALL, 128), F32),
            pltpu.VMEM((ROWS_DEV, 128), F32),
            pltpu.VMEM((2 * TALL, 2 * k), F32),
        ],
        compiler_params=params(12),
        name="apply_" + mode,
    )(*operands)


def spread(x):
    return jnp.broadcast_to(x, (8, 128))


def eliminate(rows, offset):
    groups, tiles = len(rows), len(rows[0])
    rows = [list(row) for row in rows]
    home, at = offset // 128, offset % 128
    sub = lax.broadcasted_iota(jnp.int32, (8, 128), 0)
    solved = []
    for h in range(groups):
        below = range(h + 1, groups)
        lane = at + 8 * h
        col = [{g: spread(rows[g][home][:, lane + q : lane + q + 1]) for g in range(h, groups)} for q in range(8)]
        cell = {(p, q): spread(col[p][h][q : q + 1]) for q in range(8) for p in range(q + 1)}
        row = [[spread(rows[h][t][q : q + 1]) for t in range(tiles)] for q in range(8)]
        done = []
        for m in range(0, 8, 2):
            n = m + 1
            a, b, c = cell[m, m], cell[m, n], cell[n, n]
            det = a * c - b * b
            r = pl.reciprocal(det, approx=True)
            later = range(m + 2, 8)
            u = {q: c * cell[m, q] - b * cell[n, q] for q in later}
            v = {q: a * cell[n, q] - b * cell[m, q] for q in later}
            for q in later:
                for p in range(m + 2, q + 1):
                    cell[p, q] = cell[p, q] - r * (cell[m, p] * u[q] + cell[n, p] * v[q])
            for q in later:
                for g in below:
                    col[q][g] = col[q][g] - r * (col[m][g] * u[q] + col[n][g] * v[q])
            for t in range(tiles):
                x = r * (c * row[m][t] - b * row[n][t])
                y = r * (a * row[n][t] - b * row[m][t])
                for q in later:
                    row[q][t] = row[q][t] - (cell[m, q] * x + cell[n, q] * y)
                for g in below:
                    rows[g][t] = rows[g][t] - (col[m][g] * x + col[n][g] * y)
            over = pl.reciprocal(a, approx=True)
            done.append([lax.rsqrt(a) * x for x in row[m]])
            scale = lax.rsqrt(det * over)
            done.append([scale * (x - (b * over) * w) for x, w in zip(row[n], row[m])])
        finished = []
        for t in range(tiles):
            x = done[7][t]
            for q in range(7):
                x = jnp.where(sub == q, done[q][t], x)
            finished.append(x)
        solved.append(finished)
    return solved


def tiled(x):
    return [
        [x[g * 8 : g * 8 + 8, t * 128 : t * 128 + 128] for t in range(x.shape[1] // 128)]
        for g in range(x.shape[0] // 8)
    ]


def joined(tiles):
    return jnp.concatenate([jnp.concatenate(row, axis=1) for row in tiles], axis=0)


def unit_scale(gram):
    lane = lax.broadcasted_iota(jnp.int32, gram.shape, 1)
    sub = lax.broadcasted_iota(jnp.int32, gram.shape, 0)
    kept = jnp.where(lane == sub, gram, 0.0)
    down = 1.0 / jnp.sqrt(jnp.sum(kept, axis=1, keepdims=True))
    across = jnp.sum(kept, axis=0, keepdims=True)
    across = 1.0 / jnp.sqrt(jnp.where(across == 0.0, 1.0, across))
    return gram * down * across, across


def gram_update(panel, first):
    a, b, c = split3(panel)
    left = jnp.concatenate([a, a, b, b, a, c], axis=0)
    right = jnp.concatenate([a, b, a, b, c, a], axis=0)
    parts = {
        at: lax.dot_general(left[:, at : at + 128], right, TRANS_A, preferred_element_type=F32)
        for at in range(first, panel.shape[1], 128)
    }
    return lambda at, count: parts[at // 128 * 128][at % 128 : at % 128 + count]


def inverse_factor(gram):
    k = gram.shape[0]
    lane = lax.broadcasted_iota(jnp.int32, (k, 128), 1)
    sub = lax.broadcasted_iota(jnp.int32, (k, 128), 0)
    eye = jnp.where(lane == sub, 1.0, 0.0)
    gram, across = unit_scale(jnp.concatenate([gram, jnp.zeros((k, 128 - k), F32)], axis=1))
    solved = eliminate(tiled(jnp.concatenate([gram, eye], axis=1)), 0)
    return (joined(solved)[:, 128:] * across)[:, :k]


def solve_kernel(gram_ref, image_ref, out_ref):
    for layer in range(image_ref.shape[0]):
        inverse = inverse_factor(gram_ref[layer])
        solved = jnp.dot(inverse, image_ref[layer], precision=HIGHEST, preferred_element_type=F32)
        out_ref[layer] = solved.astype(BF16)


def solve(gram, image):
    return pl.pallas_call(
        solve_kernel,
        in_specs=vmem_specs(2),
        out_specs=pl.BlockSpec(memory_space=pltpu.VMEM),
        out_shape=jax.ShapeDtypeStruct(image.shape, BF16),
        compiler_params=params(4),
        name="solve_layers",
    )(gram, image)


def cross_kernel(k, groups, *refs):
    pieces, (out_ref, stacked, packed) = refs[:-3], refs[-3:]
    g = lax.axis_index("layer")
    layers = len(pieces) // groups
    for i, piece in enumerate(pieces):
        at = ((g ^ (i % groups)) * layers + i // groups) * k
        stacked[pl.ds(pl.multiple_of(at, k), k)] = piece[...]
    gram = lax.dot_general(
        stacked[...], stacked[...], TRANS_B, precision=HIGHEST, preferred_element_type=F32
    )
    half = gram.shape[0] // 2
    first, last = gram[:half, :half], gram[half:, half:]
    row = lax.broadcasted_iota(jnp.int32, (half, half), 0) // k
    col = lax.broadcasted_iota(jnp.int32, (half, half), 1) // k
    packed[:half] = gram[:half, half:]
    packed[half : 2 * half] = jnp.where(col >= row, first, last)
    diagonal = jnp.where(col == row, last, 0.0)
    packed[2 * half :] = sum(diagonal[r * k : r * k + k] for r in range(half // k))
    rows = out_ref.shape[0]
    out_ref[...] = packed[pl.ds(pl.multiple_of((g & 1) * rows, 16), rows)]


def cross(chains):
    k, width = chains[0][0].shape
    groups = len(chains[0])
    size = len(chains) * groups * k
    pieces = [piece for chain in chains for piece in chain]
    return pl.pallas_call(
        functools.partial(cross_kernel, k, groups),
        in_specs=vmem_specs(len(pieces)),
        out_specs=vmem_specs(2),
        out_shape=[
            jax.ShapeDtypeStruct(((size + k) // 2, size // 2), F32),
            jax.ShapeDtypeStruct((size, width), F32),
        ],
        scratch_shapes=[pltpu.VMEM((size + k, size // 2), F32)],
        compiler_params=params(6),
        name="cross_gram",
    )(*pieces)


def unpack(packed, k, work):
    half = packed.shape[1]
    row = lax.broadcasted_iota(jnp.int32, (half, half), 0) // k
    col = lax.broadcasted_iota(jnp.int32, (half, half), 1) // k
    mixed = packed[half : 2 * half]
    under = jnp.where(col < row, mixed, 0.0)
    diagonal = jnp.concatenate([packed[2 * half :]] * (half // k), axis=0)
    work[:half, :half] = jnp.where(col >= row, mixed, 0.0)
    work[:half, half:] = packed[:half]
    work[half:, :half] = jnp.zeros((half, half), F32)
    work[half:, half:] = under.T + jnp.where(col == row, diagonal, 0.0)


def joint_kernel(k, *refs):
    own_ref, other_ref, images_ref, out_ref, again_ref, rounded_ref, work, packed = refs
    rows = own_ref.shape[0]
    odd = lax.axis_index("layer") & 1
    packed[pl.ds(pl.multiple_of(odd * rows, 16), rows)] = own_ref[...]
    packed[pl.ds(pl.multiple_of((1 - odd) * rows, 16), rows)] = other_ref[...]
    unpack(packed[...], k, work)
    size = work.shape[0]
    steps = size // k
    lane = lax.broadcasted_iota(jnp.int32, (k, size), 1)
    lane_128 = lax.broadcasted_iota(jnp.int32, (k, 128), 1)
    sub_128 = lax.broadcasted_iota(jnp.int32, (k, 128), 0)
    gram, across = unit_scale(work[...])
    work[...] = gram
    for s in range(steps):
        lo, hi = s * k, (s + 1) * k
        here = (lane >= lo) & (lane < hi)
        eye = jnp.where(lane_128 == sub_128 + lo % 128, 1.0, 0.0)
        solved = joined(eliminate(tiled(jnp.concatenate([work[lo:hi], eye], axis=1)), lo))
        panel, tail = solved[:, :size], solved[:, size:]
        panel = jnp.where(here, jnp.concatenate([tail] * (size // 128), axis=1), panel)
        work[lo:hi] = jnp.where(lane < hi, panel, 0.0)
        if s + 1 < steps:
            update = gram_update(panel, hi // 128 * 128)
            for r in range(s + 1, steps):
                rows = work[r * k : r * k + k]
                work[r * k : r * k + k] = jnp.where(here, 0.0, rows) - update(r * k, k)
    rows = out_ref.shape[0] * k
    own = work[pl.ds(pl.multiple_of(lax.axis_index("layer") * rows, rows), rows)] * across
    joint = jnp.dot(own, images_ref[...], precision=HIGHEST, preferred_element_type=F32)
    joint = joint.reshape(out_ref.shape)
    out_ref[...] = joint
    again_ref[...] = joint
    rounded_ref[...] = joint.astype(BF16)


def joint_solve(own, other, images, shape):
    size = images.shape[0]
    k = shape[1]
    return pl.pallas_call(
        functools.partial(joint_kernel, k),
        in_specs=vmem_specs(3),
        out_specs=vmem_specs(3),
        out_shape=[
            jax.ShapeDtypeStruct(shape, F32),
            jax.ShapeDtypeStruct(shape, F32),
            jax.ShapeDtypeStruct(shape, BF16),
        ],
        scratch_shapes=[pltpu.VMEM((size, size), F32), pltpu.VMEM((size + k, size // 2), F32)],
        compiler_params=params(8),
        name="joint_solve",
    )(own, other, images)


def around(x, axis, count):
    pieces = [x]
    for d in range(1, count):
        pieces.append(lax.ppermute(x, axis, [(m ^ d, m) for m in range(count)]))
    return pieces


def add_pieces(pieces):
    if len(pieces) == 1:
        return pieces[0]
    return (pieces[0] + pieces[1]) + (pieces[2] + pieces[3])


def per_device(shards, groups, blocks, block_rows, block_cols, counts, start):
    few = shards == 4
    layers = start.shape[0]

    def gather(x):
        return around(x, "node", shards) if few else lax.all_gather(x, "node")

    def total(x):
        return add_pieces(around(x, "node", shards)) if few else lax.psum(x, "node")

    first = gather(start.astype(BF16))
    dense = build_dense(block_rows, block_cols, counts, blocks, shards * BROWS // CHUNK_COLS)
    if few:
        images = [apply_first(layer, first, dense[layer]) for layer in range(layers)]
        images = [apply_second(gather(images[layer]), dense[layer]) for layer in range(layers)]
    else:
        image, gram = apply_dense("gram", first, dense)
        (image,) = apply_dense("plain", gather(solve(total(gram), image)), dense)
        images = [image[layer] for layer in range(layers)]
    own, stacked = cross([around(image, "layer", groups) for image in images])
    own = total(own)
    other = lax.ppermute(own, "layer", [(m ^ 1, m) for m in range(groups)])
    joint_basis, again, rounded = joint_solve(own, other, stacked, start.shape)
    if few:
        partial = apply_score(gather(rounded), again, dense)
    else:
        (partial,) = apply_dense("score", gather(rounded), dense, again)
    return joint_basis, total(partial)


def solution(mesh):
    in_specs = (
        P(("parts", "layer"), "node", None),
        P(("parts", "layer"), "node"),
        P(("parts", "layer"), "node"),
        P(("parts", "layer"), "node"),
        P(("parts", "layer"), None, "node"),
    )
    out_specs = (P(("parts", "layer"), None, "node"), P(("parts", "layer"), None, None))
    return jax.shard_map(
        functools.partial(per_device, mesh.shape["node"], mesh.shape["layer"]),
        mesh=mesh,
        in_specs=in_specs,
        out_specs=out_specs,
        check_vma=False,
    )
```

```python
import functools

import jax
import jax.numpy as jnp
from jax import lax
from jax.experimental import pallas as pl
from jax.experimental.pallas import tpu as pltpu
from jax.sharding import PartitionSpec as P

BLK = 64
ROWS_DEV = 512
BROWS = ROWS_DEV // BLK
CHUNK_COLS = 8
CHUNK_LANES = CHUNK_COLS * 2 * BLK
TALL = BROWS * BLK // 2
MIB = 1024 * 1024
F32 = jnp.float32
BF16 = jnp.bfloat16
HIGHEST = lax.Precision.HIGHEST
TRANS_B = (((1,), (1,)), ((), ()))
TRANS_A = (((0,), (0,)), ((), ()))


def params(mib):
    return pltpu.CompilerParams(vmem_limit_bytes=mib * MIB)


def vmem_specs(count):
    return [pl.BlockSpec(memory_space=pltpu.VMEM)] * count


def place(z, chunks, u, dense_ref):
    for c in range(chunks * CHUNK_COLS):
        piece = z[c * 8 : c * 8 + 8]
        piece = jnp.concatenate([piece[:, :128], piece[:, 128:]], axis=0)
        hi = piece.astype(BF16)
        lo = (piece - hi.astype(F32)).astype(BF16)
        lanes = slice((c % CHUNK_COLS) * 128, (c % CHUNK_COLS) * 128 + 128)
        dense_ref[c // CHUNK_COLS, pl.ds(pl.multiple_of(u * 16, 16), 16), lanes] = hi
        dense_ref[c // CHUNK_COLS, pl.ds(pl.multiple_of(u * 16 + TALL, 16), 16), lanes] = lo


def one_hot(rows_ref, cols_ref, counts_ref, layer, flip, base, positions):
    slot = lax.broadcasted_iota(jnp.int32, (1, rows_ref.shape[1]), 1)
    key = (cols_ref[pl.ds(layer, 1), :] ^ flip) * BROWS + rows_ref[pl.ds(layer, 1), :]
    key = jnp.where(slot < counts_ref[0, layer], key, -1)
    position = lax.broadcasted_iota(jnp.int32, (positions, key.shape[1]), 0) + base
    return jnp.where(position == key, 1.0, 0.0).astype(BF16)


def build_kernel(rows_ref, cols_ref, counts_ref, blocks_ref, dense_ref):
    chunks = dense_ref.shape[1]
    positions = chunks * CHUNK_COLS * BROWS
    base = pl.program_id(1) * positions
    onehot = one_hot(rows_ref, cols_ref, counts_ref, pl.program_id(0), 0, base, positions)

    def step(u, carry):
        cols = pl.ds(pl.multiple_of(u * 256, 256), 256)
        z = jnp.dot(onehot, blocks_ref[0, :, cols], preferred_element_type=F32)
        place(z, chunks, u, dense_ref.at[0])
        return carry

    lax.fori_loop(0, BLK * BLK // 256, step, 0)


def build_whole_kernel(rows_hbm, cols_hbm, counts_hbm, blocks_ref, *refs):
    *dense_refs, held, rows_ref, cols_ref, counts_ref, arrived, index_arrived = refs
    layers, chunks = len(dense_refs), dense_refs[0].shape[0]
    index_copies = [
        pltpu.make_async_copy(source, target, index_arrived.at[i])
        for i, (source, target) in enumerate(
            [(rows_hbm, rows_ref), (cols_hbm, cols_ref), (counts_hbm, counts_ref)]
        )
    ]
    for copy in index_copies:
        copy.start()
    pieces = arrived.shape[1]
    width = held.shape[2] // pieces
    inner = width // 256

    def fetch(layer, piece):
        cols = pl.ds(pl.multiple_of(piece * width, width), width)
        return pltpu.make_async_copy(
            blocks_ref.at[layer, :, cols], held.at[layer, :, cols], arrived.at[layer, piece]
        )

    for layer in range(layers):
        for piece in range(pieces):
            fetch(layer, piece).start()
    flip = lax.axis_index("node") * CHUNK_COLS
    for copy in index_copies:
        copy.wait()
    for layer in range(layers):
        onehot = one_hot(rows_ref, cols_ref, counts_ref, layer, flip, 0, chunks * CHUNK_COLS * BROWS)

        def step(piece, carry):
            fetch(layer, piece).wait()
            for v in range(inner):
                cols = pl.ds(pl.multiple_of(piece * width + v * 256, 256), 256)
                z = jnp.dot(onehot, held[layer, :, cols], preferred_element_type=F32)
                place(z, chunks, piece * inner + v, dense_refs[layer])
            return carry

        lax.fori_loop(0, pieces, step, 0)


def build_dense(block_rows, block_cols, counts, blocks, chunk_total):
    layers, slots, width = blocks.shape
    dense = jax.ShapeDtypeStruct((layers, chunk_total, 2 * TALL, CHUNK_LANES), BF16)
    operands = (block_rows, block_cols, counts.T, blocks)
    if chunk_total <= 4:
        pieces = 4
        return pl.pallas_call(
            build_whole_kernel,
            in_specs=[pl.BlockSpec(memory_space=pltpu.HBM)] * 4,
            out_specs=vmem_specs(layers),
            out_shape=[jax.ShapeDtypeStruct(dense.shape[1:], BF16)] * layers,
            scratch_shapes=[
                pltpu.VMEM(blocks.shape, BF16),
                pltpu.VMEM(block_rows.shape, jnp.int32),
                pltpu.VMEM(block_cols.shape, jnp.int32),
                pltpu.SMEM((1, layers), jnp.int32),
                pltpu.SemaphoreType.DMA((layers, pieces)),
                pltpu.SemaphoreType.DMA((3,)),
            ],
            compiler_params=params(28),
            name="build_dense",
        )(*[pltpu.with_memory_space_constraint(x, pltpu.HBM) for x in operands])
    return pl.pallas_call(
        build_kernel,
        grid=(layers, chunk_total // 4),
        in_specs=vmem_specs(2)
        + [
            pl.BlockSpec(memory_space=pltpu.SMEM),
            pl.BlockSpec((1, slots, width), lambda l, s: (l, 0, 0)),
        ],
        out_specs=pl.BlockSpec((1, 4, 2 * TALL, CHUNK_LANES), lambda l, s: (l, s, 0, 0)),
        out_shape=dense,
        compiler_params=params(24),
        name="build_dense",
    )(*operands)


def split3(x):
    a = x.astype(BF16)
    r = x - a.astype(F32)
    b = r.astype(BF16)
    c = (r - b.astype(F32)).astype(BF16)
    return a, b, c


def image_part(basis, dense):
    k, width = basis.shape
    basis = basis.astype(F32)
    tall = jnp.concatenate([basis, basis], axis=0).T
    lane = lax.broadcasted_iota(jnp.int32, tall.shape, 1)
    first = jnp.where(lane < k, tall, 0.0).astype(BF16)
    second = jnp.where(lane < k, 0.0, tall).astype(BF16)
    weights = []
    for c in range(width // BLK):
        weights += [first[c * BLK : c * BLK + BLK], second[c * BLK : c * BLK + BLK]]
    return jnp.dot(dense, jnp.concatenate(weights, axis=0), preferred_element_type=F32)


def to_wide(total, k, halves, tall):
    halves[:, : 2 * k] = total[:TALL] + total[TALL:]
    halves[:, 2 * k :] = jnp.zeros((TALL, 128 - 2 * k), F32)
    for b in range(BROWS):
        part = halves[pl.ds(b, BLK // 2, stride=BROWS), :]
        tall[pl.ds(BLK * b, BLK // 2, stride=2), :] = part
        tall[pl.ds(BLK * b + 1, BLK // 2, stride=2), :] = pltpu.roll(part, 128 - k, 1)
    return tall[...].T[:k]


def against(left, tall):
    k = left.shape[0]
    lane = lax.broadcasted_iota(jnp.int32, tall.shape, 1)
    a, b, c = split3(jnp.where(lane < k, tall, 0.0))
    right = a.astype(F32) + pltpu.roll(b.astype(F32), k, 1) + pltpu.roll(c.astype(F32), 2 * k, 1)
    pieces = jnp.dot(jnp.concatenate(split3(left), axis=0), right.astype(BF16), preferred_element_type=F32)
    top, middle, bottom = pieces[:k], pieces[k : 2 * k], pieces[2 * k :]
    total = top[:, :k] + (top[:, k : 2 * k] + middle[:, :k])
    return total + (middle[:, k : 2 * k] + (top[:, 2 * k : 3 * k] + bottom[:, :k]))


def apply_kernel(mode, *refs):
    basis_ref, refs = refs[0], refs[1:]
    if mode == "score":
        left_ref, refs = refs[0], refs[1:]
    dense_ref, out_ref = refs[:2]
    halves, tall, acc = refs[-3:]
    layer, chunk = pl.program_id(0), pl.program_id(1)
    total = image_part(basis_ref[chunk, layer], dense_ref[0, 0])

    @pl.when(chunk == 0)
    def _():
        acc[...] = total

    @pl.when(chunk > 0)
    def _():
        acc[...] += total

    @pl.when(chunk == pl.num_programs(1) - 1)
    def _():
        image = to_wide(acc[...], basis_ref.shape[2], halves, tall)
        if mode != "score":
            out_ref[0] = image
        if mode == "gram":
            refs[2][0] = against(image, tall[...])
        if mode == "score":
            out_ref[0] = against(left_ref[0], tall[...])


def product(a, b):
    k = a.shape[0]
    left = jnp.concatenate(split3(a), axis=0)
    right = left if b is a else jnp.concatenate(split3(b), axis=0)
    pieces = lax.dot_general(left, right, TRANS_B, preferred_element_type=F32)
    top, middle, bottom = pieces[:k], pieces[k : 2 * k], pieces[2 * k :]
    total = top[:, :k] + (top[:, k : 2 * k] + middle[:, :k])
    return total + (middle[:, k : 2 * k] + (top[:, 2 * k : 3 * k] + bottom[:, :k]))


def image_of(parts, dense_ref):
    return sum(image_part(part, dense_ref[chunk]) for chunk, part in enumerate(parts))


def first_kernel(layer, piece_count, *refs):
    pieces, (dense_ref, out_ref, halves, tall) = refs[:piece_count], refs[piece_count:]
    total = image_of([piece[layer] for piece in pieces], dense_ref)
    out_ref[...] = to_wide(total, out_ref.shape[0], halves, tall)


def second_kernel(piece_count, *refs):
    pieces, (dense_ref, out_ref, halves, tall) = refs[:piece_count], refs[piece_count:]
    image = jnp.concatenate([piece[...] for piece in pieces], axis=1)
    inverse = inverse_factor(product(image, image))
    basis = jnp.dot(inverse, image, precision=HIGHEST, preferred_element_type=F32)
    parts = [basis[:, d * ROWS_DEV : d * ROWS_DEV + ROWS_DEV] for d in range(piece_count)]
    out_ref[...] = to_wide(image_of(parts, dense_ref), out_ref.shape[0], halves, tall)


def own_kernel(basis_ref, *refs):
    *dense_refs, out_ref = refs
    for layer, dense_ref in enumerate(dense_refs):
        out_ref[layer] = image_part(basis_ref[layer], dense_ref[0])


def score_kernel(layers, piece_count, own_ref, *refs):
    pieces, left_ref, refs = refs[:piece_count], refs[piece_count], refs[piece_count + 1 :]
    dense_refs, (out_ref, halves, tall) = refs[:layers], refs[layers:]
    totals = [
        own_ref[layer]
        + sum(image_part(piece[layer], dense_refs[layer][d + 1]) for d, piece in enumerate(pieces))
        for layer in range(layers)
    ]
    wide = [
        to_wide(totals[layer], left_ref.shape[1], halves.at[layer], tall.at[layer]) for layer in range(layers)
    ]
    for layer in range(layers):
        out_ref[layer] = product(left_ref[layer], wide[layer])


def apply_whole(kernel, name, operands, out_shape, *lead):
    return pl.pallas_call(
        kernel,
        in_specs=vmem_specs(len(operands)),
        out_specs=pl.BlockSpec(memory_space=pltpu.VMEM),
        out_shape=jax.ShapeDtypeStruct(out_shape, F32),
        scratch_shapes=[pltpu.VMEM((*lead, TALL, 128), F32), pltpu.VMEM((*lead, ROWS_DEV, 128), F32)],
        compiler_params=params(14),
        cost_estimate=pl.CostEstimate(flops=0, bytes_accessed=4 * MIB, transcendentals=0),
        name=name,
    )(*operands)


def apply_first(layer, pieces, dense):
    kernel = functools.partial(first_kernel, layer, len(pieces))
    return apply_whole(kernel, "apply_first", [*pieces, dense], pieces[0].shape[1:])


def apply_second(pieces, dense):
    kernel = functools.partial(second_kernel, len(pieces))
    return apply_whole(kernel, "apply_second", [*pieces, dense], pieces[0].shape)


def apply_own(basis, dense):
    layers, k = basis.shape[:2]
    return pl.pallas_call(
        own_kernel,
        in_specs=vmem_specs(1 + layers),
        out_specs=pl.BlockSpec(memory_space=pltpu.VMEM),
        out_shape=jax.ShapeDtypeStruct((layers, 2 * TALL, 2 * k), F32),
        compiler_params=params(14),
        cost_estimate=pl.CostEstimate(flops=0, bytes_accessed=2 * MIB, transcendentals=0),
        name="apply_own",
    )(basis, *dense)


def apply_score(pieces, left, dense):
    kernel = functools.partial(score_kernel, len(dense), len(pieces) - 1)
    layers, k = left.shape[:2]
    operands = [apply_own(pieces[0], dense), *pieces[1:], left, *dense]
    return apply_whole(kernel, "apply_score", operands, (layers, k, k), layers)


def apply_dense(mode, basis, dense, left=None):
    layers, chunks = dense.shape[:2]
    k = basis.shape[-2]
    image = jax.ShapeDtypeStruct((layers, k, ROWS_DEV), F32)
    small = jax.ShapeDtypeStruct((layers, k, k), F32)
    out_shape = {"gram": [image, small], "plain": [image], "score": [small]}[mode]
    operands = [basis] + ([left] if mode == "score" else []) + [dense]
    dense_spec = pl.BlockSpec((1, 1, 2 * TALL, CHUNK_LANES), lambda l, s: (l, s, 0, 0))
    image_spec = pl.BlockSpec((1, k, ROWS_DEV), lambda l, s: (l, 0, 0))
    small_spec = pl.BlockSpec((1, k, k), lambda l, s: (l, 0, 0))
    return pl.pallas_call(
        functools.partial(apply_kernel, mode),
        grid=(layers, chunks),
        in_specs=vmem_specs(1) + ([image_spec] if mode == "score" else []) + [dense_spec],
        out_specs={"gram": [image_spec, small_spec], "plain": [image_spec], "score": [small_spec]}[mode],
        out_shape=out_shape,
        scratch_shapes=[
            pltpu.VMEM((TALL, 128), F32),
            pltpu.VMEM((ROWS_DEV, 128), F32),
            pltpu.VMEM((2 * TALL, 2 * k), F32),
        ],
        compiler_params=params(12),
        name="apply_" + mode,
    )(*operands)


def spread(x):
    return jnp.broadcast_to(x, (8, 128))


def eliminate(rows, offset):
    groups, tiles = len(rows), len(rows[0])
    rows = [list(row) for row in rows]
    home, at = offset // 128, offset % 128
    sub = lax.broadcasted_iota(jnp.int32, (8, 128), 0)
    solved = []
    for h in range(groups):
        below = range(h + 1, groups)
        lane = at + 8 * h
        col = [{g: spread(rows[g][home][:, lane + q : lane + q + 1]) for g in range(h, groups)} for q in range(8)]
        cell = {(p, q): spread(col[p][h][q : q + 1]) for q in range(8) for p in range(q + 1)}
        row = [[spread(rows[h][t][q : q + 1]) for t in range(tiles)] for q in range(8)]
        done = []
        for m in range(0, 8, 2):
            n = m + 1
            a, b, c = cell[m, m], cell[m, n], cell[n, n]
            det = a * c - b * b
            r = pl.reciprocal(det, approx=True)
            later = range(m + 2, 8)
            u = {q: c * cell[m, q] - b * cell[n, q] for q in later}
            v = {q: a * cell[n, q] - b * cell[m, q] for q in later}
            for q in later:
                for p in range(m + 2, q + 1):
                    cell[p, q] = cell[p, q] - r * (cell[m, p] * u[q] + cell[n, p] * v[q])
            for q in later:
                for g in below:
                    col[q][g] = col[q][g] - r * (col[m][g] * u[q] + col[n][g] * v[q])
            for t in range(tiles):
                x = r * (c * row[m][t] - b * row[n][t])
                y = r * (a * row[n][t] - b * row[m][t])
                for q in later:
                    row[q][t] = row[q][t] - (cell[m, q] * x + cell[n, q] * y)
                for g in below:
                    rows[g][t] = rows[g][t] - (col[m][g] * x + col[n][g] * y)
            over = pl.reciprocal(a, approx=True)
            done.append([lax.rsqrt(a) * x for x in row[m]])
            scale = lax.rsqrt(det * over)
            done.append([scale * (x - (b * over) * w) for x, w in zip(row[n], row[m])])
        finished = []
        for t in range(tiles):
            x = done[7][t]
            for q in range(7):
                x = jnp.where(sub == q, done[q][t], x)
            finished.append(x)
        solved.append(finished)
    return solved


def tiled(x):
    return [
        [x[g * 8 : g * 8 + 8, t * 128 : t * 128 + 128] for t in range(x.shape[1] // 128)]
        for g in range(x.shape[0] // 8)
    ]


def joined(tiles):
    return jnp.concatenate([jnp.concatenate(row, axis=1) for row in tiles], axis=0)


def unit_scale(gram):
    lane = lax.broadcasted_iota(jnp.int32, gram.shape, 1)
    sub = lax.broadcasted_iota(jnp.int32, gram.shape, 0)
    kept = jnp.where(lane == sub, gram, 0.0)
    down = 1.0 / jnp.sqrt(jnp.sum(kept, axis=1, keepdims=True))
    across = jnp.sum(kept, axis=0, keepdims=True)
    across = 1.0 / jnp.sqrt(jnp.where(across == 0.0, 1.0, across))
    return gram * down * across, across


def gram_update(panel, first):
    a, b, c = split3(panel)
    left = jnp.concatenate([a, a, b, b, a, c], axis=0)
    right = jnp.concatenate([a, b, a, b, c, a], axis=0)
    parts = {
        at: lax.dot_general(left[:, at : at + 128], right, TRANS_A, preferred_element_type=F32)
        for at in range(first, panel.shape[1], 128)
    }
    return lambda at, count: parts[at // 128 * 128][at % 128 : at % 128 + count]


def inverse_factor(gram):
    k = gram.shape[0]
    lane = lax.broadcasted_iota(jnp.int32, (k, 128), 1)
    sub = lax.broadcasted_iota(jnp.int32, (k, 128), 0)
    eye = jnp.where(lane == sub, 1.0, 0.0)
    gram, across = unit_scale(jnp.concatenate([gram, jnp.zeros((k, 128 - k), F32)], axis=1))
    solved = eliminate(tiled(jnp.concatenate([gram, eye], axis=1)), 0)
    return (joined(solved)[:, 128:] * across)[:, :k]


def solve_kernel(gram_ref, image_ref, out_ref):
    for layer in range(image_ref.shape[0]):
        inverse = inverse_factor(gram_ref[layer])
        solved = jnp.dot(inverse, image_ref[layer], precision=HIGHEST, preferred_element_type=F32)
        out_ref[layer] = solved.astype(BF16)


def solve(gram, image):
    return pl.pallas_call(
        solve_kernel,
        in_specs=vmem_specs(2),
        out_specs=pl.BlockSpec(memory_space=pltpu.VMEM),
        out_shape=jax.ShapeDtypeStruct(image.shape, BF16),
        compiler_params=params(4),
        name="solve_layers",
    )(gram, image)


def cross_kernel(k, groups, *refs):
    pieces, (out_ref, stacked, packed) = refs[:-3], refs[-3:]
    g = lax.axis_index("layer")
    layers = len(pieces) // groups
    for i, piece in enumerate(pieces):
        at = ((g ^ (i % groups)) * layers + i // groups) * k
        stacked[pl.ds(pl.multiple_of(at, k), k)] = piece[...]
    gram = lax.dot_general(
        stacked[...], stacked[...], TRANS_B, precision=HIGHEST, preferred_element_type=F32
    )
    half = gram.shape[0] // 2
    first, last = gram[:half, :half], gram[half:, half:]
    row = lax.broadcasted_iota(jnp.int32, (half, half), 0) // k
    col = lax.broadcasted_iota(jnp.int32, (half, half), 1) // k
    packed[:half] = gram[:half, half:]
    packed[half : 2 * half] = jnp.where(col >= row, first, last)
    diagonal = jnp.where(col == row, last, 0.0)
    packed[2 * half :] = sum(diagonal[r * k : r * k + k] for r in range(half // k))
    rows = out_ref.shape[0]
    out_ref[...] = packed[pl.ds(pl.multiple_of((g & 1) * rows, 16), rows)]


def cross(chains):
    k, width = chains[0][0].shape
    groups = len(chains[0])
    size = len(chains) * groups * k
    pieces = [piece for chain in chains for piece in chain]
    return pl.pallas_call(
        functools.partial(cross_kernel, k, groups),
        in_specs=vmem_specs(len(pieces)),
        out_specs=vmem_specs(2),
        out_shape=[
            jax.ShapeDtypeStruct(((size + k) // 2, size // 2), F32),
            jax.ShapeDtypeStruct((size, width), F32),
        ],
        scratch_shapes=[pltpu.VMEM((size + k, size // 2), F32)],
        compiler_params=params(6),
        name="cross_gram",
    )(*pieces)


def unpack(packed, k, work):
    half = packed.shape[1]
    row = lax.broadcasted_iota(jnp.int32, (half, half), 0) // k
    col = lax.broadcasted_iota(jnp.int32, (half, half), 1) // k
    mixed = packed[half : 2 * half]
    under = jnp.where(col < row, mixed, 0.0)
    diagonal = jnp.concatenate([packed[2 * half :]] * (half // k), axis=0)
    over = jnp.where(col > row, mixed, 0.0)
    work[:half, :half] = jnp.where(col >= row, mixed, over.T)
    work[:half, half:] = packed[:half]
    work[half:, :half] = jnp.zeros((half, half), F32)
    work[half:, half:] = under + under.T + jnp.where(col == row, diagonal, 0.0)


def joint_kernel(k, *refs):
    own_ref, other_ref, images_ref, out_ref, again_ref, rounded_ref, work, packed = refs
    rows = own_ref.shape[0]
    odd = lax.axis_index("layer") & 1
    packed[pl.ds(pl.multiple_of(odd * rows, 16), rows)] = own_ref[...]
    packed[pl.ds(pl.multiple_of((1 - odd) * rows, 16), rows)] = other_ref[...]
    unpack(packed[...], k, work)
    size = work.shape[0]
    band = 2 * k
    steps = size // band
    lane = lax.broadcasted_iota(jnp.int32, (band, size), 1)
    lane_128 = lax.broadcasted_iota(jnp.int32, (band, 128), 1)
    sub_128 = lax.broadcasted_iota(jnp.int32, (band, 128), 0)
    gram, across = unit_scale(work[...])
    work[...] = gram
    for s in range(steps):
        lo, hi = s * band, (s + 1) * band
        here = (lane >= lo) & (lane < hi)
        eye = jnp.where(lane_128 == sub_128 + lo % 128, 1.0, 0.0)
        solved = joined(eliminate(tiled(jnp.concatenate([work[lo:hi], eye], axis=1)), lo))
        panel, tail = solved[:, :size], solved[:, size:]
        panel = jnp.where(here, jnp.concatenate([tail] * (size // 128), axis=1), panel)
        work[lo:hi] = jnp.where(lane < hi, panel, 0.0)
        if s + 1 < steps:
            update = gram_update(panel, hi // 128 * 128)
            for r in range(s + 1, steps):
                rows = work[r * band : r * band + band]
                work[r * band : r * band + band] = jnp.where(here, 0.0, rows) - update(r * band, band)
    rows = out_ref.shape[0] * k
    own = work[pl.ds(pl.multiple_of(lax.axis_index("layer") * rows, rows), rows)] * across
    joint = jnp.dot(own, images_ref[...], precision=HIGHEST, preferred_element_type=F32)
    joint = joint.reshape(out_ref.shape)
    out_ref[...] = joint
    again_ref[...] = joint
    rounded_ref[...] = joint.astype(BF16)


def joint_solve(own, other, images, shape):
    size = images.shape[0]
    k = shape[1]
    return pl.pallas_call(
        functools.partial(joint_kernel, k),
        in_specs=vmem_specs(3),
        out_specs=vmem_specs(3),
        out_shape=[
            jax.ShapeDtypeStruct(shape, F32),
            jax.ShapeDtypeStruct(shape, F32),
            jax.ShapeDtypeStruct(shape, BF16),
        ],
        scratch_shapes=[pltpu.VMEM((size, size), F32), pltpu.VMEM((size + k, size // 2), F32)],
        compiler_params=params(8),
        name="joint_solve",
    )(own, other, images)


def around(x, axis, count):
    pieces = [x]
    for d in range(1, count):
        pieces.append(lax.ppermute(x, axis, [(m ^ d, m) for m in range(count)]))
    return pieces


def add_pieces(pieces):
    if len(pieces) == 1:
        return pieces[0]
    return (pieces[0] + pieces[1]) + (pieces[2] + pieces[3])


def per_device(shards, groups, blocks, block_rows, block_cols, counts, start):
    few = shards == 4
    layers = start.shape[0]

    def gather(x):
        return around(x, "node", shards) if few else lax.all_gather(x, "node")

    def total(x):
        return add_pieces(around(x, "node", shards)) if few else lax.psum(x, "node")

    first = gather(start.astype(BF16))
    dense = build_dense(block_rows, block_cols, counts, blocks, shards * BROWS // CHUNK_COLS)
    if few:
        images = [apply_first(layer, first, dense[layer]) for layer in range(layers)]
        images = [apply_second(gather(images[layer]), dense[layer]) for layer in range(layers)]
    else:
        image, gram = apply_dense("gram", first, dense)
        (image,) = apply_dense("plain", gather(solve(total(gram), image)), dense)
        images = [image[layer] for layer in range(layers)]
    own, stacked = cross([around(image, "layer", groups) for image in images])
    own = total(own)
    other = lax.ppermute(own, "layer", [(m ^ 1, m) for m in range(groups)])
    joint_basis, again, rounded = joint_solve(own, other, stacked, start.shape)
    if few:
        partial = apply_score(gather(rounded), again, dense)
    else:
        (partial,) = apply_dense("score", gather(rounded), dense, again)
    return joint_basis, total(partial)


def solution(mesh):
    in_specs = (
        P(("parts", "layer"), "node", None),
        P(("parts", "layer"), "node"),
        P(("parts", "layer"), "node"),
        P(("parts", "layer"), "node"),
        P(("parts", "layer"), None, "node"),
    )
    out_specs = (P(("parts", "layer"), None, "node"), P(("parts", "layer"), None, None))
    return jax.shard_map(
        functools.partial(per_device, mesh.shape["node"], mesh.shape["layer"]),
        mesh=mesh,
        in_specs=in_specs,
        out_specs=out_specs,
        check_vma=False,
    )
```

```python
import functools

import jax
import jax.numpy as jnp
from jax import lax
from jax.experimental import pallas as pl
from jax.experimental.pallas import tpu as pltpu
from jax.sharding import PartitionSpec as P

BLK = 64
ROWS_DEV = 512
BROWS = ROWS_DEV // BLK
CHUNK_COLS = 8
CHUNK_LANES = CHUNK_COLS * 2 * BLK
TALL = BROWS * BLK // 2
MIB = 1024 * 1024
F32 = jnp.float32
BF16 = jnp.bfloat16
HIGHEST = lax.Precision.HIGHEST
TRANS_B = (((1,), (1,)), ((), ()))
TRANS_A = (((0,), (0,)), ((), ()))


def params(mib):
    return pltpu.CompilerParams(vmem_limit_bytes=mib * MIB)


def vmem_specs(count):
    return [pl.BlockSpec(memory_space=pltpu.VMEM)] * count


def place(z, chunks, u, dense_ref):
    for c in range(chunks * CHUNK_COLS):
        piece = z[c * 8 : c * 8 + 8]
        piece = jnp.concatenate([piece[:, :128], piece[:, 128:]], axis=0)
        hi = piece.astype(BF16)
        lo = (piece - hi.astype(F32)).astype(BF16)
        lanes = slice((c % CHUNK_COLS) * 128, (c % CHUNK_COLS) * 128 + 128)
        dense_ref[c // CHUNK_COLS, pl.ds(pl.multiple_of(u * 16, 16), 16), lanes] = hi
        dense_ref[c // CHUNK_COLS, pl.ds(pl.multiple_of(u * 16 + TALL, 16), 16), lanes] = lo


def one_hot(rows_ref, cols_ref, counts_ref, layer, flip, base, positions):
    slot = lax.broadcasted_iota(jnp.int32, (1, rows_ref.shape[1]), 1)
    key = (cols_ref[pl.ds(layer, 1), :] ^ flip) * BROWS + rows_ref[pl.ds(layer, 1), :]
    key = jnp.where(slot < counts_ref[0, layer], key, -1)
    position = lax.broadcasted_iota(jnp.int32, (positions, key.shape[1]), 0) + base
    return jnp.where(position == key, 1.0, 0.0).astype(BF16)


def build_kernel(rows_ref, cols_ref, counts_ref, blocks_ref, dense_ref):
    chunks = dense_ref.shape[1]
    positions = chunks * CHUNK_COLS * BROWS
    base = pl.program_id(1) * positions
    onehot = one_hot(rows_ref, cols_ref, counts_ref, pl.program_id(0), 0, base, positions)

    def step(u, carry):
        cols = pl.ds(pl.multiple_of(u * 256, 256), 256)
        z = jnp.dot(onehot, blocks_ref[0, :, cols], preferred_element_type=F32)
        place(z, chunks, u, dense_ref.at[0])
        return carry

    lax.fori_loop(0, BLK * BLK // 256, step, 0)


def build_whole_kernel(rows_hbm, cols_hbm, counts_hbm, blocks_ref, *refs):
    *dense_refs, held, rows_ref, cols_ref, counts_ref, arrived, index_arrived = refs
    layers, chunks = len(dense_refs), dense_refs[0].shape[0]
    index_copies = [
        pltpu.make_async_copy(source, target, index_arrived.at[i])
        for i, (source, target) in enumerate(
            [(rows_hbm, rows_ref), (cols_hbm, cols_ref), (counts_hbm, counts_ref)]
        )
    ]
    for copy in index_copies:
        copy.start()
    pieces = arrived.shape[1]
    width = held.shape[2] // pieces
    inner = width // 256

    def fetch(layer, piece):
        cols = pl.ds(pl.multiple_of(piece * width, width), width)
        return pltpu.make_async_copy(
            blocks_ref.at[layer, :, cols], held.at[layer, :, cols], arrived.at[layer, piece]
        )

    for layer in range(layers):
        for piece in range(pieces):
            fetch(layer, piece).start()
    flip = lax.axis_index("node") * CHUNK_COLS
    for copy in index_copies:
        copy.wait()
    for layer in range(layers):
        onehot = one_hot(rows_ref, cols_ref, counts_ref, layer, flip, 0, chunks * CHUNK_COLS * BROWS)

        def step(piece, carry):
            fetch(layer, piece).wait()
            for v in range(inner):
                cols = pl.ds(pl.multiple_of(piece * width + v * 256, 256), 256)
                z = jnp.dot(onehot, held[layer, :, cols], preferred_element_type=F32)
                place(z, chunks, piece * inner + v, dense_refs[layer])
            return carry

        lax.fori_loop(0, pieces, step, 0)


def build_dense(block_rows, block_cols, counts, blocks, chunk_total):
    layers, slots, width = blocks.shape
    dense = jax.ShapeDtypeStruct((layers, chunk_total, 2 * TALL, CHUNK_LANES), BF16)
    operands = (block_rows, block_cols, counts.T, blocks)
    if chunk_total <= 4:
        pieces = 4
        return pl.pallas_call(
            build_whole_kernel,
            in_specs=[pl.BlockSpec(memory_space=pltpu.HBM)] * 4,
            out_specs=vmem_specs(layers),
            out_shape=[jax.ShapeDtypeStruct(dense.shape[1:], BF16)] * layers,
            scratch_shapes=[
                pltpu.VMEM(blocks.shape, BF16),
                pltpu.VMEM(block_rows.shape, jnp.int32),
                pltpu.VMEM(block_cols.shape, jnp.int32),
                pltpu.SMEM((1, layers), jnp.int32),
                pltpu.SemaphoreType.DMA((layers, pieces)),
                pltpu.SemaphoreType.DMA((3,)),
            ],
            compiler_params=params(28),
            name="build_dense",
        )(*[pltpu.with_memory_space_constraint(x, pltpu.HBM) for x in operands])
    return pl.pallas_call(
        build_kernel,
        grid=(layers, chunk_total // 4),
        in_specs=vmem_specs(2)
        + [
            pl.BlockSpec(memory_space=pltpu.SMEM),
            pl.BlockSpec((1, slots, width), lambda l, s: (l, 0, 0)),
        ],
        out_specs=pl.BlockSpec((1, 4, 2 * TALL, CHUNK_LANES), lambda l, s: (l, s, 0, 0)),
        out_shape=dense,
        compiler_params=params(24),
        name="build_dense",
    )(*operands)


def split3(x):
    a = x.astype(BF16)
    r = x - a.astype(F32)
    b = r.astype(BF16)
    c = (r - b.astype(F32)).astype(BF16)
    return a, b, c


def image_part(basis, dense):
    k, width = basis.shape
    basis = basis.astype(F32)
    tall = jnp.concatenate([basis, basis], axis=0).T
    lane = lax.broadcasted_iota(jnp.int32, tall.shape, 1)
    first = jnp.where(lane < k, tall, 0.0).astype(BF16)
    second = jnp.where(lane < k, 0.0, tall).astype(BF16)
    weights = []
    for c in range(width // BLK):
        weights += [first[c * BLK : c * BLK + BLK], second[c * BLK : c * BLK + BLK]]
    return jnp.dot(dense, jnp.concatenate(weights, axis=0), preferred_element_type=F32)


def to_wide(total, k, halves, tall):
    halves[:, : 2 * k] = total[:TALL] + total[TALL:]
    halves[:, 2 * k :] = jnp.zeros((TALL, 128 - 2 * k), F32)
    for b in range(BROWS):
        part = halves[pl.ds(b, BLK // 2, stride=BROWS), :]
        tall[pl.ds(BLK * b, BLK // 2, stride=2), :] = part
        tall[pl.ds(BLK * b + 1, BLK // 2, stride=2), :] = pltpu.roll(part, 128 - k, 1)
    return tall[...].T[:k]


def against(left, tall):
    k = left.shape[0]
    lane = lax.broadcasted_iota(jnp.int32, tall.shape, 1)
    a, b, c = split3(jnp.where(lane < k, tall, 0.0))
    right = a.astype(F32) + pltpu.roll(b.astype(F32), k, 1) + pltpu.roll(c.astype(F32), 2 * k, 1)
    pieces = jnp.dot(jnp.concatenate(split3(left), axis=0), right.astype(BF16), preferred_element_type=F32)
    top, middle, bottom = pieces[:k], pieces[k : 2 * k], pieces[2 * k :]
    total = top[:, :k] + (top[:, k : 2 * k] + middle[:, :k])
    return total + (middle[:, k : 2 * k] + (top[:, 2 * k : 3 * k] + bottom[:, :k]))


def apply_kernel(mode, *refs):
    basis_ref, refs = refs[0], refs[1:]
    if mode == "score":
        left_ref, refs = refs[0], refs[1:]
    dense_ref, out_ref = refs[:2]
    halves, tall, acc = refs[-3:]
    layer, chunk = pl.program_id(0), pl.program_id(1)
    total = image_part(basis_ref[chunk, layer], dense_ref[0, 0])

    @pl.when(chunk == 0)
    def _():
        acc[...] = total

    @pl.when(chunk > 0)
    def _():
        acc[...] += total

    @pl.when(chunk == pl.num_programs(1) - 1)
    def _():
        image = to_wide(acc[...], basis_ref.shape[2], halves, tall)
        if mode != "score":
            out_ref[0] = image
        if mode == "gram":
            refs[2][0] = against(image, tall[...])
        if mode == "score":
            out_ref[0] = against(left_ref[0], tall[...])


def product(a, b):
    k = a.shape[0]
    left = jnp.concatenate(split3(a), axis=0)
    right = left if b is a else jnp.concatenate(split3(b), axis=0)
    pieces = lax.dot_general(left, right, TRANS_B, preferred_element_type=F32)
    top, middle, bottom = pieces[:k], pieces[k : 2 * k], pieces[2 * k :]
    total = top[:, :k] + (top[:, k : 2 * k] + middle[:, :k])
    return total + (middle[:, k : 2 * k] + (top[:, 2 * k : 3 * k] + bottom[:, :k]))


def image_of(parts, dense_ref):
    return sum(image_part(part, dense_ref[chunk]) for chunk, part in enumerate(parts))


def first_kernel(layer, piece_count, *refs):
    pieces, (dense_ref, out_ref, halves, tall) = refs[:piece_count], refs[piece_count:]
    total = image_of([piece[layer] for piece in pieces], dense_ref)
    out_ref[...] = to_wide(total, out_ref.shape[0], halves, tall)


def second_kernel(piece_count, *refs):
    pieces, (dense_ref, out_ref, halves, tall) = refs[:piece_count], refs[piece_count:]
    image = jnp.concatenate([piece[...] for piece in pieces], axis=1)
    basis = solve_rows(product(image, image), image)
    parts = [basis[:, d * ROWS_DEV : d * ROWS_DEV + ROWS_DEV] for d in range(piece_count)]
    out_ref[...] = to_wide(image_of(parts, dense_ref), out_ref.shape[0], halves, tall)


def own_kernel(basis_ref, *refs):
    *dense_refs, out_ref = refs
    for layer, dense_ref in enumerate(dense_refs):
        out_ref[layer] = image_part(basis_ref[layer], dense_ref[0])


def score_kernel(layers, piece_count, own_ref, *refs):
    pieces, left_ref, refs = refs[:piece_count], refs[piece_count], refs[piece_count + 1 :]
    dense_refs, (out_ref, halves, tall) = refs[:layers], refs[layers:]
    totals = [
        own_ref[layer]
        + sum(image_part(piece[layer], dense_refs[layer][d + 1]) for d, piece in enumerate(pieces))
        for layer in range(layers)
    ]
    wide = [
        to_wide(totals[layer], left_ref.shape[1], halves.at[layer], tall.at[layer]) for layer in range(layers)
    ]
    for layer in range(layers):
        out_ref[layer] = product(left_ref[layer], wide[layer])


def apply_whole(kernel, name, operands, out_shape, *lead):
    return pl.pallas_call(
        kernel,
        in_specs=vmem_specs(len(operands)),
        out_specs=pl.BlockSpec(memory_space=pltpu.VMEM),
        out_shape=jax.ShapeDtypeStruct(out_shape, F32),
        scratch_shapes=[pltpu.VMEM((*lead, TALL, 128), F32), pltpu.VMEM((*lead, ROWS_DEV, 128), F32)],
        compiler_params=params(14),
        cost_estimate=pl.CostEstimate(flops=0, bytes_accessed=4 * MIB, transcendentals=0),
        name=name,
    )(*operands)


def apply_first(layer, pieces, dense):
    kernel = functools.partial(first_kernel, layer, len(pieces))
    return apply_whole(kernel, "apply_first", [*pieces, dense], pieces[0].shape[1:])


def apply_second(pieces, dense):
    kernel = functools.partial(second_kernel, len(pieces))
    return apply_whole(kernel, "apply_second", [*pieces, dense], pieces[0].shape)


def apply_own(basis, dense):
    layers, k = basis.shape[:2]
    return pl.pallas_call(
        own_kernel,
        in_specs=vmem_specs(1 + layers),
        out_specs=pl.BlockSpec(memory_space=pltpu.VMEM),
        out_shape=jax.ShapeDtypeStruct((layers, 2 * TALL, 2 * k), F32),
        compiler_params=params(14),
        cost_estimate=pl.CostEstimate(flops=0, bytes_accessed=2 * MIB, transcendentals=0),
        name="apply_own",
    )(basis, *dense)


def apply_score(pieces, left, dense):
    kernel = functools.partial(score_kernel, len(dense), len(pieces) - 1)
    layers, k = left.shape[:2]
    operands = [apply_own(pieces[0], dense), *pieces[1:], left, *dense]
    return apply_whole(kernel, "apply_score", operands, (layers, k, k), layers)


def apply_dense(mode, basis, dense, left=None):
    layers, chunks = dense.shape[:2]
    k = basis.shape[-2]
    image = jax.ShapeDtypeStruct((layers, k, ROWS_DEV), F32)
    small = jax.ShapeDtypeStruct((layers, k, k), F32)
    out_shape = {"gram": [image, small], "plain": [image], "score": [small]}[mode]
    operands = [basis] + ([left] if mode == "score" else []) + [dense]
    dense_spec = pl.BlockSpec((1, 1, 2 * TALL, CHUNK_LANES), lambda l, s: (l, s, 0, 0))
    image_spec = pl.BlockSpec((1, k, ROWS_DEV), lambda l, s: (l, 0, 0))
    small_spec = pl.BlockSpec((1, k, k), lambda l, s: (l, 0, 0))
    return pl.pallas_call(
        functools.partial(apply_kernel, mode),
        grid=(layers, chunks),
        in_specs=vmem_specs(1) + ([image_spec] if mode == "score" else []) + [dense_spec],
        out_specs={"gram": [image_spec, small_spec], "plain": [image_spec], "score": [small_spec]}[mode],
        out_shape=out_shape,
        scratch_shapes=[
            pltpu.VMEM((TALL, 128), F32),
            pltpu.VMEM((ROWS_DEV, 128), F32),
            pltpu.VMEM((2 * TALL, 2 * k), F32),
        ],
        compiler_params=params(12),
        name="apply_" + mode,
    )(*operands)


def spread(x):
    return jnp.broadcast_to(x, (8, 128))


def inverse_factor(block):
    k = block.shape[0]
    lane = lax.broadcasted_iota(jnp.int32, (k, 128), 1)
    row = lax.broadcasted_iota(jnp.int32, (k, 128), 0)
    start = jnp.where(lane < k, block, jnp.where(lane % k == row, 1.0, 0.0))
    rows = [start[g * 8 : g * 8 + 8] for g in range(k // 8)]
    sub = lax.broadcasted_iota(jnp.int32, (8, 128), 0)
    solved = []
    for h in range(k // 8):
        below = range(h + 1, k // 8)
        col = [{g: spread(rows[g][:, 8 * h + q : 8 * h + q + 1]) for g in range(h, k // 8)} for q in range(8)]
        cell = {(p, q): spread(col[p][h][q : q + 1]) for q in range(8) for p in range(q + 1)}
        row = [spread(rows[h][q : q + 1]) for q in range(8)]
        done = []
        for m in range(0, 8, 2):
            n = m + 1
            a, b, c = cell[m, m], cell[m, n], cell[n, n]
            det = a * c - b * b
            r = pl.reciprocal(det, approx=True)
            later = range(m + 2, 8)
            u = {q: c * cell[m, q] - b * cell[n, q] for q in later}
            v = {q: a * cell[n, q] - b * cell[m, q] for q in later}
            for q in later:
                for p in range(m + 2, q + 1):
                    cell[p, q] = cell[p, q] - r * (cell[m, p] * u[q] + cell[n, p] * v[q])
            for q in later:
                for g in below:
                    col[q][g] = col[q][g] - r * (col[m][g] * u[q] + col[n][g] * v[q])
            x = r * (c * row[m] - b * row[n])
            y = r * (a * row[n] - b * row[m])
            for q in later:
                row[q] = row[q] - (cell[m, q] * x + cell[n, q] * y)
            for g in below:
                rows[g] = rows[g] - (col[m][g] * x + col[n][g] * y)
            over = pl.reciprocal(a, approx=True)
            done.append(lax.rsqrt(a) * row[m])
            done.append(lax.rsqrt(det * over) * (row[n] - (b * over) * row[m]))
        finished = done[7]
        for q in range(7):
            finished = jnp.where(sub == q, done[q], finished)
        solved.append(finished)
    return jnp.concatenate(solved, axis=0)


def times(inverse, right):
    k = right.shape[0]
    a, b, c = [piece.astype(F32) for piece in split3(inverse)]
    lane = lax.broadcasted_iota(jnp.int32, inverse.shape, 1)
    major = jnp.where(lane < k, 0.0, jnp.where(lane < 3 * k, a, b)).astype(BF16)
    minor = jnp.where(lane < k, 0.0, jnp.where(lane < 2 * k, b, jnp.where(lane < 3 * k, a, c))).astype(BF16)
    p, q, r = split3(right)
    total = jnp.dot(major, jnp.concatenate([p, p, q, p], axis=0), preferred_element_type=F32)
    return total + jnp.dot(minor, jnp.concatenate([p, q, r, p], axis=0), preferred_element_type=F32)


def unit_scale(gram):
    lane = lax.broadcasted_iota(jnp.int32, gram.shape, 1)
    sub = lax.broadcasted_iota(jnp.int32, gram.shape, 0)
    kept = jnp.where(lane == sub, gram, 0.0)
    down = 1.0 / jnp.sqrt(jnp.sum(kept, axis=1, keepdims=True))
    across = jnp.sum(kept, axis=0, keepdims=True)
    across = 1.0 / jnp.sqrt(jnp.where(across == 0.0, 1.0, across))
    return gram * down * across, down, across


def solve_rows(gram, image):
    k = gram.shape[0]
    block, down, _ = unit_scale(jnp.concatenate([gram, jnp.zeros((k, 128 - k), F32)], axis=1))
    return times(inverse_factor(block), image * down)


def gram_update(panel, first):
    a, b, c = split3(panel)
    left = jnp.concatenate([a, a, b, b, a, c], axis=0)
    right = jnp.concatenate([a, b, a, b, c, a], axis=0)
    parts = {
        at: lax.dot_general(left[:, at : at + 128], right, TRANS_A, preferred_element_type=F32)
        for at in range(first, panel.shape[1], 128)
    }
    return lambda at, count: parts[at // 128 * 128][at % 128 : at % 128 + count]


def solve_kernel(gram_ref, image_ref, out_ref):
    for layer in range(image_ref.shape[0]):
        out_ref[layer] = solve_rows(gram_ref[layer], image_ref[layer]).astype(BF16)


def solve(gram, image):
    return pl.pallas_call(
        solve_kernel,
        in_specs=vmem_specs(2),
        out_specs=pl.BlockSpec(memory_space=pltpu.VMEM),
        out_shape=jax.ShapeDtypeStruct(image.shape, BF16),
        compiler_params=params(4),
        name="solve_layers",
    )(gram, image)


def cross_kernel(k, groups, *refs):
    pieces, (out_ref, stacked, packed) = refs[:-3], refs[-3:]
    g = lax.axis_index("layer")
    layers = len(pieces) // groups
    for i, piece in enumerate(pieces):
        at = ((g ^ (i % groups)) * layers + i // groups) * k
        stacked[pl.ds(pl.multiple_of(at, k), k)] = piece[...]
    gram = lax.dot_general(
        stacked[...], stacked[...], TRANS_B, precision=HIGHEST, preferred_element_type=F32
    )
    half = gram.shape[0] // 2
    first, last = gram[:half, :half], gram[half:, half:]
    row = lax.broadcasted_iota(jnp.int32, (half, half), 0) // k
    col = lax.broadcasted_iota(jnp.int32, (half, half), 1) // k
    packed[:half] = gram[:half, half:]
    packed[half : 2 * half] = jnp.where(col >= row, first, last)
    diagonal = jnp.where(col == row, last, 0.0)
    packed[2 * half :] = sum(diagonal[r * k : r * k + k] for r in range(half // k))
    rows = out_ref.shape[0]
    out_ref[...] = packed[pl.ds(pl.multiple_of((g & 1) * rows, 16), rows)]


def cross(chains):
    k, width = chains[0][0].shape
    groups = len(chains[0])
    size = len(chains) * groups * k
    pieces = [piece for chain in chains for piece in chain]
    return pl.pallas_call(
        functools.partial(cross_kernel, k, groups),
        in_specs=vmem_specs(len(pieces)),
        out_specs=vmem_specs(2),
        out_shape=[
            jax.ShapeDtypeStruct(((size + k) // 2, size // 2), F32),
            jax.ShapeDtypeStruct((size, width), F32),
        ],
        scratch_shapes=[pltpu.VMEM((size + k, size // 2), F32)],
        compiler_params=params(6),
        name="cross_gram",
    )(*pieces)


def unpack(packed, k, work):
    half = packed.shape[1]
    row = lax.broadcasted_iota(jnp.int32, (half, half), 0) // k
    col = lax.broadcasted_iota(jnp.int32, (half, half), 1) // k
    mixed = packed[half : 2 * half]
    under = jnp.where(col < row, mixed, 0.0)
    diagonal = jnp.concatenate([packed[2 * half :]] * (half // k), axis=0)
    work[:half, :half] = jnp.where(col >= row, mixed, 0.0)
    work[:half, half:] = packed[:half]
    work[half:, :half] = jnp.zeros((half, half), F32)
    work[half:, half:] = under.T + jnp.where(col == row, diagonal, 0.0)


def joint_kernel(k, *refs):
    own_ref, other_ref, images_ref, out_ref, again_ref, rounded_ref, work, packed = refs
    rows = own_ref.shape[0]
    odd = lax.axis_index("layer") & 1
    packed[pl.ds(pl.multiple_of(odd * rows, 16), rows)] = own_ref[...]
    packed[pl.ds(pl.multiple_of((1 - odd) * rows, 16), rows)] = other_ref[...]
    unpack(packed[...], k, work)
    size = work.shape[0]
    steps = size // k
    lane = lax.broadcasted_iota(jnp.int32, (k, size), 1)
    sub = lax.broadcasted_iota(jnp.int32, (k, size), 0)
    gram, _, across = unit_scale(work[...])
    work[...] = gram
    for s in range(steps):
        lo, hi = s * k, (s + 1) * k
        here = (lane >= lo) & (lane < hi)
        panel = work[lo:hi]
        tile = lo // 128 * 128
        block = pltpu.roll(panel[:, tile : tile + 128], (tile - lo) % 128, 1)
        eye = jnp.where(lane == sub + lo, 1.0, 0.0)
        panel = times(inverse_factor(block), jnp.where(here, eye, panel))
        work[lo:hi] = jnp.where(lane < hi, panel, 0.0)
        if s + 1 < steps:
            update = gram_update(panel, hi // 128 * 128)
            for r in range(s + 1, steps):
                rows = work[r * k : r * k + k]
                work[r * k : r * k + k] = jnp.where(here, 0.0, rows) - update(r * k, k)
    rows = out_ref.shape[0] * k
    own = work[pl.ds(pl.multiple_of(lax.axis_index("layer") * rows, rows), rows)] * across
    joint = jnp.dot(own, images_ref[...], precision=HIGHEST, preferred_element_type=F32)
    joint = joint.reshape(out_ref.shape)
    out_ref[...] = joint
    again_ref[...] = joint
    rounded_ref[...] = joint.astype(BF16)


def joint_solve(own, other, images, shape):
    size = images.shape[0]
    k = shape[1]
    return pl.pallas_call(
        functools.partial(joint_kernel, k),
        in_specs=vmem_specs(3),
        out_specs=vmem_specs(3),
        out_shape=[
            jax.ShapeDtypeStruct(shape, F32),
            jax.ShapeDtypeStruct(shape, F32),
            jax.ShapeDtypeStruct(shape, BF16),
        ],
        scratch_shapes=[pltpu.VMEM((size, size), F32), pltpu.VMEM((size + k, size // 2), F32)],
        compiler_params=params(8),
        name="joint_solve",
    )(own, other, images)


def around(x, axis, count):
    pieces = [x]
    for d in range(1, count):
        pieces.append(lax.ppermute(x, axis, [(m ^ d, m) for m in range(count)]))
    return pieces


def add_pieces(pieces):
    if len(pieces) == 1:
        return pieces[0]
    return (pieces[0] + pieces[1]) + (pieces[2] + pieces[3])


def per_device(shards, groups, blocks, block_rows, block_cols, counts, start):
    few = shards == 4
    layers = start.shape[0]

    def gather(x):
        return around(x, "node", shards) if few else lax.all_gather(x, "node")

    def total(x):
        return add_pieces(around(x, "node", shards)) if few else lax.psum(x, "node")

    first = gather(start.astype(BF16))
    dense = build_dense(block_rows, block_cols, counts, blocks, shards * BROWS // CHUNK_COLS)
    if few:
        images = [apply_first(layer, first, dense[layer]) for layer in range(layers)]
        images = [apply_second(gather(images[layer]), dense[layer]) for layer in range(layers)]
    else:
        image, gram = apply_dense("gram", first, dense)
        (image,) = apply_dense("plain", gather(solve(total(gram), image)), dense)
        images = [image[layer] for layer in range(layers)]
    own, stacked = cross([around(image, "layer", groups) for image in images])
    own = total(own)
    other = lax.ppermute(own, "layer", [(m ^ 1, m) for m in range(groups)])
    joint_basis, again, rounded = joint_solve(own, other, stacked, start.shape)
    if few:
        partial = apply_score(gather(rounded), again, dense)
    else:
        (partial,) = apply_dense("score", gather(rounded), dense, again)
    return joint_basis, total(partial)


def solution(mesh):
    in_specs = (
        P(("parts", "layer"), "node", None),
        P(("parts", "layer"), "node"),
        P(("parts", "layer"), "node"),
        P(("parts", "layer"), "node"),
        P(("parts", "layer"), None, "node"),
    )
    out_specs = (P(("parts", "layer"), None, "node"), P(("parts", "layer"), None, None))
    return jax.shard_map(
        functools.partial(per_device, mesh.shape["node"], mesh.shape["layer"]),
        mesh=mesh,
        in_specs=in_specs,
        out_specs=out_specs,
        check_vma=False,
    )
```

```python
import functools

import jax
import jax.numpy as jnp
from jax import lax
from jax.experimental import pallas as pl
from jax.experimental.pallas import tpu as pltpu
from jax.sharding import PartitionSpec as P

BLK = 64
ROWS_DEV = 512
BROWS = ROWS_DEV // BLK
CHUNK_COLS = 8
CHUNK_LANES = CHUNK_COLS * 2 * BLK
TALL = BROWS * BLK // 2
MIB = 1024 * 1024
F32 = jnp.float32
BF16 = jnp.bfloat16
HIGHEST = lax.Precision.HIGHEST
TRANS_B = (((1,), (1,)), ((), ()))
TRANS_A = (((0,), (0,)), ((), ()))


def params(mib):
    return pltpu.CompilerParams(vmem_limit_bytes=mib * MIB)


def vmem_specs(count):
    return [pl.BlockSpec(memory_space=pltpu.VMEM)] * count


def place(z, chunks, u, dense_ref):
    for c in range(chunks * CHUNK_COLS):
        piece = z[c * 8 : c * 8 + 8]
        piece = jnp.concatenate([piece[:, :128], piece[:, 128:]], axis=0)
        hi = piece.astype(BF16)
        lo = (piece - hi.astype(F32)).astype(BF16)
        lanes = slice((c % CHUNK_COLS) * 128, (c % CHUNK_COLS) * 128 + 128)
        dense_ref[c // CHUNK_COLS, pl.ds(pl.multiple_of(u * 16, 16), 16), lanes] = hi
        dense_ref[c // CHUNK_COLS, pl.ds(pl.multiple_of(u * 16 + TALL, 16), 16), lanes] = lo


def one_hot(rows_ref, cols_ref, counts_ref, layer, flip, base, positions):
    slot = lax.broadcasted_iota(jnp.int32, (1, rows_ref.shape[1]), 1)
    key = (cols_ref[pl.ds(layer, 1), :] ^ flip) * BROWS + rows_ref[pl.ds(layer, 1), :]
    key = jnp.where(slot < counts_ref[0, layer], key, -1)
    position = lax.broadcasted_iota(jnp.int32, (positions, key.shape[1]), 0) + base
    return jnp.where(position == key, 1.0, 0.0).astype(BF16)


def build_kernel(rows_ref, cols_ref, counts_ref, blocks_ref, dense_ref):
    chunks = dense_ref.shape[1]
    positions = chunks * CHUNK_COLS * BROWS
    base = pl.program_id(1) * positions
    onehot = one_hot(rows_ref, cols_ref, counts_ref, pl.program_id(0), 0, base, positions)

    def step(u, carry):
        cols = pl.ds(pl.multiple_of(u * 256, 256), 256)
        z = jnp.dot(onehot, blocks_ref[0, :, cols], preferred_element_type=F32)
        place(z, chunks, u, dense_ref.at[0])
        return carry

    lax.fori_loop(0, BLK * BLK // 256, step, 0)


def build_whole_kernel(rows_hbm, cols_hbm, counts_hbm, blocks_ref, *refs):
    *dense_refs, held, rows_ref, cols_ref, counts_ref, arrived, index_arrived = refs
    layers, chunks = len(dense_refs), dense_refs[0].shape[0]
    index_copies = [
        pltpu.make_async_copy(source, target, index_arrived.at[i])
        for i, (source, target) in enumerate(
            [(rows_hbm, rows_ref), (cols_hbm, cols_ref), (counts_hbm, counts_ref)]
        )
    ]
    for copy in index_copies:
        copy.start()
    pieces = arrived.shape[1]
    width = held.shape[2] // pieces
    inner = width // 256

    def fetch(layer, piece):
        cols = pl.ds(pl.multiple_of(piece * width, width), width)
        return pltpu.make_async_copy(
            blocks_ref.at[layer, :, cols], held.at[layer, :, cols], arrived.at[layer, piece]
        )

    for layer in range(layers):
        for piece in range(pieces):
            fetch(layer, piece).start()
    flip = lax.axis_index("node") * CHUNK_COLS
    for copy in index_copies:
        copy.wait()
    for layer in range(layers):
        onehot = one_hot(rows_ref, cols_ref, counts_ref, layer, flip, 0, chunks * CHUNK_COLS * BROWS)

        def step(piece, carry):
            fetch(layer, piece).wait()
            for v in range(inner):
                cols = pl.ds(pl.multiple_of(piece * width + v * 256, 256), 256)
                z = jnp.dot(onehot, held[layer, :, cols], preferred_element_type=F32)
                place(z, chunks, piece * inner + v, dense_refs[layer])
            return carry

        lax.fori_loop(0, pieces, step, 0)


def build_dense(block_rows, block_cols, counts, blocks, chunk_total):
    layers, slots, width = blocks.shape
    dense = jax.ShapeDtypeStruct((layers, chunk_total, 2 * TALL, CHUNK_LANES), BF16)
    operands = (block_rows, block_cols, counts.T, blocks)
    if chunk_total <= 4:
        pieces = 4
        return pl.pallas_call(
            build_whole_kernel,
            in_specs=[pl.BlockSpec(memory_space=pltpu.HBM)] * 4,
            out_specs=vmem_specs(layers),
            out_shape=[jax.ShapeDtypeStruct(dense.shape[1:], BF16)] * layers,
            scratch_shapes=[
                pltpu.VMEM(blocks.shape, BF16),
                pltpu.VMEM(block_rows.shape, jnp.int32),
                pltpu.VMEM(block_cols.shape, jnp.int32),
                pltpu.SMEM((1, layers), jnp.int32),
                pltpu.SemaphoreType.DMA((layers, pieces)),
                pltpu.SemaphoreType.DMA((3,)),
            ],
            compiler_params=params(28),
            name="build_dense",
        )(*[pltpu.with_memory_space_constraint(x, pltpu.HBM) for x in operands])
    return pl.pallas_call(
        build_kernel,
        grid=(layers, chunk_total // 4),
        in_specs=vmem_specs(2)
        + [
            pl.BlockSpec(memory_space=pltpu.SMEM),
            pl.BlockSpec((1, slots, width), lambda l, s: (l, 0, 0)),
        ],
        out_specs=pl.BlockSpec((1, 4, 2 * TALL, CHUNK_LANES), lambda l, s: (l, s, 0, 0)),
        out_shape=dense,
        compiler_params=params(24),
        name="build_dense",
    )(*operands)


def split3(x):
    a = x.astype(BF16)
    r = x - a.astype(F32)
    b = r.astype(BF16)
    c = (r - b.astype(F32)).astype(BF16)
    return a, b, c


def image_part(basis, dense):
    k, width = basis.shape
    basis = basis.astype(F32)
    tall = jnp.concatenate([basis, basis], axis=0).T
    lane = lax.broadcasted_iota(jnp.int32, tall.shape, 1)
    first = jnp.where(lane < k, tall, 0.0).astype(BF16)
    second = jnp.where(lane < k, 0.0, tall).astype(BF16)
    weights = []
    for c in range(width // BLK):
        weights += [first[c * BLK : c * BLK + BLK], second[c * BLK : c * BLK + BLK]]
    return jnp.dot(dense, jnp.concatenate(weights, axis=0), preferred_element_type=F32)


def to_wide(total, k, halves, tall):
    halves[:, : 2 * k] = total[:TALL] + total[TALL:]
    halves[:, 2 * k :] = jnp.zeros((TALL, 128 - 2 * k), F32)
    for b in range(BROWS):
        part = halves[pl.ds(b, BLK // 2, stride=BROWS), :]
        tall[pl.ds(BLK * b, BLK // 2, stride=2), :] = part
        tall[pl.ds(BLK * b + 1, BLK // 2, stride=2), :] = pltpu.roll(part, 128 - k, 1)
    return tall[...].T[:k]


def against(left, tall):
    k = left.shape[0]
    lane = lax.broadcasted_iota(jnp.int32, tall.shape, 1)
    a, b, c = split3(jnp.where(lane < k, tall, 0.0))
    right = a.astype(F32) + pltpu.roll(b.astype(F32), k, 1) + pltpu.roll(c.astype(F32), 2 * k, 1)
    pieces = jnp.dot(jnp.concatenate(split3(left), axis=0), right.astype(BF16), preferred_element_type=F32)
    top, middle, bottom = pieces[:k], pieces[k : 2 * k], pieces[2 * k :]
    total = top[:, :k] + (top[:, k : 2 * k] + middle[:, :k])
    return total + (middle[:, k : 2 * k] + (top[:, 2 * k : 3 * k] + bottom[:, :k]))


def apply_kernel(mode, *refs):
    basis_ref, refs = refs[0], refs[1:]
    if mode == "score":
        left_ref, refs = refs[0], refs[1:]
    dense_ref, out_ref = refs[:2]
    halves, tall, acc = refs[-3:]
    layer, chunk = pl.program_id(0), pl.program_id(1)
    total = image_part(basis_ref[chunk, layer], dense_ref[0, 0])

    @pl.when(chunk == 0)
    def _():
        acc[...] = total

    @pl.when(chunk > 0)
    def _():
        acc[...] += total

    @pl.when(chunk == pl.num_programs(1) - 1)
    def _():
        image = to_wide(acc[...], basis_ref.shape[2], halves, tall)
        if mode != "score":
            out_ref[0] = image
        if mode == "gram":
            refs[2][0] = against(image, tall[...])
        if mode == "score":
            out_ref[0] = against(left_ref[0], tall[...])


def product(a, b):
    k = a.shape[0]
    left = jnp.concatenate(split3(a), axis=0)
    right = left if b is a else jnp.concatenate(split3(b), axis=0)
    pieces = lax.dot_general(left, right, TRANS_B, preferred_element_type=F32)
    top, middle, bottom = pieces[:k], pieces[k : 2 * k], pieces[2 * k :]
    total = top[:, :k] + (top[:, k : 2 * k] + middle[:, :k])
    return total + (middle[:, k : 2 * k] + (top[:, 2 * k : 3 * k] + bottom[:, :k]))


def image_of(parts, dense_ref):
    return sum(image_part(part, dense_ref[chunk]) for chunk, part in enumerate(parts))


def first_kernel(layer, piece_count, *refs):
    pieces, (dense_ref, out_ref, halves, tall) = refs[:piece_count], refs[piece_count:]
    total = image_of([piece[layer] for piece in pieces], dense_ref)
    out_ref[...] = to_wide(total, out_ref.shape[0], halves, tall)


def second_kernel(piece_count, *refs):
    pieces, (dense_ref, out_ref, halves, tall) = refs[:piece_count], refs[piece_count:]
    image = jnp.concatenate([piece[...] for piece in pieces], axis=1)
    inverse = inverse_factor(product(image, image))
    basis = jnp.dot(inverse, image, precision=HIGHEST, preferred_element_type=F32)
    parts = [basis[:, d * ROWS_DEV : d * ROWS_DEV + ROWS_DEV] for d in range(piece_count)]
    out_ref[...] = to_wide(image_of(parts, dense_ref), out_ref.shape[0], halves, tall)


def own_kernel(basis_ref, *refs):
    *dense_refs, out_ref = refs
    for layer, dense_ref in enumerate(dense_refs):
        out_ref[layer] = image_part(basis_ref[layer], dense_ref[0])


def score_kernel(layers, piece_count, own_ref, *refs):
    pieces, left_ref, refs = refs[:piece_count], refs[piece_count], refs[piece_count + 1 :]
    dense_refs, (out_ref, halves, tall) = refs[:layers], refs[layers:]
    totals = [
        own_ref[layer]
        + sum(image_part(piece[layer], dense_refs[layer][d + 1]) for d, piece in enumerate(pieces))
        for layer in range(layers)
    ]
    wide = [
        to_wide(totals[layer], left_ref.shape[1], halves.at[layer], tall.at[layer]) for layer in range(layers)
    ]
    for layer in range(layers):
        out_ref[layer] = product(left_ref[layer], wide[layer])


def apply_whole(kernel, name, operands, out_shape, *lead):
    return pl.pallas_call(
        kernel,
        in_specs=vmem_specs(len(operands)),
        out_specs=pl.BlockSpec(memory_space=pltpu.VMEM),
        out_shape=jax.ShapeDtypeStruct(out_shape, F32),
        scratch_shapes=[pltpu.VMEM((*lead, TALL, 128), F32), pltpu.VMEM((*lead, ROWS_DEV, 128), F32)],
        compiler_params=params(14),
        cost_estimate=pl.CostEstimate(flops=0, bytes_accessed=4 * MIB, transcendentals=0),
        name=name,
    )(*operands)


def apply_first(layer, pieces, dense):
    kernel = functools.partial(first_kernel, layer, len(pieces))
    return apply_whole(kernel, "apply_first", [*pieces, dense], pieces[0].shape[1:])


def apply_second(pieces, dense):
    kernel = functools.partial(second_kernel, len(pieces))
    return apply_whole(kernel, "apply_second", [*pieces, dense], pieces[0].shape)


def apply_own(basis, dense):
    layers, k = basis.shape[:2]
    return pl.pallas_call(
        own_kernel,
        in_specs=vmem_specs(1 + layers),
        out_specs=pl.BlockSpec(memory_space=pltpu.VMEM),
        out_shape=jax.ShapeDtypeStruct((layers, 2 * TALL, 2 * k), F32),
        compiler_params=params(14),
        cost_estimate=pl.CostEstimate(flops=0, bytes_accessed=2 * MIB, transcendentals=0),
        name="apply_own",
    )(basis, *dense)


def apply_score(pieces, left, dense):
    kernel = functools.partial(score_kernel, len(dense), len(pieces) - 1)
    layers, k = left.shape[:2]
    operands = [apply_own(pieces[0], dense), *pieces[1:], left, *dense]
    return apply_whole(kernel, "apply_score", operands, (layers, k, k), layers)


def apply_dense(mode, basis, dense, left=None):
    layers, chunks = dense.shape[:2]
    k = basis.shape[-2]
    image = jax.ShapeDtypeStruct((layers, k, ROWS_DEV), F32)
    small = jax.ShapeDtypeStruct((layers, k, k), F32)
    out_shape = {"gram": [image, small], "plain": [image], "score": [small]}[mode]
    operands = [basis] + ([left] if mode == "score" else []) + [dense]
    dense_spec = pl.BlockSpec((1, 1, 2 * TALL, CHUNK_LANES), lambda l, s: (l, s, 0, 0))
    image_spec = pl.BlockSpec((1, k, ROWS_DEV), lambda l, s: (l, 0, 0))
    small_spec = pl.BlockSpec((1, k, k), lambda l, s: (l, 0, 0))
    return pl.pallas_call(
        functools.partial(apply_kernel, mode),
        grid=(layers, chunks),
        in_specs=vmem_specs(1) + ([image_spec] if mode == "score" else []) + [dense_spec],
        out_specs={"gram": [image_spec, small_spec], "plain": [image_spec], "score": [small_spec]}[mode],
        out_shape=out_shape,
        scratch_shapes=[
            pltpu.VMEM((TALL, 128), F32),
            pltpu.VMEM((ROWS_DEV, 128), F32),
            pltpu.VMEM((2 * TALL, 2 * k), F32),
        ],
        compiler_params=params(12),
        name="apply_" + mode,
    )(*operands)


def spread(x):
    return jnp.broadcast_to(x, (8, 128))


def eliminate(rows, offset):
    groups, tiles = len(rows), len(rows[0])
    rows = [list(row) for row in rows]
    home, at = offset // 128, offset % 128
    sub = lax.broadcasted_iota(jnp.int32, (8, 128), 0)
    solved = []
    for h in range(groups):
        below = range(h + 1, groups)
        lane = at + 8 * h
        col = [{g: spread(rows[g][home][:, lane + q : lane + q + 1]) for g in range(h, groups)} for q in range(8)]
        cell = {(p, q): spread(col[p][h][q : q + 1]) for q in range(8) for p in range(q + 1)}
        row = [[spread(rows[h][t][q : q + 1]) for t in range(tiles)] for q in range(8)]
        done = []
        for m in range(0, 8, 2):
            n = m + 1
            a, b, c = cell[m, m], cell[m, n], cell[n, n]
            det = a * c - b * b
            if m % 4 == 0:
                r = pl.reciprocal(det, approx=True)
            else:
                r = square * pl.reciprocal(whole, approx=True)
            later = range(m + 2, 8)
            u = {q: c * cell[m, q] - b * cell[n, q] for q in later}
            v = {q: a * cell[n, q] - b * cell[m, q] for q in later}
            taken = {(p, q): cell[m, p] * u[q] + cell[n, p] * v[q] for q in later for p in range(m + 2, q + 1)}
            if m % 4 == 0:
                i, j = m + 2, m + 3
                first, cross, last = (det * cell[pq] - taken[pq] for pq in ((i, i), (i, j), (j, j)))
                whole = first * last - cross * cross
                square = det * det
            for pq in taken:
                cell[pq] = cell[pq] - r * taken[pq]
            for q in later:
                for g in below:
                    col[q][g] = col[q][g] - r * (col[m][g] * u[q] + col[n][g] * v[q])
            for t in range(tiles):
                x = r * (c * row[m][t] - b * row[n][t])
                y = r * (a * row[n][t] - b * row[m][t])
                for q in later:
                    row[q][t] = row[q][t] - (cell[m, q] * x + cell[n, q] * y)
                for g in below:
                    rows[g][t] = rows[g][t] - (col[m][g] * x + col[n][g] * y)
            over = pl.reciprocal(a, approx=True)
            done.append([lax.rsqrt(a) * x for x in row[m]])
            scale = lax.rsqrt(det * over)
            done.append([scale * (x - (b * over) * w) for x, w in zip(row[n], row[m])])
        finished = []
        for t in range(tiles):
            x = done[7][t]
            for q in range(7):
                x = jnp.where(sub == q, done[q][t], x)
            finished.append(x)
        solved.append(finished)
    return solved


def tiled(x):
    return [
        [x[g * 8 : g * 8 + 8, t * 128 : t * 128 + 128] for t in range(x.shape[1] // 128)]
        for g in range(x.shape[0] // 8)
    ]


def joined(tiles):
    return jnp.concatenate([jnp.concatenate(row, axis=1) for row in tiles], axis=0)


def unit_scale(gram):
    lane = lax.broadcasted_iota(jnp.int32, gram.shape, 1)
    sub = lax.broadcasted_iota(jnp.int32, gram.shape, 0)
    kept = jnp.where(lane == sub, gram, 0.0)
    down = 1.0 / jnp.sqrt(jnp.sum(kept, axis=1, keepdims=True))
    across = jnp.sum(kept, axis=0, keepdims=True)
    across = 1.0 / jnp.sqrt(jnp.where(across == 0.0, 1.0, across))
    return gram * down * across, across


def gram_update(panel, first):
    a, b, c = split3(panel)
    left = jnp.concatenate([a, a, b, b, a, c], axis=0)
    right = jnp.concatenate([a, b, a, b, c, a], axis=0)
    parts = {
        at: lax.dot_general(left[:, at : at + 128], right, TRANS_A, preferred_element_type=F32)
        for at in range(first, panel.shape[1], 128)
    }
    return lambda at, count: parts[at // 128 * 128][at % 128 : at % 128 + count]


def inverse_factor(gram):
    k = gram.shape[0]
    lane = lax.broadcasted_iota(jnp.int32, (k, 128), 1)
    sub = lax.broadcasted_iota(jnp.int32, (k, 128), 0)
    eye = jnp.where(lane == sub, 1.0, 0.0)
    gram, across = unit_scale(jnp.concatenate([gram, jnp.zeros((k, 128 - k), F32)], axis=1))
    solved = eliminate(tiled(jnp.concatenate([gram, eye], axis=1)), 0)
    return (joined(solved)[:, 128:] * across)[:, :k]


def solve_kernel(gram_ref, image_ref, out_ref):
    for layer in range(image_ref.shape[0]):
        inverse = inverse_factor(gram_ref[layer])
        solved = jnp.dot(inverse, image_ref[layer], precision=HIGHEST, preferred_element_type=F32)
        out_ref[layer] = solved.astype(BF16)


def solve(gram, image):
    return pl.pallas_call(
        solve_kernel,
        in_specs=vmem_specs(2),
        out_specs=pl.BlockSpec(memory_space=pltpu.VMEM),
        out_shape=jax.ShapeDtypeStruct(image.shape, BF16),
        compiler_params=params(4),
        name="solve_layers",
    )(gram, image)


def cross_kernel(k, groups, *refs):
    pieces, (out_ref, stacked, packed) = refs[:-3], refs[-3:]
    g = lax.axis_index("layer")
    layers = len(pieces) // groups
    for i, piece in enumerate(pieces):
        at = ((g ^ (i % groups)) * layers + i // groups) * k
        stacked[pl.ds(pl.multiple_of(at, k), k)] = piece[...]
    gram = lax.dot_general(
        stacked[...], stacked[...], TRANS_B, precision=HIGHEST, preferred_element_type=F32
    )
    half = gram.shape[0] // 2
    first, last = gram[:half, :half], gram[half:, half:]
    row = lax.broadcasted_iota(jnp.int32, (half, half), 0) // k
    col = lax.broadcasted_iota(jnp.int32, (half, half), 1) // k
    packed[:half] = gram[:half, half:]
    packed[half : 2 * half] = jnp.where(col >= row, first, last)
    diagonal = jnp.where(col == row, last, 0.0)
    packed[2 * half :] = sum(diagonal[r * k : r * k + k] for r in range(half // k))
    rows = out_ref.shape[0]
    out_ref[...] = packed[pl.ds(pl.multiple_of((g & 1) * rows, 16), rows)]


def cross(chains):
    k, width = chains[0][0].shape
    groups = len(chains[0])
    size = len(chains) * groups * k
    pieces = [piece for chain in chains for piece in chain]
    return pl.pallas_call(
        functools.partial(cross_kernel, k, groups),
        in_specs=vmem_specs(len(pieces)),
        out_specs=vmem_specs(2),
        out_shape=[
            jax.ShapeDtypeStruct(((size + k) // 2, size // 2), F32),
            jax.ShapeDtypeStruct((size, width), F32),
        ],
        scratch_shapes=[pltpu.VMEM((size + k, size // 2), F32)],
        compiler_params=params(6),
        name="cross_gram",
    )(*pieces)


def unpack(packed, k, work):
    half = packed.shape[1]
    row = lax.broadcasted_iota(jnp.int32, (half, half), 0) // k
    col = lax.broadcasted_iota(jnp.int32, (half, half), 1) // k
    mixed = packed[half : 2 * half]
    under = jnp.where(col < row, mixed, 0.0)
    diagonal = jnp.concatenate([packed[2 * half :]] * (half // k), axis=0)
    work[:half, :half] = jnp.where(col >= row, mixed, 0.0)
    work[:half, half:] = packed[:half]
    work[half:, :half] = jnp.zeros((half, half), F32)
    work[half:, half:] = under.T + jnp.where(col == row, diagonal, 0.0)


def joint_kernel(k, *refs):
    own_ref, other_ref, images_ref, out_ref, again_ref, rounded_ref, work, packed = refs
    rows = own_ref.shape[0]
    odd = lax.axis_index("layer") & 1
    packed[pl.ds(pl.multiple_of(odd * rows, 16), rows)] = own_ref[...]
    packed[pl.ds(pl.multiple_of((1 - odd) * rows, 16), rows)] = other_ref[...]
    unpack(packed[...], k, work)
    size = work.shape[0]
    steps = size // k
    lane = lax.broadcasted_iota(jnp.int32, (k, size), 1)
    lane_128 = lax.broadcasted_iota(jnp.int32, (k, 128), 1)
    sub_128 = lax.broadcasted_iota(jnp.int32, (k, 128), 0)
    gram, across = unit_scale(work[...])
    work[...] = gram
    for s in range(steps):
        lo, hi = s * k, (s + 1) * k
        here = (lane >= lo) & (lane < hi)
        eye = jnp.where(lane_128 == sub_128 + lo % 128, 1.0, 0.0)
        solved = joined(eliminate(tiled(jnp.concatenate([work[lo:hi], eye], axis=1)), lo))
        panel, tail = solved[:, :size], solved[:, size:]
        panel = jnp.where(here, jnp.concatenate([tail] * (size // 128), axis=1), panel)
        work[lo:hi] = jnp.where(lane < hi, panel, 0.0)
        if s + 1 < steps:
            update = gram_update(panel, hi // 128 * 128)
            for r in range(s + 1, steps):
                rows = work[r * k : r * k + k]
                work[r * k : r * k + k] = jnp.where(here, 0.0, rows) - update(r * k, k)
    rows = out_ref.shape[0] * k
    own = work[pl.ds(pl.multiple_of(lax.axis_index("layer") * rows, rows), rows)] * across
    joint = jnp.dot(own, images_ref[...], precision=HIGHEST, preferred_element_type=F32)
    joint = joint.reshape(out_ref.shape)
    out_ref[...] = joint
    again_ref[...] = joint
    rounded_ref[...] = joint.astype(BF16)


def joint_solve(own, other, images, shape):
    size = images.shape[0]
    k = shape[1]
    return pl.pallas_call(
        functools.partial(joint_kernel, k),
        in_specs=vmem_specs(3),
        out_specs=vmem_specs(3),
        out_shape=[
            jax.ShapeDtypeStruct(shape, F32),
            jax.ShapeDtypeStruct(shape, F32),
            jax.ShapeDtypeStruct(shape, BF16),
        ],
        scratch_shapes=[pltpu.VMEM((size, size), F32), pltpu.VMEM((size + k, size // 2), F32)],
        compiler_params=params(8),
        name="joint_solve",
    )(own, other, images)


def around(x, axis, count):
    pieces = [x]
    for d in range(1, count):
        pieces.append(lax.ppermute(x, axis, [(m ^ d, m) for m in range(count)]))
    return pieces


def add_pieces(pieces):
    if len(pieces) == 1:
        return pieces[0]
    return (pieces[0] + pieces[1]) + (pieces[2] + pieces[3])


def per_device(shards, groups, blocks, block_rows, block_cols, counts, start):
    few = shards == 4
    layers = start.shape[0]

    def gather(x):
        return around(x, "node", shards) if few else lax.all_gather(x, "node")

    def total(x):
        return add_pieces(around(x, "node", shards)) if few else lax.psum(x, "node")

    first = gather(start.astype(BF16))
    dense = build_dense(block_rows, block_cols, counts, blocks, shards * BROWS // CHUNK_COLS)
    if few:
        images = [apply_first(layer, first, dense[layer]) for layer in range(layers)]
        images = [apply_second(gather(images[layer]), dense[layer]) for layer in range(layers)]
    else:
        image, gram = apply_dense("gram", first, dense)
        (image,) = apply_dense("plain", gather(solve(total(gram), image)), dense)
        images = [image[layer] for layer in range(layers)]
    own, stacked = cross([around(image, "layer", groups) for image in images])
    own = total(own)
    other = lax.ppermute(own, "layer", [(m ^ 1, m) for m in range(groups)])
    joint_basis, again, rounded = joint_solve(own, other, stacked, start.shape)
    if few:
        partial = apply_score(gather(rounded), again, dense)
    else:
        (partial,) = apply_dense("score", gather(rounded), dense, again)
    return joint_basis, total(partial)


def solution(mesh):
    in_specs = (
        P(("parts", "layer"), "node", None),
        P(("parts", "layer"), "node"),
        P(("parts", "layer"), "node"),
        P(("parts", "layer"), "node"),
        P(("parts", "layer"), None, "node"),
    )
    out_specs = (P(("parts", "layer"), None, "node"), P(("parts", "layer"), None, None))
    return jax.shard_map(
        functools.partial(per_device, mesh.shape["node"], mesh.shape["layer"]),
        mesh=mesh,
        in_specs=in_specs,
        out_specs=out_specs,
        check_vma=False,
    )
```

```python
import functools

import jax
import jax.numpy as jnp
from jax import lax
from jax.experimental import pallas as pl
from jax.experimental.pallas import tpu as pltpu
from jax.sharding import PartitionSpec as P

BLK = 64
ROWS_DEV = 512
BROWS = ROWS_DEV // BLK
CHUNK_COLS = 8
CHUNK_LANES = CHUNK_COLS * 2 * BLK
TALL = BROWS * BLK // 2
MIB = 1024 * 1024
F32 = jnp.float32
BF16 = jnp.bfloat16
HIGHEST = lax.Precision.HIGHEST
TRANS_B = (((1,), (1,)), ((), ()))
TRANS_A = (((0,), (0,)), ((), ()))
SPREAD = (2, 88, 128)


def params(mib):
    return pltpu.CompilerParams(vmem_limit_bytes=mib * MIB)


def vmem_specs(count):
    return [pl.BlockSpec(memory_space=pltpu.VMEM)] * count


def place(z, chunks, u, dense_ref):
    for c in range(chunks * CHUNK_COLS):
        piece = z[c * 8 : c * 8 + 8]
        piece = jnp.concatenate([piece[:, :128], piece[:, 128:]], axis=0)
        hi = piece.astype(BF16)
        lo = (piece - hi.astype(F32)).astype(BF16)
        lanes = slice((c % CHUNK_COLS) * 128, (c % CHUNK_COLS) * 128 + 128)
        dense_ref[c // CHUNK_COLS, pl.ds(pl.multiple_of(u * 16, 16), 16), lanes] = hi
        dense_ref[c // CHUNK_COLS, pl.ds(pl.multiple_of(u * 16 + TALL, 16), 16), lanes] = lo


def one_hot(rows_ref, cols_ref, counts_ref, layer, flip, base, positions):
    slot = lax.broadcasted_iota(jnp.int32, (1, rows_ref.shape[1]), 1)
    key = (cols_ref[pl.ds(layer, 1), :] ^ flip) * BROWS + rows_ref[pl.ds(layer, 1), :]
    key = jnp.where(slot < counts_ref[0, layer], key, -1)
    position = lax.broadcasted_iota(jnp.int32, (positions, key.shape[1]), 0) + base
    return jnp.where(position == key, 1.0, 0.0).astype(BF16)


def build_kernel(rows_ref, cols_ref, counts_ref, blocks_ref, dense_ref):
    chunks = dense_ref.shape[1]
    positions = chunks * CHUNK_COLS * BROWS
    base = pl.program_id(1) * positions
    onehot = one_hot(rows_ref, cols_ref, counts_ref, pl.program_id(0), 0, base, positions)

    def step(u, carry):
        cols = pl.ds(pl.multiple_of(u * 256, 256), 256)
        z = jnp.dot(onehot, blocks_ref[0, :, cols], preferred_element_type=F32)
        place(z, chunks, u, dense_ref.at[0])
        return carry

    lax.fori_loop(0, BLK * BLK // 256, step, 0)


def build_whole_kernel(rows_hbm, cols_hbm, counts_hbm, blocks_ref, *refs):
    *dense_refs, held, rows_ref, cols_ref, counts_ref, arrived, index_arrived = refs
    layers, chunks = len(dense_refs), dense_refs[0].shape[0]
    index_copies = [
        pltpu.make_async_copy(source, target, index_arrived.at[i])
        for i, (source, target) in enumerate(
            [(rows_hbm, rows_ref), (cols_hbm, cols_ref), (counts_hbm, counts_ref)]
        )
    ]
    for copy in index_copies:
        copy.start()
    pieces = arrived.shape[1]
    width = held.shape[2] // pieces
    inner = width // 256

    def fetch(layer, piece):
        cols = pl.ds(pl.multiple_of(piece * width, width), width)
        return pltpu.make_async_copy(
            blocks_ref.at[layer, :, cols], held.at[layer, :, cols], arrived.at[layer, piece]
        )

    for layer in range(layers):
        for piece in range(pieces):
            fetch(layer, piece).start()
    flip = lax.axis_index("node") * CHUNK_COLS
    for copy in index_copies:
        copy.wait()
    for layer in range(layers):
        onehot = one_hot(rows_ref, cols_ref, counts_ref, layer, flip, 0, chunks * CHUNK_COLS * BROWS)

        def step(piece, carry):
            fetch(layer, piece).wait()
            for v in range(inner):
                cols = pl.ds(pl.multiple_of(piece * width + v * 256, 256), 256)
                z = jnp.dot(onehot, held[layer, :, cols], preferred_element_type=F32)
                place(z, chunks, piece * inner + v, dense_refs[layer])
            return carry

        lax.fori_loop(0, pieces, step, 0)


def build_dense(block_rows, block_cols, counts, blocks, chunk_total):
    layers, slots, width = blocks.shape
    dense = jax.ShapeDtypeStruct((layers, chunk_total, 2 * TALL, CHUNK_LANES), BF16)
    operands = (block_rows, block_cols, counts.T, blocks)
    if chunk_total <= 4:
        pieces = 4
        return pl.pallas_call(
            build_whole_kernel,
            in_specs=[pl.BlockSpec(memory_space=pltpu.HBM)] * 4,
            out_specs=vmem_specs(layers),
            out_shape=[jax.ShapeDtypeStruct(dense.shape[1:], BF16)] * layers,
            scratch_shapes=[
                pltpu.VMEM(blocks.shape, BF16),
                pltpu.VMEM(block_rows.shape, jnp.int32),
                pltpu.VMEM(block_cols.shape, jnp.int32),
                pltpu.SMEM((1, layers), jnp.int32),
                pltpu.SemaphoreType.DMA((layers, pieces)),
                pltpu.SemaphoreType.DMA((3,)),
            ],
            compiler_params=params(28),
            name="build_dense",
        )(*[pltpu.with_memory_space_constraint(x, pltpu.HBM) for x in operands])
    return pl.pallas_call(
        build_kernel,
        grid=(layers, chunk_total // 4),
        in_specs=vmem_specs(2)
        + [
            pl.BlockSpec(memory_space=pltpu.SMEM),
            pl.BlockSpec((1, slots, width), lambda l, s: (l, 0, 0)),
        ],
        out_specs=pl.BlockSpec((1, 4, 2 * TALL, CHUNK_LANES), lambda l, s: (l, s, 0, 0)),
        out_shape=dense,
        compiler_params=params(24),
        name="build_dense",
    )(*operands)


def split3(x):
    a = x.astype(BF16)
    r = x - a.astype(F32)
    b = r.astype(BF16)
    c = (r - b.astype(F32)).astype(BF16)
    return a, b, c


def image_part(basis, dense):
    k, width = basis.shape
    basis = basis.astype(F32)
    tall = jnp.concatenate([basis, basis], axis=0).T
    lane = lax.broadcasted_iota(jnp.int32, tall.shape, 1)
    first = jnp.where(lane < k, tall, 0.0).astype(BF16)
    second = jnp.where(lane < k, 0.0, tall).astype(BF16)
    weights = []
    for c in range(width // BLK):
        weights += [first[c * BLK : c * BLK + BLK], second[c * BLK : c * BLK + BLK]]
    return jnp.dot(dense, jnp.concatenate(weights, axis=0), preferred_element_type=F32)


def to_wide(total, k, halves, tall):
    halves[:, : 2 * k] = total[:TALL] + total[TALL:]
    halves[:, 2 * k :] = jnp.zeros((TALL, 128 - 2 * k), F32)
    for b in range(BROWS):
        part = halves[pl.ds(b, BLK // 2, stride=BROWS), :]
        tall[pl.ds(BLK * b, BLK // 2, stride=2), :] = part
        tall[pl.ds(BLK * b + 1, BLK // 2, stride=2), :] = pltpu.roll(part, 128 - k, 1)
    return tall[...].T[:k]


def against(left, tall):
    k = left.shape[0]
    lane = lax.broadcasted_iota(jnp.int32, tall.shape, 1)
    a, b, c = split3(jnp.where(lane < k, tall, 0.0))
    right = a.astype(F32) + pltpu.roll(b.astype(F32), k, 1) + pltpu.roll(c.astype(F32), 2 * k, 1)
    pieces = jnp.dot(jnp.concatenate(split3(left), axis=0), right.astype(BF16), preferred_element_type=F32)
    top, middle, bottom = pieces[:k], pieces[k : 2 * k], pieces[2 * k :]
    total = top[:, :k] + (top[:, k : 2 * k] + middle[:, :k])
    return total + (middle[:, k : 2 * k] + (top[:, 2 * k : 3 * k] + bottom[:, :k]))


def apply_kernel(mode, *refs):
    basis_ref, refs = refs[0], refs[1:]
    if mode == "score":
        left_ref, refs = refs[0], refs[1:]
    dense_ref, out_ref = refs[:2]
    halves, tall, acc = refs[-3:]
    layer, chunk = pl.program_id(0), pl.program_id(1)
    total = image_part(basis_ref[chunk, layer], dense_ref[0, 0])

    @pl.when(chunk == 0)
    def _():
        acc[...] = total

    @pl.when(chunk > 0)
    def _():
        acc[...] += total

    @pl.when(chunk == pl.num_programs(1) - 1)
    def _():
        image = to_wide(acc[...], basis_ref.shape[2], halves, tall)
        if mode != "score":
            out_ref[0] = image
        if mode == "gram":
            refs[2][0] = against(image, tall[...])
        if mode == "score":
            out_ref[0] = against(left_ref[0], tall[...])


def product(a, b):
    k = a.shape[0]
    left = jnp.concatenate(split3(a), axis=0)
    right = left if b is a else jnp.concatenate(split3(b), axis=0)
    pieces = lax.dot_general(left, right, TRANS_B, preferred_element_type=F32)
    top, middle, bottom = pieces[:k], pieces[k : 2 * k], pieces[2 * k :]
    total = top[:, :k] + (top[:, k : 2 * k] + middle[:, :k])
    return total + (middle[:, k : 2 * k] + (top[:, 2 * k : 3 * k] + bottom[:, :k]))


def image_of(parts, dense_ref):
    return sum(image_part(part, dense_ref[chunk]) for chunk, part in enumerate(parts))


def first_kernel(layer, piece_count, *refs):
    pieces, (dense_ref, out_ref, halves, tall) = refs[:piece_count], refs[piece_count:]
    total = image_of([piece[layer] for piece in pieces], dense_ref)
    out_ref[...] = to_wide(total, out_ref.shape[0], halves, tall)


def second_kernel(piece_count, earlier_count, *refs):
    pieces, dense_ref, refs = refs[:piece_count], refs[piece_count], refs[piece_count + 1 :]
    earlier, (out_ref, halves, tall, scratch) = refs[:earlier_count], refs[earlier_count:]
    image = jnp.concatenate([piece[...] for piece in pieces], axis=1)
    inverse = inverse_factor(product(image, image), scratch)
    basis = jnp.dot(inverse, image, precision=HIGHEST, preferred_element_type=F32)
    parts = [basis[:, d * ROWS_DEV : d * ROWS_DEV + ROWS_DEV] for d in range(piece_count)]
    before = out_ref.shape[0] - 1
    for ref in earlier:
        out_ref[:before] = ref[...]
    out_ref[before] = to_wide(image_of(parts, dense_ref), out_ref.shape[1], halves, tall)


def own_kernel(basis_ref, *refs):
    *dense_refs, out_ref = refs
    for layer, dense_ref in enumerate(dense_refs):
        out_ref[layer] = image_part(basis_ref[layer], dense_ref[0])


def score_kernel(layers, piece_count, own_ref, *refs):
    pieces, left_ref, refs = refs[:piece_count], refs[piece_count], refs[piece_count + 1 :]
    dense_refs, (out_ref, halves, tall) = refs[:layers], refs[layers:]
    totals = [
        own_ref[layer]
        + sum(image_part(piece[layer], dense_refs[layer][d + 1]) for d, piece in enumerate(pieces))
        for layer in range(layers)
    ]
    wide = [
        to_wide(totals[layer], left_ref.shape[1], halves.at[layer], tall.at[layer]) for layer in range(layers)
    ]
    for layer in range(layers):
        out_ref[layer] = product(left_ref[layer], wide[layer])


def apply_whole(kernel, name, operands, out_shape, *lead, scratch=()):
    return pl.pallas_call(
        kernel,
        in_specs=vmem_specs(len(operands)),
        out_specs=pl.BlockSpec(memory_space=pltpu.VMEM),
        out_shape=jax.ShapeDtypeStruct(out_shape, F32),
        scratch_shapes=[pltpu.VMEM((*lead, TALL, 128), F32), pltpu.VMEM((*lead, ROWS_DEV, 128), F32), *scratch],
        compiler_params=params(14),
        cost_estimate=pl.CostEstimate(flops=0, bytes_accessed=4 * MIB, transcendentals=0),
        name=name,
    )(*operands)


def apply_first(layer, pieces, dense):
    kernel = functools.partial(first_kernel, layer, len(pieces))
    return apply_whole(kernel, "apply_first", [*pieces, dense], pieces[0].shape[1:])


def apply_second(pieces, dense, earlier):
    kernel = functools.partial(second_kernel, len(pieces), len(earlier))
    before = sum(array.shape[0] for array in earlier)
    shape = (before + 1, *pieces[0].shape)
    operands = [*pieces, dense, *earlier]
    return apply_whole(kernel, "apply_second", operands, shape, scratch=[pltpu.VMEM(SPREAD, F32)])


def apply_own(basis, dense):
    layers, k = basis.shape[:2]
    return pl.pallas_call(
        own_kernel,
        in_specs=vmem_specs(1 + layers),
        out_specs=pl.BlockSpec(memory_space=pltpu.VMEM),
        out_shape=jax.ShapeDtypeStruct((layers, 2 * TALL, 2 * k), F32),
        compiler_params=params(14),
        cost_estimate=pl.CostEstimate(flops=0, bytes_accessed=2 * MIB, transcendentals=0),
        name="apply_own",
    )(basis, *dense)


def apply_score(pieces, left, dense):
    kernel = functools.partial(score_kernel, len(dense), len(pieces) - 1)
    layers, k = left.shape[:2]
    operands = [apply_own(pieces[0], dense), *pieces[1:], left, *dense]
    return apply_whole(kernel, "apply_score", operands, (layers, k, k), layers)


def apply_dense(mode, basis, dense, left=None):
    layers, chunks = dense.shape[:2]
    k = basis.shape[-2]
    image = jax.ShapeDtypeStruct((layers, k, ROWS_DEV), F32)
    small = jax.ShapeDtypeStruct((layers, k, k), F32)
    out_shape = {"gram": [image, small], "plain": [image], "score": [small]}[mode]
    operands = [basis] + ([left] if mode == "score" else []) + [dense]
    dense_spec = pl.BlockSpec((1, 1, 2 * TALL, CHUNK_LANES), lambda l, s: (l, s, 0, 0))
    image_spec = pl.BlockSpec((1, k, ROWS_DEV), lambda l, s: (l, 0, 0))
    small_spec = pl.BlockSpec((1, k, k), lambda l, s: (l, 0, 0))
    return pl.pallas_call(
        functools.partial(apply_kernel, mode),
        grid=(layers, chunks),
        in_specs=vmem_specs(1) + ([image_spec] if mode == "score" else []) + [dense_spec],
        out_specs={"gram": [image_spec, small_spec], "plain": [image_spec], "score": [small_spec]}[mode],
        out_shape=out_shape,
        scratch_shapes=[
            pltpu.VMEM((TALL, 128), F32),
            pltpu.VMEM((ROWS_DEV, 128), F32),
            pltpu.VMEM((2 * TALL, 2 * k), F32),
        ],
        compiler_params=params(12),
        name="apply_" + mode,
    )(*operands)


def spread(x):
    return jnp.broadcast_to(x, (8, 128))


def eliminate(rows, offset, scratch):
    groups, tiles = len(rows), len(rows[0])
    rows = [list(row) for row in rows]
    home, at = offset // 128, offset % 128
    sub = lax.broadcasted_iota(jnp.int32, (8, 128), 0)
    solved = []
    for h in range(groups):
        below = range(h + 1, groups)
        lane = at + 8 * h
        col = [{g: spread(rows[g][home][:, lane + q : lane + q + 1]) for g in range(h, groups)} for q in range(8)]
        held = scratch.at[h % 2]
        for q in range(8):
            held[q * 8 : q * 8 + 8] = col[q][h]
        for t in range(tiles):
            held[64 + t * 8 : 72 + t * 8] = rows[h][t]
        cell = {(p, q): spread(held[p * 8 + q : p * 8 + q + 1]) for q in range(8) for p in range(q + 1)}
        row = [[spread(held[64 + t * 8 + q : 65 + t * 8 + q]) for t in range(tiles)] for q in range(8)]
        done = []
        for m in range(0, 8, 2):
            n = m + 1
            a, b, c = cell[m, m], cell[m, n], cell[n, n]
            det = a * c - b * b
            if m % 4 == 0:
                r = pl.reciprocal(det, approx=True)
            else:
                r = square * pl.reciprocal(whole, approx=True)
            later = range(m + 2, 8)
            u = {q: c * cell[m, q] - b * cell[n, q] for q in later}
            v = {q: a * cell[n, q] - b * cell[m, q] for q in later}
            taken = {(p, q): cell[m, p] * u[q] + cell[n, p] * v[q] for q in later for p in range(m + 2, q + 1)}
            if m % 4 == 0:
                i, j = m + 2, m + 3
                first, cross, last = (det * cell[pq] - taken[pq] for pq in ((i, i), (i, j), (j, j)))
                whole = first * last - cross * cross
                square = det * det
            for pq in taken:
                cell[pq] = cell[pq] - r * taken[pq]
            for q in later:
                for g in below:
                    col[q][g] = col[q][g] - r * (col[m][g] * u[q] + col[n][g] * v[q])
            for t in range(tiles):
                x = r * (c * row[m][t] - b * row[n][t])
                y = r * (a * row[n][t] - b * row[m][t])
                for q in later:
                    row[q][t] = row[q][t] - (cell[m, q] * x + cell[n, q] * y)
                for g in below:
                    rows[g][t] = rows[g][t] - (col[m][g] * x + col[n][g] * y)
            over = pl.reciprocal(a, approx=True)
            done.append([lax.rsqrt(a) * x for x in row[m]])
            scale = lax.rsqrt(det * over)
            done.append([scale * (x - (b * over) * w) for x, w in zip(row[n], row[m])])
        finished = []
        for t in range(tiles):
            x = done[7][t]
            for q in range(7):
                x = jnp.where(sub == q, done[q][t], x)
            finished.append(x)
        solved.append(finished)
    return solved


def tiled(x):
    return [
        [x[g * 8 : g * 8 + 8, t * 128 : t * 128 + 128] for t in range(x.shape[1] // 128)]
        for g in range(x.shape[0] // 8)
    ]


def joined(tiles):
    return jnp.concatenate([jnp.concatenate(row, axis=1) for row in tiles], axis=0)


def unit_scale(gram):
    lane = lax.broadcasted_iota(jnp.int32, gram.shape, 1)
    sub = lax.broadcasted_iota(jnp.int32, gram.shape, 0)
    kept = jnp.where(lane == sub, gram, 0.0)
    down = 1.0 / jnp.sqrt(jnp.sum(kept, axis=1, keepdims=True))
    across = jnp.sum(kept, axis=0, keepdims=True)
    across = 1.0 / jnp.sqrt(jnp.where(across == 0.0, 1.0, across))
    return gram * down * across, across


def gram_update(panel, first):
    a, b, c = split3(panel)
    left = jnp.concatenate([a, a, b, b, a, c], axis=0)
    right = jnp.concatenate([a, b, a, b, c, a], axis=0)
    parts = {
        at: lax.dot_general(left[:, at : at + 128], right, TRANS_A, preferred_element_type=F32)
        for at in range(first, panel.shape[1], 128)
    }
    return lambda at, count: parts[at // 128 * 128][at % 128 : at % 128 + count]


def inverse_factor(gram, scratch):
    k = gram.shape[0]
    lane = lax.broadcasted_iota(jnp.int32, (k, 128), 1)
    sub = lax.broadcasted_iota(jnp.int32, (k, 128), 0)
    eye = jnp.where(lane == sub, 1.0, 0.0)
    gram, across = unit_scale(jnp.concatenate([gram, jnp.zeros((k, 128 - k), F32)], axis=1))
    solved = eliminate(tiled(jnp.concatenate([gram, eye], axis=1)), 0, scratch)
    return (joined(solved)[:, 128:] * across)[:, :k]


def solve_kernel(gram_ref, image_ref, out_ref, scratch):
    for layer in range(image_ref.shape[0]):
        inverse = inverse_factor(gram_ref[layer], scratch.at[layer])
        solved = jnp.dot(inverse, image_ref[layer], precision=HIGHEST, preferred_element_type=F32)
        out_ref[layer] = solved.astype(BF16)


def solve(gram, image):
    return pl.pallas_call(
        solve_kernel,
        in_specs=vmem_specs(2),
        out_specs=pl.BlockSpec(memory_space=pltpu.VMEM),
        out_shape=jax.ShapeDtypeStruct(image.shape, BF16),
        scratch_shapes=[pltpu.VMEM((image.shape[0], *SPREAD), F32)],
        compiler_params=params(4),
        name="solve_layers",
    )(gram, image)


def cross_kernel(k, images_ref, out_ref, packed):
    g = lax.axis_index("layer")
    every = images_ref[...].reshape(-1, images_ref.shape[2])
    gram = lax.dot_general(every, every, TRANS_B, precision=HIGHEST, preferred_element_type=F32)
    half = gram.shape[0] // 2
    first, last = gram[:half, :half], gram[half:, half:]
    row = lax.broadcasted_iota(jnp.int32, (half, half), 0) // k
    col = lax.broadcasted_iota(jnp.int32, (half, half), 1) // k
    packed[:half] = gram[:half, half:]
    packed[half : 2 * half] = jnp.where(col >= row, first, last)
    diagonal = jnp.where(col == row, last, 0.0)
    packed[2 * half :] = sum(diagonal[r * k : r * k + k] for r in range(half // k))
    rows = out_ref.shape[0]
    out_ref[...] = packed[pl.ds(pl.multiple_of((g & 1) * rows, 16), rows)]


def cross(images):
    layers, k, _ = images.shape
    size = layers * k
    return pl.pallas_call(
        functools.partial(cross_kernel, k),
        in_specs=vmem_specs(1),
        out_specs=pl.BlockSpec(memory_space=pltpu.VMEM),
        out_shape=jax.ShapeDtypeStruct(((size + k) // 2, size // 2), F32),
        scratch_shapes=[pltpu.VMEM((size + k, size // 2), F32)],
        compiler_params=params(6),
        name="cross_gram",
    )(images)


def unpack(packed, k, work):
    half = packed.shape[1]
    row = lax.broadcasted_iota(jnp.int32, (half, half), 0) // k
    col = lax.broadcasted_iota(jnp.int32, (half, half), 1) // k
    mixed = packed[half : 2 * half]
    under = jnp.where(col < row, mixed, 0.0)
    diagonal = jnp.concatenate([packed[2 * half :]] * (half // k), axis=0)
    work[:half, :half] = jnp.where(col >= row, mixed, 0.0)
    work[:half, half:] = packed[:half]
    work[half:, :half] = jnp.zeros((half, half), F32)
    work[half:, half:] = under.T + jnp.where(col == row, diagonal, 0.0)


def joint_kernel(k, *refs):
    own_ref, other_ref, images_ref, out_ref, again_ref, rounded_ref, work, packed, scratch = refs
    rows = own_ref.shape[0]
    odd = lax.axis_index("layer") & 1
    packed[pl.ds(pl.multiple_of(odd * rows, 16), rows)] = own_ref[...]
    packed[pl.ds(pl.multiple_of((1 - odd) * rows, 16), rows)] = other_ref[...]
    unpack(packed[...], k, work)
    size = work.shape[0]
    steps = size // k
    lane = lax.broadcasted_iota(jnp.int32, (k, size), 1)
    lane_128 = lax.broadcasted_iota(jnp.int32, (k, 128), 1)
    sub_128 = lax.broadcasted_iota(jnp.int32, (k, 128), 0)
    gram, across = unit_scale(work[...])
    work[...] = gram
    for s in range(steps):
        lo, hi = s * k, (s + 1) * k
        here = (lane >= lo) & (lane < hi)
        eye = jnp.where(lane_128 == sub_128 + lo % 128, 1.0, 0.0)
        solved = joined(eliminate(tiled(jnp.concatenate([work[lo:hi], eye], axis=1)), lo, scratch.at[s % 2]))
        panel, tail = solved[:, :size], solved[:, size:]
        panel = jnp.where(here, jnp.concatenate([tail] * (size // 128), axis=1), panel)
        work[lo:hi] = jnp.where(lane < hi, panel, 0.0)
        if s + 1 < steps:
            update = gram_update(panel, hi // 128 * 128)
            for r in range(s + 1, steps):
                rows = work[r * k : r * k + k]
                work[r * k : r * k + k] = jnp.where(here, 0.0, rows) - update(r * k, k)
    rows = out_ref.shape[0] * k
    own = work[pl.ds(pl.multiple_of(lax.axis_index("layer") * rows, rows), rows)] * across
    joint = jnp.dot(own, images_ref[...].reshape(size, -1), precision=HIGHEST, preferred_element_type=F32)
    joint = joint.reshape(out_ref.shape)
    out_ref[...] = joint
    again_ref[...] = joint
    rounded_ref[...] = joint.astype(BF16)


def joint_solve(own, other, images, shape):
    k = shape[1]
    size = images.shape[0] * k
    return pl.pallas_call(
        functools.partial(joint_kernel, k),
        in_specs=vmem_specs(3),
        out_specs=vmem_specs(3),
        out_shape=[
            jax.ShapeDtypeStruct(shape, F32),
            jax.ShapeDtypeStruct(shape, F32),
            jax.ShapeDtypeStruct(shape, BF16),
        ],
        scratch_shapes=[
            pltpu.VMEM((size, size), F32),
            pltpu.VMEM((size + k, size // 2), F32),
            pltpu.VMEM((2, *SPREAD), F32),
        ],
        compiler_params=params(8),
        name="joint_solve",
    )(own, other, images)


def around(x, axis, count):
    pieces = [x]
    for d in range(1, count):
        pieces.append(lax.ppermute(x, axis, [(m ^ d, m) for m in range(count)]))
    return pieces


def add_pieces(pieces):
    if len(pieces) == 1:
        return pieces[0]
    return (pieces[0] + pieces[1]) + (pieces[2] + pieces[3])


def per_device(shards, groups, blocks, block_rows, block_cols, counts, start):
    few = shards == 4
    layers = start.shape[0]

    def gather(x):
        return around(x, "node", shards) if few else lax.all_gather(x, "node")

    def total(x):
        return add_pieces(around(x, "node", shards)) if few else lax.psum(x, "node")

    first = gather(start.astype(BF16))
    dense = build_dense(block_rows, block_cols, counts, blocks, shards * BROWS // CHUNK_COLS)
    if few:
        images = [apply_first(layer, first, dense[layer]) for layer in range(layers)]
        image = None
        for layer in range(layers):
            image = apply_second(gather(images[layer]), dense[layer], [] if image is None else [image])
    else:
        image, gram = apply_dense("gram", first, dense)
        (image,) = apply_dense("plain", gather(solve(total(gram), image)), dense)
    images = lax.all_gather(image, "layer", axis=0, tiled=True)
    own = cross(images)
    own = total(own)
    other = lax.ppermute(own, "layer", [(m ^ 1, m) for m in range(groups)])
    joint_basis, again, rounded = joint_solve(own, other, images, start.shape)
    if few:
        partial = apply_score(gather(rounded), again, dense)
    else:
        (partial,) = apply_dense("score", gather(rounded), dense, again)
    return joint_basis, total(partial)


def solution(mesh):
    in_specs = (
        P(("parts", "layer"), "node", None),
        P(("parts", "layer"), "node"),
        P(("parts", "layer"), "node"),
        P(("parts", "layer"), "node"),
        P(("parts", "layer"), None, "node"),
    )
    out_specs = (P(("parts", "layer"), None, "node"), P(("parts", "layer"), None, None))
    return jax.shard_map(
        functools.partial(per_device, mesh.shape["node"], mesh.shape["layer"]),
        mesh=mesh,
        in_specs=in_specs,
        out_specs=out_specs,
        check_vma=False,
    )
```

```python
import functools

import jax
import jax.numpy as jnp
from jax import lax
from jax.experimental import pallas as pl
from jax.experimental.pallas import tpu as pltpu
from jax.sharding import PartitionSpec as P

BLK = 64
ROWS_DEV = 512
BROWS = ROWS_DEV // BLK
CHUNK_COLS = 8
CHUNK_LANES = CHUNK_COLS * 2 * BLK
TALL = BROWS * BLK // 2
MIB = 1024 * 1024
F32 = jnp.float32
BF16 = jnp.bfloat16
HIGHEST = lax.Precision.HIGHEST
TRANS_B = (((1,), (1,)), ((), ()))
TRANS_A = (((0,), (0,)), ((), ()))
SPREAD = (2, 88, 128)


def params(mib):
    return pltpu.CompilerParams(vmem_limit_bytes=mib * MIB)


def vmem_specs(count):
    return [pl.BlockSpec(memory_space=pltpu.VMEM)] * count


def place(z, chunks, u, dense_ref):
    for c in range(chunks * CHUNK_COLS):
        piece = z[c * 8 : c * 8 + 8]
        piece = jnp.concatenate([piece[:, :128], piece[:, 128:]], axis=0)
        hi = piece.astype(BF16)
        lo = (piece - hi.astype(F32)).astype(BF16)
        lanes = slice((c % CHUNK_COLS) * 128, (c % CHUNK_COLS) * 128 + 128)
        dense_ref[c // CHUNK_COLS, pl.ds(pl.multiple_of(u * 16, 16), 16), lanes] = hi
        dense_ref[c // CHUNK_COLS, pl.ds(pl.multiple_of(u * 16 + TALL, 16), 16), lanes] = lo


def one_hot(rows_ref, cols_ref, counts_ref, layer, flip, base, positions):
    slot = lax.broadcasted_iota(jnp.int32, (1, rows_ref.shape[1]), 1)
    key = (cols_ref[pl.ds(layer, 1), :] ^ flip) * BROWS + rows_ref[pl.ds(layer, 1), :]
    key = jnp.where(slot < counts_ref[0, layer], key, -1)
    position = lax.broadcasted_iota(jnp.int32, (positions, key.shape[1]), 0) + base
    return jnp.where(position == key, 1.0, 0.0).astype(BF16)


def build_kernel(rows_ref, cols_ref, counts_ref, blocks_ref, dense_ref):
    chunks = dense_ref.shape[1]
    positions = chunks * CHUNK_COLS * BROWS
    base = pl.program_id(1) * positions
    onehot = one_hot(rows_ref, cols_ref, counts_ref, pl.program_id(0), 0, base, positions)

    def step(u, carry):
        cols = pl.ds(pl.multiple_of(u * 256, 256), 256)
        z = jnp.dot(onehot, blocks_ref[0, :, cols], preferred_element_type=F32)
        place(z, chunks, u, dense_ref.at[0])
        return carry

    lax.fori_loop(0, BLK * BLK // 256, step, 0)


def fill(onehot, held, dense_ref, piece, width):
    for v in range(width // 256):
        cols = pl.ds(pl.multiple_of(piece * width + v * 256, 256), 256)
        z = jnp.dot(onehot, held[:, cols], preferred_element_type=F32)
        place(z, dense_ref.shape[0], piece * (width // 256) + v, dense_ref)


def build_first_kernel(rows_hbm, cols_hbm, counts_hbm, blocks_ref, dense_ref, *refs):
    *refs, held, rows_ref, cols_ref, counts_ref, arrived, index_arrived = refs
    others, onehots = refs[: len(refs) // 2], refs[len(refs) // 2 :]
    index_copies = [
        pltpu.make_async_copy(source, target, index_arrived.at[i])
        for i, (source, target) in enumerate(
            [(rows_hbm, rows_ref), (cols_hbm, cols_ref), (counts_hbm, counts_ref)]
        )
    ]
    for copy in index_copies:
        copy.start()
    pieces = arrived.shape[0] - len(others)
    width = held.shape[1] // pieces

    def fetch(piece):
        cols = pl.ds(pl.multiple_of(piece * width, width), width)
        return pltpu.make_async_copy(blocks_ref.at[0, :, cols], held.at[:, cols], arrived.at[piece])

    for piece in range(pieces):
        fetch(piece).start()
    whole = [
        pltpu.make_async_copy(blocks_ref.at[i + 1], other, arrived.at[pieces + i]) for i, other in enumerate(others)
    ]
    for copy in whole:
        copy.start()
    for copy in index_copies:
        copy.wait()
    flip = lax.axis_index("node") * CHUNK_COLS
    positions = dense_ref.shape[0] * CHUNK_COLS * BROWS
    onehot = one_hot(rows_ref, cols_ref, counts_ref, 0, flip, 0, positions)
    for i, ref in enumerate(onehots):
        ref[...] = one_hot(rows_ref, cols_ref, counts_ref, i + 1, flip, 0, positions)

    def step(piece, carry):
        fetch(piece).wait()
        fill(onehot, held, dense_ref, piece, width)
        return carry

    lax.fori_loop(0, pieces, step, 0)
    for copy in whole:
        copy.wait()


def build_next_kernel(onehot_ref, blocks_ref, dense_ref):
    onehot = onehot_ref[...]
    width = blocks_ref.shape[1] // 4

    def step(piece, carry):
        fill(onehot, blocks_ref, dense_ref, piece, width)
        return carry

    lax.fori_loop(0, 4, step, 0)


def relay_kernel(x_ref, _, out_ref):
    out_ref[...] = x_ref[...]


def relay(x, after):
    return pl.pallas_call(
        relay_kernel,
        in_specs=vmem_specs(1) + [pl.BlockSpec(memory_space=pl.ANY)],
        out_specs=pl.BlockSpec(memory_space=pltpu.VMEM),
        out_shape=jax.ShapeDtypeStruct(x.shape, x.dtype),
        compiler_params=params(2),
        name="relay",
    )(x, after)


def build_first(block_rows, block_cols, counts, blocks, chunk_total):
    layers, slots, width = blocks.shape
    dense = jax.ShapeDtypeStruct((chunk_total, 2 * TALL, CHUNK_LANES), BF16)
    positions = chunk_total * CHUNK_COLS * BROWS
    operands = (block_rows, block_cols, counts.T, blocks)
    outs = pl.pallas_call(
        build_first_kernel,
        in_specs=[pl.BlockSpec(memory_space=pltpu.HBM)] * 4,
        out_specs=vmem_specs(2 * layers - 1),
        out_shape=[dense]
        + [jax.ShapeDtypeStruct((slots, width), BF16)] * (layers - 1)
        + [jax.ShapeDtypeStruct((positions, slots), BF16)] * (layers - 1),
        scratch_shapes=[
            pltpu.VMEM((slots, width), BF16),
            pltpu.VMEM(block_rows.shape, jnp.int32),
            pltpu.VMEM(block_cols.shape, jnp.int32),
            pltpu.SMEM((1, layers), jnp.int32),
            pltpu.SemaphoreType.DMA((4 + layers - 1,)),
            pltpu.SemaphoreType.DMA((3,)),
        ],
        compiler_params=params(28),
        cost_estimate=pl.CostEstimate(flops=0, bytes_accessed=12 * MIB, transcendentals=0),
        name="build_first",
    )(*[pltpu.with_memory_space_constraint(x, pltpu.HBM) for x in operands])
    return outs[0], list(zip(outs[layers:], outs[1:layers]))


def build_next(onehot, blocks, chunk_total):
    return pl.pallas_call(
        build_next_kernel,
        in_specs=vmem_specs(2),
        out_specs=pl.BlockSpec(memory_space=pltpu.VMEM),
        out_shape=jax.ShapeDtypeStruct((chunk_total, 2 * TALL, CHUNK_LANES), BF16),
        compiler_params=params(20),
        cost_estimate=pl.CostEstimate(flops=0, bytes_accessed=12 * MIB, transcendentals=0),
        name="build_next",
    )(onehot, blocks)


def build_dense(block_rows, block_cols, counts, blocks, chunk_total):
    layers, slots, width = blocks.shape
    dense = jax.ShapeDtypeStruct((layers, chunk_total, 2 * TALL, CHUNK_LANES), BF16)
    operands = (block_rows, block_cols, counts.T, blocks)
    return pl.pallas_call(
        build_kernel,
        grid=(layers, chunk_total // 4),
        in_specs=vmem_specs(2)
        + [
            pl.BlockSpec(memory_space=pltpu.SMEM),
            pl.BlockSpec((1, slots, width), lambda l, s: (l, 0, 0)),
        ],
        out_specs=pl.BlockSpec((1, 4, 2 * TALL, CHUNK_LANES), lambda l, s: (l, s, 0, 0)),
        out_shape=dense,
        compiler_params=params(24),
        name="build_dense",
    )(*operands)


def split3(x):
    a = x.astype(BF16)
    r = x - a.astype(F32)
    b = r.astype(BF16)
    c = (r - b.astype(F32)).astype(BF16)
    return a, b, c


def image_part(basis, dense):
    k, width = basis.shape
    basis = basis.astype(F32)
    tall = jnp.concatenate([basis, basis], axis=0).T
    lane = lax.broadcasted_iota(jnp.int32, tall.shape, 1)
    first = jnp.where(lane < k, tall, 0.0).astype(BF16)
    second = jnp.where(lane < k, 0.0, tall).astype(BF16)
    weights = []
    for c in range(width // BLK):
        weights += [first[c * BLK : c * BLK + BLK], second[c * BLK : c * BLK + BLK]]
    return jnp.dot(dense, jnp.concatenate(weights, axis=0), preferred_element_type=F32)


def to_wide(total, k, halves, tall):
    halves[:, : 2 * k] = total[:TALL] + total[TALL:]
    halves[:, 2 * k :] = jnp.zeros((TALL, 128 - 2 * k), F32)
    for b in range(BROWS):
        part = halves[pl.ds(b, BLK // 2, stride=BROWS), :]
        tall[pl.ds(BLK * b, BLK // 2, stride=2), :] = part
        tall[pl.ds(BLK * b + 1, BLK // 2, stride=2), :] = pltpu.roll(part, 128 - k, 1)
    return tall[...].T[:k]


def against(left, tall):
    k = left.shape[0]
    lane = lax.broadcasted_iota(jnp.int32, tall.shape, 1)
    a, b, c = split3(jnp.where(lane < k, tall, 0.0))
    right = a.astype(F32) + pltpu.roll(b.astype(F32), k, 1) + pltpu.roll(c.astype(F32), 2 * k, 1)
    pieces = jnp.dot(jnp.concatenate(split3(left), axis=0), right.astype(BF16), preferred_element_type=F32)
    top, middle, bottom = pieces[:k], pieces[k : 2 * k], pieces[2 * k :]
    total = top[:, :k] + (top[:, k : 2 * k] + middle[:, :k])
    return total + (middle[:, k : 2 * k] + (top[:, 2 * k : 3 * k] + bottom[:, :k]))


def apply_kernel(mode, *refs):
    basis_ref, refs = refs[0], refs[1:]
    if mode == "score":
        left_ref, refs = refs[0], refs[1:]
    dense_ref, out_ref = refs[:2]
    halves, tall, acc = refs[-3:]
    layer, chunk = pl.program_id(0), pl.program_id(1)
    total = image_part(basis_ref[chunk, layer], dense_ref[0, 0])

    @pl.when(chunk == 0)
    def _():
        acc[...] = total

    @pl.when(chunk > 0)
    def _():
        acc[...] += total

    @pl.when(chunk == pl.num_programs(1) - 1)
    def _():
        image = to_wide(acc[...], basis_ref.shape[2], halves, tall)
        if mode != "score":
            out_ref[0] = image
        if mode == "gram":
            refs[2][0] = against(image, tall[...])
        if mode == "score":
            out_ref[0] = against(left_ref[0], tall[...])


def product(a, b):
    k = a.shape[0]
    left = jnp.concatenate(split3(a), axis=0)
    right = left if b is a else jnp.concatenate(split3(b), axis=0)
    pieces = lax.dot_general(left, right, TRANS_B, preferred_element_type=F32)
    top, middle, bottom = pieces[:k], pieces[k : 2 * k], pieces[2 * k :]
    total = top[:, :k] + (top[:, k : 2 * k] + middle[:, :k])
    return total + (middle[:, k : 2 * k] + (top[:, 2 * k : 3 * k] + bottom[:, :k]))


def image_of(parts, dense_ref):
    return sum(image_part(part, dense_ref[chunk]) for chunk, part in enumerate(parts))


def first_kernel(layer, piece_count, *refs):
    pieces, (dense_ref, _, out_ref, halves, tall) = refs[:piece_count], refs[piece_count:]
    total = image_of([piece[layer] for piece in pieces], dense_ref)
    out_ref[...] = to_wide(total, out_ref.shape[0], halves, tall)


def second_kernel(piece_count, earlier_count, *refs):
    pieces, dense_ref, refs = refs[:piece_count], refs[piece_count], refs[piece_count + 1 :]
    earlier, (out_ref, halves, tall, scratch) = refs[:earlier_count], refs[earlier_count:]
    image = jnp.concatenate([piece[...] for piece in pieces], axis=1)
    inverse = inverse_factor(product(image, image), scratch)
    basis = jnp.dot(inverse, image, precision=HIGHEST, preferred_element_type=F32)
    parts = [basis[:, d * ROWS_DEV : d * ROWS_DEV + ROWS_DEV] for d in range(piece_count)]
    before = out_ref.shape[0] - 1
    for ref in earlier:
        out_ref[:before] = ref[...]
    out_ref[before] = to_wide(image_of(parts, dense_ref), out_ref.shape[1], halves, tall)


def some_kernel(chunk, layers, basis_ref, *refs):
    dense_refs, (*so_far, out_ref) = refs[:layers], refs[layers:]
    for layer, dense_ref in enumerate(dense_refs):
        part = image_part(basis_ref[layer], dense_ref[chunk])
        out_ref[layer] = sum((ref[layer] for ref in so_far), part)


def score_kernel(layers, chunks, so_far_ref, *refs):
    pieces, left_ref, refs = refs[: len(chunks)], refs[len(chunks)], refs[len(chunks) + 1 :]
    dense_refs, (out_ref, halves, tall) = refs[:layers], refs[layers:]
    totals = [
        so_far_ref[layer]
        + sum(image_part(piece[layer], dense_refs[layer][chunk]) for chunk, piece in zip(chunks, pieces))
        for layer in range(layers)
    ]
    wide = [
        to_wide(totals[layer], left_ref.shape[1], halves.at[layer], tall.at[layer]) for layer in range(layers)
    ]
    for layer in range(layers):
        out_ref[layer] = product(left_ref[layer], wide[layer])


def apply_whole(kernel, name, operands, out_shape, *lead, scratch=(), after=()):
    return pl.pallas_call(
        kernel,
        in_specs=vmem_specs(len(operands)) + [pl.BlockSpec(memory_space=pl.ANY)] * len(after),
        out_specs=pl.BlockSpec(memory_space=pltpu.VMEM),
        out_shape=jax.ShapeDtypeStruct(out_shape, F32),
        scratch_shapes=[pltpu.VMEM((*lead, TALL, 128), F32), pltpu.VMEM((*lead, ROWS_DEV, 128), F32), *scratch],
        compiler_params=params(14),
        cost_estimate=pl.CostEstimate(flops=0, bytes_accessed=4 * MIB, transcendentals=0),
        name=name,
    )(*operands, *after)


def apply_first(layer, pieces, dense, after):
    kernel = functools.partial(first_kernel, layer, len(pieces))
    return apply_whole(kernel, "apply_first", [*pieces, dense], pieces[0].shape[1:], after=[after])


def apply_second(pieces, dense, earlier):
    kernel = functools.partial(second_kernel, len(pieces), len(earlier))
    before = sum(array.shape[0] for array in earlier)
    shape = (before + 1, *pieces[0].shape)
    operands = [*pieces, dense, *earlier]
    return apply_whole(kernel, "apply_second", operands, shape, scratch=[pltpu.VMEM(SPREAD, F32)])


def apply_some(chunk, basis, dense, *so_far):
    layers, k = basis.shape[:2]
    return pl.pallas_call(
        functools.partial(some_kernel, chunk, layers),
        in_specs=vmem_specs(1 + layers + len(so_far)),
        out_specs=pl.BlockSpec(memory_space=pltpu.VMEM),
        out_shape=jax.ShapeDtypeStruct((layers, 2 * TALL, 2 * k), F32),
        compiler_params=params(14),
        cost_estimate=pl.CostEstimate(flops=0, bytes_accessed=2 * MIB, transcendentals=0),
        name=f"apply_some_{chunk}",
    )(basis, *dense, *so_far)


def apply_score(pieces, left, dense):
    last = len(pieces) - 1
    so_far = apply_some(last, pieces[last], dense, apply_some(0, pieces[0], dense))
    chunks = range(1, last)
    kernel = functools.partial(score_kernel, len(dense), chunks)
    layers, k = left.shape[:2]
    operands = [so_far, *pieces[1:last], left, *dense]
    return apply_whole(kernel, "apply_score", operands, (layers, k, k), layers)


def apply_dense(mode, basis, dense, left=None):
    layers, chunks = dense.shape[:2]
    k = basis.shape[-2]
    image = jax.ShapeDtypeStruct((layers, k, ROWS_DEV), F32)
    small = jax.ShapeDtypeStruct((layers, k, k), F32)
    out_shape = {"gram": [image, small], "plain": [image], "score": [small]}[mode]
    operands = [basis] + ([left] if mode == "score" else []) + [dense]
    dense_spec = pl.BlockSpec((1, 1, 2 * TALL, CHUNK_LANES), lambda l, s: (l, s, 0, 0))
    image_spec = pl.BlockSpec((1, k, ROWS_DEV), lambda l, s: (l, 0, 0))
    small_spec = pl.BlockSpec((1, k, k), lambda l, s: (l, 0, 0))
    return pl.pallas_call(
        functools.partial(apply_kernel, mode),
        grid=(layers, chunks),
        in_specs=vmem_specs(1) + ([image_spec] if mode == "score" else []) + [dense_spec],
        out_specs={"gram": [image_spec, small_spec], "plain": [image_spec], "score": [small_spec]}[mode],
        out_shape=out_shape,
        scratch_shapes=[
            pltpu.VMEM((TALL, 128), F32),
            pltpu.VMEM((ROWS_DEV, 128), F32),
            pltpu.VMEM((2 * TALL, 2 * k), F32),
        ],
        compiler_params=params(12),
        name="apply_" + mode,
    )(*operands)


def spread(x):
    return jnp.broadcast_to(x, (8, 128))


def eliminate(rows, offset, scratch):
    groups, tiles = len(rows), len(rows[0])
    rows = [list(row) for row in rows]
    home, at = offset // 128, offset % 128
    sub = lax.broadcasted_iota(jnp.int32, (8, 128), 0)
    solved = []
    for h in range(groups):
        below = range(h + 1, groups)
        lane = at + 8 * h
        col = [{g: spread(rows[g][home][:, lane + q : lane + q + 1]) for g in range(h, groups)} for q in range(8)]
        held = scratch.at[h % 2]
        for q in range(8):
            held[q * 8 : q * 8 + 8] = col[q][h]
        for t in range(tiles):
            held[64 + t * 8 : 72 + t * 8] = rows[h][t]
        cell = {(p, q): spread(held[p * 8 + q : p * 8 + q + 1]) for q in range(8) for p in range(q + 1)}
        row = [[spread(held[64 + t * 8 + q : 65 + t * 8 + q]) for t in range(tiles)] for q in range(8)]
        done = []
        for m in range(0, 8, 2):
            n = m + 1
            a, b, c = cell[m, m], cell[m, n], cell[n, n]
            det = a * c - b * b
            if m % 4 == 0:
                r = pl.reciprocal(det, approx=True)
            else:
                r = square * pl.reciprocal(whole, approx=True)
            later = range(m + 2, 8)
            u = {q: c * cell[m, q] - b * cell[n, q] for q in later}
            v = {q: a * cell[n, q] - b * cell[m, q] for q in later}
            taken = {(p, q): cell[m, p] * u[q] + cell[n, p] * v[q] for q in later for p in range(m + 2, q + 1)}
            if m % 4 == 0:
                i, j = m + 2, m + 3
                first, cross, last = (det * cell[pq] - taken[pq] for pq in ((i, i), (i, j), (j, j)))
                whole = first * last - cross * cross
                square = det * det
            for pq in taken:
                cell[pq] = cell[pq] - r * taken[pq]
            for q in later:
                for g in below:
                    col[q][g] = col[q][g] - r * (col[m][g] * u[q] + col[n][g] * v[q])
            for t in range(tiles):
                x = r * (c * row[m][t] - b * row[n][t])
                y = r * (a * row[n][t] - b * row[m][t])
                for q in later:
                    row[q][t] = row[q][t] - (cell[m, q] * x + cell[n, q] * y)
                for g in below:
                    rows[g][t] = rows[g][t] - (col[m][g] * x + col[n][g] * y)
            over = pl.reciprocal(a, approx=True)
            done.append([lax.rsqrt(a) * x for x in row[m]])
            scale = lax.rsqrt(det * over)
            done.append([scale * (x - (b * over) * w) for x, w in zip(row[n], row[m])])
        finished = []
        for t in range(tiles):
            x = done[7][t]
            for q in range(7):
                x = jnp.where(sub == q, done[q][t], x)
            finished.append(x)
        solved.append(finished)
    return solved


def tiled(x):
    return [
        [x[g * 8 : g * 8 + 8, t * 128 : t * 128 + 128] for t in range(x.shape[1] // 128)]
        for g in range(x.shape[0] // 8)
    ]


def joined(tiles):
    return jnp.concatenate([jnp.concatenate(row, axis=1) for row in tiles], axis=0)


def unit_scale(gram):
    lane = lax.broadcasted_iota(jnp.int32, gram.shape, 1)
    sub = lax.broadcasted_iota(jnp.int32, gram.shape, 0)
    kept = jnp.where(lane == sub, gram, 0.0)
    down = 1.0 / jnp.sqrt(jnp.sum(kept, axis=1, keepdims=True))
    across = jnp.sum(kept, axis=0, keepdims=True)
    across = 1.0 / jnp.sqrt(jnp.where(across == 0.0, 1.0, across))
    return gram * down * across, across


def gram_update(panel, first):
    a, b, c = split3(panel)
    left = jnp.concatenate([a, a, b, b, a, c], axis=0)
    right = jnp.concatenate([a, b, a, b, c, a], axis=0)
    parts = {
        at: lax.dot_general(left[:, at : at + 128], right, TRANS_A, preferred_element_type=F32)
        for at in range(first, panel.shape[1], 128)
    }
    return lambda at, count: parts[at // 128 * 128][at % 128 : at % 128 + count]


def inverse_factor(gram, scratch):
    k = gram.shape[0]
    lane = lax.broadcasted_iota(jnp.int32, (k, 128), 1)
    sub = lax.broadcasted_iota(jnp.int32, (k, 128), 0)
    eye = jnp.where(lane == sub, 1.0, 0.0)
    gram, across = unit_scale(jnp.concatenate([gram, jnp.zeros((k, 128 - k), F32)], axis=1))
    solved = eliminate(tiled(jnp.concatenate([gram, eye], axis=1)), 0, scratch)
    return (joined(solved)[:, 128:] * across)[:, :k]


def solve_kernel(gram_ref, image_ref, out_ref, scratch):
    for layer in range(image_ref.shape[0]):
        inverse = inverse_factor(gram_ref[layer], scratch.at[layer])
        solved = jnp.dot(inverse, image_ref[layer], precision=HIGHEST, preferred_element_type=F32)
        out_ref[layer] = solved.astype(BF16)


def solve(gram, image):
    return pl.pallas_call(
        solve_kernel,
        in_specs=vmem_specs(2),
        out_specs=pl.BlockSpec(memory_space=pltpu.VMEM),
        out_shape=jax.ShapeDtypeStruct(image.shape, BF16),
        scratch_shapes=[pltpu.VMEM((image.shape[0], *SPREAD), F32)],
        compiler_params=params(4),
        name="solve_layers",
    )(gram, image)


def cross_kernel(k, images_ref, out_ref, packed):
    g = lax.axis_index("layer")
    every = images_ref[...].reshape(-1, images_ref.shape[2])
    gram = lax.dot_general(every, every, TRANS_B, precision=HIGHEST, preferred_element_type=F32)
    half = gram.shape[0] // 2
    first, last = gram[:half, :half], gram[half:, half:]
    row = lax.broadcasted_iota(jnp.int32, (half, half), 0) // k
    col = lax.broadcasted_iota(jnp.int32, (half, half), 1) // k
    packed[:half] = gram[:half, half:]
    packed[half : 2 * half] = jnp.where(col >= row, first, last)
    diagonal = jnp.where(col == row, last, 0.0)
    packed[2 * half :] = sum(diagonal[r * k : r * k + k] for r in range(half // k))
    rows = out_ref.shape[0]
    out_ref[...] = packed[pl.ds(pl.multiple_of((g & 1) * rows, 16), rows)]


def cross(images):
    layers, k, _ = images.shape
    size = layers * k
    return pl.pallas_call(
        functools.partial(cross_kernel, k),
        in_specs=vmem_specs(1),
        out_specs=pl.BlockSpec(memory_space=pltpu.VMEM),
        out_shape=jax.ShapeDtypeStruct(((size + k) // 2, size // 2), F32),
        scratch_shapes=[pltpu.VMEM((size + k, size // 2), F32)],
        compiler_params=params(6),
        name="cross_gram",
    )(images)


def unpack(packed, k, work):
    half = packed.shape[1]
    row = lax.broadcasted_iota(jnp.int32, (half, half), 0) // k
    col = lax.broadcasted_iota(jnp.int32, (half, half), 1) // k
    mixed = packed[half : 2 * half]
    under = jnp.where(col < row, mixed, 0.0)
    diagonal = jnp.concatenate([packed[2 * half :]] * (half // k), axis=0)
    work[:half, :half] = jnp.where(col >= row, mixed, 0.0)
    work[:half, half:] = packed[:half]
    work[half:, :half] = jnp.zeros((half, half), F32)
    work[half:, half:] = under.T + jnp.where(col == row, diagonal, 0.0)


def joint_kernel(k, *refs):
    own_ref, other_ref, images_ref, out_ref, again_ref, rounded_ref, work, packed, scratch = refs
    rows = own_ref.shape[0]
    odd = lax.axis_index("layer") & 1
    packed[pl.ds(pl.multiple_of(odd * rows, 16), rows)] = own_ref[...]
    packed[pl.ds(pl.multiple_of((1 - odd) * rows, 16), rows)] = other_ref[...]
    unpack(packed[...], k, work)
    size = work.shape[0]
    steps = size // k
    lane = lax.broadcasted_iota(jnp.int32, (k, size), 1)
    lane_128 = lax.broadcasted_iota(jnp.int32, (k, 128), 1)
    sub_128 = lax.broadcasted_iota(jnp.int32, (k, 128), 0)
    gram, across = unit_scale(work[...])
    work[...] = gram
    for s in range(steps):
        lo, hi = s * k, (s + 1) * k
        here = (lane >= lo) & (lane < hi)
        eye = jnp.where(lane_128 == sub_128 + lo % 128, 1.0, 0.0)
        solved = joined(eliminate(tiled(jnp.concatenate([work[lo:hi], eye], axis=1)), lo, scratch.at[s % 2]))
        panel, tail = solved[:, :size], solved[:, size:]
        panel = jnp.where(here, jnp.concatenate([tail] * (size // 128), axis=1), panel)
        work[lo:hi] = jnp.where(lane < hi, panel, 0.0)
        if s + 1 < steps:
            update = gram_update(panel, hi // 128 * 128)
            for r in range(s + 1, steps):
                rows = work[r * k : r * k + k]
                work[r * k : r * k + k] = jnp.where(here, 0.0, rows) - update(r * k, k)
    rows = out_ref.shape[0] * k
    own = work[pl.ds(pl.multiple_of(lax.axis_index("layer") * rows, rows), rows)] * across
    joint = jnp.dot(own, images_ref[...].reshape(size, -1), precision=HIGHEST, preferred_element_type=F32)
    joint = joint.reshape(out_ref.shape)
    out_ref[...] = joint
    again_ref[...] = joint
    rounded_ref[...] = joint.astype(BF16)


def joint_solve(own, other, images, shape):
    k = shape[1]
    size = images.shape[0] * k
    return pl.pallas_call(
        functools.partial(joint_kernel, k),
        in_specs=vmem_specs(3),
        out_specs=vmem_specs(3),
        out_shape=[
            jax.ShapeDtypeStruct(shape, F32),
            jax.ShapeDtypeStruct(shape, F32),
            jax.ShapeDtypeStruct(shape, BF16),
        ],
        scratch_shapes=[
            pltpu.VMEM((size, size), F32),
            pltpu.VMEM((size + k, size // 2), F32),
            pltpu.VMEM((2, *SPREAD), F32),
        ],
        compiler_params=params(8),
        name="joint_solve",
    )(own, other, images)


def swap(x, axis, d, count):
    return lax.ppermute(x, axis, [(m ^ d, m) for m in range(count)])


def around(x, axis, count):
    return [x] + [swap(x, axis, d, count) for d in range(1, count)]


def add_pieces(pieces):
    if len(pieces) == 1:
        return pieces[0]
    return (pieces[0] + pieces[1]) + (pieces[2] + pieces[3])


def per_device(shards, groups, blocks, block_rows, block_cols, counts, start):
    few = shards == 4
    layers = start.shape[0]

    def gather(x):
        return around(x, "node", shards) if few else lax.all_gather(x, "node")

    def total(x):
        return add_pieces(around(x, "node", shards)) if few else lax.psum(x, "node")

    rounded = start.astype(BF16)
    chunk_total = shards * BROWS // CHUNK_COLS
    if few:
        near, far = swap(rounded, "node", 1, shards), swap(rounded, "node", 2, shards)
        dense_first, rest = build_first(block_rows, block_cols, counts, blocks, chunk_total)
        far = relay(far, dense_first)
        dense = [dense_first] + [build_next(*one, chunk_total) for one in rest]
        first = [rounded, near, far, swap(far, "node", 1, shards)]
        images = [apply_first(layer, first, dense[layer], dense[-1]) for layer in range(layers)]
        image = None
        for layer in range(layers):
            image = apply_second(gather(images[layer]), dense[layer], [] if image is None else [image])
    else:
        dense = build_dense(block_rows, block_cols, counts, blocks, chunk_total)
        image, gram = apply_dense("gram", gather(rounded), dense)
        (image,) = apply_dense("plain", gather(solve(total(gram), image)), dense)
    images = lax.all_gather(image, "layer", axis=0, tiled=True)
    own = cross(images)
    own = total(own)
    other = swap(own, "layer", 1, groups)
    joint_basis, again, rounded = joint_solve(own, other, images, start.shape)
    if few:
        partial = apply_score(gather(rounded), again, dense)
    else:
        (partial,) = apply_dense("score", gather(rounded), dense, again)
    return joint_basis, total(partial)


def solution(mesh):
    in_specs = (
        P(("parts", "layer"), "node", None),
        P(("parts", "layer"), "node"),
        P(("parts", "layer"), "node"),
        P(("parts", "layer"), "node"),
        P(("parts", "layer"), None, "node"),
    )
    out_specs = (P(("parts", "layer"), None, "node"), P(("parts", "layer"), None, None))
    return jax.shard_map(
        functools.partial(per_device, mesh.shape["node"], mesh.shape["layer"]),
        mesh=mesh,
        in_specs=in_specs,
        out_specs=out_specs,
        check_vma=False,
    )
```

```python
import functools

import jax
import jax.numpy as jnp
from jax import lax
from jax.experimental import pallas as pl
from jax.experimental.pallas import tpu as pltpu
from jax.sharding import PartitionSpec as P

BLK = 64
ROWS_DEV = 512
BROWS = ROWS_DEV // BLK
CHUNK_COLS = 8
CHUNK_LANES = CHUNK_COLS * 2 * BLK
TALL = BROWS * BLK // 2
MIB = 1024 * 1024
F32 = jnp.float32
BF16 = jnp.bfloat16
HIGHEST = lax.Precision.HIGHEST
TRANS_B = (((1,), (1,)), ((), ()))
TRANS_A = (((0,), (0,)), ((), ()))
SPREAD = (2, 88, 128)


def params(mib):
    return pltpu.CompilerParams(vmem_limit_bytes=mib * MIB)


def vmem_specs(count):
    return [pl.BlockSpec(memory_space=pltpu.VMEM)] * count


def place(z, chunks, u, dense_ref):
    for c in range(chunks * CHUNK_COLS):
        piece = z[c * 8 : c * 8 + 8]
        piece = jnp.concatenate([piece[:, :128], piece[:, 128:]], axis=0)
        hi = piece.astype(BF16)
        lo = (piece - hi.astype(F32)).astype(BF16)
        lanes = slice((c % CHUNK_COLS) * 128, (c % CHUNK_COLS) * 128 + 128)
        dense_ref[c // CHUNK_COLS, pl.ds(pl.multiple_of(u * 16, 16), 16), lanes] = hi
        dense_ref[c // CHUNK_COLS, pl.ds(pl.multiple_of(u * 16 + TALL, 16), 16), lanes] = lo


def one_hot(rows_ref, cols_ref, counts_ref, layer, flip, base, positions):
    slot = lax.broadcasted_iota(jnp.int32, (1, rows_ref.shape[1]), 1)
    key = (cols_ref[pl.ds(layer, 1), :] ^ flip) * BROWS + rows_ref[pl.ds(layer, 1), :]
    key = jnp.where(slot < counts_ref[0, layer], key, -1)
    position = lax.broadcasted_iota(jnp.int32, (positions, key.shape[1]), 0) + base
    return jnp.where(position == key, 1.0, 0.0).astype(BF16)


def build_kernel(rows_ref, cols_ref, counts_ref, blocks_ref, dense_ref):
    chunks = dense_ref.shape[1]
    positions = chunks * CHUNK_COLS * BROWS
    base = pl.program_id(1) * positions
    onehot = one_hot(rows_ref, cols_ref, counts_ref, pl.program_id(0), 0, base, positions)

    def step(u, carry):
        cols = pl.ds(pl.multiple_of(u * 256, 256), 256)
        z = jnp.dot(onehot, blocks_ref[0, :, cols], preferred_element_type=F32)
        place(z, chunks, u, dense_ref.at[0])
        return carry

    lax.fori_loop(0, BLK * BLK // 256, step, 0)


def fill(onehot, held, dense_ref, piece, width):
    for v in range(width // 256):
        cols = pl.ds(pl.multiple_of(piece * width + v * 256, 256), 256)
        z = jnp.dot(onehot, held[:, cols], preferred_element_type=F32)
        place(z, dense_ref.shape[0], piece * (width // 256) + v, dense_ref)


def build_whole_kernel(rows_hbm, cols_hbm, counts_hbm, blocks_ref, *refs):
    *dense_refs, held, rows_ref, cols_ref, counts_ref, arrived, index_arrived = refs
    layers, pieces = arrived.shape
    width = held.shape[2] // pieces
    ahead = 3

    def fetch(layer, piece):
        cols = pl.ds(pl.multiple_of(piece * width, width), width)
        return pltpu.make_async_copy(
            blocks_ref.at[layer, :, cols], held.at[layer, :, cols], arrived.at[layer, piece]
        )

    index_copies = [
        pltpu.make_async_copy(source, target, index_arrived.at[i])
        for i, (source, target) in enumerate(
            [(rows_hbm, rows_ref), (cols_hbm, cols_ref), (counts_hbm, counts_ref)]
        )
    ]
    for copy in index_copies:
        copy.start()
    for piece in range(ahead):
        fetch(0, piece).start()
    for copy in index_copies:
        copy.wait()
    flip = lax.axis_index("node") * CHUNK_COLS
    for layer, dense_ref in enumerate(dense_refs):
        onehot = one_hot(rows_ref, cols_ref, counts_ref, layer, flip, 0, dense_ref.shape[0] * CHUNK_COLS * BROWS)

        def step(piece, carry):
            fetch(layer, piece).wait()

            @pl.when(piece + ahead < pieces)
            def _():
                fetch(layer, piece + ahead).start()

            if layer + 1 < layers:

                @pl.when(piece + ahead >= pieces)
                def _():
                    fetch(layer + 1, piece + ahead - pieces).start()

            fill(onehot, held.at[layer], dense_ref, piece, width)
            return carry

        lax.fori_loop(0, pieces, step, 0)


def build_whole(block_rows, block_cols, counts, blocks, chunk_total):
    layers = blocks.shape[0]
    dense = jax.ShapeDtypeStruct((chunk_total, 2 * TALL, CHUNK_LANES), BF16)
    operands = (block_rows, block_cols, counts.T, blocks)
    return pl.pallas_call(
        build_whole_kernel,
        in_specs=[pl.BlockSpec(memory_space=pltpu.HBM)] * 4,
        out_specs=vmem_specs(layers),
        out_shape=[dense] * layers,
        scratch_shapes=[
            pltpu.VMEM(blocks.shape, BF16),
            pltpu.VMEM(block_rows.shape, jnp.int32),
            pltpu.VMEM(block_cols.shape, jnp.int32),
            pltpu.SMEM((1, layers), jnp.int32),
            pltpu.SemaphoreType.DMA((layers, 4)),
            pltpu.SemaphoreType.DMA((3,)),
        ],
        compiler_params=params(28),
        cost_estimate=pl.CostEstimate(flops=0, bytes_accessed=20 * MIB, transcendentals=0),
        name="build_whole",
    )(*[pltpu.with_memory_space_constraint(x, pltpu.HBM) for x in operands])


def build_dense(block_rows, block_cols, counts, blocks, chunk_total):
    layers, slots, width = blocks.shape
    dense = jax.ShapeDtypeStruct((layers, chunk_total, 2 * TALL, CHUNK_LANES), BF16)
    operands = (block_rows, block_cols, counts.T, blocks)
    return pl.pallas_call(
        build_kernel,
        grid=(layers, chunk_total // 4),
        in_specs=vmem_specs(2)
        + [
            pl.BlockSpec(memory_space=pltpu.SMEM),
            pl.BlockSpec((1, slots, width), lambda l, s: (l, 0, 0)),
        ],
        out_specs=pl.BlockSpec((1, 4, 2 * TALL, CHUNK_LANES), lambda l, s: (l, s, 0, 0)),
        out_shape=dense,
        compiler_params=params(24),
        name="build_dense",
    )(*operands)


def split3(x):
    a = x.astype(BF16)
    r = x - a.astype(F32)
    b = r.astype(BF16)
    c = (r - b.astype(F32)).astype(BF16)
    return a, b, c


def image_part(basis, dense):
    k, width = basis.shape
    basis = basis.astype(F32)
    tall = jnp.concatenate([basis, basis], axis=0).T
    lane = lax.broadcasted_iota(jnp.int32, tall.shape, 1)
    first = jnp.where(lane < k, tall, 0.0).astype(BF16)
    second = jnp.where(lane < k, 0.0, tall).astype(BF16)
    weights = []
    for c in range(width // BLK):
        weights += [first[c * BLK : c * BLK + BLK], second[c * BLK : c * BLK + BLK]]
    return jnp.dot(dense, jnp.concatenate(weights, axis=0), preferred_element_type=F32)


def to_wide(total, k, halves, tall):
    halves[:, : 2 * k] = total[:TALL] + total[TALL:]
    halves[:, 2 * k :] = jnp.zeros((TALL, 128 - 2 * k), F32)
    for b in range(BROWS):
        part = halves[pl.ds(b, BLK // 2, stride=BROWS), :]
        tall[pl.ds(BLK * b, BLK // 2, stride=2), :] = part
        tall[pl.ds(BLK * b + 1, BLK // 2, stride=2), :] = pltpu.roll(part, 128 - k, 1)
    return tall[...].T[:k]


def against(left, tall):
    k = left.shape[0]
    lane = lax.broadcasted_iota(jnp.int32, tall.shape, 1)
    a, b, c = split3(jnp.where(lane < k, tall, 0.0))
    right = a.astype(F32) + pltpu.roll(b.astype(F32), k, 1) + pltpu.roll(c.astype(F32), 2 * k, 1)
    pieces = jnp.dot(jnp.concatenate(split3(left), axis=0), right.astype(BF16), preferred_element_type=F32)
    top, middle, bottom = pieces[:k], pieces[k : 2 * k], pieces[2 * k :]
    total = top[:, :k] + (top[:, k : 2 * k] + middle[:, :k])
    return total + (middle[:, k : 2 * k] + (top[:, 2 * k : 3 * k] + bottom[:, :k]))


def apply_kernel(mode, *refs):
    basis_ref, refs = refs[0], refs[1:]
    if mode == "score":
        left_ref, refs = refs[0], refs[1:]
    dense_ref, out_ref = refs[:2]
    halves, tall, acc = refs[-3:]
    layer, chunk = pl.program_id(0), pl.program_id(1)
    total = image_part(basis_ref[chunk, layer], dense_ref[0, 0])

    @pl.when(chunk == 0)
    def _():
        acc[...] = total

    @pl.when(chunk > 0)
    def _():
        acc[...] += total

    @pl.when(chunk == pl.num_programs(1) - 1)
    def _():
        image = to_wide(acc[...], basis_ref.shape[2], halves, tall)
        if mode != "score":
            out_ref[0] = image
        if mode == "gram":
            refs[2][0] = against(image, tall[...])
        if mode == "score":
            out_ref[0] = against(left_ref[0], tall[...])


def product(a, b):
    k = a.shape[0]
    left = jnp.concatenate(split3(a), axis=0)
    right = left if b is a else jnp.concatenate(split3(b), axis=0)
    pieces = lax.dot_general(left, right, TRANS_B, preferred_element_type=F32)
    top, middle, bottom = pieces[:k], pieces[k : 2 * k], pieces[2 * k :]
    total = top[:, :k] + (top[:, k : 2 * k] + middle[:, :k])
    return total + (middle[:, k : 2 * k] + (top[:, 2 * k : 3 * k] + bottom[:, :k]))


def first_kernel(layer, chunks, *refs):
    pieces, (dense_ref, out_ref, halves, tall) = refs[: len(chunks)], refs[len(chunks) :]
    total = sum(image_part(piece[layer], dense_ref[chunk]) for chunk, piece in zip(chunks, pieces))
    out_ref[...] = to_wide(total, out_ref.shape[0], halves, tall)


def second_kernel(piece_count, earlier_count, *refs):
    pieces, dense_ref, refs = refs[:piece_count], refs[piece_count], refs[piece_count + 1 :]
    earlier, (out_ref, halves, tall, scratch) = refs[:earlier_count], refs[earlier_count:]
    image = jnp.concatenate([piece[...] for piece in pieces], axis=1)
    inverse = inverse_factor(product(image, image), scratch)
    basis = jnp.dot(inverse, image, precision=HIGHEST, preferred_element_type=F32)
    parts = [basis[:, d * ROWS_DEV : d * ROWS_DEV + ROWS_DEV] for d in range(piece_count)]
    before = out_ref.shape[0] - 1
    for ref in earlier:
        out_ref[:before] = ref[...]
    out_ref[before] = to_wide(sum(image_part(part, dense_ref[chunk]) for chunk, part in zip(ORDER, parts)), out_ref.shape[1], halves, tall)


def some_kernel(chunk, layers, basis_ref, *refs):
    dense_refs, (*so_far, out_ref) = refs[:layers], refs[layers:]
    for layer, dense_ref in enumerate(dense_refs):
        part = image_part(basis_ref[layer], dense_ref[chunk])
        out_ref[layer] = sum((ref[layer] for ref in so_far), part)


def score_kernel(layers, chunks, so_far_ref, *refs):
    pieces, left_ref, refs = refs[: len(chunks)], refs[len(chunks)], refs[len(chunks) + 1 :]
    dense_refs, (out_ref, halves, tall) = refs[:layers], refs[layers:]
    totals = [
        so_far_ref[layer]
        + sum(image_part(piece[layer], dense_refs[layer][chunk]) for chunk, piece in zip(chunks, pieces))
        for layer in range(layers)
    ]
    wide = [
        to_wide(totals[layer], left_ref.shape[1], halves.at[layer], tall.at[layer]) for layer in range(layers)
    ]
    for layer in range(layers):
        out_ref[layer] = product(left_ref[layer], wide[layer])


def apply_whole(kernel, name, operands, out_shape, *lead, scratch=()):
    return pl.pallas_call(
        kernel,
        in_specs=vmem_specs(len(operands)),
        out_specs=pl.BlockSpec(memory_space=pltpu.VMEM),
        out_shape=jax.ShapeDtypeStruct(out_shape, F32),
        scratch_shapes=[pltpu.VMEM((*lead, TALL, 128), F32), pltpu.VMEM((*lead, ROWS_DEV, 128), F32), *scratch],
        compiler_params=params(14),
        cost_estimate=pl.CostEstimate(flops=0, bytes_accessed=4 * MIB, transcendentals=0),
        name=name,
    )(*operands)


def apply_first(layer, chunks, pieces, dense):
    kernel = functools.partial(first_kernel, layer, chunks)
    return apply_whole(kernel, "apply_first", [*pieces, dense], pieces[0].shape[1:])


def apply_second(pieces, dense, earlier):
    kernel = functools.partial(second_kernel, len(pieces), len(earlier))
    before = sum(array.shape[0] for array in earlier)
    shape = (before + 1, *pieces[0].shape)
    operands = [*pieces, dense, *earlier]
    return apply_whole(kernel, "apply_second", operands, shape, scratch=[pltpu.VMEM(SPREAD, F32)])


def apply_some(chunk, basis, dense, *so_far):
    layers, k = basis.shape[:2]
    return pl.pallas_call(
        functools.partial(some_kernel, chunk, layers),
        in_specs=vmem_specs(1 + layers + len(so_far)),
        out_specs=pl.BlockSpec(memory_space=pltpu.VMEM),
        out_shape=jax.ShapeDtypeStruct((layers, 2 * TALL, 2 * k), F32),
        compiler_params=params(14),
        cost_estimate=pl.CostEstimate(flops=0, bytes_accessed=2 * MIB, transcendentals=0),
        name=f"apply_some_{chunk}",
    )(basis, *dense, *so_far)


def apply_score(pieces, left, dense):
    so_far = apply_some(ORDER[1], pieces[1], dense, apply_some(0, pieces[0], dense))
    kernel = functools.partial(score_kernel, len(dense), ORDER[2:])
    layers, k = left.shape[:2]
    operands = [so_far, *pieces[2:], left, *dense]
    return apply_whole(kernel, "apply_score", operands, (layers, k, k), layers)


def apply_dense(mode, basis, dense, left=None):
    layers, chunks = dense.shape[:2]
    k = basis.shape[-2]
    image = jax.ShapeDtypeStruct((layers, k, ROWS_DEV), F32)
    small = jax.ShapeDtypeStruct((layers, k, k), F32)
    out_shape = {"gram": [image, small], "plain": [image], "score": [small]}[mode]
    operands = [basis] + ([left] if mode == "score" else []) + [dense]
    dense_spec = pl.BlockSpec((1, 1, 2 * TALL, CHUNK_LANES), lambda l, s: (l, s, 0, 0))
    image_spec = pl.BlockSpec((1, k, ROWS_DEV), lambda l, s: (l, 0, 0))
    small_spec = pl.BlockSpec((1, k, k), lambda l, s: (l, 0, 0))
    return pl.pallas_call(
        functools.partial(apply_kernel, mode),
        grid=(layers, chunks),
        in_specs=vmem_specs(1) + ([image_spec] if mode == "score" else []) + [dense_spec],
        out_specs={"gram": [image_spec, small_spec], "plain": [image_spec], "score": [small_spec]}[mode],
        out_shape=out_shape,
        scratch_shapes=[
            pltpu.VMEM((TALL, 128), F32),
            pltpu.VMEM((ROWS_DEV, 128), F32),
            pltpu.VMEM((2 * TALL, 2 * k), F32),
        ],
        compiler_params=params(12),
        name="apply_" + mode,
    )(*operands)


def spread(x):
    return jnp.broadcast_to(x, (8, 128))


def eliminate(rows, offset, scratch):
    groups, tiles = len(rows), len(rows[0])
    rows = [list(row) for row in rows]
    home, at = offset // 128, offset % 128
    sub = lax.broadcasted_iota(jnp.int32, (8, 128), 0)
    solved = []
    for h in range(groups):
        below = range(h + 1, groups)
        lane = at + 8 * h
        col = [{g: spread(rows[g][home][:, lane + q : lane + q + 1]) for g in range(h, groups)} for q in range(8)]
        held = scratch.at[h % 2]
        for q in range(8):
            held[q * 8 : q * 8 + 8] = col[q][h]
        for t in range(tiles):
            held[64 + t * 8 : 72 + t * 8] = rows[h][t]
        cell = {(p, q): spread(held[p * 8 + q : p * 8 + q + 1]) for q in range(8) for p in range(q + 1)}
        row = [[spread(held[64 + t * 8 + q : 65 + t * 8 + q]) for t in range(tiles)] for q in range(8)]
        done = []
        for m in range(0, 8, 2):
            n = m + 1
            a, b, c = cell[m, m], cell[m, n], cell[n, n]
            det = a * c - b * b
            if m % 4 == 0:
                r = pl.reciprocal(det, approx=True)
            else:
                r = square * pl.reciprocal(whole, approx=True)
            later = range(m + 2, 8)
            u = {q: c * cell[m, q] - b * cell[n, q] for q in later}
            v = {q: a * cell[n, q] - b * cell[m, q] for q in later}
            taken = {(p, q): cell[m, p] * u[q] + cell[n, p] * v[q] for q in later for p in range(m + 2, q + 1)}
            if m % 4 == 0:
                i, j = m + 2, m + 3
                first, cross, last = (det * cell[pq] - taken[pq] for pq in ((i, i), (i, j), (j, j)))
                whole = first * last - cross * cross
                square = det * det
            for pq in taken:
                cell[pq] = cell[pq] - r * taken[pq]
            for q in later:
                for g in below:
                    col[q][g] = col[q][g] - r * (col[m][g] * u[q] + col[n][g] * v[q])
            for t in range(tiles):
                x = r * (c * row[m][t] - b * row[n][t])
                y = r * (a * row[n][t] - b * row[m][t])
                for q in later:
                    row[q][t] = row[q][t] - (cell[m, q] * x + cell[n, q] * y)
                for g in below:
                    rows[g][t] = rows[g][t] - (col[m][g] * x + col[n][g] * y)
            over = pl.reciprocal(a, approx=True)
            done.append([lax.rsqrt(a) * x for x in row[m]])
            scale = lax.rsqrt(det * over)
            done.append([scale * (x - (b * over) * w) for x, w in zip(row[n], row[m])])
        finished = []
        for t in range(tiles):
            x = done[7][t]
            for q in range(7):
                x = jnp.where(sub == q, done[q][t], x)
            finished.append(x)
        solved.append(finished)
    return solved


def tiled(x):
    return [
        [x[g * 8 : g * 8 + 8, t * 128 : t * 128 + 128] for t in range(x.shape[1] // 128)]
        for g in range(x.shape[0] // 8)
    ]


def joined(tiles):
    return jnp.concatenate([jnp.concatenate(row, axis=1) for row in tiles], axis=0)


def unit_scale(gram):
    lane = lax.broadcasted_iota(jnp.int32, gram.shape, 1)
    sub = lax.broadcasted_iota(jnp.int32, gram.shape, 0)
    kept = jnp.where(lane == sub, gram, 0.0)
    down = 1.0 / jnp.sqrt(jnp.sum(kept, axis=1, keepdims=True))
    across = jnp.sum(kept, axis=0, keepdims=True)
    across = 1.0 / jnp.sqrt(jnp.where(across == 0.0, 1.0, across))
    return gram * down * across, across


def gram_update(panel, first):
    a, b, c = split3(panel)
    left = jnp.concatenate([a, a, b, b, a, c], axis=0)
    right = jnp.concatenate([a, b, a, b, c, a], axis=0)
    parts = {
        at: lax.dot_general(left[:, at : at + 128], right, TRANS_A, preferred_element_type=F32)
        for at in range(first, panel.shape[1], 128)
    }
    return lambda at, count: parts[at // 128 * 128][at % 128 : at % 128 + count]


def inverse_factor(gram, scratch):
    k = gram.shape[0]
    lane = lax.broadcasted_iota(jnp.int32, (k, 128), 1)
    sub = lax.broadcasted_iota(jnp.int32, (k, 128), 0)
    eye = jnp.where(lane == sub, 1.0, 0.0)
    gram, across = unit_scale(jnp.concatenate([gram, jnp.zeros((k, 128 - k), F32)], axis=1))
    solved = eliminate(tiled(jnp.concatenate([gram, eye], axis=1)), 0, scratch)
    return (joined(solved)[:, 128:] * across)[:, :k]


def solve_kernel(gram_ref, image_ref, out_ref, scratch):
    for layer in range(image_ref.shape[0]):
        inverse = inverse_factor(gram_ref[layer], scratch.at[layer])
        solved = jnp.dot(inverse, image_ref[layer], precision=HIGHEST, preferred_element_type=F32)
        out_ref[layer] = solved.astype(BF16)


def solve(gram, image):
    return pl.pallas_call(
        solve_kernel,
        in_specs=vmem_specs(2),
        out_specs=pl.BlockSpec(memory_space=pltpu.VMEM),
        out_shape=jax.ShapeDtypeStruct(image.shape, BF16),
        scratch_shapes=[pltpu.VMEM((image.shape[0], *SPREAD), F32)],
        compiler_params=params(4),
        name="solve_layers",
    )(gram, image)


def cross_kernel(k, images_ref, out_ref, packed):
    g = lax.axis_index("layer")
    every = images_ref[...].reshape(-1, images_ref.shape[2])
    gram = lax.dot_general(every, every, TRANS_B, precision=HIGHEST, preferred_element_type=F32)
    half = gram.shape[0] // 2
    first, last = gram[:half, :half], gram[half:, half:]
    row = lax.broadcasted_iota(jnp.int32, (half, half), 0) // k
    col = lax.broadcasted_iota(jnp.int32, (half, half), 1) // k
    packed[:half] = gram[:half, half:]
    packed[half : 2 * half] = jnp.where(col >= row, first, last)
    diagonal = jnp.where(col == row, last, 0.0)
    packed[2 * half :] = sum(diagonal[r * k : r * k + k] for r in range(half // k))
    rows = out_ref.shape[0]
    out_ref[...] = packed[pl.ds(pl.multiple_of((g & 1) * rows, 16), rows)]


def cross(images):
    layers, k, _ = images.shape
    size = layers * k
    return pl.pallas_call(
        functools.partial(cross_kernel, k),
        in_specs=vmem_specs(1),
        out_specs=pl.BlockSpec(memory_space=pltpu.VMEM),
        out_shape=jax.ShapeDtypeStruct(((size + k) // 2, size // 2), F32),
        scratch_shapes=[pltpu.VMEM((size + k, size // 2), F32)],
        compiler_params=params(6),
        name="cross_gram",
    )(images)


def unpack(packed, k, work):
    half = packed.shape[1]
    row = lax.broadcasted_iota(jnp.int32, (half, half), 0) // k
    col = lax.broadcasted_iota(jnp.int32, (half, half), 1) // k
    mixed = packed[half : 2 * half]
    under = jnp.where(col < row, mixed, 0.0)
    diagonal = jnp.concatenate([packed[2 * half :]] * (half // k), axis=0)
    work[:half, :half] = jnp.where(col >= row, mixed, 0.0)
    work[:half, half:] = packed[:half]
    work[half:, :half] = jnp.zeros((half, half), F32)
    work[half:, half:] = under.T + jnp.where(col == row, diagonal, 0.0)


def joint_kernel(k, *refs):
    own_ref, other_ref, images_ref, out_ref, again_ref, rounded_ref, work, packed, scratch = refs
    rows = own_ref.shape[0]
    odd = lax.axis_index("layer") & 1
    packed[pl.ds(pl.multiple_of(odd * rows, 16), rows)] = own_ref[...]
    packed[pl.ds(pl.multiple_of((1 - odd) * rows, 16), rows)] = other_ref[...]
    unpack(packed[...], k, work)
    size = work.shape[0]
    steps = size // k
    lane = lax.broadcasted_iota(jnp.int32, (k, size), 1)
    lane_128 = lax.broadcasted_iota(jnp.int32, (k, 128), 1)
    sub_128 = lax.broadcasted_iota(jnp.int32, (k, 128), 0)
    gram, across = unit_scale(work[...])
    work[...] = gram
    for s in range(steps):
        lo, hi = s * k, (s + 1) * k
        here = (lane >= lo) & (lane < hi)
        eye = jnp.where(lane_128 == sub_128 + lo % 128, 1.0, 0.0)
        solved = joined(eliminate(tiled(jnp.concatenate([work[lo:hi], eye], axis=1)), lo, scratch.at[s % 2]))
        panel, tail = solved[:, :size], solved[:, size:]
        panel = jnp.where(here, jnp.concatenate([tail] * (size // 128), axis=1), panel)
        work[lo:hi] = jnp.where(lane < hi, panel, 0.0)
        if s + 1 < steps:
            update = gram_update(panel, hi // 128 * 128)
            for r in range(s + 1, steps):
                rows = work[r * k : r * k + k]
                work[r * k : r * k + k] = jnp.where(here, 0.0, rows) - update(r * k, k)
    rows = out_ref.shape[0] * k
    own = work[pl.ds(pl.multiple_of(lax.axis_index("layer") * rows, rows), rows)] * across
    joint = jnp.dot(own, images_ref[...].reshape(size, -1), precision=HIGHEST, preferred_element_type=F32)
    joint = joint.reshape(out_ref.shape)
    out_ref[...] = joint
    again_ref[...] = joint
    rounded_ref[...] = joint.astype(BF16)


def joint_solve(own, other, images, shape):
    k = shape[1]
    size = images.shape[0] * k
    return pl.pallas_call(
        functools.partial(joint_kernel, k),
        in_specs=vmem_specs(3),
        out_specs=vmem_specs(3),
        out_shape=[
            jax.ShapeDtypeStruct(shape, F32),
            jax.ShapeDtypeStruct(shape, F32),
            jax.ShapeDtypeStruct(shape, BF16),
        ],
        scratch_shapes=[
            pltpu.VMEM((size, size), F32),
            pltpu.VMEM((size + k, size // 2), F32),
            pltpu.VMEM((2, *SPREAD), F32),
        ],
        compiler_params=params(8),
        name="joint_solve",
    )(own, other, images)


def swap(x, axis, d, count):
    return lax.ppermute(x, axis, [(m ^ d, m) for m in range(count)])


ORDER = (0, 3, 2, 1)


def around(x, axis, count):
    return [x] + [swap(x, axis, d, count) for d in ORDER[1:]]


def add_pieces(pieces, flip):
    own, near, far, across = (pieces[ORDER.index(d)] for d in range(4))
    low, high = own + near, across + far
    return high + low if flip else low + high


def per_device(shards, groups, blocks, block_rows, block_cols, counts, start):
    few = shards == 4
    layers = start.shape[0]

    def gather(x):
        return around(x, "node", shards) if few else lax.all_gather(x, "node")

    def total(x, flip=False):
        return add_pieces(around(x, "node", shards), flip) if few else lax.psum(x, "node")

    rounded = start.astype(BF16)
    chunk_total = shards * BROWS // CHUNK_COLS
    if few:
        chunks = (0, 1, 3, 2)
        first = [rounded] + [swap(rounded, "node", d, shards) for d in chunks[1:]]
        dense = build_whole(block_rows, block_cols, counts, blocks, chunk_total)
        images = [apply_first(layer, chunks, first, dense[layer]) for layer in range(layers)]
        image = None
        for layer in range(layers):
            image = apply_second(gather(images[layer]), dense[layer], [] if image is None else [image])
    else:
        dense = build_dense(block_rows, block_cols, counts, blocks, chunk_total)
        image, gram = apply_dense("gram", gather(rounded), dense)
        (image,) = apply_dense("plain", gather(solve(total(gram), image)), dense)
    images = lax.all_gather(image, "layer", axis=0, tiled=True)
    own = cross(images)
    own = total(own)
    other = swap(own, "layer", 1, groups)
    joint_basis, again, rounded = joint_solve(own, other, images, start.shape)
    if few:
        partial = apply_score(gather(rounded), again, dense)
    else:
        (partial,) = apply_dense("score", gather(rounded), dense, again)
    return joint_basis, total(partial, True)


def solution(mesh):
    in_specs = (
        P(("parts", "layer"), "node", None),
        P(("parts", "layer"), "node"),
        P(("parts", "layer"), "node"),
        P(("parts", "layer"), "node"),
        P(("parts", "layer"), None, "node"),
    )
    out_specs = (P(("parts", "layer"), None, "node"), P(("parts", "layer"), None, None))
    return jax.shard_map(
        functools.partial(per_device, mesh.shape["node"], mesh.shape["layer"]),
        mesh=mesh,
        in_specs=in_specs,
        out_specs=out_specs,
        check_vma=False,
    )
```

```python
import functools

import jax
import jax.numpy as jnp
from jax import lax
from jax.experimental import pallas as pl
from jax.experimental.pallas import tpu as pltpu
from jax.sharding import PartitionSpec as P

BLK = 64
ROWS_DEV = 512
BROWS = ROWS_DEV // BLK
CHUNK_COLS = 8
CHUNK_LANES = CHUNK_COLS * 2 * BLK
TALL = BROWS * BLK // 2
MIB = 1024 * 1024
F32 = jnp.float32
BF16 = jnp.bfloat16
HIGHEST = lax.Precision.HIGHEST
TRANS_B = (((1,), (1,)), ((), ()))
TRANS_A = (((0,), (0,)), ((), ()))
SPREAD = (2, 88, 128)


def params(mib):
    return pltpu.CompilerParams(vmem_limit_bytes=mib * MIB)


def vmem_specs(count):
    return [pl.BlockSpec(memory_space=pltpu.VMEM)] * count


def place(z, chunks, u, dense_ref):
    for c in range(chunks * CHUNK_COLS):
        piece = z[c * 8 : c * 8 + 8]
        piece = jnp.concatenate([piece[:, :128], piece[:, 128:]], axis=0)
        hi = piece.astype(BF16)
        lo = (piece - hi.astype(F32)).astype(BF16)
        lanes = slice((c % CHUNK_COLS) * 128, (c % CHUNK_COLS) * 128 + 128)
        dense_ref[c // CHUNK_COLS, pl.ds(pl.multiple_of(u * 16, 16), 16), lanes] = hi
        dense_ref[c // CHUNK_COLS, pl.ds(pl.multiple_of(u * 16 + TALL, 16), 16), lanes] = lo


def one_hot(rows_ref, cols_ref, counts_ref, layer, flip, base, positions):
    slot = lax.broadcasted_iota(jnp.int32, (1, rows_ref.shape[1]), 1)
    key = (cols_ref[pl.ds(layer, 1), :] ^ flip) * BROWS + rows_ref[pl.ds(layer, 1), :]
    key = jnp.where(slot < counts_ref[0, layer], key, -1)
    position = lax.broadcasted_iota(jnp.int32, (positions, key.shape[1]), 0) + base
    return jnp.where(position == key, 1.0, 0.0).astype(BF16)


def build_kernel(rows_ref, cols_ref, counts_ref, blocks_ref, dense_ref):
    chunks = dense_ref.shape[1]
    positions = chunks * CHUNK_COLS * BROWS
    base = pl.program_id(1) * positions
    onehot = one_hot(rows_ref, cols_ref, counts_ref, pl.program_id(0), 0, base, positions)

    def step(u, carry):
        cols = pl.ds(pl.multiple_of(u * 256, 256), 256)
        z = jnp.dot(onehot, blocks_ref[0, :, cols], preferred_element_type=F32)
        place(z, chunks, u, dense_ref.at[0])
        return carry

    lax.fori_loop(0, BLK * BLK // 256, step, 0)


def fill(onehot, held, dense_ref, piece, width):
    for v in range(width // 256):
        cols = pl.ds(pl.multiple_of(piece * width + v * 256, 256), 256)
        z = jnp.dot(onehot, held[:, cols], preferred_element_type=F32)
        place(z, dense_ref.shape[0], piece * (width // 256) + v, dense_ref)


def build_whole_kernel(rows_hbm, cols_hbm, counts_hbm, blocks_ref, *refs):
    *dense_refs, held, rows_ref, cols_ref, counts_ref, arrived, index_arrived = refs
    layers, pieces = arrived.shape
    width = held.shape[2] // pieces
    ahead = 3

    def fetch(layer, piece):
        cols = pl.ds(pl.multiple_of(piece * width, width), width)
        return pltpu.make_async_copy(
            blocks_ref.at[layer, :, cols], held.at[layer, :, cols], arrived.at[layer, piece]
        )

    index_copies = [
        pltpu.make_async_copy(source, target, index_arrived.at[i])
        for i, (source, target) in enumerate(
            [(rows_hbm, rows_ref), (cols_hbm, cols_ref), (counts_hbm, counts_ref)]
        )
    ]
    for copy in index_copies:
        copy.start()
    for piece in range(ahead):
        fetch(0, piece).start()
    for copy in index_copies:
        copy.wait()
    flip = lax.axis_index("node") * CHUNK_COLS
    for layer, dense_ref in enumerate(dense_refs):
        onehot = one_hot(rows_ref, cols_ref, counts_ref, layer, flip, 0, dense_ref.shape[0] * CHUNK_COLS * BROWS)

        def step(piece, carry):
            fetch(layer, piece).wait()

            @pl.when(piece + ahead < pieces)
            def _():
                fetch(layer, piece + ahead).start()

            if layer + 1 < layers:

                @pl.when(piece + ahead >= pieces)
                def _():
                    fetch(layer + 1, piece + ahead - pieces).start()

            fill(onehot, held.at[layer], dense_ref, piece, width)
            return carry

        lax.fori_loop(0, pieces, step, 0)


def build_whole(block_rows, block_cols, counts, blocks, chunk_total):
    layers = blocks.shape[0]
    dense = jax.ShapeDtypeStruct((chunk_total, 2 * TALL, CHUNK_LANES), BF16)
    operands = (block_rows, block_cols, counts.T, blocks)
    return pl.pallas_call(
        build_whole_kernel,
        in_specs=[pl.BlockSpec(memory_space=pltpu.HBM)] * 4,
        out_specs=vmem_specs(layers),
        out_shape=[dense] * layers,
        scratch_shapes=[
            pltpu.VMEM(blocks.shape, BF16),
            pltpu.VMEM(block_rows.shape, jnp.int32),
            pltpu.VMEM(block_cols.shape, jnp.int32),
            pltpu.SMEM((1, layers), jnp.int32),
            pltpu.SemaphoreType.DMA((layers, 4)),
            pltpu.SemaphoreType.DMA((3,)),
        ],
        compiler_params=params(28),
        cost_estimate=pl.CostEstimate(flops=0, bytes_accessed=20 * MIB, transcendentals=0),
        name="build_whole",
    )(*[pltpu.with_memory_space_constraint(x, pltpu.HBM) for x in operands])


def build_dense(block_rows, block_cols, counts, blocks, chunk_total):
    layers, slots, width = blocks.shape
    dense = jax.ShapeDtypeStruct((layers, chunk_total, 2 * TALL, CHUNK_LANES), BF16)
    operands = (block_rows, block_cols, counts.T, blocks)
    return pl.pallas_call(
        build_kernel,
        grid=(layers, chunk_total // 4),
        in_specs=vmem_specs(2)
        + [
            pl.BlockSpec(memory_space=pltpu.SMEM),
            pl.BlockSpec((1, slots, width), lambda l, s: (l, 0, 0)),
        ],
        out_specs=pl.BlockSpec((1, 4, 2 * TALL, CHUNK_LANES), lambda l, s: (l, s, 0, 0)),
        out_shape=dense,
        compiler_params=params(24),
        name="build_dense",
    )(*operands)


def split3(x):
    a = x.astype(BF16)
    r = x - a.astype(F32)
    b = r.astype(BF16)
    c = (r - b.astype(F32)).astype(BF16)
    return a, b, c


def image_part(basis, dense):
    k, width = basis.shape
    basis = basis.astype(F32)
    tall = jnp.concatenate([basis, basis], axis=0).T
    lane = lax.broadcasted_iota(jnp.int32, tall.shape, 1)
    first = jnp.where(lane < k, tall, 0.0).astype(BF16)
    second = jnp.where(lane < k, 0.0, tall).astype(BF16)
    weights = []
    for c in range(width // BLK):
        weights += [first[c * BLK : c * BLK + BLK], second[c * BLK : c * BLK + BLK]]
    return jnp.dot(dense, jnp.concatenate(weights, axis=0), preferred_element_type=F32)


def to_wide(total, k, halves, tall):
    halves[:, : 2 * k] = total[:TALL] + total[TALL:]
    halves[:, 2 * k :] = jnp.zeros((TALL, 128 - 2 * k), F32)
    for b in range(BROWS):
        part = halves[pl.ds(b, BLK // 2, stride=BROWS), :]
        tall[pl.ds(BLK * b, BLK // 2, stride=2), :] = part
        tall[pl.ds(BLK * b + 1, BLK // 2, stride=2), :] = pltpu.roll(part, 128 - k, 1)
    return tall[...].T[:k]


def against(left, tall):
    k = left.shape[0]
    lane = lax.broadcasted_iota(jnp.int32, tall.shape, 1)
    a, b, c = split3(jnp.where(lane < k, tall, 0.0))
    right = a.astype(F32) + pltpu.roll(b.astype(F32), k, 1) + pltpu.roll(c.astype(F32), 2 * k, 1)
    pieces = jnp.dot(jnp.concatenate(split3(left), axis=0), right.astype(BF16), preferred_element_type=F32)
    top, middle, bottom = pieces[:k], pieces[k : 2 * k], pieces[2 * k :]
    total = top[:, :k] + (top[:, k : 2 * k] + middle[:, :k])
    return total + (middle[:, k : 2 * k] + (top[:, 2 * k : 3 * k] + bottom[:, :k]))


def apply_kernel(mode, *refs):
    basis_ref, refs = refs[0], refs[1:]
    if mode == "score":
        left_ref, refs = refs[0], refs[1:]
    dense_ref, out_ref = refs[:2]
    halves, tall, acc = refs[-3:]
    layer, chunk = pl.program_id(0), pl.program_id(1)
    total = image_part(basis_ref[chunk, layer], dense_ref[0, 0])

    @pl.when(chunk == 0)
    def _():
        acc[...] = total

    @pl.when(chunk > 0)
    def _():
        acc[...] += total

    @pl.when(chunk == pl.num_programs(1) - 1)
    def _():
        image = to_wide(acc[...], basis_ref.shape[2], halves, tall)
        if mode != "score":
            out_ref[0] = image
        if mode == "gram":
            refs[2][0] = against(image, tall[...])
        if mode == "score":
            out_ref[0] = against(left_ref[0], tall[...])


def split_dot(left, right, dims=(((1,), (0,)), ((), ()))):
    m = left.shape[0]
    a, b, c = split3(left)
    p, q, r = split3(right)

    def dot(rows, piece):
        return lax.dot_general(jnp.concatenate(rows, axis=0), piece, dims, preferred_element_type=F32)

    x, y, z = dot([a, b, c], p), dot([a, b], q), dot([a], r)
    return x[:m] + ((x[m : 2 * m] + y[:m]) + (y[m : 2 * m] + (x[2 * m :] + z)))


def product(a, b):
    k = a.shape[0]
    left = jnp.concatenate(split3(a), axis=0)
    right = left if b is a else jnp.concatenate(split3(b), axis=0)
    pieces = lax.dot_general(left, right, TRANS_B, preferred_element_type=F32)
    top, middle, bottom = pieces[:k], pieces[k : 2 * k], pieces[2 * k :]
    total = top[:, :k] + (top[:, k : 2 * k] + middle[:, :k])
    return total + (middle[:, k : 2 * k] + (top[:, 2 * k : 3 * k] + bottom[:, :k]))


def first_kernel(layer, chunks, *refs):
    pieces, (dense_ref, out_ref, halves, tall) = refs[: len(chunks)], refs[len(chunks) :]
    total = sum(image_part(piece[layer], dense_ref[chunk]) for chunk, piece in zip(chunks, pieces))
    out_ref[...] = to_wide(total, out_ref.shape[0], halves, tall)


def second_kernel(piece_count, earlier_count, *refs):
    pieces, dense_ref, refs = refs[:piece_count], refs[piece_count], refs[piece_count + 1 :]
    earlier, (out_ref, halves, tall, scratch) = refs[:earlier_count], refs[earlier_count:]
    image = jnp.concatenate([piece[...] for piece in pieces], axis=1)
    inverse = inverse_factor(product(image, image), scratch)
    basis = split_dot(inverse, image)
    parts = [basis[:, d * ROWS_DEV : d * ROWS_DEV + ROWS_DEV] for d in range(piece_count)]
    before = out_ref.shape[0] - 1
    for ref in earlier:
        out_ref[:before] = ref[...]
    out_ref[before] = to_wide(sum(image_part(part, dense_ref[chunk]) for chunk, part in zip(ORDER, parts)), out_ref.shape[1], halves, tall)


def some_kernel(chunk, layers, basis_ref, *refs):
    dense_refs, (*so_far, out_ref) = refs[:layers], refs[layers:]
    for layer, dense_ref in enumerate(dense_refs):
        part = image_part(basis_ref[layer], dense_ref[chunk])
        out_ref[layer] = sum((ref[layer] for ref in so_far), part)


def score_kernel(layers, chunks, so_far_ref, *refs):
    pieces, left_ref, refs = refs[: len(chunks)], refs[len(chunks)], refs[len(chunks) + 1 :]
    dense_refs, (out_ref, halves, tall) = refs[:layers], refs[layers:]
    totals = [
        so_far_ref[layer]
        + sum(image_part(piece[layer], dense_refs[layer][chunk]) for chunk, piece in zip(chunks, pieces))
        for layer in range(layers)
    ]
    wide = [
        to_wide(totals[layer], left_ref.shape[1], halves.at[layer], tall.at[layer]) for layer in range(layers)
    ]
    for layer in range(layers):
        out_ref[layer] = product(left_ref[layer], wide[layer])


def apply_whole(kernel, name, operands, out_shape, *lead, scratch=()):
    return pl.pallas_call(
        kernel,
        in_specs=vmem_specs(len(operands)),
        out_specs=pl.BlockSpec(memory_space=pltpu.VMEM),
        out_shape=jax.ShapeDtypeStruct(out_shape, F32),
        scratch_shapes=[pltpu.VMEM((*lead, TALL, 128), F32), pltpu.VMEM((*lead, ROWS_DEV, 128), F32), *scratch],
        compiler_params=params(14),
        cost_estimate=pl.CostEstimate(flops=0, bytes_accessed=4 * MIB, transcendentals=0),
        name=name,
    )(*operands)


def apply_first(layer, chunks, pieces, dense):
    kernel = functools.partial(first_kernel, layer, chunks)
    return apply_whole(kernel, "apply_first", [*pieces, dense], pieces[0].shape[1:])


def apply_second(pieces, dense, earlier):
    kernel = functools.partial(second_kernel, len(pieces), len(earlier))
    before = sum(array.shape[0] for array in earlier)
    shape = (before + 1, *pieces[0].shape)
    operands = [*pieces, dense, *earlier]
    return apply_whole(kernel, "apply_second", operands, shape, scratch=[pltpu.VMEM(SPREAD, F32)])


def apply_some(chunk, basis, dense, *so_far):
    layers, k = basis.shape[:2]
    return pl.pallas_call(
        functools.partial(some_kernel, chunk, layers),
        in_specs=vmem_specs(1 + layers + len(so_far)),
        out_specs=pl.BlockSpec(memory_space=pltpu.VMEM),
        out_shape=jax.ShapeDtypeStruct((layers, 2 * TALL, 2 * k), F32),
        compiler_params=params(14),
        cost_estimate=pl.CostEstimate(flops=0, bytes_accessed=2 * MIB, transcendentals=0),
        name=f"apply_some_{chunk}",
    )(basis, *dense, *so_far)


def apply_score(pieces, left, dense):
    so_far = apply_some(ORDER[1], pieces[1], dense, apply_some(0, pieces[0], dense))
    kernel = functools.partial(score_kernel, len(dense), ORDER[2:])
    layers, k = left.shape[:2]
    operands = [so_far, *pieces[2:], left, *dense]
    return apply_whole(kernel, "apply_score", operands, (layers, k, k), layers)


def apply_dense(mode, basis, dense, left=None):
    layers, chunks = dense.shape[:2]
    k = basis.shape[-2]
    image = jax.ShapeDtypeStruct((layers, k, ROWS_DEV), F32)
    small = jax.ShapeDtypeStruct((layers, k, k), F32)
    out_shape = {"gram": [image, small], "plain": [image], "score": [small]}[mode]
    operands = [basis] + ([left] if mode == "score" else []) + [dense]
    dense_spec = pl.BlockSpec((1, 1, 2 * TALL, CHUNK_LANES), lambda l, s: (l, s, 0, 0))
    image_spec = pl.BlockSpec((1, k, ROWS_DEV), lambda l, s: (l, 0, 0))
    small_spec = pl.BlockSpec((1, k, k), lambda l, s: (l, 0, 0))
    return pl.pallas_call(
        functools.partial(apply_kernel, mode),
        grid=(layers, chunks),
        in_specs=vmem_specs(1) + ([image_spec] if mode == "score" else []) + [dense_spec],
        out_specs={"gram": [image_spec, small_spec], "plain": [image_spec], "score": [small_spec]}[mode],
        out_shape=out_shape,
        scratch_shapes=[
            pltpu.VMEM((TALL, 128), F32),
            pltpu.VMEM((ROWS_DEV, 128), F32),
            pltpu.VMEM((2 * TALL, 2 * k), F32),
        ],
        compiler_params=params(12),
        name="apply_" + mode,
    )(*operands)


def spread(x):
    return jnp.broadcast_to(x, (8, 128))


def eliminate(rows, offset, scratch):
    groups, tiles = len(rows), len(rows[0])
    rows = [list(row) for row in rows]
    home, at = offset // 128, offset % 128
    sub = lax.broadcasted_iota(jnp.int32, (8, 128), 0)
    solved = []
    for h in range(groups):
        below = range(h + 1, groups)
        lane = at + 8 * h
        col = [{g: spread(rows[g][home][:, lane + q : lane + q + 1]) for g in range(h, groups)} for q in range(8)]
        held = scratch.at[h % 2]
        for q in range(8):
            held[q * 8 : q * 8 + 8] = col[q][h]
        for t in range(tiles):
            held[64 + t * 8 : 72 + t * 8] = rows[h][t]
        cell = {(p, q): spread(held[p * 8 + q : p * 8 + q + 1]) for q in range(8) for p in range(q + 1)}
        row = [[spread(held[64 + t * 8 + q : 65 + t * 8 + q]) for t in range(tiles)] for q in range(8)]
        done = []
        for m in range(0, 8, 2):
            n = m + 1
            a, b, c = cell[m, m], cell[m, n], cell[n, n]
            det = a * c - b * b
            if m % 4 == 0:
                r = pl.reciprocal(det, approx=True)
            else:
                r = square * pl.reciprocal(whole, approx=True)
            later = range(m + 2, 8)
            u = {q: c * cell[m, q] - b * cell[n, q] for q in later}
            v = {q: a * cell[n, q] - b * cell[m, q] for q in later}
            taken = {(p, q): cell[m, p] * u[q] + cell[n, p] * v[q] for q in later for p in range(m + 2, q + 1)}
            if m % 4 == 0:
                i, j = m + 2, m + 3
                first, cross, last = (det * cell[pq] - taken[pq] for pq in ((i, i), (i, j), (j, j)))
                whole = first * last - cross * cross
                square = det * det
            for pq in taken:
                cell[pq] = cell[pq] - r * taken[pq]
            for q in later:
                for g in below:
                    col[q][g] = col[q][g] - r * (col[m][g] * u[q] + col[n][g] * v[q])
            for t in range(tiles):
                x = r * (c * row[m][t] - b * row[n][t])
                y = r * (a * row[n][t] - b * row[m][t])
                for q in later:
                    row[q][t] = row[q][t] - (cell[m, q] * x + cell[n, q] * y)
                for g in below:
                    rows[g][t] = rows[g][t] - (col[m][g] * x + col[n][g] * y)
            over = pl.reciprocal(a, approx=True)
            done.append([lax.rsqrt(a) * x for x in row[m]])
            scale = lax.rsqrt(det * over)
            done.append([scale * (x - (b * over) * w) for x, w in zip(row[n], row[m])])
        finished = []
        for t in range(tiles):
            x = done[7][t]
            for q in range(7):
                x = jnp.where(sub == q, done[q][t], x)
            finished.append(x)
        solved.append(finished)
    return solved


def tiled(x):
    return [
        [x[g * 8 : g * 8 + 8, t * 128 : t * 128 + 128] for t in range(x.shape[1] // 128)]
        for g in range(x.shape[0] // 8)
    ]


def joined(tiles):
    return jnp.concatenate([jnp.concatenate(row, axis=1) for row in tiles], axis=0)


def unit_scale(gram):
    lane = lax.broadcasted_iota(jnp.int32, gram.shape, 1)
    sub = lax.broadcasted_iota(jnp.int32, gram.shape, 0)
    kept = jnp.where(lane == sub, gram, 0.0)
    down = 1.0 / jnp.sqrt(jnp.sum(kept, axis=1, keepdims=True))
    across = jnp.sum(kept, axis=0, keepdims=True)
    across = 1.0 / jnp.sqrt(jnp.where(across == 0.0, 1.0, across))
    return gram * down * across, across


def gram_update(panel, first):
    a, b, c = split3(panel)
    left = jnp.concatenate([a, a, b, b, a, c], axis=0)
    right = jnp.concatenate([a, b, a, b, c, a], axis=0)
    parts = {
        at: lax.dot_general(left[:, at : at + 128], right, TRANS_A, preferred_element_type=F32)
        for at in range(first, panel.shape[1], 128)
    }
    return lambda at, count: parts[at // 128 * 128][at % 128 : at % 128 + count]


def inverse_factor(gram, scratch):
    k = gram.shape[0]
    lane = lax.broadcasted_iota(jnp.int32, (k, 128), 1)
    sub = lax.broadcasted_iota(jnp.int32, (k, 128), 0)
    eye = jnp.where(lane == sub, 1.0, 0.0)
    gram, across = unit_scale(jnp.concatenate([gram, jnp.zeros((k, 128 - k), F32)], axis=1))
    solved = eliminate(tiled(jnp.concatenate([gram, eye], axis=1)), 0, scratch)
    return (joined(solved)[:, 128:] * across)[:, :k]


def solve_kernel(gram_ref, image_ref, out_ref, scratch):
    for layer in range(image_ref.shape[0]):
        inverse = inverse_factor(gram_ref[layer], scratch.at[layer])
        solved = jnp.dot(inverse, image_ref[layer], precision=HIGHEST, preferred_element_type=F32)
        out_ref[layer] = solved.astype(BF16)


def solve(gram, image):
    return pl.pallas_call(
        solve_kernel,
        in_specs=vmem_specs(2),
        out_specs=pl.BlockSpec(memory_space=pltpu.VMEM),
        out_shape=jax.ShapeDtypeStruct(image.shape, BF16),
        scratch_shapes=[pltpu.VMEM((image.shape[0], *SPREAD), F32)],
        compiler_params=params(4),
        name="solve_layers",
    )(gram, image)


def cross_kernel(k, images_ref, out_ref, packed):
    g = lax.axis_index("layer")
    every = images_ref[...].reshape(-1, images_ref.shape[2])
    gram = split_dot(every, every, TRANS_B)
    half = gram.shape[0] // 2
    first, last = gram[:half, :half], gram[half:, half:]
    row = lax.broadcasted_iota(jnp.int32, (half, half), 0) // k
    col = lax.broadcasted_iota(jnp.int32, (half, half), 1) // k
    packed[:half] = gram[:half, half:]
    packed[half : 2 * half] = jnp.where(col >= row, first, last)
    diagonal = jnp.where(col == row, last, 0.0)
    packed[2 * half :] = sum(diagonal[r * k : r * k + k] for r in range(half // k))
    rows = out_ref.shape[0]
    out_ref[...] = packed[pl.ds(pl.multiple_of((g & 1) * rows, 16), rows)]


def cross(images):
    layers, k, _ = images.shape
    size = layers * k
    return pl.pallas_call(
        functools.partial(cross_kernel, k),
        in_specs=vmem_specs(1),
        out_specs=pl.BlockSpec(memory_space=pltpu.VMEM),
        out_shape=jax.ShapeDtypeStruct(((size + k) // 2, size // 2), F32),
        scratch_shapes=[pltpu.VMEM((size + k, size // 2), F32)],
        compiler_params=params(6),
        name="cross_gram",
    )(images)


def unpack(packed, k, work):
    half = packed.shape[1]
    row = lax.broadcasted_iota(jnp.int32, (half, half), 0) // k
    col = lax.broadcasted_iota(jnp.int32, (half, half), 1) // k
    mixed = packed[half : 2 * half]
    under = jnp.where(col < row, mixed, 0.0)
    diagonal = jnp.concatenate([packed[2 * half :]] * (half // k), axis=0)
    work[:half, :half] = jnp.where(col >= row, mixed, 0.0)
    work[:half, half:] = packed[:half]
    work[half:, :half] = jnp.zeros((half, half), F32)
    work[half:, half:] = under.T + jnp.where(col == row, diagonal, 0.0)


def joint_kernel(k, *refs):
    own_ref, other_ref, images_ref, out_ref, again_ref, rounded_ref, work, packed, scratch = refs
    rows = own_ref.shape[0]
    odd = lax.axis_index("layer") & 1
    packed[pl.ds(pl.multiple_of(odd * rows, 16), rows)] = own_ref[...]
    packed[pl.ds(pl.multiple_of((1 - odd) * rows, 16), rows)] = other_ref[...]
    unpack(packed[...], k, work)
    size = work.shape[0]
    steps = size // k
    lane = lax.broadcasted_iota(jnp.int32, (k, size), 1)
    lane_128 = lax.broadcasted_iota(jnp.int32, (k, 128), 1)
    sub_128 = lax.broadcasted_iota(jnp.int32, (k, 128), 0)
    gram, across = unit_scale(work[...])
    work[...] = gram
    for s in range(steps):
        lo, hi = s * k, (s + 1) * k
        here = (lane >= lo) & (lane < hi)
        eye = jnp.where(lane_128 == sub_128 + lo % 128, 1.0, 0.0)
        solved = joined(eliminate(tiled(jnp.concatenate([work[lo:hi], eye], axis=1)), lo, scratch.at[s % 2]))
        panel, tail = solved[:, :size], solved[:, size:]
        panel = jnp.where(here, jnp.concatenate([tail] * (size // 128), axis=1), panel)
        work[lo:hi] = jnp.where(lane < hi, panel, 0.0)
        if s + 1 < steps:
            update = gram_update(panel, hi // 128 * 128)
            for r in range(s + 1, steps):
                rows = work[r * k : r * k + k]
                work[r * k : r * k + k] = jnp.where(here, 0.0, rows) - update(r * k, k)
    rows = out_ref.shape[0] * k
    own = work[pl.ds(pl.multiple_of(lax.axis_index("layer") * rows, rows), rows)] * across
    joint = split_dot(own, images_ref[...].reshape(size, -1))
    joint = joint.reshape(out_ref.shape)
    out_ref[...] = joint
    again_ref[...] = joint
    rounded_ref[...] = joint.astype(BF16)


def joint_solve(own, other, images, shape):
    k = shape[1]
    size = images.shape[0] * k
    return pl.pallas_call(
        functools.partial(joint_kernel, k),
        in_specs=vmem_specs(3),
        out_specs=vmem_specs(3),
        out_shape=[
            jax.ShapeDtypeStruct(shape, F32),
            jax.ShapeDtypeStruct(shape, F32),
            jax.ShapeDtypeStruct(shape, BF16),
        ],
        scratch_shapes=[
            pltpu.VMEM((size, size), F32),
            pltpu.VMEM((size + k, size // 2), F32),
            pltpu.VMEM((2, *SPREAD), F32),
        ],
        compiler_params=params(8),
        name="joint_solve",
    )(own, other, images)


def swap(x, axis, d, count):
    return lax.ppermute(x, axis, [(m ^ d, m) for m in range(count)])


ORDER = (0, 3, 2, 1)


def around(x, axis, count):
    return [x] + [swap(x, axis, d, count) for d in ORDER[1:]]


def add_pieces(pieces, flip):
    own, near, far, across = (pieces[ORDER.index(d)] for d in range(4))
    low, high = own + near, across + far
    return high + low if flip else low + high


def per_device(shards, groups, blocks, block_rows, block_cols, counts, start):
    few = shards == 4
    layers = start.shape[0]

    def gather(x):
        return around(x, "node", shards) if few else lax.all_gather(x, "node")

    def total(x, flip=False):
        return add_pieces(around(x, "node", shards), flip) if few else lax.psum(x, "node")

    rounded = start.astype(BF16)
    chunk_total = shards * BROWS // CHUNK_COLS
    if few:
        chunks = (0, 1, 3, 2)
        first = [rounded] + [swap(rounded, "node", d, shards) for d in chunks[1:]]
        dense = build_whole(block_rows, block_cols, counts, blocks, chunk_total)
        images = [apply_first(layer, chunks, first, dense[layer]) for layer in range(layers)]
        image = None
        for layer in range(layers):
            image = apply_second(gather(images[layer]), dense[layer], [] if image is None else [image])
    else:
        dense = build_dense(block_rows, block_cols, counts, blocks, chunk_total)
        image, gram = apply_dense("gram", gather(rounded), dense)
        (image,) = apply_dense("plain", gather(solve(total(gram), image)), dense)
    images = lax.all_gather(image, "layer", axis=0, tiled=True)
    own = cross(images)
    own = total(own)
    other = swap(own, "layer", 1, groups)
    joint_basis, again, rounded = joint_solve(own, other, images, start.shape)
    if few:
        partial = apply_score(gather(rounded), again, dense)
    else:
        (partial,) = apply_dense("score", gather(rounded), dense, again)
    return joint_basis, total(partial, True)


def solution(mesh):
    in_specs = (
        P(("parts", "layer"), "node", None),
        P(("parts", "layer"), "node"),
        P(("parts", "layer"), "node"),
        P(("parts", "layer"), "node"),
        P(("parts", "layer"), None, "node"),
    )
    out_specs = (P(("parts", "layer"), None, "node"), P(("parts", "layer"), None, None))
    return jax.shard_map(
        functools.partial(per_device, mesh.shape["node"], mesh.shape["layer"]),
        mesh=mesh,
        in_specs=in_specs,
        out_specs=out_specs,
        check_vma=False,
    )
```

```python
import functools

import jax
import jax.numpy as jnp
from jax import lax
from jax.experimental import pallas as pl
from jax.experimental.pallas import tpu as pltpu
from jax.sharding import PartitionSpec as P

BLK = 64
ROWS_DEV = 512
BROWS = ROWS_DEV // BLK
CHUNK_COLS = 8
CHUNK_LANES = CHUNK_COLS * 2 * BLK
TALL = BROWS * BLK // 2
MIB = 1024 * 1024
F32 = jnp.float32
BF16 = jnp.bfloat16
HIGHEST = lax.Precision.HIGHEST
TRANS_B = (((1,), (1,)), ((), ()))
TRANS_A = (((0,), (0,)), ((), ()))
SPREAD = (2, 88, 128)


def params(mib):
    return pltpu.CompilerParams(vmem_limit_bytes=mib * MIB)


def vmem_specs(count):
    return [pl.BlockSpec(memory_space=pltpu.VMEM)] * count


def place(z, chunks, u, dense_ref):
    for c in range(chunks * CHUNK_COLS):
        piece = z[c * 8 : c * 8 + 8]
        piece = jnp.concatenate([piece[:, :128], piece[:, 128:]], axis=0)
        hi = piece.astype(BF16)
        lo = (piece - hi.astype(F32)).astype(BF16)
        lanes = slice((c % CHUNK_COLS) * 128, (c % CHUNK_COLS) * 128 + 128)
        dense_ref[c // CHUNK_COLS, pl.ds(pl.multiple_of(u * 16, 16), 16), lanes] = hi
        dense_ref[c // CHUNK_COLS, pl.ds(pl.multiple_of(u * 16 + TALL, 16), 16), lanes] = lo


def one_hot(rows_ref, cols_ref, counts_ref, layer, flip, base, positions):
    slot = lax.broadcasted_iota(jnp.int32, (1, rows_ref.shape[1]), 1)
    key = (cols_ref[pl.ds(layer, 1), :] ^ flip) * BROWS + rows_ref[pl.ds(layer, 1), :]
    key = jnp.where(slot < counts_ref[0, layer], key, -1)
    position = lax.broadcasted_iota(jnp.int32, (positions, key.shape[1]), 0) + base
    return jnp.where(position == key, 1.0, 0.0).astype(BF16)


def build_kernel(rows_ref, cols_ref, counts_ref, blocks_ref, dense_ref):
    chunks = dense_ref.shape[1]
    positions = chunks * CHUNK_COLS * BROWS
    base = pl.program_id(1) * positions
    onehot = one_hot(rows_ref, cols_ref, counts_ref, pl.program_id(0), 0, base, positions)

    def step(u, carry):
        cols = pl.ds(pl.multiple_of(u * 256, 256), 256)
        z = jnp.dot(onehot, blocks_ref[0, :, cols], preferred_element_type=F32)
        place(z, chunks, u, dense_ref.at[0])
        return carry

    lax.fori_loop(0, BLK * BLK // 256, step, 0)


def fill(onehot, held, dense_ref, piece, width):
    for v in range(width // 256):
        cols = pl.ds(pl.multiple_of(piece * width + v * 256, 256), 256)
        z = jnp.dot(onehot, held[:, cols], preferred_element_type=F32)
        place(z, dense_ref.shape[0], piece * (width // 256) + v, dense_ref)


def build_whole_kernel(rows_hbm, cols_hbm, counts_hbm, blocks_ref, *refs):
    *dense_refs, held, rows_ref, cols_ref, counts_ref, arrived, index_arrived = refs
    layers, pieces = arrived.shape
    width = held.shape[2] // pieces
    ahead = 3

    def fetch(layer, piece):
        cols = pl.ds(pl.multiple_of(piece * width, width), width)
        return pltpu.make_async_copy(
            blocks_ref.at[layer, :, cols], held.at[layer, :, cols], arrived.at[layer, piece]
        )

    index_copies = [
        pltpu.make_async_copy(source, target, index_arrived.at[i])
        for i, (source, target) in enumerate(
            [(rows_hbm, rows_ref), (cols_hbm, cols_ref), (counts_hbm, counts_ref)]
        )
    ]
    for copy in index_copies:
        copy.start()
    for piece in range(ahead):
        fetch(0, piece).start()
    for copy in index_copies:
        copy.wait()
    flip = lax.axis_index("node") * CHUNK_COLS
    for layer, dense_ref in enumerate(dense_refs):
        onehot = one_hot(rows_ref, cols_ref, counts_ref, layer, flip, 0, dense_ref.shape[0] * CHUNK_COLS * BROWS)

        def step(piece, carry):
            fetch(layer, piece).wait()

            @pl.when(piece + ahead < pieces)
            def _():
                fetch(layer, piece + ahead).start()

            if layer + 1 < layers:

                @pl.when(piece + ahead >= pieces)
                def _():
                    fetch(layer + 1, piece + ahead - pieces).start()

            fill(onehot, held.at[layer], dense_ref, piece, width)
            return carry

        lax.fori_loop(0, pieces, step, 0)


def build_whole(block_rows, block_cols, counts, blocks, chunk_total):
    layers = blocks.shape[0]
    dense = jax.ShapeDtypeStruct((chunk_total, 2 * TALL, CHUNK_LANES), BF16)
    operands = (block_rows, block_cols, counts.T, blocks)
    return pl.pallas_call(
        build_whole_kernel,
        in_specs=[pl.BlockSpec(memory_space=pltpu.HBM)] * 4,
        out_specs=vmem_specs(layers),
        out_shape=[dense] * layers,
        scratch_shapes=[
            pltpu.VMEM(blocks.shape, BF16),
            pltpu.VMEM(block_rows.shape, jnp.int32),
            pltpu.VMEM(block_cols.shape, jnp.int32),
            pltpu.SMEM((1, layers), jnp.int32),
            pltpu.SemaphoreType.DMA((layers, 4)),
            pltpu.SemaphoreType.DMA((3,)),
        ],
        compiler_params=params(28),
        cost_estimate=pl.CostEstimate(flops=0, bytes_accessed=20 * MIB, transcendentals=0),
        name="build_whole",
    )(*[pltpu.with_memory_space_constraint(x, pltpu.HBM) for x in operands])


def build_dense(block_rows, block_cols, counts, blocks, chunk_total):
    layers, slots, width = blocks.shape
    dense = jax.ShapeDtypeStruct((layers, chunk_total, 2 * TALL, CHUNK_LANES), BF16)
    operands = (block_rows, block_cols, counts.T, blocks)
    return pl.pallas_call(
        build_kernel,
        grid=(layers, chunk_total // 4),
        in_specs=vmem_specs(2)
        + [
            pl.BlockSpec(memory_space=pltpu.SMEM),
            pl.BlockSpec((1, slots, width), lambda l, s: (l, 0, 0)),
        ],
        out_specs=pl.BlockSpec((1, 4, 2 * TALL, CHUNK_LANES), lambda l, s: (l, s, 0, 0)),
        out_shape=dense,
        compiler_params=params(24),
        name="build_dense",
    )(*operands)


def split3(x):
    a = x.astype(BF16)
    r = x - a.astype(F32)
    b = r.astype(BF16)
    c = (r - b.astype(F32)).astype(BF16)
    return a, b, c


def image_part(basis, dense):
    k, width = basis.shape
    basis = basis.astype(F32)
    tall = jnp.concatenate([basis, basis], axis=0).T
    lane = lax.broadcasted_iota(jnp.int32, tall.shape, 1)
    first = jnp.where(lane < k, tall, 0.0).astype(BF16)
    second = jnp.where(lane < k, 0.0, tall).astype(BF16)
    weights = []
    for c in range(width // BLK):
        weights += [first[c * BLK : c * BLK + BLK], second[c * BLK : c * BLK + BLK]]
    return jnp.dot(dense, jnp.concatenate(weights, axis=0), preferred_element_type=F32)


def to_wide(total, k, halves, tall):
    halves[:, : 2 * k] = total[:TALL] + total[TALL:]
    halves[:, 2 * k :] = jnp.zeros((TALL, 128 - 2 * k), F32)
    for b in range(BROWS):
        part = halves[pl.ds(b, BLK // 2, stride=BROWS), :]
        tall[pl.ds(BLK * b, BLK // 2, stride=2), :] = part
        tall[pl.ds(BLK * b + 1, BLK // 2, stride=2), :] = pltpu.roll(part, 128 - k, 1)
    return tall[...].T[:k]


def against(left, tall):
    k = left.shape[0]
    lane = lax.broadcasted_iota(jnp.int32, tall.shape, 1)
    a, b, c = split3(jnp.where(lane < k, tall, 0.0))
    right = a.astype(F32) + pltpu.roll(b.astype(F32), k, 1) + pltpu.roll(c.astype(F32), 2 * k, 1)
    pieces = jnp.dot(jnp.concatenate(split3(left), axis=0), right.astype(BF16), preferred_element_type=F32)
    top, middle, bottom = pieces[:k], pieces[k : 2 * k], pieces[2 * k :]
    total = top[:, :k] + (top[:, k : 2 * k] + middle[:, :k])
    return total + (middle[:, k : 2 * k] + (top[:, 2 * k : 3 * k] + bottom[:, :k]))


def apply_kernel(mode, *refs):
    basis_ref, refs = refs[0], refs[1:]
    if mode == "score":
        left_ref, refs = refs[0], refs[1:]
    dense_ref, out_ref = refs[:2]
    halves, tall, acc = refs[-3:]
    layer, chunk = pl.program_id(0), pl.program_id(1)
    total = image_part(basis_ref[chunk, layer], dense_ref[0, 0])

    @pl.when(chunk == 0)
    def _():
        acc[...] = total

    @pl.when(chunk > 0)
    def _():
        acc[...] += total

    @pl.when(chunk == pl.num_programs(1) - 1)
    def _():
        image = to_wide(acc[...], basis_ref.shape[2], halves, tall)
        if mode != "score":
            out_ref[0] = image
        if mode == "gram":
            refs[2][0] = against(image, tall[...])
        if mode == "score":
            out_ref[0] = against(left_ref[0], tall[...])


def split_dot(left, right, dims=(((1,), (0,)), ((), ()))):
    m = left.shape[0]
    a, b, c = split3(left)
    p, q, r = split3(right)

    def dot(rows, piece):
        return lax.dot_general(jnp.concatenate(rows, axis=0), piece, dims, preferred_element_type=F32)

    x, y, z = dot([a, b, c], p), dot([a, b], q), dot([a], r)
    return x[:m] + ((x[m : 2 * m] + y[:m]) + (y[m : 2 * m] + (x[2 * m :] + z)))


def product(a, b):
    k = a.shape[0]
    left = jnp.concatenate(split3(a), axis=0)
    right = left if b is a else jnp.concatenate(split3(b), axis=0)
    pieces = lax.dot_general(left, right, TRANS_B, preferred_element_type=F32)
    top, middle, bottom = pieces[:k], pieces[k : 2 * k], pieces[2 * k :]
    total = top[:, :k] + (top[:, k : 2 * k] + middle[:, :k])
    return total + (middle[:, k : 2 * k] + (top[:, 2 * k : 3 * k] + bottom[:, :k]))


def first_kernel(layer, chunks, *refs):
    pieces, (dense_ref, out_ref, halves, tall) = refs[: len(chunks)], refs[len(chunks) :]
    total = sum(image_part(piece[layer], dense_ref[chunk]) for chunk, piece in zip(chunks, pieces))
    out_ref[...] = to_wide(total, out_ref.shape[0], halves, tall)


def second_kernel(piece_count, earlier_count, *refs):
    pieces, dense_ref, refs = refs[:piece_count], refs[piece_count], refs[piece_count + 1 :]
    earlier, (out_ref, halves, tall, scratch) = refs[:earlier_count], refs[earlier_count:]
    image = jnp.concatenate([piece[...] for piece in pieces], axis=1)
    inverse = inverse_factor(product(image, image), scratch)
    basis = jnp.dot(inverse, image, precision=HIGHEST, preferred_element_type=F32)
    parts = [basis[:, d * ROWS_DEV : d * ROWS_DEV + ROWS_DEV] for d in range(piece_count)]
    before = out_ref.shape[0] - 1
    for ref in earlier:
        out_ref[:before] = ref[...]
    out_ref[before] = to_wide(sum(image_part(part, dense_ref[chunk]) for chunk, part in zip(ORDER, parts)), out_ref.shape[1], halves, tall)


def turn(left, tall, halves):
    k, nodes = left.shape
    tall[...] = jnp.concatenate([left, jnp.zeros((128 - k, nodes), F32)], axis=0).T
    for b in range(BROWS):
        even = tall[pl.ds(BLK * b, BLK // 2, stride=2), :]
        odd = tall[pl.ds(BLK * b + 1, BLK // 2, stride=2), :]
        halves[pl.ds(b, BLK // 2, stride=BROWS), :] = even + pltpu.roll(odd, k, 1)
    return halves[...].T[: 2 * k]


def own_kernel(layers, basis_ref, left_ref, *refs):
    dense_refs, (out_ref, turned_ref, tall, halves) = refs[:layers], refs[layers:]
    for layer, dense_ref in enumerate(dense_refs):
        out_ref[layer] = image_part(basis_ref[layer], dense_ref[0])
    for layer in range(layers):
        turned_ref[layer] = turn(left_ref[layer], tall.at[layer], halves.at[layer])


def some_kernel(chunk, layers, basis_ref, *refs):
    dense_refs, (so_far_ref, out_ref) = refs[:layers], refs[layers:]
    for layer, dense_ref in enumerate(dense_refs):
        out_ref[layer] = so_far_ref[layer] + image_part(basis_ref[layer], dense_ref[chunk])


def score_kernel(layers, chunks, so_far_ref, *refs):
    pieces, turned_ref, refs = refs[: len(chunks)], refs[len(chunks)], refs[len(chunks) + 1 :]
    dense_refs, out_ref = refs[:layers], refs[layers]
    k = out_ref.shape[1]
    totals = [
        so_far_ref[layer]
        + sum(image_part(piece[layer], dense_refs[layer][chunk]) for chunk, piece in zip(chunks, pieces))
        for layer in range(layers)
    ]
    halves = [total[:TALL] + total[TALL:] for total in totals]
    for layer in range(layers):
        pairs = split_dot(turned_ref[layer], halves[layer])
        out_ref[layer] = pairs[:k, :k] + pairs[k : 2 * k, k : 2 * k]


def apply_whole(kernel, name, operands, out_shape, *lead, scratch=()):
    return pl.pallas_call(
        kernel,
        in_specs=vmem_specs(len(operands)),
        out_specs=pl.BlockSpec(memory_space=pltpu.VMEM),
        out_shape=jax.ShapeDtypeStruct(out_shape, F32),
        scratch_shapes=[pltpu.VMEM((*lead, TALL, 128), F32), pltpu.VMEM((*lead, ROWS_DEV, 128), F32), *scratch],
        compiler_params=params(14),
        cost_estimate=pl.CostEstimate(flops=0, bytes_accessed=4 * MIB, transcendentals=0),
        name=name,
    )(*operands)


def apply_first(layer, chunks, pieces, dense):
    kernel = functools.partial(first_kernel, layer, chunks)
    return apply_whole(kernel, "apply_first", [*pieces, dense], pieces[0].shape[1:])


def apply_second(pieces, dense, earlier):
    kernel = functools.partial(second_kernel, len(pieces), len(earlier))
    before = sum(array.shape[0] for array in earlier)
    shape = (before + 1, *pieces[0].shape)
    operands = [*pieces, dense, *earlier]
    return apply_whole(kernel, "apply_second", operands, shape, scratch=[pltpu.VMEM(SPREAD, F32)])


def part_cost():
    return pl.CostEstimate(flops=0, bytes_accessed=2 * MIB, transcendentals=0)


def apply_own(basis, left, dense):
    layers, k, _ = basis.shape
    return pl.pallas_call(
        functools.partial(own_kernel, layers),
        in_specs=vmem_specs(2 + layers),
        out_specs=vmem_specs(2),
        out_shape=[
            jax.ShapeDtypeStruct((layers, 2 * TALL, 2 * k), F32),
            jax.ShapeDtypeStruct((layers, 2 * k, TALL), F32),
        ],
        scratch_shapes=[pltpu.VMEM((layers, ROWS_DEV, 128), F32), pltpu.VMEM((layers, TALL, 128), F32)],
        compiler_params=params(14),
        cost_estimate=part_cost(),
        name="apply_own",
    )(basis, left, *dense)


def apply_some(chunk, basis, dense, so_far):
    return pl.pallas_call(
        functools.partial(some_kernel, chunk, len(dense)),
        in_specs=vmem_specs(2 + len(dense)),
        out_specs=pl.BlockSpec(memory_space=pltpu.VMEM),
        out_shape=jax.ShapeDtypeStruct(so_far.shape, F32),
        compiler_params=params(14),
        cost_estimate=part_cost(),
        name=f"apply_some_{chunk}",
    )(basis, *dense, so_far)


def apply_score(pieces, left, dense):
    layers, k, _ = left.shape
    so_far, turned = apply_own(pieces[0], left, dense)
    so_far = apply_some(ORDER[1], pieces[1], dense, so_far)
    operands = [so_far, *pieces[2:], turned, *dense]
    return pl.pallas_call(
        functools.partial(score_kernel, len(dense), ORDER[2:]),
        in_specs=vmem_specs(len(operands)),
        out_specs=pl.BlockSpec(memory_space=pltpu.VMEM),
        out_shape=jax.ShapeDtypeStruct((layers, k, k), F32),
        compiler_params=params(14),
        cost_estimate=part_cost(),
        name="apply_score",
    )(*operands)


def apply_dense(mode, basis, dense, left=None):
    layers, chunks = dense.shape[:2]
    k = basis.shape[-2]
    image = jax.ShapeDtypeStruct((layers, k, ROWS_DEV), F32)
    small = jax.ShapeDtypeStruct((layers, k, k), F32)
    out_shape = {"gram": [image, small], "plain": [image], "score": [small]}[mode]
    operands = [basis] + ([left] if mode == "score" else []) + [dense]
    dense_spec = pl.BlockSpec((1, 1, 2 * TALL, CHUNK_LANES), lambda l, s: (l, s, 0, 0))
    image_spec = pl.BlockSpec((1, k, ROWS_DEV), lambda l, s: (l, 0, 0))
    small_spec = pl.BlockSpec((1, k, k), lambda l, s: (l, 0, 0))
    return pl.pallas_call(
        functools.partial(apply_kernel, mode),
        grid=(layers, chunks),
        in_specs=vmem_specs(1) + ([image_spec] if mode == "score" else []) + [dense_spec],
        out_specs={"gram": [image_spec, small_spec], "plain": [image_spec], "score": [small_spec]}[mode],
        out_shape=out_shape,
        scratch_shapes=[
            pltpu.VMEM((TALL, 128), F32),
            pltpu.VMEM((ROWS_DEV, 128), F32),
            pltpu.VMEM((2 * TALL, 2 * k), F32),
        ],
        compiler_params=params(12),
        name="apply_" + mode,
    )(*operands)


def spread(x):
    return jnp.broadcast_to(x, (8, 128))


def eliminate(rows, offset, scratch):
    groups, tiles = len(rows), len(rows[0])
    rows = [list(row) for row in rows]
    home, at = offset // 128, offset % 128
    sub = lax.broadcasted_iota(jnp.int32, (8, 128), 0)
    solved = []
    for h in range(groups):
        below = range(h + 1, groups)
        lane = at + 8 * h
        col = [{g: spread(rows[g][home][:, lane + q : lane + q + 1]) for g in range(h, groups)} for q in range(8)]
        held = scratch.at[h % 2]
        for q in range(8):
            held[q * 8 : q * 8 + 8] = col[q][h]
        for t in range(tiles):
            held[64 + t * 8 : 72 + t * 8] = rows[h][t]
        cell = {(p, q): spread(held[p * 8 + q : p * 8 + q + 1]) for q in range(8) for p in range(q + 1)}
        row = [[spread(held[64 + t * 8 + q : 65 + t * 8 + q]) for t in range(tiles)] for q in range(8)]
        done = []
        for m in range(0, 8, 2):
            n = m + 1
            a, b, c = cell[m, m], cell[m, n], cell[n, n]
            det = a * c - b * b
            if m % 4 == 0:
                r = pl.reciprocal(det, approx=True)
            else:
                r = square * pl.reciprocal(whole, approx=True)
            later = range(m + 2, 8)
            u = {q: c * cell[m, q] - b * cell[n, q] for q in later}
            v = {q: a * cell[n, q] - b * cell[m, q] for q in later}
            taken = {(p, q): cell[m, p] * u[q] + cell[n, p] * v[q] for q in later for p in range(m + 2, q + 1)}
            if m % 4 == 0:
                i, j = m + 2, m + 3
                first, cross, last = (det * cell[pq] - taken[pq] for pq in ((i, i), (i, j), (j, j)))
                whole = first * last - cross * cross
                square = det * det
            for pq in taken:
                cell[pq] = cell[pq] - r * taken[pq]
            for q in later:
                for g in below:
                    col[q][g] = col[q][g] - r * (col[m][g] * u[q] + col[n][g] * v[q])
            for t in range(tiles):
                x = r * (c * row[m][t] - b * row[n][t])
                y = r * (a * row[n][t] - b * row[m][t])
                for q in later:
                    row[q][t] = row[q][t] - (cell[m, q] * x + cell[n, q] * y)
                for g in below:
                    rows[g][t] = rows[g][t] - (col[m][g] * x + col[n][g] * y)
            over = pl.reciprocal(a, approx=True)
            done.append([lax.rsqrt(a) * x for x in row[m]])
            scale = lax.rsqrt(det * over)
            done.append([scale * (x - (b * over) * w) for x, w in zip(row[n], row[m])])
        finished = []
        for t in range(tiles):
            x = done[7][t]
            for q in range(7):
                x = jnp.where(sub == q, done[q][t], x)
            finished.append(x)
        solved.append(finished)
    return solved


def tiled(x):
    return [
        [x[g * 8 : g * 8 + 8, t * 128 : t * 128 + 128] for t in range(x.shape[1] // 128)]
        for g in range(x.shape[0] // 8)
    ]


def joined(tiles):
    return jnp.concatenate([jnp.concatenate(row, axis=1) for row in tiles], axis=0)


def unit_scale(gram):
    lane = lax.broadcasted_iota(jnp.int32, gram.shape, 1)
    sub = lax.broadcasted_iota(jnp.int32, gram.shape, 0)
    kept = jnp.where(lane == sub, gram, 0.0)
    down = 1.0 / jnp.sqrt(jnp.sum(kept, axis=1, keepdims=True))
    across = jnp.sum(kept, axis=0, keepdims=True)
    across = 1.0 / jnp.sqrt(jnp.where(across == 0.0, 1.0, across))
    return gram * down * across, across


def gram_update(panel, first):
    a, b, c = split3(panel)
    left = jnp.concatenate([a, a, b, b, a, c], axis=0)
    right = jnp.concatenate([a, b, a, b, c, a], axis=0)
    parts = {
        at: lax.dot_general(left[:, at : at + 128], right, TRANS_A, preferred_element_type=F32)
        for at in range(first, panel.shape[1], 128)
    }
    return lambda at, count: parts[at // 128 * 128][at % 128 : at % 128 + count]


def inverse_factor(gram, scratch):
    k = gram.shape[0]
    lane = lax.broadcasted_iota(jnp.int32, (k, 128), 1)
    sub = lax.broadcasted_iota(jnp.int32, (k, 128), 0)
    eye = jnp.where(lane == sub, 1.0, 0.0)
    gram, across = unit_scale(jnp.concatenate([gram, jnp.zeros((k, 128 - k), F32)], axis=1))
    solved = eliminate(tiled(jnp.concatenate([gram, eye], axis=1)), 0, scratch)
    return (joined(solved)[:, 128:] * across)[:, :k]


def solve_kernel(gram_ref, image_ref, out_ref, scratch):
    for layer in range(image_ref.shape[0]):
        inverse = inverse_factor(gram_ref[layer], scratch.at[layer])
        solved = jnp.dot(inverse, image_ref[layer], precision=HIGHEST, preferred_element_type=F32)
        out_ref[layer] = solved.astype(BF16)


def solve(gram, image):
    return pl.pallas_call(
        solve_kernel,
        in_specs=vmem_specs(2),
        out_specs=pl.BlockSpec(memory_space=pltpu.VMEM),
        out_shape=jax.ShapeDtypeStruct(image.shape, BF16),
        scratch_shapes=[pltpu.VMEM((image.shape[0], *SPREAD), F32)],
        compiler_params=params(4),
        name="solve_layers",
    )(gram, image)


def cross_kernel(k, images_ref, out_ref, packed):
    g = lax.axis_index("layer")
    every = images_ref[...].reshape(-1, images_ref.shape[2])
    gram = split_dot(every, every, TRANS_B)
    half = gram.shape[0] // 2
    first, last = gram[:half, :half], gram[half:, half:]
    row = lax.broadcasted_iota(jnp.int32, (half, half), 0) // k
    col = lax.broadcasted_iota(jnp.int32, (half, half), 1) // k
    packed[:half] = gram[:half, half:]
    packed[half : 2 * half] = jnp.where(col >= row, first, last)
    diagonal = jnp.where(col == row, last, 0.0)
    packed[2 * half :] = sum(diagonal[r * k : r * k + k] for r in range(half // k))
    rows = out_ref.shape[0]
    out_ref[...] = packed[pl.ds(pl.multiple_of((g & 1) * rows, 16), rows)]


def cross(images):
    layers, k, _ = images.shape
    size = layers * k
    return pl.pallas_call(
        functools.partial(cross_kernel, k),
        in_specs=vmem_specs(1),
        out_specs=pl.BlockSpec(memory_space=pltpu.VMEM),
        out_shape=jax.ShapeDtypeStruct(((size + k) // 2, size // 2), F32),
        scratch_shapes=[pltpu.VMEM((size + k, size // 2), F32)],
        compiler_params=params(6),
        name="cross_gram",
    )(images)


def unpack(packed, k, work):
    half = packed.shape[1]
    row = lax.broadcasted_iota(jnp.int32, (half, half), 0) // k
    col = lax.broadcasted_iota(jnp.int32, (half, half), 1) // k
    mixed = packed[half : 2 * half]
    under = jnp.where(col < row, mixed, 0.0)
    diagonal = jnp.concatenate([packed[2 * half :]] * (half // k), axis=0)
    work[:half, :half] = jnp.where(col >= row, mixed, 0.0)
    work[:half, half:] = packed[:half]
    work[half:, :half] = jnp.zeros((half, half), F32)
    work[half:, half:] = under.T + jnp.where(col == row, diagonal, 0.0)


def joint_kernel(k, *refs):
    own_ref, other_ref, images_ref, out_ref, again_ref, rounded_ref, work, packed, scratch = refs
    rows = own_ref.shape[0]
    odd = lax.axis_index("layer") & 1
    packed[pl.ds(pl.multiple_of(odd * rows, 16), rows)] = own_ref[...]
    packed[pl.ds(pl.multiple_of((1 - odd) * rows, 16), rows)] = other_ref[...]
    unpack(packed[...], k, work)
    size = work.shape[0]
    steps = size // k
    lane = lax.broadcasted_iota(jnp.int32, (k, size), 1)
    lane_128 = lax.broadcasted_iota(jnp.int32, (k, 128), 1)
    sub_128 = lax.broadcasted_iota(jnp.int32, (k, 128), 0)
    gram, across = unit_scale(work[...])
    work[...] = gram
    for s in range(steps):
        lo, hi = s * k, (s + 1) * k
        here = (lane >= lo) & (lane < hi)
        eye = jnp.where(lane_128 == sub_128 + lo % 128, 1.0, 0.0)
        solved = joined(eliminate(tiled(jnp.concatenate([work[lo:hi], eye], axis=1)), lo, scratch.at[s % 2]))
        panel, tail = solved[:, :size], solved[:, size:]
        panel = jnp.where(here, jnp.concatenate([tail] * (size // 128), axis=1), panel)
        work[lo:hi] = jnp.where(lane < hi, panel, 0.0)
        if s + 1 < steps:
            update = gram_update(panel, hi // 128 * 128)
            for r in range(s + 1, steps):
                rows = work[r * k : r * k + k]
                work[r * k : r * k + k] = jnp.where(here, 0.0, rows) - update(r * k, k)
    rows = out_ref.shape[0] * k
    own = work[pl.ds(pl.multiple_of(lax.axis_index("layer") * rows, rows), rows)] * across
    joint = split_dot(own, images_ref[...].reshape(size, -1))
    joint = joint.reshape(out_ref.shape)
    out_ref[...] = joint
    again_ref[...] = joint
    rounded_ref[...] = joint.astype(BF16)


def joint_solve(own, other, images, shape):
    k = shape[1]
    size = images.shape[0] * k
    return pl.pallas_call(
        functools.partial(joint_kernel, k),
        in_specs=vmem_specs(3),
        out_specs=vmem_specs(3),
        out_shape=[
            jax.ShapeDtypeStruct(shape, F32),
            jax.ShapeDtypeStruct(shape, F32),
            jax.ShapeDtypeStruct(shape, BF16),
        ],
        scratch_shapes=[
            pltpu.VMEM((size, size), F32),
            pltpu.VMEM((size + k, size // 2), F32),
            pltpu.VMEM((2, *SPREAD), F32),
        ],
        compiler_params=params(8),
        name="joint_solve",
    )(own, other, images)


def swap(x, axis, d, count):
    return lax.ppermute(x, axis, [(m ^ d, m) for m in range(count)])


ORDER = (0, 3, 2, 1)


def around(x, axis, count):
    return [x] + [swap(x, axis, d, count) for d in ORDER[1:]]


def add_pieces(pieces):
    own, near, far, across = (pieces[ORDER.index(d)] for d in range(4))
    return (own + near) + (across + far)


def per_device(shards, groups, blocks, block_rows, block_cols, counts, start):
    few = shards == 4
    layers = start.shape[0]

    def gather(x):
        return around(x, "node", shards) if few else lax.all_gather(x, "node")

    def total(x):
        return add_pieces(around(x, "node", shards)) if few else lax.psum(x, "node")

    rounded = start.astype(BF16)
    chunk_total = shards * BROWS // CHUNK_COLS
    if few:
        chunks = (0, 1, 3, 2)
        first = [rounded] + [swap(rounded, "node", d, shards) for d in chunks[1:]]
        dense = build_whole(block_rows, block_cols, counts, blocks, chunk_total)
        images = [apply_first(layer, chunks, first, dense[layer]) for layer in range(layers)]
        image = None
        for layer in range(layers):
            image = apply_second(gather(images[layer]), dense[layer], [] if image is None else [image])
    else:
        dense = build_dense(block_rows, block_cols, counts, blocks, chunk_total)
        image, gram = apply_dense("gram", gather(rounded), dense)
        (image,) = apply_dense("plain", gather(solve(total(gram), image)), dense)
    images = lax.all_gather(image, "layer", axis=0, tiled=True)
    own = cross(images)
    own = total(own)
    other = swap(own, "layer", 1, groups)
    joint_basis, again, rounded = joint_solve(own, other, images, start.shape)
    if few:
        partial = apply_score(gather(rounded), again, dense)
    else:
        (partial,) = apply_dense("score", gather(rounded), dense, again)
    return joint_basis, total(partial)


def solution(mesh):
    in_specs = (
        P(("parts", "layer"), "node", None),
        P(("parts", "layer"), "node"),
        P(("parts", "layer"), "node"),
        P(("parts", "layer"), "node"),
        P(("parts", "layer"), None, "node"),
    )
    out_specs = (P(("parts", "layer"), None, "node"), P(("parts", "layer"), None, None))
    return jax.shard_map(
        functools.partial(per_device, mesh.shape["node"], mesh.shape["layer"]),
        mesh=mesh,
        in_specs=in_specs,
        out_specs=out_specs,
        check_vma=False,
    )
```

```python
import functools

import jax
import jax.numpy as jnp
from jax import lax
from jax.experimental import pallas as pl
from jax.experimental.pallas import tpu as pltpu
from jax.sharding import PartitionSpec as P

BLK = 64
ROWS_DEV = 512
BROWS = ROWS_DEV // BLK
CHUNK_COLS = 8
CHUNK_LANES = CHUNK_COLS * 2 * BLK
TALL = BROWS * BLK // 2
MIB = 1024 * 1024
F32 = jnp.float32
BF16 = jnp.bfloat16
HIGHEST = lax.Precision.HIGHEST
TRANS_B = (((1,), (1,)), ((), ()))
TRANS_A = (((0,), (0,)), ((), ()))
SPREAD = (2, 88, 128)
TAIL = 16


def params(mib):
    return pltpu.CompilerParams(vmem_limit_bytes=mib * MIB)


def vmem_specs(count):
    return [pl.BlockSpec(memory_space=pltpu.VMEM)] * count


def place(z, chunks, u, dense_ref):
    for c in range(chunks * CHUNK_COLS):
        piece = z[c * 8 : c * 8 + 8]
        piece = jnp.concatenate([piece[:, :128], piece[:, 128:]], axis=0)
        hi = piece.astype(BF16)
        lo = (piece - hi.astype(F32)).astype(BF16)
        lanes = slice((c % CHUNK_COLS) * 128, (c % CHUNK_COLS) * 128 + 128)
        dense_ref[c // CHUNK_COLS, pl.ds(pl.multiple_of(u * 16, 16), 16), lanes] = hi
        dense_ref[c // CHUNK_COLS, pl.ds(pl.multiple_of(u * 16 + TALL, 16), 16), lanes] = lo


def one_hot(rows_ref, cols_ref, counts_ref, layer, flip, base, positions):
    slot = lax.broadcasted_iota(jnp.int32, (1, rows_ref.shape[1]), 1)
    key = (cols_ref[pl.ds(layer, 1), :] ^ flip) * BROWS + rows_ref[pl.ds(layer, 1), :]
    key = jnp.where(slot < counts_ref[0, layer], key, -1)
    position = lax.broadcasted_iota(jnp.int32, (positions, key.shape[1]), 0) + base
    return jnp.where(position == key, 1.0, 0.0).astype(BF16)


def build_kernel(rows_ref, cols_ref, counts_ref, blocks_ref, dense_ref):
    chunks = dense_ref.shape[1]
    positions = chunks * CHUNK_COLS * BROWS
    base = pl.program_id(1) * positions
    onehot = one_hot(rows_ref, cols_ref, counts_ref, pl.program_id(0), 0, base, positions)

    def step(u, carry):
        cols = pl.ds(pl.multiple_of(u * 256, 256), 256)
        z = jnp.dot(onehot, blocks_ref[0, :, cols], preferred_element_type=F32)
        place(z, chunks, u, dense_ref.at[0])
        return carry

    lax.fori_loop(0, BLK * BLK // 256, step, 0)


def fill(onehot, held, dense_ref, piece, width):
    for v in range(width // 256):
        cols = pl.ds(pl.multiple_of(piece * width + v * 256, 256), 256)
        z = jnp.dot(onehot, held[:, cols], preferred_element_type=F32)
        place(z, dense_ref.shape[0], piece * (width // 256) + v, dense_ref)


def build_whole_kernel(rows_hbm, cols_hbm, counts_hbm, blocks_ref, *refs):
    *dense_refs, held, rows_ref, cols_ref, counts_ref, arrived, index_arrived = refs
    layers, pieces = arrived.shape
    width = held.shape[2] // pieces
    ahead = 3

    def fetch(layer, piece):
        cols = pl.ds(pl.multiple_of(piece * width, width), width)
        return pltpu.make_async_copy(
            blocks_ref.at[layer, :, cols], held.at[layer, :, cols], arrived.at[layer, piece]
        )

    index_copies = [
        pltpu.make_async_copy(source, target, index_arrived.at[i])
        for i, (source, target) in enumerate(
            [(rows_hbm, rows_ref), (cols_hbm, cols_ref), (counts_hbm, counts_ref)]
        )
    ]
    for copy in index_copies:
        copy.start()
    for piece in range(ahead):
        fetch(0, piece).start()
    for copy in index_copies:
        copy.wait()
    flip = lax.axis_index("node") * CHUNK_COLS
    for layer, dense_ref in enumerate(dense_refs):
        onehot = one_hot(rows_ref, cols_ref, counts_ref, layer, flip, 0, dense_ref.shape[0] * CHUNK_COLS * BROWS)

        def step(piece, carry):
            fetch(layer, piece).wait()

            @pl.when(piece + ahead < pieces)
            def _():
                fetch(layer, piece + ahead).start()

            if layer + 1 < layers:

                @pl.when(piece + ahead >= pieces)
                def _():
                    fetch(layer + 1, piece + ahead - pieces).start()

            fill(onehot, held.at[layer], dense_ref, piece, width)
            return carry

        lax.fori_loop(0, pieces, step, 0)


def build_whole(block_rows, block_cols, counts, blocks, chunk_total):
    layers = blocks.shape[0]
    dense = jax.ShapeDtypeStruct((chunk_total, 2 * TALL, CHUNK_LANES), BF16)
    operands = (block_rows, block_cols, counts.T, blocks)
    return pl.pallas_call(
        build_whole_kernel,
        in_specs=[pl.BlockSpec(memory_space=pltpu.HBM)] * 4,
        out_specs=vmem_specs(layers),
        out_shape=[dense] * layers,
        scratch_shapes=[
            pltpu.VMEM(blocks.shape, BF16),
            pltpu.VMEM(block_rows.shape, jnp.int32),
            pltpu.VMEM(block_cols.shape, jnp.int32),
            pltpu.SMEM((1, layers), jnp.int32),
            pltpu.SemaphoreType.DMA((layers, 4)),
            pltpu.SemaphoreType.DMA((3,)),
        ],
        compiler_params=params(28),
        cost_estimate=pl.CostEstimate(flops=0, bytes_accessed=20 * MIB, transcendentals=0),
        name="build_whole",
    )(*[pltpu.with_memory_space_constraint(x, pltpu.HBM) for x in operands])


def build_dense(block_rows, block_cols, counts, blocks, chunk_total):
    layers, slots, width = blocks.shape
    dense = jax.ShapeDtypeStruct((layers, chunk_total, 2 * TALL, CHUNK_LANES), BF16)
    operands = (block_rows, block_cols, counts.T, blocks)
    return pl.pallas_call(
        build_kernel,
        grid=(layers, chunk_total // 4),
        in_specs=vmem_specs(2)
        + [
            pl.BlockSpec(memory_space=pltpu.SMEM),
            pl.BlockSpec((1, slots, width), lambda l, s: (l, 0, 0)),
        ],
        out_specs=pl.BlockSpec((1, 4, 2 * TALL, CHUNK_LANES), lambda l, s: (l, s, 0, 0)),
        out_shape=dense,
        compiler_params=params(24),
        name="build_dense",
    )(*operands)


def split3(x):
    a = x.astype(BF16)
    r = x - a.astype(F32)
    b = r.astype(BF16)
    c = (r - b.astype(F32)).astype(BF16)
    return a, b, c


def image_part(basis, dense):
    k, width = basis.shape
    basis = basis.astype(F32)
    tall = jnp.concatenate([basis, basis], axis=0).T
    lane = lax.broadcasted_iota(jnp.int32, tall.shape, 1)
    first = jnp.where(lane < k, tall, 0.0).astype(BF16)
    second = jnp.where(lane < k, 0.0, tall).astype(BF16)
    weights = []
    for c in range(width // BLK):
        weights += [first[c * BLK : c * BLK + BLK], second[c * BLK : c * BLK + BLK]]
    return jnp.dot(dense, jnp.concatenate(weights, axis=0), preferred_element_type=F32)


def to_wide(total, k, halves, tall):
    halves[:, : 2 * k] = total[:TALL] + total[TALL:]
    halves[:, 2 * k :] = jnp.zeros((TALL, 128 - 2 * k), F32)
    for b in range(BROWS):
        part = halves[pl.ds(b, BLK // 2, stride=BROWS), :]
        tall[pl.ds(BLK * b, BLK // 2, stride=2), :] = part
        tall[pl.ds(BLK * b + 1, BLK // 2, stride=2), :] = pltpu.roll(part, 128 - k, 1)
    return tall[...].T[:k]


def against(left, tall):
    k = left.shape[0]
    lane = lax.broadcasted_iota(jnp.int32, tall.shape, 1)
    a, b, c = split3(jnp.where(lane < k, tall, 0.0))
    right = a.astype(F32) + pltpu.roll(b.astype(F32), k, 1) + pltpu.roll(c.astype(F32), 2 * k, 1)
    pieces = jnp.dot(jnp.concatenate(split3(left), axis=0), right.astype(BF16), preferred_element_type=F32)
    top, middle, bottom = pieces[:k], pieces[k : 2 * k], pieces[2 * k :]
    total = top[:, :k] + (top[:, k : 2 * k] + middle[:, :k])
    return total + (middle[:, k : 2 * k] + (top[:, 2 * k : 3 * k] + bottom[:, :k]))


def apply_kernel(mode, *refs):
    basis_ref, refs = refs[0], refs[1:]
    if mode == "score":
        left_ref, refs = refs[0], refs[1:]
    dense_ref, out_ref = refs[:2]
    halves, tall, acc = refs[-3:]
    layer, chunk = pl.program_id(0), pl.program_id(1)
    total = image_part(basis_ref[chunk, layer], dense_ref[0, 0])

    @pl.when(chunk == 0)
    def _():
        acc[...] = total

    @pl.when(chunk > 0)
    def _():
        acc[...] += total

    @pl.when(chunk == pl.num_programs(1) - 1)
    def _():
        image = to_wide(acc[...], basis_ref.shape[2], halves, tall)
        if mode != "score":
            out_ref[0] = image
        if mode == "gram":
            refs[2][0] = against(image, tall[...])
        if mode == "score":
            out_ref[0] = against(left_ref[0], tall[...])


def split_dot(left, right, dims=(((1,), (0,)), ((), ()))):
    m = left.shape[0]
    a, b, c = split3(left)
    p, q, r = split3(right)

    def dot(rows, piece):
        return lax.dot_general(jnp.concatenate(rows, axis=0), piece, dims, preferred_element_type=F32)

    x, y, z = dot([a, b, c], p), dot([a, b], q), dot([a], r)
    return x[:m] + ((x[m : 2 * m] + y[:m]) + (y[m : 2 * m] + (x[2 * m :] + z)))


def product(a, b):
    k = a.shape[0]
    left = jnp.concatenate(split3(a), axis=0)
    right = left if b is a else jnp.concatenate(split3(b), axis=0)
    pieces = lax.dot_general(left, right, TRANS_B, preferred_element_type=F32)
    top, middle, bottom = pieces[:k], pieces[k : 2 * k], pieces[2 * k :]
    total = top[:, :k] + (top[:, k : 2 * k] + middle[:, :k])
    return total + (middle[:, k : 2 * k] + (top[:, 2 * k : 3 * k] + bottom[:, :k]))


def first_kernel(layer, chunks, *refs):
    pieces, (dense_ref, out_ref, halves, tall) = refs[: len(chunks)], refs[len(chunks) :]
    total = sum(image_part(piece[layer], dense_ref[chunk]) for chunk, piece in zip(chunks, pieces))
    out_ref[...] = to_wide(total, out_ref.shape[0], halves, tall)


def second_kernel(piece_count, earlier_count, *refs):
    pieces, dense_ref, refs = refs[:piece_count], refs[piece_count], refs[piece_count + 1 :]
    earlier, (out_ref, halves, tall, scratch) = refs[:earlier_count], refs[earlier_count:]
    image = jnp.concatenate([piece[...] for piece in pieces], axis=1)
    inverse = inverse_factor(product(image, image), scratch)
    basis = jnp.dot(inverse, image, precision=HIGHEST, preferred_element_type=F32)
    parts = [basis[:, d * ROWS_DEV : d * ROWS_DEV + ROWS_DEV] for d in range(piece_count)]
    before = out_ref.shape[0] - 1
    for ref in earlier:
        out_ref[:before] = ref[...]
    out_ref[before] = to_wide(sum(image_part(part, dense_ref[chunk]) for chunk, part in zip(ORDER, parts)), out_ref.shape[1], halves, tall)


def turn(left, tall, halves):
    k, nodes = left.shape
    tall[...] = jnp.concatenate([left, jnp.zeros((128 - k, nodes), F32)], axis=0).T
    for b in range(BROWS):
        even = tall[pl.ds(BLK * b, BLK // 2, stride=2), :]
        odd = tall[pl.ds(BLK * b + 1, BLK // 2, stride=2), :]
        halves[pl.ds(b, BLK // 2, stride=BROWS), :] = even + pltpu.roll(odd, k, 1)
    return halves[...].T[: 2 * k]


def own_kernel(layers, basis_ref, left_ref, *refs):
    dense_refs, (out_ref, turned_ref, tall, halves) = refs[:layers], refs[layers:]
    for layer, dense_ref in enumerate(dense_refs):
        out_ref[layer] = image_part(basis_ref[layer], dense_ref[0])
    for layer in range(layers):
        turned_ref[layer] = turn(left_ref[layer], tall.at[layer], halves.at[layer])


def some_kernel(chunk, layers, basis_ref, *refs):
    dense_refs, (so_far_ref, out_ref) = refs[:layers], refs[layers:]
    for layer, dense_ref in enumerate(dense_refs):
        out_ref[layer] = so_far_ref[layer] + image_part(basis_ref[layer], dense_ref[chunk])


def score_kernel(layers, chunks, so_far_ref, *refs):
    pieces, turned_ref, refs = refs[: len(chunks)], refs[len(chunks)], refs[len(chunks) + 1 :]
    dense_refs, out_ref = refs[:layers], refs[layers]
    k = out_ref.shape[1]
    totals = [
        so_far_ref[layer]
        + sum(image_part(piece[layer], dense_refs[layer][chunk]) for chunk, piece in zip(chunks, pieces))
        for layer in range(layers)
    ]
    halves = [total[:TALL] + total[TALL:] for total in totals]
    for layer in range(layers):
        pairs = split_dot(turned_ref[layer], halves[layer])
        out_ref[layer] = pairs[:k, :k] + pairs[k : 2 * k, k : 2 * k]


def apply_whole(kernel, name, operands, out_shape, *lead, scratch=()):
    return pl.pallas_call(
        kernel,
        in_specs=vmem_specs(len(operands)),
        out_specs=pl.BlockSpec(memory_space=pltpu.VMEM),
        out_shape=jax.ShapeDtypeStruct(out_shape, F32),
        scratch_shapes=[pltpu.VMEM((*lead, TALL, 128), F32), pltpu.VMEM((*lead, ROWS_DEV, 128), F32), *scratch],
        compiler_params=params(14),
        cost_estimate=pl.CostEstimate(flops=0, bytes_accessed=4 * MIB, transcendentals=0),
        name=name,
    )(*operands)


def apply_first(layer, chunks, pieces, dense):
    kernel = functools.partial(first_kernel, layer, chunks)
    return apply_whole(kernel, "apply_first", [*pieces, dense], pieces[0].shape[1:])


def apply_second(pieces, dense, earlier):
    kernel = functools.partial(second_kernel, len(pieces), len(earlier))
    before = sum(array.shape[0] for array in earlier)
    shape = (before + 1, *pieces[0].shape)
    operands = [*pieces, dense, *earlier]
    return apply_whole(kernel, "apply_second", operands, shape, scratch=[pltpu.VMEM(SPREAD, F32)])


def part_cost():
    return pl.CostEstimate(flops=0, bytes_accessed=2 * MIB, transcendentals=0)


def apply_own(basis, left, dense):
    layers, k, _ = basis.shape
    return pl.pallas_call(
        functools.partial(own_kernel, layers),
        in_specs=vmem_specs(2 + layers),
        out_specs=vmem_specs(2),
        out_shape=[
            jax.ShapeDtypeStruct((layers, 2 * TALL, 2 * k), F32),
            jax.ShapeDtypeStruct((layers, 2 * k, TALL), F32),
        ],
        scratch_shapes=[pltpu.VMEM((layers, ROWS_DEV, 128), F32), pltpu.VMEM((layers, TALL, 128), F32)],
        compiler_params=params(14),
        cost_estimate=part_cost(),
        name="apply_own",
    )(basis, left, *dense)


def apply_some(chunk, basis, dense, so_far):
    return pl.pallas_call(
        functools.partial(some_kernel, chunk, len(dense)),
        in_specs=vmem_specs(2 + len(dense)),
        out_specs=pl.BlockSpec(memory_space=pltpu.VMEM),
        out_shape=jax.ShapeDtypeStruct(so_far.shape, F32),
        compiler_params=params(14),
        cost_estimate=part_cost(),
        name=f"apply_some_{chunk}",
    )(basis, *dense, so_far)


def apply_score(pieces, left, dense):
    layers, k, _ = left.shape
    so_far, turned = apply_own(pieces[0], left, dense)
    so_far = apply_some(ORDER[1], pieces[1], dense, so_far)
    operands = [so_far, *pieces[2:], turned, *dense]
    return pl.pallas_call(
        functools.partial(score_kernel, len(dense), ORDER[2:]),
        in_specs=vmem_specs(len(operands)),
        out_specs=pl.BlockSpec(memory_space=pltpu.VMEM),
        out_shape=jax.ShapeDtypeStruct((layers, k, k), F32),
        compiler_params=params(14),
        cost_estimate=part_cost(),
        name="apply_score",
    )(*operands)


def apply_dense(mode, basis, dense, left=None):
    layers, chunks = dense.shape[:2]
    k = basis.shape[-2]
    image = jax.ShapeDtypeStruct((layers, k, ROWS_DEV), F32)
    small = jax.ShapeDtypeStruct((layers, k, k), F32)
    out_shape = {"gram": [image, small], "plain": [image], "score": [small]}[mode]
    operands = [basis] + ([left] if mode == "score" else []) + [dense]
    dense_spec = pl.BlockSpec((1, 1, 2 * TALL, CHUNK_LANES), lambda l, s: (l, s, 0, 0))
    image_spec = pl.BlockSpec((1, k, ROWS_DEV), lambda l, s: (l, 0, 0))
    small_spec = pl.BlockSpec((1, k, k), lambda l, s: (l, 0, 0))
    return pl.pallas_call(
        functools.partial(apply_kernel, mode),
        grid=(layers, chunks),
        in_specs=vmem_specs(1) + ([image_spec] if mode == "score" else []) + [dense_spec],
        out_specs={"gram": [image_spec, small_spec], "plain": [image_spec], "score": [small_spec]}[mode],
        out_shape=out_shape,
        scratch_shapes=[
            pltpu.VMEM((TALL, 128), F32),
            pltpu.VMEM((ROWS_DEV, 128), F32),
            pltpu.VMEM((2 * TALL, 2 * k), F32),
        ],
        compiler_params=params(12),
        name="apply_" + mode,
    )(*operands)


def spread(x):
    return jnp.broadcast_to(x, (8, 128))


def eliminate(rows, offset, scratch):
    groups, tiles = len(rows), len(rows[0])
    rows = [list(row) for row in rows]
    home, at = offset // 128, offset % 128
    sub = lax.broadcasted_iota(jnp.int32, (8, 128), 0)
    solved = []
    for h in range(groups):
        below = range(h + 1, groups)
        lane = at + 8 * h
        col = [{g: spread(rows[g][home][:, lane + q : lane + q + 1]) for g in range(h, groups)} for q in range(8)]
        held = scratch.at[h % 2]
        for q in range(8):
            held[q * 8 : q * 8 + 8] = col[q][h]
        for t in range(tiles):
            held[64 + t * 8 : 72 + t * 8] = rows[h][t]
        cell = {(p, q): spread(held[p * 8 + q : p * 8 + q + 1]) for q in range(8) for p in range(q + 1)}
        row = [[spread(held[64 + t * 8 + q : 65 + t * 8 + q]) for t in range(tiles)] for q in range(8)]
        done = []
        for m in range(0, 8, 2):
            n = m + 1
            a, b, c = cell[m, m], cell[m, n], cell[n, n]
            det = a * c - b * b
            if m % 4 == 0:
                r = pl.reciprocal(det, approx=True)
            else:
                r = square * pl.reciprocal(whole, approx=True)
            later = range(m + 2, 8)
            u = {q: c * cell[m, q] - b * cell[n, q] for q in later}
            v = {q: a * cell[n, q] - b * cell[m, q] for q in later}
            taken = {(p, q): cell[m, p] * u[q] + cell[n, p] * v[q] for q in later for p in range(m + 2, q + 1)}
            if m % 4 == 0:
                i, j = m + 2, m + 3
                first, cross, last = (det * cell[pq] - taken[pq] for pq in ((i, i), (i, j), (j, j)))
                whole = first * last - cross * cross
                square = det * det
            for pq in taken:
                cell[pq] = cell[pq] - r * taken[pq]
            for q in later:
                for g in below:
                    col[q][g] = col[q][g] - r * (col[m][g] * u[q] + col[n][g] * v[q])
            for t in range(tiles):
                x = r * (c * row[m][t] - b * row[n][t])
                y = r * (a * row[n][t] - b * row[m][t])
                for q in later:
                    row[q][t] = row[q][t] - (cell[m, q] * x + cell[n, q] * y)
                for g in below:
                    rows[g][t] = rows[g][t] - (col[m][g] * x + col[n][g] * y)
            over = pl.reciprocal(a, approx=True)
            done.append([lax.rsqrt(a) * x for x in row[m]])
            scale = lax.rsqrt(det * over)
            done.append([scale * (x - (b * over) * w) for x, w in zip(row[n], row[m])])
        finished = []
        for t in range(tiles):
            x = done[7][t]
            for q in range(7):
                x = jnp.where(sub == q, done[q][t], x)
            finished.append(x)
        solved.append(finished)
    return solved


def tiled(x):
    return [
        [x[g * 8 : g * 8 + 8, t * 128 : t * 128 + 128] for t in range(x.shape[1] // 128)]
        for g in range(x.shape[0] // 8)
    ]


def joined(tiles):
    return jnp.concatenate([jnp.concatenate(row, axis=1) for row in tiles], axis=0)


def unit_scale(gram):
    lane = lax.broadcasted_iota(jnp.int32, gram.shape, 1)
    sub = lax.broadcasted_iota(jnp.int32, gram.shape, 0)
    kept = jnp.where(lane == sub, gram, 0.0)
    down = 1.0 / jnp.sqrt(jnp.sum(kept, axis=1, keepdims=True))
    across = jnp.sum(kept, axis=0, keepdims=True)
    across = 1.0 / jnp.sqrt(jnp.where(across == 0.0, 1.0, across))
    return gram * down * across, across


def gram_update(panel, first):
    a, b, c = split3(panel)
    left = jnp.concatenate([a, a, b, b, a, c], axis=0)
    right = jnp.concatenate([a, b, a, b, c, a], axis=0)
    parts = {
        at: lax.dot_general(left[:, at : at + 128], right, TRANS_A, preferred_element_type=F32)
        for at in range(first, panel.shape[1], 128)
    }
    return lambda at, count: parts[at // 128 * 128][at % 128 : at % 128 + count]


def inverse_factor(gram, scratch):
    k = gram.shape[0]
    lane = lax.broadcasted_iota(jnp.int32, (k, 128), 1)
    sub = lax.broadcasted_iota(jnp.int32, (k, 128), 0)
    eye = jnp.where(lane == sub, 1.0, 0.0)
    gram, across = unit_scale(jnp.concatenate([gram, jnp.zeros((k, 128 - k), F32)], axis=1))
    solved = eliminate(tiled(jnp.concatenate([gram, eye], axis=1)), 0, scratch)
    return (joined(solved)[:, 128:] * across)[:, :k]


def solve_kernel(gram_ref, image_ref, out_ref, scratch):
    for layer in range(image_ref.shape[0]):
        inverse = inverse_factor(gram_ref[layer], scratch.at[layer])
        solved = jnp.dot(inverse, image_ref[layer], precision=HIGHEST, preferred_element_type=F32)
        out_ref[layer] = solved.astype(BF16)


def solve(gram, image):
    return pl.pallas_call(
        solve_kernel,
        in_specs=vmem_specs(2),
        out_specs=pl.BlockSpec(memory_space=pltpu.VMEM),
        out_shape=jax.ShapeDtypeStruct(image.shape, BF16),
        scratch_shapes=[pltpu.VMEM((image.shape[0], *SPREAD), F32)],
        compiler_params=params(4),
        name="solve_layers",
    )(gram, image)


def cross_kernel(images_ref, out_ref, packed):
    g = lax.axis_index("layer")
    every = images_ref[...].reshape(-1, images_ref.shape[2])
    gram = split_dot(every, every, TRANS_B)
    half = gram.shape[0] // 2
    first, last = gram[:half, :half], gram[half:, half:]
    row = lax.broadcasted_iota(jnp.int32, (half, half), 0)
    col = lax.broadcasted_iota(jnp.int32, (half, half), 1)
    packed[:half] = gram[:half, half:]
    packed[half : 2 * half] = jnp.where(col >= row, first, last)
    diagonal = jnp.sum(jnp.where(col == row, last, 0.0), axis=0, keepdims=True)
    packed[2 * half :] = jnp.broadcast_to(diagonal, (TAIL, half))
    rows = out_ref.shape[0]
    out_ref[...] = packed[pl.ds(pl.multiple_of((g & 1) * rows, 8), rows)]


def cross(images):
    layers, k, _ = images.shape
    size = layers * k
    return pl.pallas_call(
        cross_kernel,
        in_specs=vmem_specs(1),
        out_specs=pl.BlockSpec(memory_space=pltpu.VMEM),
        out_shape=jax.ShapeDtypeStruct(((size + TAIL) // 2, size // 2), F32),
        scratch_shapes=[pltpu.VMEM((size + TAIL, size // 2), F32)],
        compiler_params=params(6),
        name="cross_gram",
    )(images)


def unpack(packed, work):
    half = packed.shape[1]
    row = lax.broadcasted_iota(jnp.int32, (half, half), 0)
    col = lax.broadcasted_iota(jnp.int32, (half, half), 1)
    mixed = packed[half : 2 * half]
    over, under = jnp.where(col > row, mixed, 0.0), jnp.where(col < row, mixed, 0.0)
    work[:half, :half] = jnp.where(col >= row, mixed, over.T)
    work[:half, half:] = packed[:half]
    work[half:, :half] = jnp.zeros((half, half), F32)
    work[half:, half:] = under + under.T + jnp.where(col == row, packed[2 * half : 2 * half + 1], 0.0)


def joint_kernel(k, *refs):
    own_ref, other_ref, images_ref, out_ref, again_ref, rounded_ref, work, packed, scratch = refs
    rows = own_ref.shape[0]
    odd = lax.axis_index("layer") & 1
    packed[pl.ds(pl.multiple_of(odd * rows, 8), rows)] = own_ref[...]
    packed[pl.ds(pl.multiple_of((1 - odd) * rows, 8), rows)] = other_ref[...]
    unpack(packed[...], work)
    size = work.shape[0]
    steps = size // k
    lane = lax.broadcasted_iota(jnp.int32, (k, size), 1)
    lane_128 = lax.broadcasted_iota(jnp.int32, (k, 128), 1)
    sub_128 = lax.broadcasted_iota(jnp.int32, (k, 128), 0)
    gram, across = unit_scale(work[...])
    work[...] = gram
    for s in range(steps):
        lo, hi = s * k, (s + 1) * k
        here = (lane >= lo) & (lane < hi)
        eye = jnp.where(lane_128 == sub_128 + lo % 128, 1.0, 0.0)
        solved = joined(eliminate(tiled(jnp.concatenate([work[lo:hi], eye], axis=1)), lo, scratch.at[s % 2]))
        panel, tail = solved[:, :size], solved[:, size:]
        panel = jnp.where(here, jnp.concatenate([tail] * (size // 128), axis=1), panel)
        work[lo:hi] = jnp.where(lane < hi, panel, 0.0)
        if s + 1 < steps:
            update = gram_update(panel, hi // 128 * 128)
            for r in range(s + 1, steps):
                rows = work[r * k : r * k + k]
                work[r * k : r * k + k] = jnp.where(here, 0.0, rows) - update(r * k, k)
    rows = out_ref.shape[0] * k
    own = work[pl.ds(pl.multiple_of(lax.axis_index("layer") * rows, rows), rows)] * across
    joint = split_dot(own, images_ref[...].reshape(size, -1))
    joint = joint.reshape(out_ref.shape)
    out_ref[...] = joint
    again_ref[...] = joint
    rounded_ref[...] = joint.astype(BF16)


def joint_solve(own, other, images, shape):
    k = shape[1]
    size = images.shape[0] * k
    return pl.pallas_call(
        functools.partial(joint_kernel, k),
        in_specs=vmem_specs(3),
        out_specs=vmem_specs(3),
        out_shape=[
            jax.ShapeDtypeStruct(shape, F32),
            jax.ShapeDtypeStruct(shape, F32),
            jax.ShapeDtypeStruct(shape, BF16),
        ],
        scratch_shapes=[
            pltpu.VMEM((size, size), F32),
            pltpu.VMEM((size + TAIL, size // 2), F32),
            pltpu.VMEM((2, *SPREAD), F32),
        ],
        compiler_params=params(8),
        name="joint_solve",
    )(own, other, images)


def swap(x, axis, d, count):
    return lax.ppermute(x, axis, [(m ^ d, m) for m in range(count)])


ORDER = (0, 3, 2, 1)


def around(x, axis, count):
    return [x] + [swap(x, axis, d, count) for d in ORDER[1:]]


def add_pieces(pieces):
    own, near, far, across = (pieces[ORDER.index(d)] for d in range(4))
    return (own + near) + (across + far)


def per_device(shards, groups, blocks, block_rows, block_cols, counts, start):
    few = shards == 4
    layers = start.shape[0]

    def gather(x):
        return around(x, "node", shards) if few else lax.all_gather(x, "node")

    def total(x):
        return add_pieces(around(x, "node", shards)) if few else lax.psum(x, "node")

    rounded = start.astype(BF16)
    chunk_total = shards * BROWS // CHUNK_COLS
    if few:
        chunks = (0, 1, 3, 2)
        first = [rounded] + [swap(rounded, "node", d, shards) for d in chunks[1:]]
        dense = build_whole(block_rows, block_cols, counts, blocks, chunk_total)
        images = [apply_first(layer, chunks, first, dense[layer]) for layer in range(layers)]
        image = None
        for layer in range(layers):
            image = apply_second(gather(images[layer]), dense[layer], [] if image is None else [image])
    else:
        dense = build_dense(block_rows, block_cols, counts, blocks, chunk_total)
        image, gram = apply_dense("gram", gather(rounded), dense)
        (image,) = apply_dense("plain", gather(solve(total(gram), image)), dense)
    images = lax.all_gather(image, "layer", axis=0, tiled=True)
    own = cross(images)
    own = total(own)
    other = swap(own, "layer", 1, groups)
    joint_basis, again, rounded = joint_solve(own, other, images, start.shape)
    if few:
        partial = apply_score(gather(rounded), again, dense)
    else:
        (partial,) = apply_dense("score", gather(rounded), dense, again)
    return joint_basis, total(partial)


def solution(mesh):
    in_specs = (
        P(("parts", "layer"), "node", None),
        P(("parts", "layer"), "node"),
        P(("parts", "layer"), "node"),
        P(("parts", "layer"), "node"),
        P(("parts", "layer"), None, "node"),
    )
    out_specs = (P(("parts", "layer"), None, "node"), P(("parts", "layer"), None, None))
    return jax.shard_map(
        functools.partial(per_device, mesh.shape["node"], mesh.shape["layer"]),
        mesh=mesh,
        in_specs=in_specs,
        out_specs=out_specs,
        check_vma=False,
    )
```

```python
import functools

import jax
import jax.numpy as jnp
from jax import lax
from jax.experimental import pallas as pl
from jax.experimental.pallas import tpu as pltpu
from jax.sharding import PartitionSpec as P

BLK = 64
ROWS_DEV = 512
BROWS = ROWS_DEV // BLK
CHUNK_COLS = 8
CHUNK_LANES = CHUNK_COLS * 2 * BLK
TALL = BROWS * BLK // 2
MIB = 1024 * 1024
F32 = jnp.float32
BF16 = jnp.bfloat16
HIGHEST = lax.Precision.HIGHEST
TRANS_B = (((1,), (1,)), ((), ()))
TRANS_A = (((0,), (0,)), ((), ()))
SPREAD = (2, 88, 128)
TAIL = 16


def params(mib):
    return pltpu.CompilerParams(vmem_limit_bytes=mib * MIB)


def vmem_specs(count):
    return [pl.BlockSpec(memory_space=pltpu.VMEM)] * count


def place(z, chunks, u, dense_ref):
    for c in range(chunks * CHUNK_COLS):
        piece = z[c * 8 : c * 8 + 8]
        piece = jnp.concatenate([piece[:, :128], piece[:, 128:]], axis=0)
        hi = piece.astype(BF16)
        lo = (piece - hi.astype(F32)).astype(BF16)
        lanes = slice((c % CHUNK_COLS) * 128, (c % CHUNK_COLS) * 128 + 128)
        dense_ref[c // CHUNK_COLS, pl.ds(pl.multiple_of(u * 16, 16), 16), lanes] = hi
        dense_ref[c // CHUNK_COLS, pl.ds(pl.multiple_of(u * 16 + TALL, 16), 16), lanes] = lo


def one_hot(rows_ref, cols_ref, counts_ref, layer, flip, base, positions):
    slot = lax.broadcasted_iota(jnp.int32, (1, rows_ref.shape[1]), 1)
    key = (cols_ref[pl.ds(layer, 1), :] ^ flip) * BROWS + rows_ref[pl.ds(layer, 1), :]
    key = jnp.where(slot < counts_ref[0, layer], key, -1)
    position = lax.broadcasted_iota(jnp.int32, (positions, key.shape[1]), 0) + base
    return jnp.where(position == key, 1.0, 0.0).astype(BF16)


def build_kernel(rows_ref, cols_ref, counts_ref, blocks_ref, dense_ref):
    chunks = dense_ref.shape[1]
    positions = chunks * CHUNK_COLS * BROWS
    base = pl.program_id(1) * positions
    onehot = one_hot(rows_ref, cols_ref, counts_ref, pl.program_id(0), 0, base, positions)

    def step(u, carry):
        cols = pl.ds(pl.multiple_of(u * 256, 256), 256)
        z = jnp.dot(onehot, blocks_ref[0, :, cols], preferred_element_type=F32)
        place(z, chunks, u, dense_ref.at[0])
        return carry

    lax.fori_loop(0, BLK * BLK // 256, step, 0)


def fill(onehot, held, dense_ref, piece, width):
    for v in range(width // 256):
        cols = pl.ds(pl.multiple_of(piece * width + v * 256, 256), 256)
        z = jnp.dot(onehot, held[:, cols], preferred_element_type=F32)
        place(z, dense_ref.shape[0], piece * (width // 256) + v, dense_ref)


def build_whole_kernel(rows_hbm, cols_hbm, counts_hbm, blocks_ref, *refs):
    *dense_refs, held, rows_ref, cols_ref, counts_ref, arrived, index_arrived = refs
    layers, pieces = arrived.shape
    width = held.shape[2] // pieces
    ahead = 3

    def fetch(layer, piece):
        cols = pl.ds(pl.multiple_of(piece * width, width), width)
        return pltpu.make_async_copy(
            blocks_ref.at[layer, :, cols], held.at[layer, :, cols], arrived.at[layer, piece]
        )

    index_copies = [
        pltpu.make_async_copy(source, target, index_arrived.at[i])
        for i, (source, target) in enumerate(
            [(rows_hbm, rows_ref), (cols_hbm, cols_ref), (counts_hbm, counts_ref)]
        )
    ]
    for copy in index_copies:
        copy.start()
    for piece in range(ahead):
        fetch(0, piece).start()
    for copy in index_copies:
        copy.wait()
    flip = lax.axis_index("node") * CHUNK_COLS
    positions = dense_refs[0].shape[0] * CHUNK_COLS * BROWS
    onehots = [one_hot(rows_ref, cols_ref, counts_ref, layer, flip, 0, positions) for layer in range(layers)]
    for layer, (dense_ref, onehot) in enumerate(zip(dense_refs, onehots)):

        def step(piece, carry):
            fetch(layer, piece).wait()

            @pl.when(piece + ahead < pieces)
            def _():
                fetch(layer, piece + ahead).start()

            if layer + 1 < layers:

                @pl.when(piece + ahead >= pieces)
                def _():
                    fetch(layer + 1, piece + ahead - pieces).start()

            fill(onehot, held.at[layer], dense_ref, piece, width)
            return carry

        lax.fori_loop(0, pieces, step, 0)


def build_whole(block_rows, block_cols, counts, blocks, chunk_total):
    layers = blocks.shape[0]
    dense = jax.ShapeDtypeStruct((chunk_total, 2 * TALL, CHUNK_LANES), BF16)
    operands = (block_rows, block_cols, counts.T, blocks)
    return pl.pallas_call(
        build_whole_kernel,
        in_specs=[pl.BlockSpec(memory_space=pltpu.HBM)] * 4,
        out_specs=vmem_specs(layers),
        out_shape=[dense] * layers,
        scratch_shapes=[
            pltpu.VMEM(blocks.shape, BF16),
            pltpu.VMEM(block_rows.shape, jnp.int32),
            pltpu.VMEM(block_cols.shape, jnp.int32),
            pltpu.SMEM((1, layers), jnp.int32),
            pltpu.SemaphoreType.DMA((layers, 4)),
            pltpu.SemaphoreType.DMA((3,)),
        ],
        compiler_params=params(28),
        cost_estimate=pl.CostEstimate(flops=0, bytes_accessed=20 * MIB, transcendentals=0),
        name="build_whole",
    )(*[pltpu.with_memory_space_constraint(x, pltpu.HBM) for x in operands])


def build_dense(block_rows, block_cols, counts, blocks, chunk_total):
    layers, slots, width = blocks.shape
    dense = jax.ShapeDtypeStruct((layers, chunk_total, 2 * TALL, CHUNK_LANES), BF16)
    operands = (block_rows, block_cols, counts.T, blocks)
    return pl.pallas_call(
        build_kernel,
        grid=(layers, chunk_total // 4),
        in_specs=vmem_specs(2)
        + [
            pl.BlockSpec(memory_space=pltpu.SMEM),
            pl.BlockSpec((1, slots, width), lambda l, s: (l, 0, 0)),
        ],
        out_specs=pl.BlockSpec((1, 4, 2 * TALL, CHUNK_LANES), lambda l, s: (l, s, 0, 0)),
        out_shape=dense,
        compiler_params=params(24),
        name="build_dense",
    )(*operands)


def split3(x):
    a = x.astype(BF16)
    r = x - a.astype(F32)
    b = r.astype(BF16)
    c = (r - b.astype(F32)).astype(BF16)
    return a, b, c


def image_part(basis, dense):
    k, width = basis.shape
    basis = basis.astype(F32)
    tall = jnp.concatenate([basis, basis], axis=0).T
    lane = lax.broadcasted_iota(jnp.int32, tall.shape, 1)
    first = jnp.where(lane < k, tall, 0.0).astype(BF16)
    second = jnp.where(lane < k, 0.0, tall).astype(BF16)
    weights = []
    for c in range(width // BLK):
        weights += [first[c * BLK : c * BLK + BLK], second[c * BLK : c * BLK + BLK]]
    return jnp.dot(dense, jnp.concatenate(weights, axis=0), preferred_element_type=F32)


def to_wide(total, k, halves, tall):
    halves[:, : 2 * k] = total[:TALL] + total[TALL:]
    halves[:, 2 * k :] = jnp.zeros((TALL, 128 - 2 * k), F32)
    for b in range(BROWS):
        part = halves[pl.ds(b, BLK // 2, stride=BROWS), :]
        tall[pl.ds(BLK * b, BLK // 2, stride=2), :] = part
        tall[pl.ds(BLK * b + 1, BLK // 2, stride=2), :] = pltpu.roll(part, 128 - k, 1)
    return tall[...].T[:k]


def against(left, tall):
    k = left.shape[0]
    lane = lax.broadcasted_iota(jnp.int32, tall.shape, 1)
    a, b, c = split3(jnp.where(lane < k, tall, 0.0))
    right = a.astype(F32) + pltpu.roll(b.astype(F32), k, 1) + pltpu.roll(c.astype(F32), 2 * k, 1)
    pieces = jnp.dot(jnp.concatenate(split3(left), axis=0), right.astype(BF16), preferred_element_type=F32)
    top, middle, bottom = pieces[:k], pieces[k : 2 * k], pieces[2 * k :]
    total = top[:, :k] + (top[:, k : 2 * k] + middle[:, :k])
    return total + (middle[:, k : 2 * k] + (top[:, 2 * k : 3 * k] + bottom[:, :k]))


def apply_kernel(mode, *refs):
    basis_ref, refs = refs[0], refs[1:]
    if mode == "score":
        left_ref, refs = refs[0], refs[1:]
    dense_ref, out_ref = refs[:2]
    halves, tall, acc = refs[-3:]
    layer, chunk = pl.program_id(0), pl.program_id(1)
    total = image_part(basis_ref[chunk, layer], dense_ref[0, 0])

    @pl.when(chunk == 0)
    def _():
        acc[...] = total

    @pl.when(chunk > 0)
    def _():
        acc[...] += total

    @pl.when(chunk == pl.num_programs(1) - 1)
    def _():
        image = to_wide(acc[...], basis_ref.shape[2], halves, tall)
        if mode != "score":
            out_ref[0] = image
        if mode == "gram":
            refs[2][0] = against(image, tall[...])
        if mode == "score":
            out_ref[0] = against(left_ref[0], tall[...])


def split_dot(left, right, dims=(((1,), (0,)), ((), ()))):
    m = left.shape[0]
    a, b, c = split3(left)
    p, q, r = split3(right)

    def dot(rows, piece):
        return lax.dot_general(jnp.concatenate(rows, axis=0), piece, dims, preferred_element_type=F32)

    x, y, z = dot([a, b, c], p), dot([a, b], q), dot([a], r)
    return x[:m] + ((x[m : 2 * m] + y[:m]) + (y[m : 2 * m] + (x[2 * m :] + z)))


def product(a, b):
    k = a.shape[0]
    left = jnp.concatenate(split3(a), axis=0)
    right = left if b is a else jnp.concatenate(split3(b), axis=0)
    pieces = lax.dot_general(left, right, TRANS_B, preferred_element_type=F32)
    top, middle, bottom = pieces[:k], pieces[k : 2 * k], pieces[2 * k :]
    total = top[:, :k] + (top[:, k : 2 * k] + middle[:, :k])
    return total + (middle[:, k : 2 * k] + (top[:, 2 * k : 3 * k] + bottom[:, :k]))


def first_kernel(layer, chunks, *refs):
    pieces, (dense_ref, out_ref, halves, tall) = refs[: len(chunks)], refs[len(chunks) :]
    total = sum(image_part(piece[layer], dense_ref[chunk]) for chunk, piece in zip(chunks, pieces))
    out_ref[...] = to_wide(total, out_ref.shape[0], halves, tall)


def second_kernel(piece_count, earlier_count, *refs):
    pieces, dense_ref, refs = refs[:piece_count], refs[piece_count], refs[piece_count + 1 :]
    earlier, (out_ref, halves, tall, scratch) = refs[:earlier_count], refs[earlier_count:]
    image = jnp.concatenate([piece[...] for piece in pieces], axis=1)
    inverse = inverse_factor(product(image, image), scratch)
    basis = jnp.dot(inverse, image, precision=HIGHEST, preferred_element_type=F32)
    parts = [basis[:, d * ROWS_DEV : d * ROWS_DEV + ROWS_DEV] for d in range(piece_count)]
    before = out_ref.shape[0] - 1
    for ref in earlier:
        out_ref[:before] = ref[...]
    out_ref[before] = to_wide(sum(image_part(part, dense_ref[chunk]) for chunk, part in zip(ORDER, parts)), out_ref.shape[1], halves, tall)


def turn(left, tall, halves):
    k, nodes = left.shape
    tall[...] = jnp.concatenate([left, jnp.zeros((128 - k, nodes), F32)], axis=0).T
    for b in range(BROWS):
        even = tall[pl.ds(BLK * b, BLK // 2, stride=2), :]
        odd = tall[pl.ds(BLK * b + 1, BLK // 2, stride=2), :]
        halves[pl.ds(b, BLK // 2, stride=BROWS), :] = even + pltpu.roll(odd, k, 1)
    return halves[...].T[: 2 * k]


def own_kernel(layers, basis_ref, left_ref, *refs):
    dense_refs, (out_ref, turned_ref, tall, halves) = refs[:layers], refs[layers:]
    for layer, dense_ref in enumerate(dense_refs):
        out_ref[layer] = image_part(basis_ref[layer], dense_ref[0])
    for layer in range(layers):
        turned_ref[layer] = turn(left_ref[layer], tall.at[layer], halves.at[layer])


def some_kernel(chunk, layers, basis_ref, *refs):
    dense_refs, (so_far_ref, out_ref) = refs[:layers], refs[layers:]
    for layer, dense_ref in enumerate(dense_refs):
        out_ref[layer] = so_far_ref[layer] + image_part(basis_ref[layer], dense_ref[chunk])


def score_kernel(layers, chunks, so_far_ref, *refs):
    pieces, turned_ref, refs = refs[: len(chunks)], refs[len(chunks)], refs[len(chunks) + 1 :]
    dense_refs, out_ref = refs[:layers], refs[layers]
    k = out_ref.shape[1]
    totals = [
        so_far_ref[layer]
        + sum(image_part(piece[layer], dense_refs[layer][chunk]) for chunk, piece in zip(chunks, pieces))
        for layer in range(layers)
    ]
    halves = [total[:TALL] + total[TALL:] for total in totals]
    for layer in range(layers):
        pairs = split_dot(turned_ref[layer], halves[layer])
        out_ref[layer] = pairs[:k, :k] + pairs[k : 2 * k, k : 2 * k]


def apply_whole(kernel, name, operands, out_shape, *lead, scratch=()):
    return pl.pallas_call(
        kernel,
        in_specs=vmem_specs(len(operands)),
        out_specs=pl.BlockSpec(memory_space=pltpu.VMEM),
        out_shape=jax.ShapeDtypeStruct(out_shape, F32),
        scratch_shapes=[pltpu.VMEM((*lead, TALL, 128), F32), pltpu.VMEM((*lead, ROWS_DEV, 128), F32), *scratch],
        compiler_params=params(14),
        cost_estimate=pl.CostEstimate(flops=0, bytes_accessed=4 * MIB, transcendentals=0),
        name=name,
    )(*operands)


def apply_first(layer, chunks, pieces, dense):
    kernel = functools.partial(first_kernel, layer, chunks)
    return apply_whole(kernel, "apply_first", [*pieces, dense], pieces[0].shape[1:])


def apply_second(pieces, dense, earlier):
    kernel = functools.partial(second_kernel, len(pieces), len(earlier))
    before = sum(array.shape[0] for array in earlier)
    shape = (before + 1, *pieces[0].shape)
    operands = [*pieces, dense, *earlier]
    return apply_whole(kernel, "apply_second", operands, shape, scratch=[pltpu.VMEM(SPREAD, F32)])


def part_cost():
    return pl.CostEstimate(flops=0, bytes_accessed=2 * MIB, transcendentals=0)


def apply_own(basis, left, dense):
    layers, k, _ = basis.shape
    return pl.pallas_call(
        functools.partial(own_kernel, layers),
        in_specs=vmem_specs(2 + layers),
        out_specs=vmem_specs(2),
        out_shape=[
            jax.ShapeDtypeStruct((layers, 2 * TALL, 2 * k), F32),
            jax.ShapeDtypeStruct((layers, 2 * k, TALL), F32),
        ],
        scratch_shapes=[pltpu.VMEM((layers, ROWS_DEV, 128), F32), pltpu.VMEM((layers, TALL, 128), F32)],
        compiler_params=params(14),
        cost_estimate=part_cost(),
        name="apply_own",
    )(basis, left, *dense)


def apply_some(chunk, basis, dense, so_far):
    return pl.pallas_call(
        functools.partial(some_kernel, chunk, len(dense)),
        in_specs=vmem_specs(2 + len(dense)),
        out_specs=pl.BlockSpec(memory_space=pltpu.VMEM),
        out_shape=jax.ShapeDtypeStruct(so_far.shape, F32),
        compiler_params=params(14),
        cost_estimate=part_cost(),
        name=f"apply_some_{chunk}",
    )(basis, *dense, so_far)


def apply_score(pieces, left, dense):
    layers, k, _ = left.shape
    so_far, turned = apply_own(pieces[0], left, dense)
    so_far = apply_some(ORDER[1], pieces[1], dense, so_far)
    operands = [so_far, *pieces[2:], turned, *dense]
    return pl.pallas_call(
        functools.partial(score_kernel, len(dense), ORDER[2:]),
        in_specs=vmem_specs(len(operands)),
        out_specs=pl.BlockSpec(memory_space=pltpu.VMEM),
        out_shape=jax.ShapeDtypeStruct((layers, k, k), F32),
        compiler_params=params(14),
        cost_estimate=part_cost(),
        name="apply_score",
    )(*operands)


def apply_dense(mode, basis, dense, left=None):
    layers, chunks = dense.shape[:2]
    k = basis.shape[-2]
    image = jax.ShapeDtypeStruct((layers, k, ROWS_DEV), F32)
    small = jax.ShapeDtypeStruct((layers, k, k), F32)
    out_shape = {"gram": [image, small], "plain": [image], "score": [small]}[mode]
    operands = [basis] + ([left] if mode == "score" else []) + [dense]
    dense_spec = pl.BlockSpec((1, 1, 2 * TALL, CHUNK_LANES), lambda l, s: (l, s, 0, 0))
    image_spec = pl.BlockSpec((1, k, ROWS_DEV), lambda l, s: (l, 0, 0))
    small_spec = pl.BlockSpec((1, k, k), lambda l, s: (l, 0, 0))
    return pl.pallas_call(
        functools.partial(apply_kernel, mode),
        grid=(layers, chunks),
        in_specs=vmem_specs(1) + ([image_spec] if mode == "score" else []) + [dense_spec],
        out_specs={"gram": [image_spec, small_spec], "plain": [image_spec], "score": [small_spec]}[mode],
        out_shape=out_shape,
        scratch_shapes=[
            pltpu.VMEM((TALL, 128), F32),
            pltpu.VMEM((ROWS_DEV, 128), F32),
            pltpu.VMEM((2 * TALL, 2 * k), F32),
        ],
        compiler_params=params(12),
        name="apply_" + mode,
    )(*operands)


def spread(x):
    return jnp.broadcast_to(x, (8, 128))


def eliminate(rows, offset, scratch):
    groups, tiles = len(rows), len(rows[0])
    rows = [list(row) for row in rows]
    home, at = offset // 128, offset % 128
    sub = lax.broadcasted_iota(jnp.int32, (8, 128), 0)
    solved = []
    for h in range(groups):
        below = range(h + 1, groups)
        lane = at + 8 * h
        col = [{g: spread(rows[g][home][:, lane + q : lane + q + 1]) for g in range(h, groups)} for q in range(8)]
        held = scratch.at[h % 2]
        for q in range(8):
            held[q * 8 : q * 8 + 8] = col[q][h]
        for t in range(tiles):
            held[64 + t * 8 : 72 + t * 8] = rows[h][t]
        cell = {(p, q): spread(held[p * 8 + q : p * 8 + q + 1]) for q in range(8) for p in range(q + 1)}
        row = [[spread(held[64 + t * 8 + q : 65 + t * 8 + q]) for t in range(tiles)] for q in range(8)]
        done = []
        for m in range(0, 8, 2):
            n = m + 1
            a, b, c = cell[m, m], cell[m, n], cell[n, n]
            det = a * c - b * b
            if m % 4 == 0:
                r = pl.reciprocal(det, approx=True)
            else:
                r = square * pl.reciprocal(whole, approx=True)
            later = range(m + 2, 8)
            u = {q: c * cell[m, q] - b * cell[n, q] for q in later}
            v = {q: a * cell[n, q] - b * cell[m, q] for q in later}
            taken = {(p, q): cell[m, p] * u[q] + cell[n, p] * v[q] for q in later for p in range(m + 2, q + 1)}
            if m % 4 == 0:
                i, j = m + 2, m + 3
                first, cross, last = (det * cell[pq] - taken[pq] for pq in ((i, i), (i, j), (j, j)))
                whole = first * last - cross * cross
                square = det * det
            for pq in taken:
                cell[pq] = cell[pq] - r * taken[pq]
            for q in later:
                for g in below:
                    col[q][g] = col[q][g] - r * (col[m][g] * u[q] + col[n][g] * v[q])
            for t in range(tiles):
                x = r * (c * row[m][t] - b * row[n][t])
                y = r * (a * row[n][t] - b * row[m][t])
                for q in later:
                    row[q][t] = row[q][t] - (cell[m, q] * x + cell[n, q] * y)
                for g in below:
                    rows[g][t] = rows[g][t] - (col[m][g] * x + col[n][g] * y)
            over = pl.reciprocal(a, approx=True)
            done.append([lax.rsqrt(a) * x for x in row[m]])
            scale = lax.rsqrt(det * over)
            done.append([scale * (x - (b * over) * w) for x, w in zip(row[n], row[m])])
        finished = []
        for t in range(tiles):
            x = done[7][t]
            for q in range(7):
                x = jnp.where(sub == q, done[q][t], x)
            finished.append(x)
        solved.append(finished)
    return solved


def tiled(x):
    return [
        [x[g * 8 : g * 8 + 8, t * 128 : t * 128 + 128] for t in range(x.shape[1] // 128)]
        for g in range(x.shape[0] // 8)
    ]


def joined(tiles):
    return jnp.concatenate([jnp.concatenate(row, axis=1) for row in tiles], axis=0)


def unit_scale(gram):
    lane = lax.broadcasted_iota(jnp.int32, gram.shape, 1)
    sub = lax.broadcasted_iota(jnp.int32, gram.shape, 0)
    kept = jnp.where(lane == sub, gram, 0.0)
    down = 1.0 / jnp.sqrt(jnp.sum(kept, axis=1, keepdims=True))
    across = jnp.sum(kept, axis=0, keepdims=True)
    across = 1.0 / jnp.sqrt(jnp.where(across == 0.0, 1.0, across))
    return gram * down * across, across


def gram_update(panel, first):
    a, b, c = split3(panel)
    left = jnp.concatenate([a, a, b, b, a, c], axis=0)
    right = jnp.concatenate([a, b, a, b, c, a], axis=0)
    parts = {
        at: lax.dot_general(left[:, at : at + 128], right, TRANS_A, preferred_element_type=F32)
        for at in range(first, panel.shape[1], 128)
    }
    return lambda at, count: parts[at // 128 * 128][at % 128 : at % 128 + count]


def inverse_factor(gram, scratch):
    k = gram.shape[0]
    lane = lax.broadcasted_iota(jnp.int32, (k, 128), 1)
    sub = lax.broadcasted_iota(jnp.int32, (k, 128), 0)
    eye = jnp.where(lane == sub, 1.0, 0.0)
    gram, across = unit_scale(jnp.concatenate([gram, jnp.zeros((k, 128 - k), F32)], axis=1))
    solved = eliminate(tiled(jnp.concatenate([gram, eye], axis=1)), 0, scratch)
    return (joined(solved)[:, 128:] * across)[:, :k]


def solve_kernel(gram_ref, image_ref, out_ref, scratch):
    for layer in range(image_ref.shape[0]):
        inverse = inverse_factor(gram_ref[layer], scratch.at[layer])
        solved = jnp.dot(inverse, image_ref[layer], precision=HIGHEST, preferred_element_type=F32)
        out_ref[layer] = solved.astype(BF16)


def solve(gram, image):
    return pl.pallas_call(
        solve_kernel,
        in_specs=vmem_specs(2),
        out_specs=pl.BlockSpec(memory_space=pltpu.VMEM),
        out_shape=jax.ShapeDtypeStruct(image.shape, BF16),
        scratch_shapes=[pltpu.VMEM((image.shape[0], *SPREAD), F32)],
        compiler_params=params(4),
        name="solve_layers",
    )(gram, image)


def cross_kernel(images_ref, out_ref, packed):
    g = lax.axis_index("layer")
    every = images_ref[...].reshape(-1, images_ref.shape[2])
    gram = split_dot(every, every, TRANS_B)
    half = gram.shape[0] // 2
    first, last = gram[:half, :half], gram[half:, half:]
    row = lax.broadcasted_iota(jnp.int32, (half, half), 0)
    col = lax.broadcasted_iota(jnp.int32, (half, half), 1)
    packed[:half] = gram[:half, half:]
    packed[half : 2 * half] = jnp.where(col >= row, first, last)
    diagonal = jnp.sum(jnp.where(col == row, last, 0.0), axis=0, keepdims=True)
    packed[2 * half :] = jnp.broadcast_to(diagonal, (TAIL, half))
    rows = out_ref.shape[0]
    out_ref[...] = packed[pl.ds(pl.multiple_of((g & 1) * rows, 8), rows)]


def cross(images):
    layers, k, _ = images.shape
    size = layers * k
    return pl.pallas_call(
        cross_kernel,
        in_specs=vmem_specs(1),
        out_specs=pl.BlockSpec(memory_space=pltpu.VMEM),
        out_shape=jax.ShapeDtypeStruct(((size + TAIL) // 2, size // 2), F32),
        scratch_shapes=[pltpu.VMEM((size + TAIL, size // 2), F32)],
        compiler_params=params(6),
        name="cross_gram",
    )(images)


def unpack(packed, work):
    half = packed.shape[1]
    row = lax.broadcasted_iota(jnp.int32, (half, half), 0)
    col = lax.broadcasted_iota(jnp.int32, (half, half), 1)
    mixed = packed[half : 2 * half]
    over, under = jnp.where(col > row, mixed, 0.0), jnp.where(col < row, mixed, 0.0)
    work[:half, :half] = jnp.where(col >= row, mixed, over.T)
    work[:half, half:] = packed[:half]
    work[half:, :half] = jnp.zeros((half, half), F32)
    work[half:, half:] = under + under.T + jnp.where(col == row, packed[2 * half : 2 * half + 1], 0.0)


def joint_kernel(k, *refs):
    own_ref, other_ref, images_ref, out_ref, again_ref, rounded_ref, work, packed, scratch = refs
    rows = own_ref.shape[0]
    odd = lax.axis_index("layer") & 1
    packed[pl.ds(pl.multiple_of(odd * rows, 8), rows)] = own_ref[...]
    packed[pl.ds(pl.multiple_of((1 - odd) * rows, 8), rows)] = other_ref[...]
    unpack(packed[...], work)
    size = work.shape[0]
    steps = size // k
    lane = lax.broadcasted_iota(jnp.int32, (k, size), 1)
    lane_128 = lax.broadcasted_iota(jnp.int32, (k, 128), 1)
    sub_128 = lax.broadcasted_iota(jnp.int32, (k, 128), 0)
    gram, across = unit_scale(work[...])
    work[...] = gram
    for s in range(steps):
        lo, hi = s * k, (s + 1) * k
        here = (lane >= lo) & (lane < hi)
        eye = jnp.where(lane_128 == sub_128 + lo % 128, 1.0, 0.0)
        solved = joined(eliminate(tiled(jnp.concatenate([work[lo:hi], eye], axis=1)), lo, scratch.at[s % 2]))
        panel, tail = solved[:, :size], solved[:, size:]
        panel = jnp.where(here, jnp.concatenate([tail] * (size // 128), axis=1), panel)
        work[lo:hi] = jnp.where(lane < hi, panel, 0.0)
        if s + 1 < steps:
            update = gram_update(panel, hi // 128 * 128)
            for r in range(s + 1, steps):
                rows = work[r * k : r * k + k]
                work[r * k : r * k + k] = jnp.where(here, 0.0, rows) - update(r * k, k)
    rows = out_ref.shape[0] * k
    own = work[pl.ds(pl.multiple_of(lax.axis_index("layer") * rows, rows), rows)] * across
    joint = split_dot(own, images_ref[...].reshape(size, -1))
    joint = joint.reshape(out_ref.shape)
    out_ref[...] = joint
    again_ref[...] = joint
    rounded_ref[...] = joint.astype(BF16)


def joint_solve(own, other, images, shape):
    k = shape[1]
    size = images.shape[0] * k
    return pl.pallas_call(
        functools.partial(joint_kernel, k),
        in_specs=vmem_specs(3),
        out_specs=vmem_specs(3),
        out_shape=[
            jax.ShapeDtypeStruct(shape, F32),
            jax.ShapeDtypeStruct(shape, F32),
            jax.ShapeDtypeStruct(shape, BF16),
        ],
        scratch_shapes=[
            pltpu.VMEM((size, size), F32),
            pltpu.VMEM((size + TAIL, size // 2), F32),
            pltpu.VMEM((2, *SPREAD), F32),
        ],
        compiler_params=params(8),
        name="joint_solve",
    )(own, other, images)


def swap(x, axis, d, count):
    return lax.ppermute(x, axis, [(m ^ d, m) for m in range(count)])


ORDER = (0, 3, 2, 1)


def around(x, axis, count):
    return [x] + [swap(x, axis, d, count) for d in ORDER[1:]]


def add_pieces(pieces):
    own, near, far, across = (pieces[ORDER.index(d)] for d in range(4))
    return (own + near) + (across + far)


def per_device(shards, groups, blocks, block_rows, block_cols, counts, start):
    few = shards == 4
    layers = start.shape[0]

    def gather(x):
        return around(x, "node", shards) if few else lax.all_gather(x, "node")

    def total(x):
        return add_pieces(around(x, "node", shards)) if few else lax.psum(x, "node")

    rounded = start.astype(BF16)
    chunk_total = shards * BROWS // CHUNK_COLS
    if few:
        chunks = (0, 1, 3, 2)
        first = [rounded] + [swap(rounded, "node", d, shards) for d in chunks[1:]]
        dense = build_whole(block_rows, block_cols, counts, blocks, chunk_total)
        images = [apply_first(layer, chunks, first, dense[layer]) for layer in range(layers)]
        image = None
        for layer in range(layers):
            image = apply_second(gather(images[layer]), dense[layer], [] if image is None else [image])
    else:
        dense = build_dense(block_rows, block_cols, counts, blocks, chunk_total)
        image, gram = apply_dense("gram", gather(rounded), dense)
        (image,) = apply_dense("plain", gather(solve(total(gram), image)), dense)
    images = lax.all_gather(image, "layer", axis=0, tiled=True)
    own = cross(images)
    own = total(own)
    other = swap(own, "layer", 1, groups)
    joint_basis, again, rounded = joint_solve(own, other, images, start.shape)
    if few:
        partial = apply_score(gather(rounded), again, dense)
    else:
        (partial,) = apply_dense("score", gather(rounded), dense, again)
    return joint_basis, total(partial)


def solution(mesh):
    in_specs = (
        P(("parts", "layer"), "node", None),
        P(("parts", "layer"), "node"),
        P(("parts", "layer"), "node"),
        P(("parts", "layer"), "node"),
        P(("parts", "layer"), None, "node"),
    )
    out_specs = (P(("parts", "layer"), None, "node"), P(("parts", "layer"), None, None))
    return jax.shard_map(
        functools.partial(per_device, mesh.shape["node"], mesh.shape["layer"]),
        mesh=mesh,
        in_specs=in_specs,
        out_specs=out_specs,
        check_vma=False,
    )
```
